128 devices in a mesh: blk: 16 (over z, y), sub: 8 (over x, core).
Axes of the slice: x: 4, y: 4, z: 4, core: 2. Of those that a mesh axis runs over, the one named last changes fastest.
Arguments:
- synthetic: bfloat16 [16384, 3, 1024], P(('blk', 'sub')), may hold values from -6 to 6
- observed: bfloat16 [16384, 3, 1024], P(('blk', 'sub')), may hold values from -6 to 6
- pair_first: int32 [256, 1024], P('blk', 'sub'), may hold values from 0 to 16383, as said below
- pair_second: int32 [256, 1024], P('blk', 'sub'), may hold values from 0 to 16383, as said below
- pair_mask: int32 [256, 1024], P('blk', 'sub'), may hold values 0 or 1
- pair_weight: float32 [256, 1024], P('blk', 'sub'), may hold values from 0.2 to 2
- station_owner: int32 [16384, 1], P(('blk', 'sub')), may hold values from 0 to 127; in each aligned block of 128 rows (0 to 127, 128 to 255, ...) at most 2 rows name the same one
- station_element: int32 [16384], P(('blk', 'sub')), may hold values from 0 to 127
Outputs:
- delivered: float32 [16384, 3, 1024], P(('blk', 'sub'))
The draws below stay inside these ranges and needn't reach their ends.
Inputs may be any that keep to these rules, and one draw needn't show every extreme that they name: `pair_first`: the slots of block j name first stations of block j, stations j * 64 to j * 64 + 63. `pair_second`: the second station is the first plus 1 to 63; where that passes the last station it is taken modulo 64 inside the first station's block. `station_owner`: among the 128 stations of one device, at most 2 have the same owner, and some owner has exactly 2.
All inputs are finite; a program needn't handle non-finite values. No bound on the sum of `pair_mask` on one device may be relied on, other than what follows from the above.
Results may differ from the reference program's by a relative error of at most 0.0045.
Values may be sent and summed in bfloat16 or wider, within the bound.
A program may use at most 128 MiB of HBM per device.

```python
import math
import jax
import jax.numpy as jnp
import numpy as np
from jax import lax

STA_DEV = 128
PB = 1024
ELEM_DEV = 128
NT = 1024
NF = 128
BLOCK = 64
STATIONS = 16384
BLOCKS = 256
ELEMENTS = 16384
SLOTS = 2
DEVICES = 128


def pair_offsets(key):
    inner_index = jax.random.randint(jax.random.fold_in(key, 11), (BLOCKS, PB), 0, BLOCK)
    offset_step = jax.random.randint(jax.random.fold_in(key, 12), (BLOCKS, PB), 1, BLOCK)
    return (inner_index, offset_step)


def draw_pair_first(key, part):
    inner_index, offset_step = pair_offsets(key)
    block_base = jnp.arange(BLOCKS, dtype=jnp.int32)[:, None] * BLOCK
    return (block_base + inner_index).astype(jnp.int32)


def draw_pair_second(key, part):
    inner_index, offset_step = pair_offsets(key)
    block_base = jnp.arange(BLOCKS, dtype=jnp.int32)[:, None] * BLOCK
    forward = block_base + inner_index + offset_step
    wrapped = block_base + (inner_index + offset_step) % BLOCK
    return jnp.where(forward < STATIONS, forward, wrapped).astype(jnp.int32)


def plant(drawn, stream_key, smallest, top_value):
    index_at = [jax.random.randint(jax.random.fold_in(stream_key, axis), (), 0, length) for axis, length in enumerate(drawn.shape)]
    widest = drawn.shape.index(max(drawn.shape))
    beside = index_at[:widest] + [(index_at[widest] + 1) % drawn.shape[widest]] + index_at[widest + 1:]
    return drawn.at[tuple(index_at)].set(smallest).at[tuple(beside)].set(top_value)


def shard_levels(own_key, extent, split, least, top_value):
    factor_of, own = 1.0, jax.random.fold_in(own_key, 6)
    for axis_at, parts in split:
        steps = jnp.exp(jax.random.uniform(jax.random.fold_in(own, axis_at), (parts,), jnp.float32, least / len(split), top_value / len(split)))
        factor_of = factor_of * jnp.repeat(steps, extent[axis_at] // parts).reshape([-1 if axis == axis_at else 1 for axis in range(len(extent))])
    return factor_of


def assign_block(rng, own, number, rows, count, top, limit, lean):
    order = jax.random.permutation(rng, count)
    packed, usual = load_shares(count, rows * top, limit, lean, True), load_shares(count, rows * top, limit, lean, False)
    places = jnp.arange(count)

    def named(sizes, rotation):
        used = int((sizes > 0).sum())
        fixed = max(1, used // 4)
        moved = fixed + (places - fixed + rotation * (used - fixed)) % max(1, count - fixed)
        return jnp.zeros((count,), jnp.int32).at[order[jnp.where(places < fixed, places, moved)]].set(jnp.asarray(sizes, jnp.int32))

    sizes = jnp.where(number % 4 == 0, named(packed, number // 4), named(usual, number - number // 4 - 1))
    mixed = jax.random.permutation(jax.random.fold_in(own, 3), count)
    donor, sink = mixed[0:count // 2 * 2:2], mixed[1:count // 2 * 2:2]
    room = jnp.minimum(sizes[donor] - 1, limit - sizes[sink]) // 2
    room = jnp.where((donor == order[0]) | (sink == order[0]) | (sizes[sink] == 0), 0, jnp.maximum(room, 0))
    moved = jax.random.randint(jax.random.fold_in(own, 4), (count // 2,), 0, 1 << 20) % (room + 1)
    sizes = sizes.at[donor].add(-moved).at[sink].add(moved)
    labels = jnp.searchsorted(jnp.cumsum(sizes), jnp.arange(rows * top), side="right").astype(jnp.int32)
    listing = labels.reshape(top, rows).T
    listing = listing[jax.random.permutation(jax.random.fold_in(own, 1), rows)]
    rotation = jax.random.randint(jax.random.fold_in(own, 2), (rows, 1), 0, top)
    return jnp.take_along_axis(listing, (jnp.arange(top)[None, :] + rotation) % top, axis=1)


def load_shares(amount, total, most, slope, full):
    weights = [(1 << 20) // math.isqrt(rank ** slope) + 1 for rank in range(1, amount + 1)]
    largest = most if full else min(most, max(-(-total // amount), total * weights[0] // sum(weights)))
    least = 1 if total - largest >= amount - 1 else 0
    counts, spare = [largest] + [least] * (amount - 1), total - largest - least * (amount - 1)
    while spare > 0:
        movable = [i for i in range(1, amount) if counts[i] < largest] or [i for i in range(1, amount) if counts[i] < most]
        mass, left = sum([weights[i] for i in movable]), spare
        for i in movable:
            extra = min(most - counts[i], max(1, left * weights[i] // mass), spare)
            counts[i] = counts[i] + extra
            spare = spare - extra
    return np.array(counts)


def centred(stream_key, extent, scale, reach, split=(), kind=jnp.bfloat16):
    values = jax.random.normal(stream_key, extent, jnp.float32) * scale
    if len(split) > 0:
        values = shard_levels(stream_key, extent, split, -0.22, 0.18) * values
    return jnp.clip(values, min=-reach, max=reach).astype(kind)


def setup_inputs(seed: int = 0) -> dict:
    key_list = jax.random.split(jax.random.key(seed), 9)
    synthetic = centred(key_list[0], (STATIONS, 3, NT), 1.0, 6.0, ((0, 128),))
    observed = centred(key_list[1], (STATIONS, 3, NT), 1.0, 6.0, ((0, 128),))
    pair_first = draw_pair_first(jax.random.fold_in(key_list[8], 71), 0)
    pair_second = draw_pair_second(jax.random.fold_in(key_list[8], 71), 0)
    pair_mask = plant((jax.random.randint(key_list[4], (BLOCKS, PB), 0, 4) < 3).astype(jnp.int32), jax.random.fold_in(key_list[4], 1), 0, 1)
    pair_weight = jnp.clip(jnp.exp(math.log(2.0) - 2.3025851 * jax.random.uniform(key_list[5], (BLOCKS, PB), jnp.float32) ** shard_levels(key_list[5], (BLOCKS, PB), ((0, 16), (1, 8)), -0.2, 0.2)), 0.2, 2.0)
    station_owner_keys = jax.random.split(jax.random.fold_in(key_list[6], 1), STATIONS // STA_DEV)
    station_owner_turns = jax.random.permutation(jax.random.fold_in(key_list[6], 3), STATIONS // STA_DEV)
    station_owner = jax.vmap(lambda own, number: assign_block(jax.random.fold_in(key_list[6], 2), own, number, STA_DEV, DEVICES, 1, SLOTS, 2))(station_owner_keys, station_owner_turns).reshape((STATIONS, 1))
    station_element = plant(jax.random.randint(key_list[7], (STATIONS,), 0, ELEM_DEV), jax.random.fold_in(key_list[7], 1), 0, ELEM_DEV - 1).astype(jnp.int32)
    return {"synthetic": synthetic, "observed": observed, "pair_first": pair_first, "pair_second": pair_second, "pair_mask": pair_mask, "pair_weight": pair_weight, "station_owner": station_owner, "station_element": station_element}


def dft_tables(samples, freqs):
    sample_index = jnp.arange(samples, dtype=jnp.int32)
    orders = jnp.arange(freqs, dtype=jnp.int32)
    phase_index = sample_index[:, None] * orders[None, :] % samples
    angles = phase_index.astype(jnp.float32) * (2.0 * math.pi / samples)
    norm_scale = 1.0 / math.sqrt(samples)
    cosine = jnp.cos(angles) * norm_scale
    sine_part = jnp.sin(angles) * norm_scale
    forward_table = jnp.concatenate([cosine, -sine_part], axis=1).astype(jnp.bfloat16)
    doubled = jnp.where(orders == 0, 1.0, 2.0).astype(jnp.float32)
    inverse_table = jnp.concatenate([cosine.T * doubled[:, None], -sine_part.T * doubled[:, None]], axis=0)
    return (forward_table, inverse_table)

def spectra(traces, forward_table):
    station_count = traces.shape[0]
    stacked = traces.reshape(station_count * 3, traces.shape[2])
    result = jnp.dot(stacked, forward_table, preferred_element_type=jnp.float32).astype(jnp.bfloat16)
    return result.reshape(station_count, 3, 2, forward_table.shape[1] // 2)

def pair_terms(first_rows, second_rows, weights):
    left_side = first_rows.astype(jnp.float32)
    right_side = second_rows.astype(jnp.float32)
    left_re = left_side[:, :, 0]
    left_im = left_side[:, :, 1]
    right_re = right_side[:, :, 0]
    right_im = right_side[:, :, 1]
    cross_re = left_re * right_re + left_im * right_im
    cross_im = left_im * right_re - left_re * right_im
    weighted = weights[:, None, None]
    resid_re = (cross_re[:, :3] - cross_re[:, 3:]) * weighted
    resid_im = (cross_im[:, :3] - cross_im[:, 3:]) * weighted
    first_re = resid_re * right_re[:, :3] - resid_im * right_im[:, :3]
    first_im = resid_re * right_im[:, :3] + resid_im * right_re[:, :3]
    second_re = resid_re * left_re[:, :3] + resid_im * left_im[:, :3]
    second_im = resid_re * left_im[:, :3] - resid_im * left_re[:, :3]
    return (jnp.stack([first_re, first_im], axis=2), jnp.stack([second_re, second_im], axis=2))

def reference(synthetic, observed, pair_first, pair_second, pair_mask, pair_weight, station_owner, station_element):
    forward_table, inverse_table = dft_tables(NT, NF)
    spectrum_table = jnp.concatenate([spectra(synthetic, forward_table), spectra(observed, forward_table)], axis=1)
    effective = pair_weight * pair_mask.astype(jnp.float32)

    def block_step(totals, inputs):
        firsts, seconds, weights = inputs
        first_terms, second_terms = pair_terms(spectrum_table[firsts], spectrum_table[seconds], weights)
        totals = totals.at[firsts].add(first_terms).at[seconds].add(second_terms)
        return (totals, None)
    start_totals = jnp.zeros((STATIONS, 3, 2, NF), jnp.float32)
    totals, unused = lax.scan(block_step, start_totals, (pair_first, pair_second, effective))
    adjoint = jnp.dot(totals.reshape(STATIONS * 3, 2 * NF), inverse_table, precision=lax.Precision.HIGHEST, preferred_element_type=jnp.float32).reshape(STATIONS, 3, NT)
    targets = (station_owner[:, 0] * ELEM_DEV + station_element).astype(jnp.int32)
    return jnp.zeros((ELEMENTS, 3, NT), jnp.float32).at[targets].add(adjoint)
```

```python
import functools
import math

import jax
import jax.numpy as jnp
import numpy as np
from jax import lax
from jax.experimental import pallas as pl
from jax.experimental.pallas import tpu as pltpu
from jax.sharding import PartitionSpec as P

MESH = pl.DeviceIdType.MESH
NF = 128
BLOCK = 64
F32 = jnp.float32
BF16 = jnp.bfloat16


def dft_tables(samples, freqs):
    phase = (np.arange(samples)[:, None] * np.arange(freqs)[None, :]) % samples
    angles = phase.astype(np.float64) * (2.0 * math.pi / samples)
    scale = 1.0 / math.sqrt(samples)
    cosine, sine = np.cos(angles) * scale, np.sin(angles) * scale
    forward = np.concatenate([cosine, -sine], axis=1).astype(np.float32)
    doubled = np.where(np.arange(freqs) == 0, 1.0, 2.0)[:, None]
    inverse = np.concatenate([cosine.T * doubled, -sine.T * doubled], axis=0)
    return forward.astype(jnp.bfloat16), inverse.astype(np.float32)


def in_two(x):
    high = x.astype(BF16)
    return high, (x - high.astype(F32)).astype(BF16)


def dot_rows(a, b):
    return lax.dot_general(a, b, (((1,), (1,)), ((), ())), preferred_element_type=F32)


def dot_plain(a, b):
    return jnp.dot(a, b, preferred_element_type=F32)


def features(pair):
    xr, xi = pair[0][:, :NF].astype(F32), pair[0][:, NF:].astype(F32)
    o_r, o_i = pair[1][:, :NF].astype(F32), pair[1][:, NF:].astype(F32)
    dr, di = xr - o_r, xi - o_i
    parts = [dr * xr + di * xi, dr * xi - di * xr, o_r * xr + o_i * xi, o_r * xi - o_i * xr]
    both = [in_two(p) for p in parts]
    return jnp.concatenate(
        [jnp.concatenate([b[i] for b in both], axis=1) for i in range(2)], axis=0
    )


def for_features(links):
    high, low = in_two(links)
    return jnp.concatenate(
        [jnp.concatenate([high, high], axis=1), jnp.concatenate([low, low], axis=1)], axis=0
    )


def linked(links, values):
    rows = links.shape[0] // 2
    both = dot_plain(links, values)
    return both[:rows] + both[rows:]


def spread(rows, count, shift):
    index = lax.broadcasted_iota(jnp.int32, (count, NF), 0) + shift
    return jnp.concatenate(
        [(index == rows[s : s + 1]).astype(F32).astype(BF16) for s in range(rows.shape[0])], axis=1
    )


def spread_weights(rows, weights, count, shift):
    index = lax.broadcasted_iota(jnp.int32, (count, NF), 0) + shift
    parts = []
    for part in in_two(weights):
        wide = part.astype(F32)
        parts.append(
            jnp.concatenate(
                [
                    jnp.where(index == rows[s : s + 1], wide[s : s + 1], 0.0).astype(BF16)
                    for s in range(rows.shape[0])
                ],
                axis=1,
            )
        )
    return jnp.concatenate(parts, axis=0)


def exchange_kernel(
    blks,
    subs,
    syn_hbm,
    obs_hbm,
    table_hbm,
    first_hbm,
    second_hbm,
    mask_hbm,
    weight_hbm,
    owner_hbm,
    element_hbm,
    summed,
    traces,
    table,
    first,
    second,
    mask,
    weight,
    owner,
    element,
    spec,
    halo,
    list_out,
    list_over,
    lists,
    lists_prev,
    near_out,
    near_labels,
    label_out,
    labels,
    group_out,
    group_in,
    far_out,
    far_in,
    load_sems,
    list_send,
    list_recv,
    over_send,
    over_recv,
    halo_send,
    halo_recv,
    near_send,
    near_recv,
    label_send,
    label_recv,
    group_send,
    group_recv,
    far_send,
    far_recv,
):
    devices = blks * subs
    blk, sub = lax.axis_index("blk"), lax.axis_index("sub")
    me = blk * subs + sub
    rows = spec.shape[1]
    blocks = first.shape[0]
    group_rows, far_rows = 2 * blks, 2 * subs

    def around(at, step, size):
        there = at + step
        return jnp.where(there >= size, there - size, there)

    subs_there = [around(sub, step, subs) for step in range(1, subs)]
    blks_there = [around(blk, step, blks) for step in range(1, blks)]
    blk_after, blk_before = blks_there[0], blks_there[-1]
    after = (jnp.where(sub == subs - 1, blk_after, blk), subs_there[0])
    before = (jnp.where(sub == 0, blk_before, blk), subs_there[-1])

    pairs = [
        (first_hbm, first),
        (second_hbm, second),
        (mask_hbm, mask),
        (weight_hbm, weight),
        (table_hbm, table),
        (syn_hbm.at[0], traces.at[0, pl.ds(0, rows)]),
        (obs_hbm.at[0], traces.at[0, pl.ds(rows, rows)]),
        (syn_hbm.at[1], traces.at[1, pl.ds(0, rows)]),
        (obs_hbm.at[1], traces.at[1, pl.ds(rows, rows)]),
        (syn_hbm.at[2], traces.at[2, pl.ds(0, rows)]),
        (obs_hbm.at[2], traces.at[2, pl.ds(rows, rows)]),
        (owner_hbm, owner),
        (element_hbm, element),
    ]
    loads = [
        pltpu.make_async_copy(src, dst, load_sems.at[i]) for i, (src, dst) in enumerate(pairs)
    ]
    for load in loads:
        load.start()

    barrier = pltpu.get_barrier_semaphore()

    def greet(there):
        pl.semaphore_signal(barrier, inc=1, device_id=there, device_id_type=MESH)

    for there in subs_there:
        greet((blk, there))
    for there in blks_there:
        greet((there, sub))

    @pl.when(sub == 0)
    def _():
        for s in range(1, subs):
            greet((blk_before, s))

    @pl.when(sub == subs - 1)
    def _():
        greet((blk_after, 0))

    for i in range(4):
        loads[i].wait()
    base = (blk * blocks + lax.broadcasted_iota(jnp.int32, (blocks, NF), 0)) * BLOCK
    code = ((first[...] - base) * (2 * BLOCK) + (second[...] - base)).astype(F32)
    slot_weight = weight[...] * mask[...].astype(F32)
    zero_row = jnp.zeros((1, NF), F32)
    for s in range(subs):
        lines = [max(2 * s - 1, 0), 2 * s, 2 * s + 1]
        list_out[s] = jnp.concatenate(
            [code[i : i + 1] for i in lines]
            + [slot_weight[i : i + 1] for i in lines]
            + [zero_row] * 2,
            axis=0,
        )
    list_over[...] = jnp.concatenate(
        [code[blocks - 1 : blocks]]
        + [zero_row] * 2
        + [slot_weight[blocks - 1 : blocks]]
        + [zero_row] * 4,
        axis=0,
    )
    lists[sub] = list_out[sub]

    def transform(c):
        both = dot_plain(traces[c], table[...]).astype(BF16)
        spec[2 * c] = both[:rows]
        spec[2 * c + 1] = both[rows:]

    for i in range(4, 7):
        loads[i].wait()
    transform(0)

    pl.semaphore_wait(barrier, subs + blks - 1)

    def halo_copies(c):
        q = pl.ds(2 * c, 2)
        return [
            pltpu.make_async_remote_copy(
                src_ref=spec.at[q, pl.ds(0, BLOCK)],
                dst_ref=halo.at[q, pl.ds(BLOCK, BLOCK)],
                send_sem=halo_send.at[0, c],
                recv_sem=halo_recv.at[0, c],
                device_id=before,
                device_id_type=MESH,
            ),
            pltpu.make_async_remote_copy(
                src_ref=spec.at[q, pl.ds(rows - BLOCK, BLOCK)],
                dst_ref=halo.at[q, pl.ds(0, BLOCK)],
                send_sem=halo_send.at[1, c],
                recv_sem=halo_recv.at[1, c],
                device_id=after,
                device_id_type=MESH,
            ),
        ]

    halos = [halo_copies(c) for c in range(3)]
    for there in subs_there:
        pltpu.make_async_remote_copy(
            src_ref=list_out.at[there],
            dst_ref=lists.at[sub],
            send_sem=list_send,
            recv_sem=list_recv,
            device_id=(blk, there),
            device_id_type=MESH,
        ).start()
    over = pltpu.make_async_remote_copy(
        src_ref=list_over,
        dst_ref=lists_prev.at[sub],
        send_sem=over_send,
        recv_sem=over_recv,
        device_id=(blk_after, 0),
        device_id_type=MESH,
    )
    over.start()
    for copy in halos[0]:
        copy.start()
    for c in (1, 2):
        loads[5 + 2 * c].wait()
        loads[6 + 2 * c].wait()
        transform(c)
        for copy in halos[c]:
            copy.start()

    loads[11].wait()
    loads[12].wait()
    lane = lax.broadcasted_iota(jnp.int32, (rows, rows), 1)
    line = lax.broadcasted_iota(jnp.int32, (rows, rows), 0)
    owner_row = owner[...]

    def column(row):
        return jnp.sum(jnp.where(lane == line, row, 0), axis=1, keepdims=True)

    owner_column, element_column = column(owner_row), column(element[...]).astype(F32)
    same = owner_column == owner_row
    rank_row = jnp.sum(jnp.where(same & (line < lane), 1, 0), axis=0, keepdims=True)
    rank_column = jnp.sum(jnp.where(same & (lane < line), 1, 0), axis=1, keepdims=True)
    label_rows = []
    for k in range(2):
        chosen = ((owner_column == lane) & (rank_column == k)).astype(F32)
        label_rows.append(
            jnp.sum(chosen * (element_column - rows), axis=0, keepdims=True) + float(rows)
        )
    near_out[...] = jnp.concatenate(label_rows + [zero_row] * 6, axis=0)
    near_labels[sub] = near_out[...]
    for there in subs_there:
        pltpu.make_async_remote_copy(
            src_ref=near_out,
            dst_ref=near_labels.at[sub],
            send_sem=near_send,
            recv_sem=near_recv,
            device_id=(blk, there),
            device_id_type=MESH,
        ).start()
    sub_bits, blk_bits = subs.bit_length() - 1, blks.bit_length() - 1
    target = (owner_row & (subs - 1)) * group_rows + rank_row * blks + (owner_row >> sub_bits)
    slot = lax.broadcasted_iota(jnp.int32, (2 * devices, rows), 0)
    placement = (slot == target).astype(F32).astype(BF16)

    def stations(c):
        return (spec[2 * c], spec[2 * c + 1])

    own = [features(stations(c)) for c in range(3)]

    others = pl.ds(0, subs - 1)
    pltpu.make_async_copy(lists.at[others], lists.at[others], list_recv).wait()

    @pl.when(sub == 0)
    def _():
        pltpu.make_async_copy(lists_prev, lists_prev, over_recv).wait()

    @pl.when(sub != 0)
    def _():
        lists_prev[...] = lists[...]

    def unpacked(ref, k):
        codes = ref[:, k, :].astype(jnp.int32)
        return codes >> 7, codes & 127, ref[:, 3 + k, :]

    first0, second0, weight0 = unpacked(lists_prev, 0)
    first1, second1, weight1 = unpacked(lists, 1)
    first2, second2, weight2 = unpacked(lists, 2)
    to_prev = dot_rows(spread_weights(second0, weight0, BLOCK, BLOCK), spread(first0, rows, 0))
    upper = dot_rows(spread(first1, BLOCK, 0), spread_weights(second1, weight1, rows, 0))
    lower = dot_rows(spread(first2, BLOCK, 0), spread_weights(second2, weight2, rows, 0))
    to_prev = to_prev[:BLOCK] + to_prev[BLOCK:]
    upper = upper[:, :rows] + upper[:, rows:]
    lower = lower[:, :rows] + lower[:, rows:]
    half = lax.broadcasted_iota(jnp.int32, (BLOCK, rows), 1) >= BLOCK
    inside = jnp.where(half, pltpu.roll(lower, BLOCK, 1), 0.0)
    one_way = jnp.concatenate([upper, inside], axis=0)
    link_own = for_features(one_way + one_way.T)
    link_halo = for_features(jnp.concatenate([to_prev, jnp.where(half, lower, 0.0)], axis=0))
    inner = [linked(link_own, own[c]) for c in range(3)]

    pltpu.make_async_copy(near_labels.at[others], near_labels.at[others], near_recv).wait()
    group_labels = jnp.concatenate([near_labels[:, 0, :], near_labels[:, 1, :]], axis=0)
    label_out[...] = group_labels
    labels[blk] = group_labels
    for there in blks_there:
        pltpu.make_async_remote_copy(
            src_ref=label_out,
            dst_ref=labels.at[blk],
            send_sem=label_send,
            recv_sem=label_recv,
            device_id=(there, sub),
            device_id_type=MESH,
        ).start()

    row_out = lax.broadcasted_iota(jnp.int32, (2 * devices, 2 * devices), 0)
    row_in = lax.broadcasted_iota(jnp.int32, (2 * devices, 2 * devices), 1)
    wanted = (
        ((row_out & (subs - 1)) << (blk_bits + 1))
        + (((row_out >> sub_bits) & 1) << blk_bits)
        + (row_out >> (sub_bits + 1))
    )
    turned = (row_in == wanted).astype(F32).astype(BF16)

    for c in range(3):
        for copy in halos[c]:
            copy.wait_recv()
        sums = inner[c] + linked(link_halo, features((halo[2 * c], halo[2 * c + 1])))
        g1r, g1i, g2r, g2i = (sums[:, i * NF : (i + 1) * NF] for i in range(4))
        x, o = stations(c)
        xr, xi = x[:, :NF].astype(F32), x[:, NF:].astype(F32)
        dr, di = xr - o[:, :NF].astype(F32), xi - o[:, NF:].astype(F32)
        real = (xr * g1r - xi * g1i) + (dr * g2r - di * g2i)
        imag = (xr * g1i + xi * g1r) + (dr * g2i + di * g2r)
        adjoint = jnp.concatenate([real, imag], axis=1).astype(BF16)
        group_out[c] = dot_plain(placement, adjoint).astype(BF16)
        mine = pl.ds(pl.multiple_of(sub * group_rows, group_rows), group_rows)
        group_in[c, mine] = group_out[c, mine]
        for there in subs_there:
            theirs = pl.ds(pl.multiple_of(there * group_rows, group_rows), group_rows)
            pltpu.make_async_remote_copy(
                src_ref=group_out.at[c, theirs],
                dst_ref=group_in.at[c, mine],
                send_sem=group_send.at[c],
                recv_sem=group_recv.at[c],
                device_id=(blk, there),
                device_id_type=MESH,
            ).start()

    some = pl.ds(0, blks - 1)
    pltpu.make_async_copy(labels.at[some], labels.at[some], label_recv).wait()
    table_of_labels = labels[...].reshape(2 * devices, NF)
    row_lane = lax.broadcasted_iota(jnp.int32, (2 * devices, NF), 1)
    label = jnp.sum(jnp.where(row_lane == me, table_of_labels, 0.0), axis=1, keepdims=True)
    collect = (label == row_lane.astype(F32)).astype(F32).T.astype(BF16)

    part = pl.ds(0, (subs - 1) * group_rows)
    here = pl.ds(pl.multiple_of(blk * far_rows, far_rows), far_rows)
    for c in range(3):
        pltpu.make_async_copy(group_in.at[c, part], group_in.at[c, part], group_recv.at[c]).wait()
        far_out[c] = dot_plain(turned, group_in[c]).astype(BF16)
        far_in[c, here] = far_out[c, here]
        for there in blks_there:
            theirs = pl.ds(pl.multiple_of(there * far_rows, far_rows), far_rows)
            pltpu.make_async_remote_copy(
                src_ref=far_out.at[c, theirs],
                dst_ref=far_in.at[c, here],
                send_sem=far_send.at[c],
                recv_sem=far_recv.at[c],
                device_id=(there, sub),
                device_id_type=MESH,
            ).start()

    far_part = pl.ds(0, (blks - 1) * far_rows)
    for c in range(3):
        pltpu.make_async_copy(far_in.at[c, far_part], far_in.at[c, far_part], far_recv.at[c]).wait()
        summed[c] = dot_plain(collect, far_in[c])

    for c in range(3):
        for copy in halos[c]:
            copy.wait_send()
        pltpu.make_async_copy(
            group_out.at[c, part], group_out.at[c, part], group_send.at[c]
        ).wait()
        pltpu.make_async_copy(
            far_out.at[c, far_part], far_out.at[c, far_part], far_send.at[c]
        ).wait()
    pltpu.make_async_copy(list_out.at[others], list_out.at[others], list_send).wait()
    pltpu.make_async_copy(near_labels.at[others], near_labels.at[others], near_send).wait()
    pltpu.make_async_copy(labels.at[some], labels.at[some], label_send).wait()
    over.wait_send()


def exchange(blks, subs, syn, obs, table, first, second, mask, weight, owner, element):
    devices = blks * subs
    samples, rows = syn.shape[2], syn.shape[1]
    in_hbm = pl.BlockSpec(memory_space=pltpu.HBM)
    dma = pltpu.SemaphoreType.DMA
    moved = pltpu.VMEM((3, 2 * devices, 2 * NF), BF16)
    return pl.pallas_call(
        functools.partial(exchange_kernel, blks, subs),
        out_shape=jax.ShapeDtypeStruct((3, rows, 2 * NF), F32),
        in_specs=[in_hbm] * 9,
        out_specs=pl.BlockSpec(memory_space=pltpu.VMEM),
        scratch_shapes=[
            pltpu.VMEM((3, 2 * rows, samples), BF16),
            pltpu.VMEM(table.shape, BF16),
            pltpu.VMEM(first.shape, jnp.int32),
            pltpu.VMEM(second.shape, jnp.int32),
            pltpu.VMEM(mask.shape, jnp.int32),
            pltpu.VMEM(weight.shape, F32),
            pltpu.VMEM(owner.shape, jnp.int32),
            pltpu.VMEM(element.shape, jnp.int32),
            pltpu.VMEM((6, rows, 2 * NF), BF16),
            pltpu.VMEM((6, 2 * BLOCK, 2 * NF), BF16),
            pltpu.VMEM((subs, 8, NF), F32),
            pltpu.VMEM((8, NF), F32),
            pltpu.VMEM((subs, 8, NF), F32),
            pltpu.VMEM((subs, 8, NF), F32),
            pltpu.VMEM((8, NF), F32),
            pltpu.VMEM((subs, 8, NF), F32),
            pltpu.VMEM((2 * subs, NF), F32),
            pltpu.VMEM((blks, 2 * subs, NF), F32),
            moved,
            moved,
            moved,
            moved,
            dma((13,)),
            dma,
            dma,
            dma,
            dma,
            dma((2, 3)),
            dma((2, 3)),
            dma,
            dma,
            dma,
            dma,
            dma((3,)),
            dma((3,)),
            dma((3,)),
            dma((3,)),
        ],
        compiler_params=pltpu.CompilerParams(
            collective_id=0, has_side_effects=True, vmem_limit_bytes=60 * 2**20
        ),
        cost_estimate=pl.CostEstimate(
            flops=2 * 10**9, bytes_accessed=3 * 10**6, transcendentals=0
        ),
        name="exchange",
    )(syn, obs, table, first, second, mask, weight, owner, element)


def finish_kernel(summed, table_high, table_low, out, result, sems):
    components, elements, width = summed.shape
    count = components * elements
    samples = result.shape[1]
    chunk = samples // sems.shape[0]
    high, low = in_two(summed[...].reshape(count, width))
    parts = jnp.concatenate([high, low], axis=0)
    copies = []
    for n in range(sems.shape[0]):
        columns = pl.ds(n * chunk, chunk)
        both = dot_plain(parts, table_high[:, columns])
        result[:, columns] = both[:count] + (
            both[count:] + dot_plain(high, table_low[:, columns])
        )
        copies.append(
            pltpu.make_async_copy(result.at[:, columns], out.at[:, columns], sems.at[n])
        )
        copies[-1].start()
    for copy in copies:
        copy.wait()


def finish(summed, table_high, table_low):
    components, elements, width = summed.shape
    samples = table_high.shape[1]
    in_vmem = pl.BlockSpec(memory_space=pltpu.VMEM)
    out = pl.pallas_call(
        finish_kernel,
        out_shape=jax.ShapeDtypeStruct((components * elements, samples), F32),
        in_specs=[in_vmem] * 3,
        out_specs=pl.BlockSpec(memory_space=pl.ANY),
        scratch_shapes=[
            pltpu.VMEM((components * elements, samples), F32),
            pltpu.SemaphoreType.DMA((4,)),
        ],
        compiler_params=pltpu.CompilerParams(vmem_limit_bytes=40 * 2**20),
        cost_estimate=pl.CostEstimate(
            flops=7 * 10**8, bytes_accessed=3 * 10**6, transcendentals=0
        ),
        name="finish",
    )(summed, table_high, table_low)
    return out.reshape(components, elements, samples)


def on_device(
    blks,
    subs,
    synthetic,
    observed,
    pair_first,
    pair_second,
    pair_mask,
    pair_weight,
    station_owner,
    station_element,
):
    rows, _, samples = synthetic.shape
    forward, inverse = dft_tables(samples, NF)
    inverse_high = inverse.astype(jnp.bfloat16)
    inverse_low = (inverse - inverse_high.astype(np.float32)).astype(jnp.bfloat16)
    summed = exchange(
        blks,
        subs,
        jnp.transpose(synthetic, (1, 0, 2)),
        jnp.transpose(observed, (1, 0, 2)),
        jnp.asarray(forward),
        pair_first,
        pair_second,
        pair_mask,
        pair_weight,
        station_owner.reshape(1, rows),
        station_element.reshape(1, rows),
    )
    out = finish(summed, jnp.asarray(inverse_high), jnp.asarray(inverse_low))
    return jnp.transpose(out, (1, 0, 2))


def solution(mesh):
    blks, subs = mesh.shape["blk"], mesh.shape["sub"]
    return jax.shard_map(
        functools.partial(on_device, blks, subs),
        mesh=mesh,
        in_specs=(
            P(("blk", "sub"), None, None),
            P(("blk", "sub"), None, None),
            P("blk", "sub"),
            P("blk", "sub"),
            P("blk", "sub"),
            P("blk", "sub"),
            P(("blk", "sub"), None),
            P(("blk", "sub")),
        ),
        out_specs=P(("blk", "sub"), None, None),
        check_vma=False,
    )
```

```python
import functools
import math

import jax
import jax.numpy as jnp
import numpy as np
from jax import lax
from jax.experimental import pallas as pl
from jax.experimental.pallas import tpu as pltpu
from jax.sharding import PartitionSpec as P

MESH = pl.DeviceIdType.MESH
NF = 128
BLOCK = 64
TILE = 16
F32 = jnp.float32
BF16 = jnp.bfloat16


def dft_tables(samples, freqs):
    phase = (np.arange(samples)[:, None] * np.arange(freqs)[None, :]) % samples
    angles = phase.astype(np.float64) * (2.0 * math.pi / samples)
    scale = 1.0 / math.sqrt(samples)
    cosine, sine = np.cos(angles) * scale, np.sin(angles) * scale
    forward = np.concatenate([cosine, -sine], axis=1).astype(np.float32)
    doubled = np.where(np.arange(freqs) == 0, 1.0, 2.0)[:, None]
    inverse = np.concatenate([cosine.T * doubled, -sine.T * doubled], axis=0)
    return forward.astype(jnp.bfloat16), inverse.astype(np.float32)


def in_two(x):
    high = x.astype(BF16)
    return high, (x - high.astype(F32)).astype(BF16)


def dot_rows(a, b):
    return lax.dot_general(a, b, (((1,), (1,)), ((), ())), preferred_element_type=F32)


def dot_plain(a, b):
    return jnp.dot(a, b, preferred_element_type=F32)


def features(pair):
    xr, xi = pair[0][:, :NF].astype(F32), pair[0][:, NF:].astype(F32)
    o_r, o_i = pair[1][:, :NF].astype(F32), pair[1][:, NF:].astype(F32)
    dr, di = xr - o_r, xi - o_i
    parts = [dr * xr + di * xi, dr * xi - di * xr, o_r * xr + o_i * xi, o_r * xi - o_i * xr]
    both = [in_two(p) for p in parts]
    return jnp.concatenate(
        [jnp.concatenate([b[i] for b in both], axis=1) for i in range(2)], axis=0
    )


def for_features(links):
    high, low = in_two(links)
    return jnp.concatenate(
        [jnp.concatenate([high, high], axis=1), jnp.concatenate([low, low], axis=1)], axis=0
    )


def linked(links, values):
    rows = links.shape[0] // 2
    both = dot_plain(links, values)
    return both[:rows] + both[rows:]


def spread(rows, count, shift):
    index = lax.broadcasted_iota(jnp.int32, (count, NF), 0) + shift
    return jnp.concatenate(
        [(index == rows[s : s + 1]).astype(F32).astype(BF16) for s in range(rows.shape[0])], axis=1
    )


def spread_weights(rows, weights, count, shift):
    index = lax.broadcasted_iota(jnp.int32, (count, NF), 0) + shift
    parts = []
    for part in in_two(weights):
        wide = part.astype(F32)
        parts.append(
            jnp.concatenate(
                [
                    jnp.where(index == rows[s : s + 1], wide[s : s + 1], 0.0).astype(BF16)
                    for s in range(rows.shape[0])
                ],
                axis=1,
            )
        )
    return jnp.concatenate(parts, axis=0)


def exchange_kernel(
    blks,
    subs,
    syn_hbm,
    obs_hbm,
    table_hbm,
    first_hbm,
    second_hbm,
    mask_hbm,
    weight_hbm,
    owner_hbm,
    element_hbm,
    summed,
    traces,
    table,
    first,
    second,
    mask,
    weight,
    owner,
    element,
    spec,
    halo,
    list_out,
    list_over,
    lists,
    lists_prev,
    wide,
    outgoing,
    received,
    wide_in,
    load_sems,
    list_send,
    list_recv,
    over_send,
    over_recv,
    halo_send,
    halo_recv,
    joined,
    all_send,
    all_recv,
):
    devices = blks * subs
    blk, sub = lax.axis_index("blk"), lax.axis_index("sub")
    me = blk * subs + sub
    rows = spec.shape[1]
    blocks = first.shape[0]
    def around(at, step, size):
        there = at + step
        return jnp.where(there >= size, there - size, there)

    subs_there = [around(sub, step, subs) for step in range(1, subs)]
    blks_there = [around(blk, step, blks) for step in range(1, blks)]
    blk_after, blk_before = blks_there[0], blks_there[-1]
    after = (jnp.where(sub == subs - 1, blk_after, blk), subs_there[0])
    before = (jnp.where(sub == 0, blk_before, blk), subs_there[-1])

    pairs = [
        (first_hbm, first),
        (second_hbm, second),
        (mask_hbm, mask),
        (weight_hbm, weight),
        (table_hbm, table),
        (syn_hbm.at[0], traces.at[0, pl.ds(0, rows)]),
        (obs_hbm.at[0], traces.at[0, pl.ds(rows, rows)]),
        (syn_hbm.at[1], traces.at[1, pl.ds(0, rows)]),
        (obs_hbm.at[1], traces.at[1, pl.ds(rows, rows)]),
        (syn_hbm.at[2], traces.at[2, pl.ds(0, rows)]),
        (obs_hbm.at[2], traces.at[2, pl.ds(rows, rows)]),
        (owner_hbm, owner),
        (element_hbm, element),
    ]
    loads = [
        pltpu.make_async_copy(src, dst, load_sems.at[i]) for i, (src, dst) in enumerate(pairs)
    ]
    for load in loads:
        load.start()

    barrier = pltpu.get_barrier_semaphore()

    def greet(there):
        pl.semaphore_signal(barrier, inc=1, device_id=there, device_id_type=MESH)

    for there in subs_there:
        greet((blk, there))
    for there in blks_there:
        greet((there, sub))

    @pl.when(sub == 0)
    def _():
        for s in range(1, subs):
            greet((blk_before, s))

    @pl.when(sub == subs - 1)
    def _():
        greet((blk_after, 0))

    for i in range(4):
        loads[i].wait()
    base = (blk * blocks + lax.broadcasted_iota(jnp.int32, (blocks, NF), 0)) * BLOCK
    code = ((first[...] - base) * (2 * BLOCK) + (second[...] - base)).astype(F32)
    slot_weight = weight[...] * mask[...].astype(F32)
    zero_row = jnp.zeros((1, NF), F32)
    for s in range(subs):
        lines = [max(2 * s - 1, 0), 2 * s, 2 * s + 1]
        list_out[s] = jnp.concatenate(
            [code[i : i + 1] for i in lines]
            + [slot_weight[i : i + 1] for i in lines]
            + [zero_row] * 2,
            axis=0,
        )
    list_over[...] = jnp.concatenate(
        [code[blocks - 1 : blocks]]
        + [zero_row] * 2
        + [slot_weight[blocks - 1 : blocks]]
        + [zero_row] * 4,
        axis=0,
    )
    lists[sub] = list_out[sub]

    def transform(c):
        both = dot_plain(traces[c], table[...]).astype(BF16)
        spec[2 * c] = both[:rows]
        spec[2 * c + 1] = both[rows:]

    for i in range(4, 7):
        loads[i].wait()
    transform(0)

    pl.semaphore_wait(barrier, subs + blks - 1)
    for there in subs_there:
        pl.semaphore_signal(joined, inc=1, device_id=(blk, there), device_id_type=MESH)

    def halo_copies(c):
        q = pl.ds(2 * c, 2)
        return [
            pltpu.make_async_remote_copy(
                src_ref=spec.at[q, pl.ds(0, BLOCK)],
                dst_ref=halo.at[q, pl.ds(BLOCK, BLOCK)],
                send_sem=halo_send.at[0, c],
                recv_sem=halo_recv.at[0, c],
                device_id=before,
                device_id_type=MESH,
            ),
            pltpu.make_async_remote_copy(
                src_ref=spec.at[q, pl.ds(rows - BLOCK, BLOCK)],
                dst_ref=halo.at[q, pl.ds(0, BLOCK)],
                send_sem=halo_send.at[1, c],
                recv_sem=halo_recv.at[1, c],
                device_id=after,
                device_id_type=MESH,
            ),
        ]

    halos = [halo_copies(c) for c in range(3)]
    for there in subs_there:
        pltpu.make_async_remote_copy(
            src_ref=list_out.at[there],
            dst_ref=lists.at[sub],
            send_sem=list_send,
            recv_sem=list_recv,
            device_id=(blk, there),
            device_id_type=MESH,
        ).start()
    over = pltpu.make_async_remote_copy(
        src_ref=list_over,
        dst_ref=lists_prev.at[sub],
        send_sem=over_send,
        recv_sem=over_recv,
        device_id=(blk_after, 0),
        device_id_type=MESH,
    )
    over.start()
    for copy in halos[0]:
        copy.start()
    for c in (1, 2):
        loads[5 + 2 * c].wait()
        loads[6 + 2 * c].wait()
        transform(c)
        for copy in halos[c]:
            copy.start()

    loads[11].wait()
    loads[12].wait()
    lane = lax.broadcasted_iota(jnp.int32, (rows, rows), 1)
    line = lax.broadcasted_iota(jnp.int32, (rows, rows), 0)
    owner_row = owner[...]
    owner_column = jnp.sum(jnp.where(lane == line, owner_row, 0), axis=1, keepdims=True)
    rank_row = jnp.sum(
        jnp.where((owner_column == owner_row) & (line < lane), 1, 0), axis=0, keepdims=True
    )
    slot = lax.broadcasted_iota(jnp.int32, (2 * devices, rows), 0)
    chosen = (slot == rank_row * devices + owner_row).astype(F32)
    placement = chosen.astype(BF16)
    label = jnp.sum(chosen * (element[...].astype(F32) - rows), axis=1, keepdims=True) + rows
    for k in range(2):
        mine = label[k * devices : (k + 1) * devices]
        wide[pl.ds(8 * k + 6, devices, stride=TILE), :] = jnp.broadcast_to(mine, (devices, NF))
        wide[pl.ds(8 * k + 7, devices, stride=TILE), :] = jnp.zeros((devices, NF), F32)

    def stations(c):
        return (spec[2 * c], spec[2 * c + 1])

    own = [features(stations(c)) for c in range(3)]

    others = pl.ds(0, subs - 1)
    pltpu.make_async_copy(lists.at[others], lists.at[others], list_recv).wait()

    @pl.when(sub == 0)
    def _():
        pltpu.make_async_copy(lists_prev, lists_prev, over_recv).wait()

    @pl.when(sub != 0)
    def _():
        lists_prev[...] = lists[...]

    def unpacked(ref, k):
        codes = ref[:, k, :].astype(jnp.int32)
        return codes >> 7, codes & 127, ref[:, 3 + k, :]

    first0, second0, weight0 = unpacked(lists_prev, 0)
    first1, second1, weight1 = unpacked(lists, 1)
    first2, second2, weight2 = unpacked(lists, 2)
    to_prev = dot_rows(spread_weights(second0, weight0, BLOCK, BLOCK), spread(first0, rows, 0))
    upper = dot_rows(spread(first1, BLOCK, 0), spread_weights(second1, weight1, rows, 0))
    lower = dot_rows(spread(first2, BLOCK, 0), spread_weights(second2, weight2, rows, 0))
    to_prev = to_prev[:BLOCK] + to_prev[BLOCK:]
    upper = upper[:, :rows] + upper[:, rows:]
    lower = lower[:, :rows] + lower[:, rows:]
    half = lax.broadcasted_iota(jnp.int32, (BLOCK, rows), 1) >= BLOCK
    inside = jnp.where(half, pltpu.roll(lower, BLOCK, 1), 0.0)
    one_way = jnp.concatenate([upper, inside], axis=0)
    link_own = for_features(one_way + one_way.T)
    link_halo = for_features(jnp.concatenate([to_prev, jnp.where(half, lower, 0.0)], axis=0))
    inner = [linked(link_own, own[c]) for c in range(3)]

    for c in range(3):
        for copy in halos[c]:
            copy.wait_recv()
        sums = inner[c] + linked(link_halo, features((halo[2 * c], halo[2 * c + 1])))
        g1r, g1i, g2r, g2i = (sums[:, i * NF : (i + 1) * NF] for i in range(4))
        x, o = stations(c)
        xr, xi = x[:, :NF].astype(F32), x[:, NF:].astype(F32)
        dr, di = xr - o[:, :NF].astype(F32), xi - o[:, NF:].astype(F32)
        real = (xr * g1r - xi * g1i) + (dr * g2r - di * g2i)
        imag = (xr * g1i + xi * g1r) + (dr * g2i + di * g2r)
        adjoint = jnp.concatenate([real, imag], axis=1).astype(BF16)
        moved = dot_plain(placement, adjoint)
        for k in range(2):
            for i in range(2):
                wide[pl.ds(8 * k + 2 * c + i, devices, stride=TILE), :] = moved[
                    k * devices : (k + 1) * devices, i * NF : (i + 1) * NF
                ]
    outgoing[...] = wide[...].astype(BF16).reshape(outgoing.shape)
    received[me] = outgoing[me]

    pl.semaphore_wait(joined, subs - 1)

    def deliver(blk_to, sub_to):
        to = blk_to * subs + sub_to
        pltpu.make_async_remote_copy(
            src_ref=outgoing.at[to],
            dst_ref=received.at[me],
            send_sem=all_send,
            recv_sem=all_recv,
            device_id=(blk_to, sub_to),
            device_id_type=MESH,
        ).start()

    def deliver_far(step, carry):
        there = around(blk, step, blks)
        for sub_to in [sub] + subs_there:
            deliver(there, sub_to)
        return carry

    lax.fori_loop(1, blks, deliver_far, 0)
    for there in subs_there:
        deliver(blk, there)

    most = pl.ds(0, devices - 1)
    pltpu.make_async_copy(received.at[most], received.at[most], all_recv).wait()
    wide_in[...] = received[...].astype(F32).reshape(wide_in.shape)

    def picked(row):
        return wide_in[pl.ds(row, devices, stride=TILE), :]

    labels = jnp.concatenate([picked(6), picked(14)], axis=0)
    element_lane = lax.broadcasted_iota(jnp.int32, (2 * devices, NF), 1).astype(F32)
    collect = (labels == element_lane).astype(F32).astype(BF16)
    for c in range(3):
        values = jnp.concatenate(
            [
                jnp.concatenate([picked(8 * k + 2 * c), picked(8 * k + 2 * c + 1)], axis=1)
                for k in range(2)
            ],
            axis=0,
        ).astype(BF16)
        summed[c] = lax.dot_general(
            collect, values, (((0,), (0,)), ((), ())), preferred_element_type=F32
        )

    for c in range(3):
        for copy in halos[c]:
            copy.wait_send()
    pltpu.make_async_copy(list_out.at[others], list_out.at[others], list_send).wait()
    over.wait_send()
    pltpu.make_async_copy(outgoing.at[most], outgoing.at[most], all_send).wait()


def exchange(blks, subs, syn, obs, table, first, second, mask, weight, owner, element):
    devices = blks * subs
    samples, rows = syn.shape[2], syn.shape[1]
    in_hbm = pl.BlockSpec(memory_space=pltpu.HBM)
    dma = pltpu.SemaphoreType.DMA
    return pl.pallas_call(
        functools.partial(exchange_kernel, blks, subs),
        out_shape=jax.ShapeDtypeStruct((3, rows, 2 * NF), F32),
        in_specs=[in_hbm] * 9,
        out_specs=pl.BlockSpec(memory_space=pltpu.VMEM),
        scratch_shapes=[
            pltpu.VMEM((3, 2 * rows, samples), BF16),
            pltpu.VMEM(table.shape, BF16),
            pltpu.VMEM(first.shape, jnp.int32),
            pltpu.VMEM(second.shape, jnp.int32),
            pltpu.VMEM(mask.shape, jnp.int32),
            pltpu.VMEM(weight.shape, F32),
            pltpu.VMEM(owner.shape, jnp.int32),
            pltpu.VMEM(element.shape, jnp.int32),
            pltpu.VMEM((6, rows, 2 * NF), BF16),
            pltpu.VMEM((6, 2 * BLOCK, 2 * NF), BF16),
            pltpu.VMEM((subs, 8, NF), F32),
            pltpu.VMEM((8, NF), F32),
            pltpu.VMEM((subs, 8, NF), F32),
            pltpu.VMEM((subs, 8, NF), F32),
            pltpu.VMEM((devices * TILE, NF), F32),
            pltpu.VMEM((devices, TILE, NF), BF16),
            pltpu.VMEM((devices, TILE, NF), BF16),
            pltpu.VMEM((devices * TILE, NF), F32),
            dma((13,)),
            dma,
            dma,
            dma,
            dma,
            dma((2, 3)),
            dma((2, 3)),
            pltpu.SemaphoreType.REGULAR,
            dma,
            dma,
        ],
        compiler_params=pltpu.CompilerParams(
            collective_id=0, has_side_effects=True, vmem_limit_bytes=60 * 2**20
        ),
        cost_estimate=pl.CostEstimate(
            flops=2 * 10**9, bytes_accessed=3 * 10**6, transcendentals=0
        ),
        name="exchange",
    )(syn, obs, table, first, second, mask, weight, owner, element)


def finish_kernel(summed, table_high, table_low, out, result, sems):
    components, elements, width = summed.shape
    count = components * elements
    samples = result.shape[1]
    chunk = samples // sems.shape[0]
    high, low = in_two(summed[...].reshape(count, width))
    parts = jnp.concatenate([high, low], axis=0)
    copies = []
    for n in range(sems.shape[0]):
        columns = pl.ds(n * chunk, chunk)
        both = dot_plain(parts, table_high[:, columns])
        result[:, columns] = both[:count] + (
            both[count:] + dot_plain(high, table_low[:, columns])
        )
        copies.append(
            pltpu.make_async_copy(result.at[:, columns], out.at[:, columns], sems.at[n])
        )
        copies[-1].start()
    for copy in copies:
        copy.wait()


def finish(summed, table_high, table_low):
    components, elements, width = summed.shape
    samples = table_high.shape[1]
    in_vmem = pl.BlockSpec(memory_space=pltpu.VMEM)
    out = pl.pallas_call(
        finish_kernel,
        out_shape=jax.ShapeDtypeStruct((components * elements, samples), F32),
        in_specs=[in_vmem] * 3,
        out_specs=pl.BlockSpec(memory_space=pl.ANY),
        scratch_shapes=[
            pltpu.VMEM((components * elements, samples), F32),
            pltpu.SemaphoreType.DMA((4,)),
        ],
        compiler_params=pltpu.CompilerParams(vmem_limit_bytes=40 * 2**20),
        cost_estimate=pl.CostEstimate(
            flops=7 * 10**8, bytes_accessed=3 * 10**6, transcendentals=0
        ),
        name="finish",
    )(summed, table_high, table_low)
    return out.reshape(components, elements, samples)


def on_device(
    blks,
    subs,
    synthetic,
    observed,
    pair_first,
    pair_second,
    pair_mask,
    pair_weight,
    station_owner,
    station_element,
):
    rows, _, samples = synthetic.shape
    forward, inverse = dft_tables(samples, NF)
    inverse_high = inverse.astype(jnp.bfloat16)
    inverse_low = (inverse - inverse_high.astype(np.float32)).astype(jnp.bfloat16)
    summed = exchange(
        blks,
        subs,
        jnp.transpose(synthetic, (1, 0, 2)),
        jnp.transpose(observed, (1, 0, 2)),
        jnp.asarray(forward),
        pair_first,
        pair_second,
        pair_mask,
        pair_weight,
        station_owner.reshape(1, rows),
        station_element.reshape(1, rows),
    )
    out = finish(summed, jnp.asarray(inverse_high), jnp.asarray(inverse_low))
    return jnp.transpose(out, (1, 0, 2))


def solution(mesh):
    blks, subs = mesh.shape["blk"], mesh.shape["sub"]
    return jax.shard_map(
        functools.partial(on_device, blks, subs),
        mesh=mesh,
        in_specs=(
            P(("blk", "sub"), None, None),
            P(("blk", "sub"), None, None),
            P("blk", "sub"),
            P("blk", "sub"),
            P("blk", "sub"),
            P("blk", "sub"),
            P(("blk", "sub"), None),
            P(("blk", "sub")),
        ),
        out_specs=P(("blk", "sub"), None, None),
        check_vma=False,
    )
```

```python
import functools
import itertools
import math

import jax
import jax.numpy as jnp
import numpy as np
from jax import lax
from jax.experimental import pallas as pl
from jax.experimental.pallas import tpu as pltpu
from jax.sharding import PartitionSpec as P

MESH = pl.DeviceIdType.MESH
NF = 128
BLOCK = 64
TILE = 16
F32 = jnp.float32
BF16 = jnp.bfloat16


def dft_tables(samples, freqs):
    phase = (np.arange(samples)[:, None] * np.arange(freqs)[None, :]) % samples
    angles = phase.astype(np.float64) * (2.0 * math.pi / samples)
    scale = 1.0 / math.sqrt(samples)
    cosine, sine = np.cos(angles) * scale, np.sin(angles) * scale
    forward = np.concatenate([cosine, -sine], axis=1).astype(np.float32)
    doubled = np.where(np.arange(freqs) == 0, 1.0, 2.0)[:, None]
    inverse = np.concatenate([cosine.T * doubled, -sine.T * doubled], axis=0)
    return forward.astype(jnp.bfloat16), inverse.astype(np.float32).astype(jnp.bfloat16)


def in_two(x):
    high = x.astype(BF16)
    return high, (x - high.astype(F32)).astype(BF16)


def dot_rows(a, b):
    return lax.dot_general(a, b, (((1,), (1,)), ((), ())), preferred_element_type=F32)


def dot_plain(a, b):
    return jnp.dot(a, b, preferred_element_type=F32)


def features(pair):
    xr, xi = pair[0][:, :NF].astype(F32), pair[0][:, NF:].astype(F32)
    o_r, o_i = pair[1][:, :NF].astype(F32), pair[1][:, NF:].astype(F32)
    dr, di = xr - o_r, xi - o_i
    parts = [dr * xr + di * xi, dr * xi - di * xr, o_r * xr + o_i * xi, o_r * xi - o_i * xr]
    both = [in_two(p) for p in parts]
    return jnp.concatenate(
        [jnp.concatenate([b[i] for b in both], axis=1) for i in range(2)], axis=0
    )


def for_features(links):
    high, low = in_two(links)
    return jnp.concatenate(
        [jnp.concatenate([high, high], axis=1), jnp.concatenate([low, low], axis=1)], axis=0
    )


def linked(links, values):
    rows = links.shape[0] // 2
    both = dot_plain(links, values)
    return both[:rows] + both[rows:]


def spread(rows, count, shift):
    index = lax.broadcasted_iota(jnp.int32, (count, NF), 0) + shift
    return jnp.concatenate(
        [(index == rows[s : s + 1]).astype(F32).astype(BF16) for s in range(rows.shape[0])], axis=1
    )


def spread_weights(rows, weights, count, shift):
    index = lax.broadcasted_iota(jnp.int32, (count, NF), 0) + shift
    parts = []
    for part in in_two(weights):
        wide = part.astype(F32)
        parts.append(
            jnp.concatenate(
                [
                    jnp.where(index == rows[s : s + 1], wide[s : s + 1], 0.0).astype(BF16)
                    for s in range(rows.shape[0])
                ],
                axis=1,
            )
        )
    return jnp.concatenate(parts, axis=0)


def spread_order():
    left = list(itertools.product(range(4), range(4), range(4), range(2)))[1:]
    ways = {0: (0.0, 0.0), 1: (1.0, 0.0), 2: (1.0, 1.0), 3: (0.0, 1.0)}

    def links(step):
        return np.array([way for axis in step[:3] for way in ways[axis]])

    used, order = np.zeros(6), []
    while left:
        step = min(left, key=lambda t: (np.max(used + links(t)), -np.sum(links(t)), t))
        left.remove(step)
        used = used + links(step)
        order.append(step)
    return order


def exchange_kernel(
    blks,
    subs,
    syn_hbm,
    obs_hbm,
    table_hbm,
    first_hbm,
    second_hbm,
    mask_hbm,
    weight_hbm,
    owner_hbm,
    element_hbm,
    summed,
    traces,
    table,
    first,
    second,
    mask,
    weight,
    owner,
    element,
    spec,
    halo,
    list_out,
    list_over,
    lists,
    lists_prev,
    wide,
    outgoing,
    received,
    wide_in,
    load_sems,
    list_send,
    list_recv,
    over_send,
    over_recv,
    halo_send,
    halo_recv,
    joined,
    all_send,
    all_recv,
):
    devices = blks * subs
    blk, sub = lax.axis_index("blk"), lax.axis_index("sub")
    me = blk * subs + sub
    rows = spec.shape[1]
    blocks = first.shape[0]
    def around(at, step, size):
        there = at + step
        return jnp.where(there >= size, there - size, there)

    subs_there = [around(sub, step, subs) for step in range(1, subs)]
    blks_there = [around(blk, step, blks) for step in range(1, blks)]
    blk_after, blk_before = blks_there[0], blks_there[-1]
    after = (jnp.where(sub == subs - 1, blk_after, blk), subs_there[0])
    before = (jnp.where(sub == 0, blk_before, blk), subs_there[-1])

    pairs = [
        (first_hbm, first),
        (second_hbm, second),
        (mask_hbm, mask),
        (weight_hbm, weight),
        (table_hbm, table),
        (syn_hbm.at[0], traces.at[0, pl.ds(0, rows)]),
        (obs_hbm.at[0], traces.at[0, pl.ds(rows, rows)]),
        (syn_hbm.at[1], traces.at[1, pl.ds(0, rows)]),
        (obs_hbm.at[1], traces.at[1, pl.ds(rows, rows)]),
        (syn_hbm.at[2], traces.at[2, pl.ds(0, rows)]),
        (obs_hbm.at[2], traces.at[2, pl.ds(rows, rows)]),
        (owner_hbm, owner),
        (element_hbm, element),
    ]
    loads = [
        pltpu.make_async_copy(src, dst, load_sems.at[i]) for i, (src, dst) in enumerate(pairs)
    ]
    for load in loads:
        load.start()

    barrier = pltpu.get_barrier_semaphore()

    def greet(there):
        pl.semaphore_signal(barrier, inc=1, device_id=there, device_id_type=MESH)

    for there in subs_there:
        greet((blk, there))
    for there in blks_there:
        greet((there, sub))

    @pl.when(sub == 0)
    def _():
        for s in range(1, subs):
            greet((blk_before, s))

    @pl.when(sub == subs - 1)
    def _():
        greet((blk_after, 0))

    for i in range(4):
        loads[i].wait()
    base = (blk * blocks + lax.broadcasted_iota(jnp.int32, (blocks, NF), 0)) * BLOCK
    code = ((first[...] - base) * (2 * BLOCK) + (second[...] - base)).astype(F32)
    slot_weight = weight[...] * mask[...].astype(F32)
    zero_row = jnp.zeros((1, NF), F32)
    for s in range(subs):
        lines = [max(2 * s - 1, 0), 2 * s, 2 * s + 1]
        list_out[s] = jnp.concatenate(
            [code[i : i + 1] for i in lines]
            + [slot_weight[i : i + 1] for i in lines]
            + [zero_row] * 2,
            axis=0,
        )
    list_over[...] = jnp.concatenate(
        [code[blocks - 1 : blocks]]
        + [zero_row] * 2
        + [slot_weight[blocks - 1 : blocks]]
        + [zero_row] * 4,
        axis=0,
    )
    lists[sub] = list_out[sub]

    pl.semaphore_wait(barrier, subs + blks - 1)
    for there in subs_there:
        pltpu.make_async_remote_copy(
            src_ref=list_out.at[there],
            dst_ref=lists.at[sub],
            send_sem=list_send,
            recv_sem=list_recv,
            device_id=(blk, there),
            device_id_type=MESH,
        ).start()
    over = pltpu.make_async_remote_copy(
        src_ref=list_over,
        dst_ref=lists_prev.at[sub],
        send_sem=over_send,
        recv_sem=over_recv,
        device_id=(blk_after, 0),
        device_id_type=MESH,
    )
    over.start()

    def transform(c):
        both = dot_plain(traces[c], table[...]).astype(BF16)
        spec[2 * c] = both[:rows]
        spec[2 * c + 1] = both[rows:]

    for i in range(4, 7):
        loads[i].wait()
    transform(0)

    def halo_copies(c):
        q = pl.ds(2 * c, 2)
        return [
            pltpu.make_async_remote_copy(
                src_ref=spec.at[q, pl.ds(0, BLOCK)],
                dst_ref=halo.at[q, pl.ds(BLOCK, BLOCK)],
                send_sem=halo_send.at[0, c],
                recv_sem=halo_recv.at[0, c],
                device_id=before,
                device_id_type=MESH,
            ),
            pltpu.make_async_remote_copy(
                src_ref=spec.at[q, pl.ds(rows - BLOCK, BLOCK)],
                dst_ref=halo.at[q, pl.ds(0, BLOCK)],
                send_sem=halo_send.at[1, c],
                recv_sem=halo_recv.at[1, c],
                device_id=after,
                device_id_type=MESH,
            ),
        ]

    halos = [halo_copies(c) for c in range(3)]
    for copy in halos[0]:
        copy.start()
    for c in (1, 2):
        loads[5 + 2 * c].wait()
        loads[6 + 2 * c].wait()
        transform(c)
        for copy in halos[c]:
            copy.start()

    for there in subs_there:
        pl.semaphore_signal(joined, inc=1, device_id=(blk, there), device_id_type=MESH)

    loads[11].wait()
    loads[12].wait()
    lane = lax.broadcasted_iota(jnp.int32, (rows, rows), 1)
    line = lax.broadcasted_iota(jnp.int32, (rows, rows), 0)
    owner_row = owner[...]
    owner_column = jnp.sum(jnp.where(lane == line, owner_row, 0), axis=1, keepdims=True)
    rank_row = jnp.sum(
        jnp.where((owner_column == owner_row) & (line < lane), 1, 0), axis=0, keepdims=True
    )
    slot = lax.broadcasted_iota(jnp.int32, (2 * devices, rows), 0)
    chosen = (slot == rank_row * devices + owner_row).astype(F32)
    placement = chosen.astype(BF16)
    label = jnp.sum(chosen * (element[...].astype(F32) - rows), axis=1, keepdims=True) + rows
    for k in range(2):
        mine = label[k * devices : (k + 1) * devices]
        wide[pl.ds(8 * k + 6, devices, stride=TILE), :] = jnp.broadcast_to(mine, (devices, NF))
        wide[pl.ds(8 * k + 7, devices, stride=TILE), :] = jnp.zeros((devices, NF), F32)

    def stations(c):
        return (spec[2 * c], spec[2 * c + 1])

    own = [features(stations(c)) for c in range(3)]

    others = pl.ds(0, subs - 1)
    pltpu.make_async_copy(lists.at[others], lists.at[others], list_recv).wait()

    @pl.when(sub == 0)
    def _():
        pltpu.make_async_copy(lists_prev, lists_prev, over_recv).wait()

    @pl.when(sub != 0)
    def _():
        lists_prev[...] = lists[...]

    def unpacked(ref, k):
        codes = ref[:, k, :].astype(jnp.int32)
        return codes >> 7, codes & 127, ref[:, 3 + k, :]

    first0, second0, weight0 = unpacked(lists_prev, 0)
    first1, second1, weight1 = unpacked(lists, 1)
    first2, second2, weight2 = unpacked(lists, 2)
    to_prev = dot_rows(spread_weights(second0, weight0, BLOCK, BLOCK), spread(first0, rows, 0))
    upper = dot_rows(spread(first1, BLOCK, 0), spread_weights(second1, weight1, rows, 0))
    lower = dot_rows(spread(first2, BLOCK, 0), spread_weights(second2, weight2, rows, 0))
    to_prev = to_prev[:BLOCK] + to_prev[BLOCK:]
    upper = upper[:, :rows] + upper[:, rows:]
    lower = lower[:, :rows] + lower[:, rows:]
    half = lax.broadcasted_iota(jnp.int32, (BLOCK, rows), 1) >= BLOCK
    inside = jnp.where(half, pltpu.roll(lower, BLOCK, 1), 0.0)
    one_way = jnp.concatenate([upper, inside], axis=0)
    link_own = for_features(one_way + one_way.T)
    link_halo = for_features(jnp.concatenate([to_prev, jnp.where(half, lower, 0.0)], axis=0))
    inner = [linked(link_own, own[c]) for c in range(3)]

    for c in range(3):
        for copy in halos[c]:
            copy.wait_recv()
        sums = inner[c] + linked(link_halo, features((halo[2 * c], halo[2 * c + 1])))
        g1r, g1i, g2r, g2i = (sums[:, i * NF : (i + 1) * NF] for i in range(4))
        x, o = stations(c)
        xr, xi = x[:, :NF].astype(F32), x[:, NF:].astype(F32)
        dr, di = xr - o[:, :NF].astype(F32), xi - o[:, NF:].astype(F32)
        real = (xr * g1r - xi * g1i) + (dr * g2r - di * g2i)
        imag = (xr * g1i + xi * g1r) + (dr * g2i + di * g2r)
        adjoint = jnp.concatenate([real, imag], axis=1).astype(BF16)
        moved = dot_plain(placement, adjoint)
        for k in range(2):
            for i in range(2):
                wide[pl.ds(8 * k + 2 * c + i, devices, stride=TILE), :] = moved[
                    k * devices : (k + 1) * devices, i * NF : (i + 1) * NF
                ]
    outgoing[...] = wide[...].astype(BF16).reshape(outgoing.shape)
    received[me] = outgoing[me]

    pl.semaphore_wait(joined, subs - 1)

    def turns(at, size):
        return [at] + [around(at, step, size) for step in range(1, size)]

    z_to, y_to = turns(lax.div(blk, 4), 4), turns(lax.rem(blk, 4), 4)
    x_to, core_to = turns(lax.div(sub, 2), 4), turns(lax.rem(sub, 2), 2)
    for dz, dy, dx, core in spread_order():
        blk_to, sub_to = z_to[dz] * 4 + y_to[dy], x_to[dx] * 2 + core_to[core]
        pltpu.make_async_remote_copy(
            src_ref=outgoing.at[blk_to * subs + sub_to],
            dst_ref=received.at[me],
            send_sem=all_send,
            recv_sem=all_recv,
            device_id=(blk_to, sub_to),
            device_id_type=MESH,
        ).start()

    most = pl.ds(0, devices - 1)
    pltpu.make_async_copy(received.at[most], received.at[most], all_recv).wait()
    wide_in[...] = received[...].astype(F32).reshape(wide_in.shape)

    def picked(row):
        return wide_in[pl.ds(row, devices, stride=TILE), :]

    labels = jnp.concatenate([picked(6), picked(14)], axis=0)
    element_lane = lax.broadcasted_iota(jnp.int32, (2 * devices, NF), 1).astype(F32)
    collect = (labels == element_lane).astype(F32).astype(BF16)
    for c in range(3):
        values = jnp.concatenate(
            [
                jnp.concatenate([picked(8 * k + 2 * c), picked(8 * k + 2 * c + 1)], axis=1)
                for k in range(2)
            ],
            axis=0,
        ).astype(BF16)
        summed[c] = lax.dot_general(
            collect, values, (((0,), (0,)), ((), ())), preferred_element_type=F32
        )

    for c in range(3):
        for copy in halos[c]:
            copy.wait_send()
    pltpu.make_async_copy(list_out.at[others], list_out.at[others], list_send).wait()
    over.wait_send()
    pltpu.make_async_copy(outgoing.at[most], outgoing.at[most], all_send).wait()


def exchange(blks, subs, syn, obs, table, first, second, mask, weight, owner, element):
    devices = blks * subs
    samples, rows = syn.shape[2], syn.shape[1]
    in_hbm = pl.BlockSpec(memory_space=pltpu.HBM)
    dma = pltpu.SemaphoreType.DMA
    return pl.pallas_call(
        functools.partial(exchange_kernel, blks, subs),
        out_shape=pltpu.VMEM((3, rows, 2 * NF), F32),
        in_specs=[in_hbm] * 9,
        out_specs=pl.BlockSpec(memory_space=pltpu.VMEM),
        scratch_shapes=[
            pltpu.VMEM((3, 2 * rows, samples), BF16),
            pltpu.VMEM(table.shape, BF16),
            pltpu.VMEM(first.shape, jnp.int32),
            pltpu.VMEM(second.shape, jnp.int32),
            pltpu.VMEM(mask.shape, jnp.int32),
            pltpu.VMEM(weight.shape, F32),
            pltpu.VMEM(owner.shape, jnp.int32),
            pltpu.VMEM(element.shape, jnp.int32),
            pltpu.VMEM((6, rows, 2 * NF), BF16),
            pltpu.VMEM((6, 2 * BLOCK, 2 * NF), BF16),
            pltpu.VMEM((subs, 8, NF), F32),
            pltpu.VMEM((8, NF), F32),
            pltpu.VMEM((subs, 8, NF), F32),
            pltpu.VMEM((subs, 8, NF), F32),
            pltpu.VMEM((devices * TILE, NF), F32),
            pltpu.VMEM((devices, TILE, NF), BF16),
            pltpu.VMEM((devices, TILE, NF), BF16),
            pltpu.VMEM((devices * TILE, NF), F32),
            dma((13,)),
            dma,
            dma,
            dma,
            dma,
            dma((2, 3)),
            dma((2, 3)),
            pltpu.SemaphoreType.REGULAR,
            dma,
            dma,
        ],
        compiler_params=pltpu.CompilerParams(
            collective_id=0, has_side_effects=True, vmem_limit_bytes=60 * 2**20
        ),
        cost_estimate=pl.CostEstimate(
            flops=2 * 10**9, bytes_accessed=3 * 10**6, transcendentals=0
        ),
        name="exchange",
    )(syn, obs, table, first, second, mask, weight, owner, element)


def finish_kernel(summed, table, out, result, sems):
    components, elements, width = summed.shape
    count = components * elements
    samples = result.shape[1]
    chunk = samples // sems.shape[0]
    values = summed[...].reshape(count, width).astype(BF16)
    copies = []
    for n in range(sems.shape[0]):
        columns = pl.ds(n * chunk, chunk)
        result[:, columns] = dot_plain(values, table[:, columns])
        copies.append(
            pltpu.make_async_copy(result.at[:, columns], out.at[:, columns], sems.at[n])
        )
        copies[-1].start()
    for copy in copies:
        copy.wait()


def finish(summed, table):
    components, elements, width = summed.shape
    samples = table.shape[1]
    in_vmem = pl.BlockSpec(memory_space=pltpu.VMEM)
    out = pl.pallas_call(
        finish_kernel,
        out_shape=jax.ShapeDtypeStruct((components * elements, samples), F32),
        in_specs=[in_vmem] * 2,
        out_specs=pl.BlockSpec(memory_space=pl.ANY),
        scratch_shapes=[
            pltpu.VMEM((components * elements, samples), F32),
            pltpu.SemaphoreType.DMA((4,)),
        ],
        compiler_params=pltpu.CompilerParams(vmem_limit_bytes=40 * 2**20),
        cost_estimate=pl.CostEstimate(
            flops=7 * 10**8, bytes_accessed=3 * 10**6, transcendentals=0
        ),
        name="finish",
    )(summed, table)
    return out.reshape(components, elements, samples)


def on_device(
    blks,
    subs,
    synthetic,
    observed,
    pair_first,
    pair_second,
    pair_mask,
    pair_weight,
    station_owner,
    station_element,
):
    rows, _, samples = synthetic.shape
    forward, inverse = dft_tables(samples, NF)
    summed = exchange(
        blks,
        subs,
        jnp.transpose(synthetic, (1, 0, 2)),
        jnp.transpose(observed, (1, 0, 2)),
        jnp.asarray(forward),
        pair_first,
        pair_second,
        pair_mask,
        pair_weight,
        station_owner.reshape(1, rows),
        station_element.reshape(1, rows),
    )
    out = finish(summed, jnp.asarray(inverse))
    return jnp.transpose(out, (1, 0, 2))


def solution(mesh):
    blks, subs = mesh.shape["blk"], mesh.shape["sub"]
    return jax.shard_map(
        functools.partial(on_device, blks, subs),
        mesh=mesh,
        in_specs=(
            P(("blk", "sub"), None, None),
            P(("blk", "sub"), None, None),
            P("blk", "sub"),
            P("blk", "sub"),
            P("blk", "sub"),
            P("blk", "sub"),
            P(("blk", "sub"), None),
            P(("blk", "sub")),
        ),
        out_specs=P(("blk", "sub"), None, None),
        check_vma=False,
    )
```

```python
import functools
import itertools
import math

import jax
import jax.numpy as jnp
import numpy as np
from jax import lax
from jax.experimental import pallas as pl
from jax.experimental.pallas import tpu as pltpu
from jax.sharding import PartitionSpec as P

MESH = pl.DeviceIdType.MESH
NF = 128
BLOCK = 64
F32 = jnp.float32
BF16 = jnp.bfloat16


def dft_tables(samples, freqs):
    phase = (np.arange(samples)[:, None] * np.arange(freqs)[None, :]) % samples
    angles = phase.astype(np.float64) * (2.0 * math.pi / samples)
    scale = 1.0 / math.sqrt(samples)
    cosine, sine = np.cos(angles) * scale, np.sin(angles) * scale
    forward = np.concatenate([cosine, -sine], axis=1).astype(np.float32)
    doubled = np.where(np.arange(freqs) == 0, 1.0, 2.0)[:, None]
    inverse = np.concatenate([cosine.T * doubled, -sine.T * doubled], axis=0)
    return forward.astype(jnp.bfloat16), inverse.astype(np.float32).astype(jnp.bfloat16)


def in_two(x):
    high = x.astype(BF16)
    return high, (x - high.astype(F32)).astype(BF16)


def dot_rows(a, b):
    return lax.dot_general(a, b, (((1,), (1,)), ((), ())), preferred_element_type=F32)


def dot_plain(a, b):
    return jnp.dot(a, b, preferred_element_type=F32)


def features(pair):
    xr, xi = pair[0][:, :NF].astype(F32), pair[0][:, NF:].astype(F32)
    o_r, o_i = pair[1][:, :NF].astype(F32), pair[1][:, NF:].astype(F32)
    dr, di = xr - o_r, xi - o_i
    parts = [dr * xr + di * xi, dr * xi - di * xr, o_r * xr + o_i * xi, o_r * xi - o_i * xr]
    both = [in_two(p) for p in parts]
    return jnp.concatenate(
        [jnp.concatenate([b[i] for b in both], axis=1) for i in range(2)], axis=0
    )


def for_features(links):
    high, low = in_two(links)
    return jnp.concatenate(
        [jnp.concatenate([high, high], axis=1), jnp.concatenate([low, low], axis=1)], axis=0
    )


def linked(links, values):
    rows = links.shape[0] // 2
    both = dot_plain(links, values)
    return both[:rows] + both[rows:]


def spread(rows, count, shift):
    index = lax.broadcasted_iota(jnp.int32, (count, NF), 0) + shift
    return jnp.concatenate(
        [(index == rows[s : s + 1]).astype(F32).astype(BF16) for s in range(rows.shape[0])], axis=1
    )


def spread_weights(rows, weights, count, shift):
    index = lax.broadcasted_iota(jnp.int32, (count, NF), 0) + shift
    parts = []
    for part in in_two(weights):
        wide = part.astype(F32)
        parts.append(
            jnp.concatenate(
                [
                    jnp.where(index == rows[s : s + 1], wide[s : s + 1], 0.0).astype(BF16)
                    for s in range(rows.shape[0])
                ],
                axis=1,
            )
        )
    return jnp.concatenate(parts, axis=0)


def spread_order():
    left = list(itertools.product(range(4), range(4), range(4), range(2)))[1:]
    ways = {0: (0.0, 0.0), 1: (1.0, 0.0), 2: (1.0, 1.0), 3: (0.0, 1.0)}

    def links(step):
        return np.array([way for axis in step[:3] for way in ways[axis]])

    used, order = np.zeros(6), []
    while left:
        step = min(left, key=lambda t: (np.max(used + links(t)), -np.sum(links(t)), t))
        left.remove(step)
        used = used + links(step)
        order.append(step)
    return order


def exchange_kernel(
    blks,
    subs,
    syn_hbm,
    obs_hbm,
    table_hbm,
    first_hbm,
    second_hbm,
    mask_hbm,
    weight_hbm,
    owner_hbm,
    element_hbm,
    summed,
    traces,
    table,
    first,
    second,
    mask,
    weight,
    owner,
    element,
    spec,
    halo,
    list_out,
    list_over,
    lists,
    lists_prev,
    near_out,
    near_labels,
    far_out,
    labels,
    outgoing,
    received,
    load_sems,
    list_send,
    list_recv,
    over_send,
    over_recv,
    halo_send,
    halo_recv,
    joined,
    near_send,
    near_recv,
    far_send,
    far_recv,
    all_send,
    all_recv,
):
    devices = blks * subs
    blk, sub = lax.axis_index("blk"), lax.axis_index("sub")
    me = blk * subs + sub
    rows = spec.shape[1]
    blocks = first.shape[0]
    def around(at, step, size):
        there = at + step
        return jnp.where(there >= size, there - size, there)

    subs_there = [around(sub, step, subs) for step in range(1, subs)]
    blks_there = [around(blk, step, blks) for step in range(1, blks)]
    blk_after, blk_before = blks_there[0], blks_there[-1]
    after = (jnp.where(sub == subs - 1, blk_after, blk), subs_there[0])
    before = (jnp.where(sub == 0, blk_before, blk), subs_there[-1])

    pairs = [
        (first_hbm, first),
        (second_hbm, second),
        (mask_hbm, mask),
        (weight_hbm, weight),
        (table_hbm, table),
        (syn_hbm.at[0], traces.at[0, pl.ds(0, rows)]),
        (obs_hbm.at[0], traces.at[0, pl.ds(rows, rows)]),
        (syn_hbm.at[1], traces.at[1, pl.ds(0, rows)]),
        (obs_hbm.at[1], traces.at[1, pl.ds(rows, rows)]),
        (syn_hbm.at[2], traces.at[2, pl.ds(0, rows)]),
        (obs_hbm.at[2], traces.at[2, pl.ds(rows, rows)]),
        (owner_hbm, owner),
        (element_hbm, element),
    ]
    loads = [
        pltpu.make_async_copy(src, dst, load_sems.at[i]) for i, (src, dst) in enumerate(pairs)
    ]
    for load in loads:
        load.start()

    barrier = pltpu.get_barrier_semaphore()

    def greet(there):
        pl.semaphore_signal(barrier, inc=1, device_id=there, device_id_type=MESH)

    for there in subs_there:
        greet((blk, there))
    for there in blks_there:
        greet((there, sub))

    @pl.when(sub == 0)
    def _():
        for s in range(1, subs):
            greet((blk_before, s))

    @pl.when(sub == subs - 1)
    def _():
        greet((blk_after, 0))

    for i in range(4):
        loads[i].wait()
    base = (blk * blocks + lax.broadcasted_iota(jnp.int32, (blocks, NF), 0)) * BLOCK
    code = ((first[...] - base) * (2 * BLOCK) + (second[...] - base)).astype(F32)
    slot_weight = weight[...] * mask[...].astype(F32)
    zero_row = jnp.zeros((1, NF), F32)
    for s in range(subs):
        lines = [max(2 * s - 1, 0), 2 * s, 2 * s + 1]
        list_out[s] = jnp.concatenate(
            [code[i : i + 1] for i in lines]
            + [slot_weight[i : i + 1] for i in lines]
            + [zero_row] * 2,
            axis=0,
        )
    list_over[...] = jnp.concatenate(
        [code[blocks - 1 : blocks]]
        + [zero_row] * 2
        + [slot_weight[blocks - 1 : blocks]]
        + [zero_row] * 4,
        axis=0,
    )
    lists[sub] = list_out[sub]

    pl.semaphore_wait(barrier, subs + blks - 1)
    for there in subs_there:
        pltpu.make_async_remote_copy(
            src_ref=list_out.at[there],
            dst_ref=lists.at[sub],
            send_sem=list_send,
            recv_sem=list_recv,
            device_id=(blk, there),
            device_id_type=MESH,
        ).start()
    over = pltpu.make_async_remote_copy(
        src_ref=list_over,
        dst_ref=lists_prev.at[sub],
        send_sem=over_send,
        recv_sem=over_recv,
        device_id=(blk_after, 0),
        device_id_type=MESH,
    )
    over.start()

    def transform(c):
        both = dot_plain(traces[c], table[...]).astype(BF16)
        spec[2 * c] = both[:rows]
        spec[2 * c + 1] = both[rows:]

    for i in range(4, 7):
        loads[i].wait()
    transform(0)

    def halo_copies(c):
        q = pl.ds(2 * c, 2)
        return [
            pltpu.make_async_remote_copy(
                src_ref=spec.at[q, pl.ds(0, BLOCK)],
                dst_ref=halo.at[q, pl.ds(BLOCK, BLOCK)],
                send_sem=halo_send.at[0, c],
                recv_sem=halo_recv.at[0, c],
                device_id=before,
                device_id_type=MESH,
            ),
            pltpu.make_async_remote_copy(
                src_ref=spec.at[q, pl.ds(rows - BLOCK, BLOCK)],
                dst_ref=halo.at[q, pl.ds(0, BLOCK)],
                send_sem=halo_send.at[1, c],
                recv_sem=halo_recv.at[1, c],
                device_id=after,
                device_id_type=MESH,
            ),
        ]

    halos = [halo_copies(c) for c in range(3)]
    for copy in halos[0]:
        copy.start()
    for c in (1, 2):
        loads[5 + 2 * c].wait()
        loads[6 + 2 * c].wait()
        transform(c)
        for copy in halos[c]:
            copy.start()

    for there in subs_there:
        pl.semaphore_signal(joined, inc=1, device_id=(blk, there), device_id_type=MESH)

    loads[11].wait()
    loads[12].wait()
    lane = lax.broadcasted_iota(jnp.int32, (rows, rows), 1)
    line = lax.broadcasted_iota(jnp.int32, (rows, rows), 0)
    owner_row = owner[...]

    def column(row):
        return jnp.sum(jnp.where(lane == line, row, 0), axis=1, keepdims=True)

    owner_column, element_column = column(owner_row), column(element[...]).astype(F32)
    same = owner_column == owner_row
    rank_column = jnp.sum(jnp.where(same & (lane < line), 1, 0), axis=1, keepdims=True)
    label_rows = []
    for k in range(2):
        chosen = ((owner_column == lane) & (rank_column == k)).astype(F32)
        label_rows.append(
            jnp.sum(chosen * (element_column - rows), axis=0, keepdims=True) + float(rows)
        )
    near_out[...] = jnp.concatenate(label_rows + [zero_row] * 6, axis=0)
    near_labels[sub] = near_out[...]
    for there in subs_there:
        pltpu.make_async_remote_copy(
            src_ref=near_out,
            dst_ref=near_labels.at[sub],
            send_sem=near_send,
            recv_sem=near_recv,
            device_id=(blk, there),
            device_id_type=MESH,
        ).start()

    rank_row = jnp.sum(jnp.where(same & (line < lane), 1, 0), axis=0, keepdims=True)
    target = owner_row * 4 + rank_row * 2
    slot = lax.broadcasted_iota(jnp.int32, (4 * devices, 2 * rows), 0)
    placement = (slot == jnp.concatenate([target, target + 1], axis=1)).astype(F32).astype(BF16)

    def stations(c):
        return (spec[2 * c], spec[2 * c + 1])

    own = [features(stations(c)) for c in range(3)]

    others = pl.ds(0, subs - 1)
    pltpu.make_async_copy(lists.at[others], lists.at[others], list_recv).wait()

    @pl.when(sub == 0)
    def _():
        pltpu.make_async_copy(lists_prev, lists_prev, over_recv).wait()

    @pl.when(sub != 0)
    def _():
        lists_prev[...] = lists[...]

    def unpacked(ref, k):
        codes = ref[:, k, :].astype(jnp.int32)
        return codes >> 7, codes & 127, ref[:, 3 + k, :]

    first0, second0, weight0 = unpacked(lists_prev, 0)
    first1, second1, weight1 = unpacked(lists, 1)
    first2, second2, weight2 = unpacked(lists, 2)
    to_prev = dot_rows(spread_weights(second0, weight0, BLOCK, BLOCK), spread(first0, rows, 0))
    upper = dot_rows(spread(first1, BLOCK, 0), spread_weights(second1, weight1, rows, 0))
    lower = dot_rows(spread(first2, BLOCK, 0), spread_weights(second2, weight2, rows, 0))
    to_prev = to_prev[:BLOCK] + to_prev[BLOCK:]
    upper = upper[:, :rows] + upper[:, rows:]
    lower = lower[:, :rows] + lower[:, rows:]
    half = lax.broadcasted_iota(jnp.int32, (BLOCK, rows), 1) >= BLOCK
    inside = jnp.where(half, pltpu.roll(lower, BLOCK, 1), 0.0)
    one_way = jnp.concatenate([upper, inside], axis=0)
    link_own = for_features(one_way + one_way.T)
    link_halo = for_features(jnp.concatenate([to_prev, jnp.where(half, lower, 0.0)], axis=0))
    inner = [linked(link_own, own[c]) for c in range(3)]

    pltpu.make_async_copy(near_labels.at[others], near_labels.at[others], near_recv).wait()
    far_out[...] = jnp.concatenate(
        [near_labels[:, 0, :], near_labels[:, 1, :]], axis=0
    ).astype(BF16)
    labels[blk] = far_out[...]
    for there in blks_there:
        pltpu.make_async_remote_copy(
            src_ref=far_out,
            dst_ref=labels.at[blk],
            send_sem=far_send,
            recv_sem=far_recv,
            device_id=(there, sub),
            device_id_type=MESH,
        ).start()

    for c in range(3):
        for copy in halos[c]:
            copy.wait_recv()
        sums = inner[c] + linked(link_halo, features((halo[2 * c], halo[2 * c + 1])))
        g1r, g1i, g2r, g2i = (sums[:, i * NF : (i + 1) * NF] for i in range(4))
        x, o = stations(c)
        xr, xi = x[:, :NF].astype(F32), x[:, NF:].astype(F32)
        dr, di = xr - o[:, :NF].astype(F32), xi - o[:, NF:].astype(F32)
        real = (xr * g1r - xi * g1i) + (dr * g2r - di * g2i)
        imag = (xr * g1i + xi * g1r) + (dr * g2i + di * g2r)
        adjoint = jnp.concatenate([real, imag], axis=0).astype(BF16)
        outgoing[:, c] = dot_plain(placement, adjoint).astype(BF16).reshape(devices, 4, NF)
    received[me] = outgoing[me]

    pl.semaphore_wait(joined, subs - 1)

    def turns(at, size):
        return [at] + [around(at, step, size) for step in range(1, size)]

    z_to, y_to = turns(lax.div(blk, 4), 4), turns(lax.rem(blk, 4), 4)
    x_to, core_to = turns(lax.div(sub, 2), 4), turns(lax.rem(sub, 2), 2)
    for dz, dy, dx, core in spread_order():
        blk_to, sub_to = z_to[dz] * 4 + y_to[dy], x_to[dx] * 2 + core_to[core]
        pltpu.make_async_remote_copy(
            src_ref=outgoing.at[blk_to * subs + sub_to],
            dst_ref=received.at[me],
            send_sem=all_send,
            recv_sem=all_recv,
            device_id=(blk_to, sub_to),
            device_id_type=MESH,
        ).start()

    some = pl.ds(0, blks - 1)
    pltpu.make_async_copy(labels.at[some], labels.at[some], far_recv).wait()
    by_owner = labels[...].reshape(2 * devices, NF)
    arrived = lax.broadcasted_iota(jnp.int32, (2 * devices, 4 * devices), 1)
    held = lax.broadcasted_iota(jnp.int32, (2 * devices, 4 * devices), 0)
    sub_bits = subs.bit_length() - 1
    wanted = (
        ((arrived >> (sub_bits + 2)) << (sub_bits + 1))
        + (((arrived >> 1) & 1) << sub_bits)
        + ((arrived >> 2) & (subs - 1))
    )
    repeated = lax.dot_general(
        by_owner,
        (held == wanted).astype(F32).astype(BF16),
        (((0,), (0,)), ((), ())),
        preferred_element_type=F32,
    )
    owner_line = lax.broadcasted_iota(jnp.int32, repeated.shape, 0)
    label = jnp.sum(jnp.where(owner_line == me, repeated, 0.0), axis=0, keepdims=True)
    collect = jnp.concatenate(
        [
            ((label == owner_line.astype(F32)) & ((arrived[:rows] & 1) == i)).astype(F32)
            for i in range(2)
        ],
        axis=0,
    ).astype(BF16)
    most = pl.ds(0, devices - 1)
    pltpu.make_async_copy(received.at[most], received.at[most], all_recv).wait()
    for c in range(3):
        sums = dot_plain(collect, received[:, c].reshape(4 * devices, NF)).astype(BF16)
        summed[c * rows : (c + 1) * rows, :NF] = sums[:rows]
        summed[c * rows : (c + 1) * rows, NF:] = sums[rows:]

    for c in range(3):
        for copy in halos[c]:
            copy.wait_send()
    pltpu.make_async_copy(list_out.at[others], list_out.at[others], list_send).wait()
    over.wait_send()
    pltpu.make_async_copy(near_labels.at[others], near_labels.at[others], near_send).wait()
    pltpu.make_async_copy(labels.at[some], labels.at[some], far_send).wait()
    pltpu.make_async_copy(outgoing.at[most], outgoing.at[most], all_send).wait()


def exchange(blks, subs, syn, obs, table, first, second, mask, weight, owner, element):
    devices = blks * subs
    samples, rows = syn.shape[2], syn.shape[1]
    in_hbm = pl.BlockSpec(memory_space=pltpu.HBM)
    dma = pltpu.SemaphoreType.DMA
    return pl.pallas_call(
        functools.partial(exchange_kernel, blks, subs),
        out_shape=pltpu.VMEM((3 * rows, 2 * NF), BF16),
        in_specs=[in_hbm] * 9,
        out_specs=pl.BlockSpec(memory_space=pltpu.VMEM),
        scratch_shapes=[
            pltpu.VMEM((3, 2 * rows, samples), BF16),
            pltpu.VMEM(table.shape, BF16),
            pltpu.VMEM(first.shape, jnp.int32),
            pltpu.VMEM(second.shape, jnp.int32),
            pltpu.VMEM(mask.shape, jnp.int32),
            pltpu.VMEM(weight.shape, F32),
            pltpu.VMEM(owner.shape, jnp.int32),
            pltpu.VMEM(element.shape, jnp.int32),
            pltpu.VMEM((6, rows, 2 * NF), BF16),
            pltpu.VMEM((6, 2 * BLOCK, 2 * NF), BF16),
            pltpu.VMEM((subs, 8, NF), F32),
            pltpu.VMEM((8, NF), F32),
            pltpu.VMEM((subs, 8, NF), F32),
            pltpu.VMEM((subs, 8, NF), F32),
            pltpu.VMEM((8, NF), F32),
            pltpu.VMEM((subs, 8, NF), F32),
            pltpu.VMEM((2 * subs, NF), BF16),
            pltpu.VMEM((blks, 2 * subs, NF), BF16),
            pltpu.VMEM((devices, 3, 4, NF), BF16),
            pltpu.VMEM((devices, 3, 4, NF), BF16),
            dma((13,)),
            dma,
            dma,
            dma,
            dma,
            dma((2, 3)),
            dma((2, 3)),
            pltpu.SemaphoreType.REGULAR,
            dma,
            dma,
            dma,
            dma,
            dma,
            dma,
        ],
        compiler_params=pltpu.CompilerParams(
            collective_id=0, has_side_effects=True, vmem_limit_bytes=60 * 2**20
        ),
        cost_estimate=pl.CostEstimate(
            flops=2 * 10**9, bytes_accessed=3 * 10**6, transcendentals=0
        ),
        name="exchange",
    )(syn, obs, table, first, second, mask, weight, owner, element)


def finish_kernel(summed, table, out, result, sems):
    samples = result.shape[1]
    chunk = samples // sems.shape[0]
    copies = []
    for n in range(sems.shape[0]):
        columns = pl.ds(n * chunk, chunk)
        result[:, columns] = dot_plain(summed[...], table[:, columns])
        copies.append(
            pltpu.make_async_copy(result.at[:, columns], out.at[:, columns], sems.at[n])
        )
        copies[-1].start()
    for copy in copies:
        copy.wait()


def finish(summed, table):
    count, samples = summed.shape[0], table.shape[1]
    in_vmem = pl.BlockSpec(memory_space=pltpu.VMEM)
    out = pl.pallas_call(
        finish_kernel,
        out_shape=jax.ShapeDtypeStruct((count, samples), F32),
        in_specs=[in_vmem] * 2,
        out_specs=pl.BlockSpec(memory_space=pl.ANY),
        scratch_shapes=[
            pltpu.VMEM((count, samples), F32),
            pltpu.SemaphoreType.DMA((4,)),
        ],
        compiler_params=pltpu.CompilerParams(vmem_limit_bytes=40 * 2**20),
        cost_estimate=pl.CostEstimate(
            flops=7 * 10**8, bytes_accessed=3 * 10**6, transcendentals=0
        ),
        name="finish",
    )(summed, table)
    return out.reshape(3, count // 3, samples)


def on_device(
    blks,
    subs,
    synthetic,
    observed,
    pair_first,
    pair_second,
    pair_mask,
    pair_weight,
    station_owner,
    station_element,
):
    rows, _, samples = synthetic.shape
    forward, inverse = dft_tables(samples, NF)
    summed = exchange(
        blks,
        subs,
        jnp.transpose(synthetic, (1, 0, 2)),
        jnp.transpose(observed, (1, 0, 2)),
        jnp.asarray(forward),
        pair_first,
        pair_second,
        pair_mask,
        pair_weight,
        station_owner.reshape(1, rows),
        station_element.reshape(1, rows),
    )
    out = finish(summed, jnp.asarray(inverse))
    return jnp.transpose(out, (1, 0, 2))


def solution(mesh):
    blks, subs = mesh.shape["blk"], mesh.shape["sub"]
    return jax.shard_map(
        functools.partial(on_device, blks, subs),
        mesh=mesh,
        in_specs=(
            P(("blk", "sub"), None, None),
            P(("blk", "sub"), None, None),
            P("blk", "sub"),
            P("blk", "sub"),
            P("blk", "sub"),
            P("blk", "sub"),
            P(("blk", "sub"), None),
            P(("blk", "sub")),
        ),
        out_specs=P(("blk", "sub"), None, None),
        check_vma=False,
    )
```

```python
import functools
import itertools
import math

import jax
import jax.numpy as jnp
import numpy as np
from jax import lax
from jax.experimental import pallas as pl
from jax.experimental.pallas import tpu as pltpu
from jax.sharding import PartitionSpec as P

MESH = pl.DeviceIdType.MESH
NF = 128
BLOCK = 64
F32 = jnp.float32
BF16 = jnp.bfloat16


def dft_tables(samples, freqs):
    phase = (np.arange(samples)[:, None] * np.arange(freqs)[None, :]) % samples
    angles = phase.astype(np.float64) * (2.0 * math.pi / samples)
    scale = 1.0 / math.sqrt(samples)
    cosine, sine = np.cos(angles) * scale, np.sin(angles) * scale
    forward = np.concatenate([cosine, -sine], axis=1).astype(np.float32)
    doubled = np.where(np.arange(freqs) == 0, 1.0, 2.0)[:, None]
    inverse = np.concatenate([cosine.T * doubled, -sine.T * doubled], axis=0)
    return forward.astype(jnp.bfloat16), inverse.astype(np.float32).astype(jnp.bfloat16)


def in_two(x):
    high = x.astype(BF16)
    return high, (x - high.astype(F32)).astype(BF16)


def dot_rows(a, b):
    return lax.dot_general(a, b, (((1,), (1,)), ((), ())), preferred_element_type=F32)


def dot_plain(a, b):
    return jnp.dot(a, b, preferred_element_type=F32)


def features(pair):
    xr, xi = pair[0][:, :NF].astype(F32), pair[0][:, NF:].astype(F32)
    o_r, o_i = pair[1][:, :NF].astype(F32), pair[1][:, NF:].astype(F32)
    dr, di = xr - o_r, xi - o_i
    parts = [dr * xr + di * xi, dr * xi - di * xr, o_r * xr + o_i * xi, o_r * xi - o_i * xr]
    both = [in_two(p) for p in parts]
    return jnp.concatenate(
        [jnp.concatenate([b[i] for b in both], axis=1) for i in range(2)], axis=0
    )


def for_features(links):
    high, low = in_two(links)
    return jnp.concatenate(
        [jnp.concatenate([high, high], axis=1), jnp.concatenate([low, low], axis=1)], axis=0
    )


def linked(links, values):
    rows = links.shape[0] // 2
    both = dot_plain(links, values)
    return both[:rows] + both[rows:]


def spread(rows, count, shift):
    index = lax.broadcasted_iota(jnp.int32, (count, NF), 0) + shift
    return jnp.concatenate(
        [(index == rows[s : s + 1]).astype(F32).astype(BF16) for s in range(rows.shape[0])], axis=1
    )


def spread_weights(rows, weights, count, shift):
    index = lax.broadcasted_iota(jnp.int32, (count, NF), 0) + shift
    parts = []
    for part in in_two(weights):
        wide = part.astype(F32)
        parts.append(
            jnp.concatenate(
                [
                    jnp.where(index == rows[s : s + 1], wide[s : s + 1], 0.0).astype(BF16)
                    for s in range(rows.shape[0])
                ],
                axis=1,
            )
        )
    return jnp.concatenate(parts, axis=0)


def spread_order():
    left = list(itertools.product(range(4), range(4), range(4), range(2)))[1:]
    ways = {0: (0.0, 0.0), 1: (1.0, 0.0), 2: (1.0, 1.0), 3: (0.0, 1.0)}

    def links(step):
        return np.array([way for axis in step[:3] for way in ways[axis]])

    used, order = np.zeros(6), []
    while left:
        step = min(left, key=lambda t: (np.max(used + links(t)), -np.sum(links(t)), t))
        left.remove(step)
        used = used + links(step)
        order.append(step)
    return order


def exchange_kernel(
    blks,
    subs,
    syn_hbm,
    obs_hbm,
    table_hbm,
    first_hbm,
    second_hbm,
    mask_hbm,
    weight_hbm,
    owner_hbm,
    element_hbm,
    summed,
    traces,
    table,
    first,
    second,
    mask,
    weight,
    owner,
    element,
    spec,
    halo,
    list_out,
    list_over,
    lists,
    lists_prev,
    labels,
    outgoing,
    received,
    load_sems,
    list_send,
    list_recv,
    over_send,
    over_recv,
    halo_send,
    halo_recv,
    joined,
    y_send,
    y_recv,
    z_send,
    z_recv,
    all_send,
    all_recv,
):
    devices = blks * subs
    blk, sub = lax.axis_index("blk"), lax.axis_index("sub")
    me = blk * subs + sub
    rows = spec.shape[1]
    blocks = first.shape[0]
    def around(at, step, size):
        there = at + step
        return jnp.where(there >= size, there - size, there)

    subs_there = [around(sub, step, subs) for step in range(1, subs)]
    blks_there = [around(blk, step, blks) for step in range(1, blks)]
    blk_after, blk_before = blks_there[0], blks_there[-1]
    after = (jnp.where(sub == subs - 1, blk_after, blk), subs_there[0])
    before = (jnp.where(sub == 0, blk_before, blk), subs_there[-1])

    pairs = [
        (owner_hbm, owner),
        (element_hbm, element),
        (first_hbm, first),
        (second_hbm, second),
        (mask_hbm, mask),
        (weight_hbm, weight),
        (table_hbm, table),
        (syn_hbm.at[0], traces.at[0, pl.ds(0, rows)]),
        (obs_hbm.at[0], traces.at[0, pl.ds(rows, rows)]),
        (syn_hbm.at[1], traces.at[1, pl.ds(0, rows)]),
        (obs_hbm.at[1], traces.at[1, pl.ds(rows, rows)]),
        (syn_hbm.at[2], traces.at[2, pl.ds(0, rows)]),
        (obs_hbm.at[2], traces.at[2, pl.ds(rows, rows)]),
    ]
    loads = [
        pltpu.make_async_copy(src, dst, load_sems.at[i]) for i, (src, dst) in enumerate(pairs)
    ]
    for load in loads:
        load.start()

    barrier = pltpu.get_barrier_semaphore()

    def greet(there):
        pl.semaphore_signal(barrier, inc=1, device_id=there, device_id_type=MESH)

    for there in subs_there:
        greet((blk, there))
    for there in blks_there:
        greet((there, sub))

    @pl.when(sub == 0)
    def _():
        for s in range(1, subs):
            greet((blk_before, s))

    @pl.when(sub == subs - 1)
    def _():
        greet((blk_after, 0))

    for i in range(2):
        loads[i].wait()
    lane = lax.broadcasted_iota(jnp.int32, (rows, rows), 1)
    line = lax.broadcasted_iota(jnp.int32, (rows, rows), 0)
    owner_row = owner[...]

    def column(row):
        return jnp.sum(jnp.where(lane == line, row, 0), axis=1, keepdims=True)

    owner_column, element_column = column(owner_row), column(element[...]).astype(F32)
    same = owner_column == owner_row
    rank_column = jnp.sum(jnp.where(same & (lane < line), 1, 0), axis=1, keepdims=True)
    label_rows = []
    for k in range(2):
        chosen = ((owner_column == lane) & (rank_column == k)).astype(F32)
        label_rows.append(
            jnp.sum(chosen * (element_column - rows), axis=0, keepdims=True) + float(rows)
        )

    for i in range(2, 6):
        loads[i].wait()
    base = (blk * blocks + lax.broadcasted_iota(jnp.int32, (blocks, NF), 0)) * BLOCK
    code = ((first[...] - base) * (2 * BLOCK) + (second[...] - base)).astype(F32)
    slot_weight = weight[...] * mask[...].astype(F32)
    zero_row = jnp.zeros((1, NF), F32)
    for s in range(subs):
        lines = [max(2 * s - 1, 0), 2 * s, 2 * s + 1]
        list_out[s] = jnp.concatenate(
            [code[i : i + 1] for i in lines]
            + [slot_weight[i : i + 1] for i in lines]
            + label_rows,
            axis=0,
        )
    list_over[...] = jnp.concatenate(
        [code[blocks - 1 : blocks]]
        + [zero_row] * 2
        + [slot_weight[blocks - 1 : blocks]]
        + [zero_row] * 4,
        axis=0,
    )
    lists[sub] = list_out[sub]

    pl.semaphore_wait(barrier, subs + blks - 1)
    for there in subs_there:
        pltpu.make_async_remote_copy(
            src_ref=list_out.at[there],
            dst_ref=lists.at[sub],
            send_sem=list_send,
            recv_sem=list_recv,
            device_id=(blk, there),
            device_id_type=MESH,
        ).start()
    over = pltpu.make_async_remote_copy(
        src_ref=list_over,
        dst_ref=lists_prev.at[sub],
        send_sem=over_send,
        recv_sem=over_recv,
        device_id=(blk_after, 0),
        device_id_type=MESH,
    )
    over.start()

    def transform(c):
        both = dot_plain(traces[c], table[...]).astype(BF16)
        spec[2 * c] = both[:rows]
        spec[2 * c + 1] = both[rows:]

    for i in range(6, 9):
        loads[i].wait()
    transform(0)

    def halo_copies(c):
        q = pl.ds(2 * c, 2)
        return [
            pltpu.make_async_remote_copy(
                src_ref=spec.at[q, pl.ds(0, BLOCK)],
                dst_ref=halo.at[q, pl.ds(BLOCK, BLOCK)],
                send_sem=halo_send.at[0, c],
                recv_sem=halo_recv.at[0, c],
                device_id=before,
                device_id_type=MESH,
            ),
            pltpu.make_async_remote_copy(
                src_ref=spec.at[q, pl.ds(rows - BLOCK, BLOCK)],
                dst_ref=halo.at[q, pl.ds(0, BLOCK)],
                send_sem=halo_send.at[1, c],
                recv_sem=halo_recv.at[1, c],
                device_id=after,
                device_id_type=MESH,
            ),
        ]

    halos = [halo_copies(c) for c in range(3)]
    for copy in halos[0]:
        copy.start()
    for c in (1, 2):
        loads[7 + 2 * c].wait()
        loads[8 + 2 * c].wait()
        transform(c)
        for copy in halos[c]:
            copy.start()

    for there in subs_there:
        pl.semaphore_signal(joined, inc=1, device_id=(blk, there), device_id_type=MESH)

    rank_row = jnp.sum(jnp.where(same & (line < lane), 1, 0), axis=0, keepdims=True)
    target = owner_row * 4 + rank_row * 2
    slot = lax.broadcasted_iota(jnp.int32, (4 * devices, 2 * rows), 0)
    placement = (slot == jnp.concatenate([target, target + 1], axis=1)).astype(F32).astype(BF16)

    def stations(c):
        return (spec[2 * c], spec[2 * c + 1])

    own = [features(stations(c)) for c in range(3)]

    others = pl.ds(0, subs - 1)
    pltpu.make_async_copy(lists.at[others], lists.at[others], list_recv).wait()

    z, y = lax.div(blk, 4), lax.rem(blk, 4)
    labels[z, y] = jnp.concatenate([lists[:, 6, :], lists[:, 7, :]], axis=0).astype(BF16)
    for step in range(1, 4):
        pltpu.make_async_remote_copy(
            src_ref=labels.at[z, y],
            dst_ref=labels.at[z, y],
            send_sem=y_send,
            recv_sem=y_recv,
            device_id=(z * 4 + around(y, step, 4), sub),
            device_id_type=MESH,
        ).start()

    @pl.when(sub == 0)
    def _():
        pltpu.make_async_copy(lists_prev, lists_prev, over_recv).wait()

    @pl.when(sub != 0)
    def _():
        lists_prev[...] = lists[...]

    def unpacked(ref, k):
        codes = ref[:, k, :].astype(jnp.int32)
        return codes >> 7, codes & 127, ref[:, 3 + k, :]

    first0, second0, weight0 = unpacked(lists_prev, 0)
    first1, second1, weight1 = unpacked(lists, 1)
    first2, second2, weight2 = unpacked(lists, 2)
    to_prev = dot_rows(spread_weights(second0, weight0, BLOCK, BLOCK), spread(first0, rows, 0))
    upper = dot_rows(spread(first1, BLOCK, 0), spread_weights(second1, weight1, rows, 0))
    lower = dot_rows(spread(first2, BLOCK, 0), spread_weights(second2, weight2, rows, 0))
    to_prev = to_prev[:BLOCK] + to_prev[BLOCK:]
    upper = upper[:, :rows] + upper[:, rows:]
    lower = lower[:, :rows] + lower[:, rows:]
    half = lax.broadcasted_iota(jnp.int32, (BLOCK, rows), 1) >= BLOCK
    inside = jnp.where(half, pltpu.roll(lower, BLOCK, 1), 0.0)
    one_way = jnp.concatenate([upper, inside], axis=0)
    link_own = for_features(one_way + one_way.T)
    link_halo = for_features(jnp.concatenate([to_prev, jnp.where(half, lower, 0.0)], axis=0))
    inner = [linked(link_own, own[c]) for c in range(3)]

    some = pl.ds(0, 3)
    pltpu.make_async_copy(labels.at[0, some], labels.at[0, some], y_recv).wait()
    for step in range(1, 4):
        pltpu.make_async_remote_copy(
            src_ref=labels.at[z],
            dst_ref=labels.at[z],
            send_sem=z_send,
            recv_sem=z_recv,
            device_id=(around(z, step, 4) * 4 + y, sub),
            device_id_type=MESH,
        ).start()

    for c in range(3):
        for copy in halos[c]:
            copy.wait_recv()
        sums = inner[c] + linked(link_halo, features((halo[2 * c], halo[2 * c + 1])))
        g1r, g1i, g2r, g2i = (sums[:, i * NF : (i + 1) * NF] for i in range(4))
        x, o = stations(c)
        xr, xi = x[:, :NF].astype(F32), x[:, NF:].astype(F32)
        dr, di = xr - o[:, :NF].astype(F32), xi - o[:, NF:].astype(F32)
        real = (xr * g1r - xi * g1i) + (dr * g2r - di * g2i)
        imag = (xr * g1i + xi * g1r) + (dr * g2i + di * g2r)
        adjoint = jnp.concatenate([real, imag], axis=0).astype(BF16)
        outgoing[:, c] = dot_plain(placement, adjoint).astype(BF16).reshape(devices, 4, NF)
    received[me] = outgoing[me]

    pl.semaphore_wait(joined, subs - 1)

    def turns(at, size):
        return [at] + [around(at, step, size) for step in range(1, size)]

    z_to, y_to = turns(z, 4), turns(y, 4)
    x_to, core_to = turns(lax.div(sub, 2), 4), turns(lax.rem(sub, 2), 2)
    for dz, dy, dx, core in spread_order():
        blk_to, sub_to = z_to[dz] * 4 + y_to[dy], x_to[dx] * 2 + core_to[core]
        pltpu.make_async_remote_copy(
            src_ref=outgoing.at[blk_to * subs + sub_to],
            dst_ref=received.at[me],
            send_sem=all_send,
            recv_sem=all_recv,
            device_id=(blk_to, sub_to),
            device_id_type=MESH,
        ).start()

    pltpu.make_async_copy(labels.at[some], labels.at[some], z_recv).wait()
    by_owner = labels[...].reshape(2 * devices, NF)
    arrived = lax.broadcasted_iota(jnp.int32, (2 * devices, 4 * devices), 1)
    held = lax.broadcasted_iota(jnp.int32, (2 * devices, 4 * devices), 0)
    sub_bits = subs.bit_length() - 1
    wanted = (
        ((arrived >> (sub_bits + 2)) << (sub_bits + 1))
        + (((arrived >> 1) & 1) << sub_bits)
        + ((arrived >> 2) & (subs - 1))
    )
    repeated = lax.dot_general(
        by_owner,
        (held == wanted).astype(F32).astype(BF16),
        (((0,), (0,)), ((), ())),
        preferred_element_type=F32,
    )
    owner_line = lax.broadcasted_iota(jnp.int32, repeated.shape, 0)
    label = jnp.sum(jnp.where(owner_line == me, repeated, 0.0), axis=0, keepdims=True)
    collect = jnp.concatenate(
        [
            ((label == owner_line.astype(F32)) & ((arrived[:rows] & 1) == i)).astype(F32)
            for i in range(2)
        ],
        axis=0,
    ).astype(BF16)
    most = pl.ds(0, devices - 1)
    pltpu.make_async_copy(received.at[most], received.at[most], all_recv).wait()
    for c in range(3):
        sums = dot_plain(collect, received[:, c].reshape(4 * devices, NF)).astype(BF16)
        summed[c * rows : (c + 1) * rows, :NF] = sums[:rows]
        summed[c * rows : (c + 1) * rows, NF:] = sums[rows:]

    for c in range(3):
        for copy in halos[c]:
            copy.wait_send()
    pltpu.make_async_copy(list_out.at[others], list_out.at[others], list_send).wait()
    over.wait_send()
    pltpu.make_async_copy(labels.at[0, some], labels.at[0, some], y_send).wait()
    pltpu.make_async_copy(labels.at[some], labels.at[some], z_send).wait()
    pltpu.make_async_copy(outgoing.at[most], outgoing.at[most], all_send).wait()


def exchange(blks, subs, syn, obs, table, first, second, mask, weight, owner, element):
    devices = blks * subs
    samples, rows = syn.shape[2], syn.shape[1]
    in_hbm = pl.BlockSpec(memory_space=pltpu.HBM)
    dma = pltpu.SemaphoreType.DMA
    return pl.pallas_call(
        functools.partial(exchange_kernel, blks, subs),
        out_shape=pltpu.VMEM((3 * rows, 2 * NF), BF16),
        in_specs=[in_hbm] * 9,
        out_specs=pl.BlockSpec(memory_space=pltpu.VMEM),
        scratch_shapes=[
            pltpu.VMEM((3, 2 * rows, samples), BF16),
            pltpu.VMEM(table.shape, BF16),
            pltpu.VMEM(first.shape, jnp.int32),
            pltpu.VMEM(second.shape, jnp.int32),
            pltpu.VMEM(mask.shape, jnp.int32),
            pltpu.VMEM(weight.shape, F32),
            pltpu.VMEM(owner.shape, jnp.int32),
            pltpu.VMEM(element.shape, jnp.int32),
            pltpu.VMEM((6, rows, 2 * NF), BF16),
            pltpu.VMEM((6, 2 * BLOCK, 2 * NF), BF16),
            pltpu.VMEM((subs, 8, NF), F32),
            pltpu.VMEM((8, NF), F32),
            pltpu.VMEM((subs, 8, NF), F32),
            pltpu.VMEM((subs, 8, NF), F32),
            pltpu.VMEM((4, blks // 4, 2 * subs, NF), BF16),
            pltpu.VMEM((devices, 3, 4, NF), BF16),
            pltpu.VMEM((devices, 3, 4, NF), BF16),
            dma((13,)),
            dma,
            dma,
            dma,
            dma,
            dma((2, 3)),
            dma((2, 3)),
            pltpu.SemaphoreType.REGULAR,
            dma,
            dma,
            dma,
            dma,
            dma,
            dma,
        ],
        compiler_params=pltpu.CompilerParams(
            collective_id=0, has_side_effects=True, vmem_limit_bytes=60 * 2**20
        ),
        cost_estimate=pl.CostEstimate(
            flops=2 * 10**9, bytes_accessed=3 * 10**6, transcendentals=0
        ),
        name="exchange",
    )(syn, obs, table, first, second, mask, weight, owner, element)


def finish_kernel(summed, table, out, result, sems):
    samples = result.shape[1]
    chunk = samples // sems.shape[0]
    copies = []
    for n in range(sems.shape[0]):
        columns = pl.ds(n * chunk, chunk)
        result[:, columns] = dot_plain(summed[...], table[:, columns])
        copies.append(
            pltpu.make_async_copy(result.at[:, columns], out.at[:, columns], sems.at[n])
        )
        copies[-1].start()
    for copy in copies:
        copy.wait()


def finish(summed, table):
    count, samples = summed.shape[0], table.shape[1]
    in_vmem = pl.BlockSpec(memory_space=pltpu.VMEM)
    out = pl.pallas_call(
        finish_kernel,
        out_shape=jax.ShapeDtypeStruct((count, samples), F32),
        in_specs=[in_vmem] * 2,
        out_specs=pl.BlockSpec(memory_space=pl.ANY),
        scratch_shapes=[
            pltpu.VMEM((count, samples), F32),
            pltpu.SemaphoreType.DMA((4,)),
        ],
        compiler_params=pltpu.CompilerParams(vmem_limit_bytes=40 * 2**20),
        cost_estimate=pl.CostEstimate(
            flops=7 * 10**8, bytes_accessed=3 * 10**6, transcendentals=0
        ),
        name="finish",
    )(summed, table)
    return out.reshape(3, count // 3, samples)


def on_device(
    blks,
    subs,
    synthetic,
    observed,
    pair_first,
    pair_second,
    pair_mask,
    pair_weight,
    station_owner,
    station_element,
):
    rows, _, samples = synthetic.shape
    forward, inverse = dft_tables(samples, NF)
    summed = exchange(
        blks,
        subs,
        jnp.transpose(synthetic, (1, 0, 2)),
        jnp.transpose(observed, (1, 0, 2)),
        jnp.asarray(forward),
        pair_first,
        pair_second,
        pair_mask,
        pair_weight,
        station_owner.reshape(1, rows),
        station_element.reshape(1, rows),
    )
    out = finish(summed, jnp.asarray(inverse))
    return jnp.transpose(out, (1, 0, 2))


def solution(mesh):
    blks, subs = mesh.shape["blk"], mesh.shape["sub"]
    return jax.shard_map(
        functools.partial(on_device, blks, subs),
        mesh=mesh,
        in_specs=(
            P(("blk", "sub"), None, None),
            P(("blk", "sub"), None, None),
            P("blk", "sub"),
            P("blk", "sub"),
            P("blk", "sub"),
            P("blk", "sub"),
            P(("blk", "sub"), None),
            P(("blk", "sub")),
        ),
        out_specs=P(("blk", "sub"), None, None),
        check_vma=False,
    )
```

```python
import functools
import itertools
import math

import jax
import jax.numpy as jnp
import numpy as np
from jax import lax
from jax.experimental import pallas as pl
from jax.experimental.pallas import tpu as pltpu
from jax.sharding import PartitionSpec as P

MESH = pl.DeviceIdType.MESH
NF = 128
BLOCK = 64
F32 = jnp.float32
BF16 = jnp.bfloat16


def dft_tables(samples, freqs):
    phase = (np.arange(samples)[:, None] * np.arange(freqs)[None, :]) % samples
    angles = phase.astype(np.float64) * (2.0 * math.pi / samples)
    scale = 1.0 / math.sqrt(samples)
    cosine, sine = np.cos(angles) * scale, np.sin(angles) * scale
    forward = np.concatenate([cosine, -sine], axis=1).astype(np.float32)
    doubled = np.where(np.arange(freqs) == 0, 1.0, 2.0)[:, None]
    inverse = np.concatenate([cosine.T * doubled, -sine.T * doubled], axis=0)
    return forward.astype(jnp.bfloat16), inverse.astype(np.float32).astype(jnp.bfloat16)


def in_two(x):
    high = x.astype(BF16)
    return high, (x - high.astype(F32)).astype(BF16)


def dot_rows(a, b):
    return lax.dot_general(a, b, (((1,), (1,)), ((), ())), preferred_element_type=F32)


def dot_plain(a, b):
    return jnp.dot(a, b, preferred_element_type=F32)


def features(pair):
    xr, xi = pair[0][:, :NF].astype(F32), pair[0][:, NF:].astype(F32)
    o_r, o_i = pair[1][:, :NF].astype(F32), pair[1][:, NF:].astype(F32)
    dr, di = xr - o_r, xi - o_i
    parts = [dr * xr + di * xi, dr * xi - di * xr, o_r * xr + o_i * xi, o_r * xi - o_i * xr]
    both = [in_two(p) for p in parts]
    return jnp.concatenate(
        [jnp.concatenate([b[i] for b in both], axis=1) for i in range(2)], axis=0
    )


def for_features(links):
    high, low = in_two(links)
    return jnp.concatenate(
        [jnp.concatenate([high, high], axis=1), jnp.concatenate([low, low], axis=1)], axis=0
    )


def linked(links, values):
    rows = links.shape[0] // 2
    both = dot_plain(links, values)
    return both[:rows] + both[rows:]


def spread(rows, count, shift):
    index = lax.broadcasted_iota(jnp.int32, (count, NF), 0) + shift
    return jnp.concatenate(
        [(index == rows[s : s + 1]).astype(F32).astype(BF16) for s in range(rows.shape[0])], axis=1
    )


def spread_weights(rows, weights, count, shift):
    index = lax.broadcasted_iota(jnp.int32, (count, NF), 0) + shift
    parts = []
    for part in in_two(weights):
        wide = part.astype(F32)
        parts.append(
            jnp.concatenate(
                [
                    jnp.where(index == rows[s : s + 1], wide[s : s + 1], 0.0).astype(BF16)
                    for s in range(rows.shape[0])
                ],
                axis=1,
            )
        )
    return jnp.concatenate(parts, axis=0)


def spread_order():
    left = list(itertools.product(range(2), range(4), range(4), range(2)))[1:]
    ways = {0: (0.0, 0.0), 1: (1.0, 0.0), 2: (1.0, 1.0), 3: (0.0, 1.0)}

    def links(step):
        return np.array([way for axis in step[:3] for way in ways[axis]])

    used, order = np.zeros(6), []
    while left:
        step = min(left, key=lambda t: (np.max(used + links(t)), -np.sum(links(t)), t))
        left.remove(step)
        used = used + links(step)
        order.append(step)
    return order


def exchange_kernel(
    blks,
    subs,
    syn_hbm,
    obs_hbm,
    table_hbm,
    first_hbm,
    second_hbm,
    mask_hbm,
    weight_hbm,
    owner_hbm,
    element_hbm,
    summed,
    traces,
    table,
    first,
    second,
    mask,
    weight,
    owner,
    element,
    spec,
    halo,
    list_out,
    list_over,
    lists,
    lists_prev,
    labels,
    outgoing,
    gathered,
    received,
    load_sems,
    list_send,
    list_recv,
    over_send,
    over_recv,
    halo_send,
    halo_recv,
    joined,
    y_send,
    y_recv,
    z_send,
    z_recv,
    sibling_send,
    sibling_recv,
    all_send,
    all_recv,
):
    devices = blks * subs
    blk, sub = lax.axis_index("blk"), lax.axis_index("sub")
    me = blk * subs + sub
    core, served = lax.rem(sub, 2), devices // 2
    sibling = sub + 1 - 2 * core
    rows = spec.shape[1]
    blocks = first.shape[0]
    def around(at, step, size):
        there = at + step
        return jnp.where(there >= size, there - size, there)

    subs_there = [around(sub, step, subs) for step in range(1, subs)]
    blks_there = [around(blk, step, blks) for step in range(1, blks)]
    blk_after, blk_before = blks_there[0], blks_there[-1]
    after = (jnp.where(sub == subs - 1, blk_after, blk), subs_there[0])
    before = (jnp.where(sub == 0, blk_before, blk), subs_there[-1])

    pairs = [
        (owner_hbm, owner),
        (element_hbm, element),
        (first_hbm, first),
        (second_hbm, second),
        (mask_hbm, mask),
        (weight_hbm, weight),
        (table_hbm, table),
        (syn_hbm.at[0], traces.at[0, pl.ds(0, rows)]),
        (obs_hbm.at[0], traces.at[0, pl.ds(rows, rows)]),
        (syn_hbm.at[1], traces.at[1, pl.ds(0, rows)]),
        (obs_hbm.at[1], traces.at[1, pl.ds(rows, rows)]),
        (syn_hbm.at[2], traces.at[2, pl.ds(0, rows)]),
        (obs_hbm.at[2], traces.at[2, pl.ds(rows, rows)]),
    ]
    loads = [
        pltpu.make_async_copy(src, dst, load_sems.at[i]) for i, (src, dst) in enumerate(pairs)
    ]
    for load in loads:
        load.start()

    barrier = pltpu.get_barrier_semaphore()

    def greet(there):
        pl.semaphore_signal(barrier, inc=1, device_id=there, device_id_type=MESH)

    for there in subs_there:
        greet((blk, there))
    for there in blks_there:
        greet((there, sub))

    @pl.when(sub == 0)
    def _():
        for s in range(1, subs):
            greet((blk_before, s))

    @pl.when(sub == subs - 1)
    def _():
        greet((blk_after, 0))

    for i in range(2):
        loads[i].wait()
    lane = lax.broadcasted_iota(jnp.int32, (rows, rows), 1)
    line = lax.broadcasted_iota(jnp.int32, (rows, rows), 0)
    owner_row = owner[...]

    def column(row):
        return jnp.sum(jnp.where(lane == line, row, 0), axis=1, keepdims=True)

    owner_column, element_column = column(owner_row), column(element[...]).astype(F32)
    same = owner_column == owner_row
    rank_column = jnp.sum(jnp.where(same & (lane < line), 1, 0), axis=1, keepdims=True)
    label_rows = []
    for k in range(2):
        chosen = ((owner_column == lane) & (rank_column == k)).astype(F32)
        label_rows.append(
            jnp.sum(chosen * (element_column - rows), axis=0, keepdims=True) + float(rows)
        )

    for i in range(2, 6):
        loads[i].wait()
    base = (blk * blocks + lax.broadcasted_iota(jnp.int32, (blocks, NF), 0)) * BLOCK
    code = ((first[...] - base) * (2 * BLOCK) + (second[...] - base)).astype(F32)
    slot_weight = weight[...] * mask[...].astype(F32)
    zero_row = jnp.zeros((1, NF), F32)
    for s in range(subs):
        lines = [max(2 * s - 1, 0), 2 * s, 2 * s + 1]
        list_out[s] = jnp.concatenate(
            [code[i : i + 1] for i in lines]
            + [slot_weight[i : i + 1] for i in lines]
            + label_rows,
            axis=0,
        )
    list_over[...] = jnp.concatenate(
        [code[blocks - 1 : blocks]]
        + [zero_row] * 2
        + [slot_weight[blocks - 1 : blocks]]
        + [zero_row] * 4,
        axis=0,
    )
    lists[sub] = list_out[sub]

    pl.semaphore_wait(barrier, subs + blks - 1)
    for there in subs_there:
        pltpu.make_async_remote_copy(
            src_ref=list_out.at[there],
            dst_ref=lists.at[sub],
            send_sem=list_send,
            recv_sem=list_recv,
            device_id=(blk, there),
            device_id_type=MESH,
        ).start()
    over = pltpu.make_async_remote_copy(
        src_ref=list_over,
        dst_ref=lists_prev.at[sub],
        send_sem=over_send,
        recv_sem=over_recv,
        device_id=(blk_after, 0),
        device_id_type=MESH,
    )
    over.start()

    def transform(c):
        both = dot_plain(traces[c], table[...]).astype(BF16)
        spec[2 * c] = both[:rows]
        spec[2 * c + 1] = both[rows:]

    for i in range(6, 9):
        loads[i].wait()
    transform(0)

    def halo_copies(c):
        q = pl.ds(2 * c, 2)
        return [
            pltpu.make_async_remote_copy(
                src_ref=spec.at[q, pl.ds(0, BLOCK)],
                dst_ref=halo.at[q, pl.ds(BLOCK, BLOCK)],
                send_sem=halo_send.at[0, c],
                recv_sem=halo_recv.at[0, c],
                device_id=before,
                device_id_type=MESH,
            ),
            pltpu.make_async_remote_copy(
                src_ref=spec.at[q, pl.ds(rows - BLOCK, BLOCK)],
                dst_ref=halo.at[q, pl.ds(0, BLOCK)],
                send_sem=halo_send.at[1, c],
                recv_sem=halo_recv.at[1, c],
                device_id=after,
                device_id_type=MESH,
            ),
        ]

    halos = [halo_copies(c) for c in range(3)]
    for copy in halos[0]:
        copy.start()
    for c in (1, 2):
        loads[7 + 2 * c].wait()
        loads[8 + 2 * c].wait()
        transform(c)
        for copy in halos[c]:
            copy.start()

    for there in subs_there:
        pl.semaphore_signal(joined, inc=1, device_id=(blk, there), device_id_type=MESH)

    rank_row = jnp.sum(jnp.where(same & (line < lane), 1, 0), axis=0, keepdims=True)
    target = (owner_row ^ (core * served)) * 4 + rank_row * 2
    slot = lax.broadcasted_iota(jnp.int32, (4 * devices, 2 * rows), 0)
    placement = (slot == jnp.concatenate([target, target + 1], axis=1)).astype(F32).astype(BF16)

    def sort_out(c, values):
        tiles = values.astype(BF16).reshape(2, served, 4, NF)
        gathered[:, core, c] = tiles[0]
        outgoing[c] = tiles[1]
        copy = pltpu.make_async_remote_copy(
            src_ref=outgoing.at[c],
            dst_ref=gathered.at[:, core, c],
            send_sem=sibling_send.at[c],
            recv_sem=sibling_recv.at[c],
            device_id=(blk, sibling),
            device_id_type=MESH,
        )
        copy.start()
        return copy

    def stations(c):
        return (spec[2 * c], spec[2 * c + 1])

    own = [features(stations(c)) for c in range(3)]

    others = pl.ds(0, subs - 1)
    pltpu.make_async_copy(lists.at[others], lists.at[others], list_recv).wait()

    z, y = lax.div(blk, 4), lax.rem(blk, 4)
    labels[z, y] = jnp.concatenate([lists[:, 6, :], lists[:, 7, :]], axis=0).astype(BF16)
    for step in range(1, 4):
        pltpu.make_async_remote_copy(
            src_ref=labels.at[z, y],
            dst_ref=labels.at[z, y],
            send_sem=y_send,
            recv_sem=y_recv,
            device_id=(z * 4 + around(y, step, 4), sub),
            device_id_type=MESH,
        ).start()

    @pl.when(sub == 0)
    def _():
        pltpu.make_async_copy(lists_prev, lists_prev, over_recv).wait()

    @pl.when(sub != 0)
    def _():
        lists_prev[...] = lists[...]

    def unpacked(ref, k):
        codes = ref[:, k, :].astype(jnp.int32)
        return codes >> 7, codes & 127, ref[:, 3 + k, :]

    first0, second0, weight0 = unpacked(lists_prev, 0)
    first1, second1, weight1 = unpacked(lists, 1)
    first2, second2, weight2 = unpacked(lists, 2)
    to_prev = dot_rows(spread_weights(second0, weight0, BLOCK, BLOCK), spread(first0, rows, 0))
    upper = dot_rows(spread(first1, BLOCK, 0), spread_weights(second1, weight1, rows, 0))
    lower = dot_rows(spread(first2, BLOCK, 0), spread_weights(second2, weight2, rows, 0))
    to_prev = to_prev[:BLOCK] + to_prev[BLOCK:]
    upper = upper[:, :rows] + upper[:, rows:]
    lower = lower[:, :rows] + lower[:, rows:]
    half = lax.broadcasted_iota(jnp.int32, (BLOCK, rows), 1) >= BLOCK
    inside = jnp.where(half, pltpu.roll(lower, BLOCK, 1), 0.0)
    one_way = jnp.concatenate([upper, inside], axis=0)
    link_own = for_features(one_way + one_way.T)
    link_halo = for_features(jnp.concatenate([to_prev, jnp.where(half, lower, 0.0)], axis=0))
    inner = [linked(link_own, own[c]) for c in range(3)]

    some = pl.ds(0, 3)
    pltpu.make_async_copy(labels.at[0, some], labels.at[0, some], y_recv).wait()
    for step in range(1, 4):
        pltpu.make_async_remote_copy(
            src_ref=labels.at[z],
            dst_ref=labels.at[z],
            send_sem=z_send,
            recv_sem=z_recv,
            device_id=(around(z, step, 4) * 4 + y, sub),
            device_id_type=MESH,
        ).start()

    sorted_out = []
    for c in range(3):
        for copy in halos[c]:
            copy.wait_recv()
        sums = inner[c] + linked(link_halo, features((halo[2 * c], halo[2 * c + 1])))
        g1r, g1i, g2r, g2i = (sums[:, i * NF : (i + 1) * NF] for i in range(4))
        x, o = stations(c)
        xr, xi = x[:, :NF].astype(F32), x[:, NF:].astype(F32)
        dr, di = xr - o[:, :NF].astype(F32), xi - o[:, NF:].astype(F32)
        real = (xr * g1r - xi * g1i) + (dr * g2r - di * g2i)
        imag = (xr * g1i + xi * g1r) + (dr * g2i + di * g2r)
        adjoint = jnp.concatenate([real, imag], axis=0).astype(BF16)
        sorted_out.append(sort_out(c, dot_plain(placement, adjoint)))

    pl.semaphore_wait(joined, subs - 1)
    for copy in sorted_out:
        copy.wait_recv()

    def turns(at, size):
        return [at] + [around(at, step, size) for step in range(1, size)]

    x = lax.div(sub, 2)
    z_near = lax.rem(z, 2)
    near_to, y_to, x_to, core_to = [z_near, 1 - z_near], turns(y, 4), turns(x, 4), turns(core, 2)
    home = lax.div(z, 2) == core
    chip = lax.div(me, 2)

    def deliver(step):
        dz, dy, dx, dcore = step
        blk_to, sub_to = near_to[dz] * 4 + y_to[dy], x_to[dx] * 2 + core_to[dcore]
        return gathered.at[blk_to * subs + sub_to], (core * 8 + blk_to, sub_to)

    def deliver_away(step):
        tile, there = deliver(step)
        pltpu.make_async_remote_copy(
            src_ref=tile,
            dst_ref=received.at[chip],
            send_sem=all_send,
            recv_sem=all_recv,
            device_id=there,
            device_id_type=MESH,
        ).start()

    for step in spread_order():
        deliver_away(step)

    @pl.when(home)
    def _():
        tile, _ = deliver((0, 0, 0, 0))
        kept = pltpu.make_async_copy(tile, received.at[chip], load_sems.at[0])
        kept.start()
        kept.wait()

    @pl.when(jnp.logical_not(home))
    def _():
        deliver_away((0, 0, 0, 0))

    pltpu.make_async_copy(labels.at[some], labels.at[some], z_recv).wait()
    by_owner = labels[...].reshape(2 * devices, NF)
    arrived = lax.broadcasted_iota(jnp.int32, (2 * devices, 4 * devices), 1)
    held = lax.broadcasted_iota(jnp.int32, (2 * devices, 4 * devices), 0)
    sub_bits = subs.bit_length() - 1
    wanted = (
        ((arrived >> (sub_bits + 2)) << (sub_bits + 1))
        + (((arrived >> 1) & 1) << sub_bits)
        + ((arrived >> 2) & (subs - 1))
    )
    repeated = lax.dot_general(
        by_owner,
        (held == wanted).astype(F32).astype(BF16),
        (((0,), (0,)), ((), ())),
        preferred_element_type=F32,
    )
    owner_line = lax.broadcasted_iota(jnp.int32, repeated.shape, 0)
    label = jnp.sum(jnp.where(owner_line == me, repeated, 0.0), axis=0, keepdims=True)
    collect = jnp.concatenate(
        [
            ((label == owner_line.astype(F32)) & ((arrived[:rows] & 1) == i)).astype(F32)
            for i in range(2)
        ],
        axis=0,
    ).astype(BF16)
    most = pl.ds(0, served - 1)

    def wait_for(ref, sem):
        @pl.when(home)
        def _():
            pltpu.make_async_copy(ref.at[most], ref.at[most], sem).wait()

        @pl.when(jnp.logical_not(home))
        def _():
            pltpu.make_async_copy(ref, ref, sem).wait()

    wait_for(received, all_recv)
    for c in range(3):
        sums = dot_plain(collect, received[:, :, c].reshape(4 * devices, NF)).astype(BF16)
        summed[c * rows : (c + 1) * rows, :NF] = sums[:rows]
        summed[c * rows : (c + 1) * rows, NF:] = sums[rows:]

    for c in range(3):
        for copy in halos[c]:
            copy.wait_send()
    pltpu.make_async_copy(list_out.at[others], list_out.at[others], list_send).wait()
    over.wait_send()
    pltpu.make_async_copy(labels.at[0, some], labels.at[0, some], y_send).wait()
    pltpu.make_async_copy(labels.at[some], labels.at[some], z_send).wait()
    for copy in sorted_out:
        copy.wait_send()
    wait_for(gathered, all_send)


def exchange(blks, subs, syn, obs, table, first, second, mask, weight, owner, element):
    devices = blks * subs
    samples, rows = syn.shape[2], syn.shape[1]
    in_hbm = pl.BlockSpec(memory_space=pltpu.HBM)
    dma = pltpu.SemaphoreType.DMA
    return pl.pallas_call(
        functools.partial(exchange_kernel, blks, subs),
        out_shape=pltpu.VMEM((3 * rows, 2 * NF), BF16),
        in_specs=[in_hbm] * 9,
        out_specs=pl.BlockSpec(memory_space=pltpu.VMEM),
        scratch_shapes=[
            pltpu.VMEM((3, 2 * rows, samples), BF16),
            pltpu.VMEM(table.shape, BF16),
            pltpu.VMEM(first.shape, jnp.int32),
            pltpu.VMEM(second.shape, jnp.int32),
            pltpu.VMEM(mask.shape, jnp.int32),
            pltpu.VMEM(weight.shape, F32),
            pltpu.VMEM(owner.shape, jnp.int32),
            pltpu.VMEM(element.shape, jnp.int32),
            pltpu.VMEM((6, rows, 2 * NF), BF16),
            pltpu.VMEM((6, 2 * BLOCK, 2 * NF), BF16),
            pltpu.VMEM((subs, 8, NF), F32),
            pltpu.VMEM((8, NF), F32),
            pltpu.VMEM((subs, 8, NF), F32),
            pltpu.VMEM((subs, 8, NF), F32),
            pltpu.VMEM((4, blks // 4, 2 * subs, NF), BF16),
            pltpu.VMEM((3, devices // 2, 4, NF), BF16),
            pltpu.VMEM((devices // 2, 2, 3, 4, NF), BF16),
            pltpu.VMEM((devices // 2, 2, 3, 4, NF), BF16),
            dma((13,)),
            dma,
            dma,
            dma,
            dma,
            dma((2, 3)),
            dma((2, 3)),
            pltpu.SemaphoreType.REGULAR,
            dma,
            dma,
            dma,
            dma,
            dma((3,)),
            dma((3,)),
            dma,
            dma,
        ],
        compiler_params=pltpu.CompilerParams(
            collective_id=0, has_side_effects=True, vmem_limit_bytes=60 * 2**20
        ),
        cost_estimate=pl.CostEstimate(
            flops=2 * 10**9, bytes_accessed=3 * 10**6, transcendentals=0
        ),
        name="exchange",
    )(syn, obs, table, first, second, mask, weight, owner, element)


def finish_kernel(summed, table, out, result, sems):
    samples = result.shape[1]
    chunk = samples // sems.shape[0]
    copies = []
    for n in range(sems.shape[0]):
        columns = pl.ds(n * chunk, chunk)
        result[:, columns] = dot_plain(summed[...], table[:, columns])
        copies.append(
            pltpu.make_async_copy(result.at[:, columns], out.at[:, columns], sems.at[n])
        )
        copies[-1].start()
    for copy in copies:
        copy.wait()


def finish(summed, table):
    count, samples = summed.shape[0], table.shape[1]
    in_vmem = pl.BlockSpec(memory_space=pltpu.VMEM)
    out = pl.pallas_call(
        finish_kernel,
        out_shape=jax.ShapeDtypeStruct((count, samples), F32),
        in_specs=[in_vmem] * 2,
        out_specs=pl.BlockSpec(memory_space=pl.ANY),
        scratch_shapes=[
            pltpu.VMEM((count, samples), F32),
            pltpu.SemaphoreType.DMA((4,)),
        ],
        compiler_params=pltpu.CompilerParams(vmem_limit_bytes=40 * 2**20),
        cost_estimate=pl.CostEstimate(
            flops=7 * 10**8, bytes_accessed=3 * 10**6, transcendentals=0
        ),
        name="finish",
    )(summed, table)
    return out.reshape(3, count // 3, samples)


def on_device(
    blks,
    subs,
    synthetic,
    observed,
    pair_first,
    pair_second,
    pair_mask,
    pair_weight,
    station_owner,
    station_element,
):
    rows, _, samples = synthetic.shape
    forward, inverse = dft_tables(samples, NF)
    summed = exchange(
        blks,
        subs,
        jnp.transpose(synthetic, (1, 0, 2)),
        jnp.transpose(observed, (1, 0, 2)),
        jnp.asarray(forward),
        pair_first,
        pair_second,
        pair_mask,
        pair_weight,
        station_owner.reshape(1, rows),
        station_element.reshape(1, rows),
    )
    out = finish(summed, jnp.asarray(inverse))
    return jnp.transpose(out, (1, 0, 2))


def solution(mesh):
    blks, subs = mesh.shape["blk"], mesh.shape["sub"]
    return jax.shard_map(
        functools.partial(on_device, blks, subs),
        mesh=mesh,
        in_specs=(
            P(("blk", "sub"), None, None),
            P(("blk", "sub"), None, None),
            P("blk", "sub"),
            P("blk", "sub"),
            P("blk", "sub"),
            P("blk", "sub"),
            P(("blk", "sub"), None),
            P(("blk", "sub")),
        ),
        out_specs=P(("blk", "sub"), None, None),
        check_vma=False,
    )
```

```python
import functools
import itertools
import math

import jax
import jax.numpy as jnp
import numpy as np
from jax import lax
from jax.experimental import pallas as pl
from jax.experimental.pallas import tpu as pltpu
from jax.sharding import PartitionSpec as P

MESH = pl.DeviceIdType.MESH
NF = 128
BLOCK = 64
F32 = jnp.float32
BF16 = jnp.bfloat16


def dft_tables(samples, freqs):
    phase = (np.arange(samples)[:, None] * np.arange(freqs)[None, :]) % samples
    angles = phase.astype(np.float64) * (2.0 * math.pi / samples)
    scale = 1.0 / math.sqrt(samples)
    cosine, sine = np.cos(angles) * scale, np.sin(angles) * scale
    forward = np.concatenate([cosine, -sine], axis=1).astype(np.float32)
    doubled = np.where(np.arange(freqs) == 0, 1.0, 2.0)[:, None]
    inverse = np.concatenate([cosine.T * doubled, -sine.T * doubled], axis=0)
    return forward.astype(jnp.bfloat16), inverse.astype(np.float32).astype(jnp.bfloat16)


def in_two(x):
    high = x.astype(BF16)
    return high, (x - high.astype(F32)).astype(BF16)


def dot_rows(a, b):
    return lax.dot_general(a, b, (((1,), (1,)), ((), ())), preferred_element_type=F32)


def dot_plain(a, b):
    return jnp.dot(a, b, preferred_element_type=F32)


def features(pair):
    xr, xi = pair[0][:, :NF].astype(F32), pair[0][:, NF:].astype(F32)
    o_r, o_i = pair[1][:, :NF].astype(F32), pair[1][:, NF:].astype(F32)
    dr, di = xr - o_r, xi - o_i
    parts = [dr * xr + di * xi, dr * xi - di * xr, o_r * xr + o_i * xi, o_r * xi - o_i * xr]
    both = [in_two(p) for p in parts]
    return jnp.concatenate(
        [jnp.concatenate([b[i] for b in both], axis=1) for i in range(2)], axis=0
    )


def for_features(links):
    high, low = in_two(links)
    return jnp.concatenate(
        [jnp.concatenate([high, high], axis=1), jnp.concatenate([low, low], axis=1)], axis=0
    )


def linked(links, values):
    rows = links.shape[0] // 2
    both = dot_plain(links, values)
    return both[:rows] + both[rows:]


def spread(rows, count, shift):
    index = lax.broadcasted_iota(jnp.int32, (count, NF), 0) + shift
    return jnp.concatenate(
        [(index == rows[s : s + 1]).astype(F32).astype(BF16) for s in range(rows.shape[0])], axis=1
    )


def spread_weights(rows, weights, count, shift):
    index = lax.broadcasted_iota(jnp.int32, (count, NF), 0) + shift
    parts = []
    for part in in_two(weights):
        wide = part.astype(F32)
        parts.append(
            jnp.concatenate(
                [
                    jnp.where(index == rows[s : s + 1], wide[s : s + 1], 0.0).astype(BF16)
                    for s in range(rows.shape[0])
                ],
                axis=1,
            )
        )
    return jnp.concatenate(parts, axis=0)


def spread_order():
    left = list(itertools.product(range(4), range(4), range(4), range(2)))[1:]
    ways = {0: (0.0, 0.0), 1: (1.0, 0.0), 2: (1.0, 1.0), 3: (0.0, 1.0)}

    def links(step):
        return np.array([way for axis in step[:3] for way in ways[axis]])

    used, order = np.zeros(6), []
    while left:
        step = min(left, key=lambda t: (np.max(used + links(t)), -np.sum(links(t)), t))
        left.remove(step)
        used = used + links(step)
        order.append(step)
    return order


def exchange_kernel(
    blks,
    subs,
    syn_hbm,
    obs_hbm,
    table_hbm,
    first_hbm,
    second_hbm,
    mask_hbm,
    weight_hbm,
    owner_hbm,
    element_hbm,
    summed,
    traces,
    table,
    first,
    second,
    mask,
    weight,
    owner,
    element,
    spec,
    halo,
    list_out,
    list_over,
    lists,
    lists_prev,
    labels,
    outgoing,
    received,
    load_sems,
    list_send,
    list_recv,
    over_send,
    over_recv,
    halo_send,
    halo_recv,
    joined,
    y_send,
    y_recv,
    z_send,
    z_recv,
    all_send,
    all_recv,
):
    devices = blks * subs
    blk, sub = lax.axis_index("blk"), lax.axis_index("sub")
    me = blk * subs + sub
    rows = spec.shape[1]
    blocks = first.shape[0]
    def around(at, step, size):
        there = at + step
        return jnp.where(there >= size, there - size, there)

    subs_there = [around(sub, step, subs) for step in range(1, subs)]
    blks_there = [around(blk, step, blks) for step in range(1, blks)]
    blk_after, blk_before = blks_there[0], blks_there[-1]
    after = (jnp.where(sub == subs - 1, blk_after, blk), subs_there[0])
    before = (jnp.where(sub == 0, blk_before, blk), subs_there[-1])

    pairs = [
        (owner_hbm, owner),
        (element_hbm, element),
        (first_hbm, first),
        (second_hbm, second),
        (mask_hbm, mask),
        (weight_hbm, weight),
        (table_hbm, table),
        (syn_hbm.at[0], traces.at[0, pl.ds(0, rows)]),
        (obs_hbm.at[0], traces.at[0, pl.ds(rows, rows)]),
        (syn_hbm.at[1], traces.at[1, pl.ds(0, rows)]),
        (obs_hbm.at[1], traces.at[1, pl.ds(rows, rows)]),
        (syn_hbm.at[2], traces.at[2, pl.ds(0, rows)]),
        (obs_hbm.at[2], traces.at[2, pl.ds(rows, rows)]),
    ]
    loads = [
        pltpu.make_async_copy(src, dst, load_sems.at[i]) for i, (src, dst) in enumerate(pairs)
    ]
    for load in loads:
        load.start()

    barrier = pltpu.get_barrier_semaphore()

    def greet(there):
        pl.semaphore_signal(barrier, inc=1, device_id=there, device_id_type=MESH)

    for there in subs_there:
        greet((blk, there))
    for there in blks_there:
        greet((there, sub))

    @pl.when(sub == 0)
    def _():
        for s in range(1, subs):
            greet((blk_before, s))

    @pl.when(sub == subs - 1)
    def _():
        greet((blk_after, 0))

    for i in range(2):
        loads[i].wait()
    lane = lax.broadcasted_iota(jnp.int32, (rows, rows), 1)
    line = lax.broadcasted_iota(jnp.int32, (rows, rows), 0)
    owner_row = owner[...]

    def column(row):
        return jnp.sum(jnp.where(lane == line, row, 0), axis=1, keepdims=True)

    owner_column, element_column = column(owner_row), column(element[...]).astype(F32)
    same = owner_column == owner_row
    rank_column = jnp.sum(jnp.where(same & (lane < line), 1, 0), axis=1, keepdims=True)
    label_rows = []
    for k in range(2):
        chosen = ((owner_column == lane) & (rank_column == k)).astype(F32)
        label_rows.append(
            jnp.sum(chosen * (element_column - rows), axis=0, keepdims=True) + float(rows)
        )

    for i in range(2, 6):
        loads[i].wait()
    base = (blk * blocks + lax.broadcasted_iota(jnp.int32, (blocks, NF), 0)) * BLOCK
    code = ((first[...] - base) * (2 * BLOCK) + (second[...] - base)).astype(F32)
    slot_weight = weight[...] * mask[...].astype(F32)
    zero_row = jnp.zeros((1, NF), F32)
    for s in range(subs):
        lines = [max(2 * s - 1, 0), 2 * s, 2 * s + 1]
        list_out[s] = jnp.concatenate(
            [code[i : i + 1] for i in lines]
            + [slot_weight[i : i + 1] for i in lines]
            + label_rows,
            axis=0,
        )
    list_over[...] = jnp.concatenate(
        [code[blocks - 1 : blocks]]
        + [zero_row] * 2
        + [slot_weight[blocks - 1 : blocks]]
        + [zero_row] * 4,
        axis=0,
    )
    lists[sub] = list_out[sub]

    pl.semaphore_wait(barrier, subs + blks - 1)
    for there in subs_there:
        pltpu.make_async_remote_copy(
            src_ref=list_out.at[there],
            dst_ref=lists.at[sub],
            send_sem=list_send,
            recv_sem=list_recv,
            device_id=(blk, there),
            device_id_type=MESH,
        ).start()
    over = pltpu.make_async_remote_copy(
        src_ref=list_over,
        dst_ref=lists_prev.at[sub],
        send_sem=over_send,
        recv_sem=over_recv,
        device_id=(blk_after, 0),
        device_id_type=MESH,
    )
    over.start()

    def transform(c):
        both = dot_plain(traces[c], table[...]).astype(BF16)
        spec[2 * c] = both[:rows]
        spec[2 * c + 1] = both[rows:]

    for i in range(6, 9):
        loads[i].wait()
    transform(0)

    def halo_copies(c):
        q = pl.ds(2 * c, 2)
        return [
            pltpu.make_async_remote_copy(
                src_ref=spec.at[q, pl.ds(0, BLOCK)],
                dst_ref=halo.at[q, pl.ds(BLOCK, BLOCK)],
                send_sem=halo_send.at[0, c],
                recv_sem=halo_recv.at[0, c],
                device_id=before,
                device_id_type=MESH,
            ),
            pltpu.make_async_remote_copy(
                src_ref=spec.at[q, pl.ds(rows - BLOCK, BLOCK)],
                dst_ref=halo.at[q, pl.ds(0, BLOCK)],
                send_sem=halo_send.at[1, c],
                recv_sem=halo_recv.at[1, c],
                device_id=after,
                device_id_type=MESH,
            ),
        ]

    halos = [halo_copies(c) for c in range(3)]
    for copy in halos[0]:
        copy.start()
    for c in (1, 2):
        loads[7 + 2 * c].wait()
        loads[8 + 2 * c].wait()
        transform(c)
        for copy in halos[c]:
            copy.start()

    for there in subs_there:
        pl.semaphore_signal(joined, inc=1, device_id=(blk, there), device_id_type=MESH)

    rank_row = jnp.sum(jnp.where(same & (line < lane), 1, 0), axis=0, keepdims=True)
    target = owner_row * 4 + rank_row * 2
    slot = lax.broadcasted_iota(jnp.int32, (4 * devices, 2 * rows), 0)
    placement = (slot == jnp.concatenate([target, target + 1], axis=1)).astype(F32).astype(BF16)

    def stations(c):
        return (spec[2 * c], spec[2 * c + 1])

    own = [features(stations(c)) for c in range(3)]

    others = pl.ds(0, subs - 1)
    pltpu.make_async_copy(lists.at[others], lists.at[others], list_recv).wait()

    z, y = lax.div(blk, 4), lax.rem(blk, 4)
    labels[z, y] = jnp.concatenate([lists[:, 6, :], lists[:, 7, :]], axis=0).astype(BF16)
    for step in range(1, 4):
        pltpu.make_async_remote_copy(
            src_ref=labels.at[z, y],
            dst_ref=labels.at[z, y],
            send_sem=y_send,
            recv_sem=y_recv,
            device_id=(z * 4 + around(y, step, 4), sub),
            device_id_type=MESH,
        ).start()

    @pl.when(sub == 0)
    def _():
        pltpu.make_async_copy(lists_prev, lists_prev, over_recv).wait()

    @pl.when(sub != 0)
    def _():
        lists_prev[...] = lists[...]

    def unpacked(ref, k):
        codes = ref[:, k, :].astype(jnp.int32)
        return codes >> 7, codes & 127, ref[:, 3 + k, :]

    first0, second0, weight0 = unpacked(lists_prev, 0)
    first1, second1, weight1 = unpacked(lists, 1)
    first2, second2, weight2 = unpacked(lists, 2)
    to_prev = dot_rows(spread_weights(second0, weight0, BLOCK, BLOCK), spread(first0, rows, 0))
    upper = dot_rows(spread(first1, BLOCK, 0), spread_weights(second1, weight1, rows, 0))
    lower = dot_rows(spread(first2, BLOCK, 0), spread_weights(second2, weight2, rows, 0))
    to_prev = to_prev[:BLOCK] + to_prev[BLOCK:]
    upper = upper[:, :rows] + upper[:, rows:]
    lower = lower[:, :rows] + lower[:, rows:]
    half = lax.broadcasted_iota(jnp.int32, (BLOCK, rows), 1) >= BLOCK
    inside = jnp.where(half, pltpu.roll(lower, BLOCK, 1), 0.0)
    one_way = jnp.concatenate([upper, inside], axis=0)
    link_own = for_features(one_way + one_way.T)
    link_halo = for_features(jnp.concatenate([to_prev, jnp.where(half, lower, 0.0)], axis=0))
    inner = [linked(link_own, own[c]) for c in range(3)]

    for c in range(3):
        for copy in halos[c]:
            copy.wait_recv()
        sums = inner[c] + linked(link_halo, features((halo[2 * c], halo[2 * c + 1])))
        g1r, g1i, g2r, g2i = (sums[:, i * NF : (i + 1) * NF] for i in range(4))
        x, o = stations(c)
        xr, xi = x[:, :NF].astype(F32), x[:, NF:].astype(F32)
        dr, di = xr - o[:, :NF].astype(F32), xi - o[:, NF:].astype(F32)
        real = (xr * g1r - xi * g1i) + (dr * g2r - di * g2i)
        imag = (xr * g1i + xi * g1r) + (dr * g2i + di * g2r)
        adjoint = jnp.concatenate([real, imag], axis=0).astype(BF16)
        outgoing[:, c] = dot_plain(placement, adjoint).astype(BF16).reshape(devices, 4, NF)
    received[me] = outgoing[me]

    pl.semaphore_wait(joined, subs - 1)

    def turns(at, size):
        return [at] + [around(at, step, size) for step in range(1, size)]

    z_to, y_to = turns(z, 4), turns(y, 4)
    x_to, core_to = turns(lax.div(sub, 2), 4), turns(lax.rem(sub, 2), 2)
    def deliver(step):
        dz, dy, dx, core = step
        blk_to, sub_to = z_to[dz] * 4 + y_to[dy], x_to[dx] * 2 + core_to[core]
        pltpu.make_async_remote_copy(
            src_ref=outgoing.at[blk_to * subs + sub_to],
            dst_ref=received.at[me],
            send_sem=all_send,
            recv_sem=all_recv,
            device_id=(blk_to, sub_to),
            device_id_type=MESH,
        ).start()

    order = spread_order()
    for step in order[:32]:
        deliver(step)
    some = pl.ds(0, 3)
    pltpu.make_async_copy(labels.at[0, some], labels.at[0, some], y_recv).wait()
    for step in range(1, 4):
        pltpu.make_async_remote_copy(
            src_ref=labels.at[z],
            dst_ref=labels.at[z],
            send_sem=z_send,
            recv_sem=z_recv,
            device_id=(around(z, step, 4) * 4 + y, sub),
            device_id_type=MESH,
        ).start()

    for step in order[32:]:
        deliver(step)

    pltpu.make_async_copy(labels.at[some], labels.at[some], z_recv).wait()
    by_owner = labels[...].reshape(2 * devices, NF)
    arrived = lax.broadcasted_iota(jnp.int32, (2 * devices, 4 * devices), 1)
    held = lax.broadcasted_iota(jnp.int32, (2 * devices, 4 * devices), 0)
    sub_bits = subs.bit_length() - 1
    wanted = (
        ((arrived >> (sub_bits + 2)) << (sub_bits + 1))
        + (((arrived >> 1) & 1) << sub_bits)
        + ((arrived >> 2) & (subs - 1))
    )
    repeated = lax.dot_general(
        by_owner,
        (held == wanted).astype(F32).astype(BF16),
        (((0,), (0,)), ((), ())),
        preferred_element_type=F32,
    )
    owner_line = lax.broadcasted_iota(jnp.int32, repeated.shape, 0)
    label = jnp.sum(jnp.where(owner_line == me, repeated, 0.0), axis=0, keepdims=True)
    collect = jnp.concatenate(
        [
            ((label == owner_line.astype(F32)) & ((arrived[:rows] & 1) == i)).astype(F32)
            for i in range(2)
        ],
        axis=0,
    ).astype(BF16)
    most = pl.ds(0, devices - 1)
    pltpu.make_async_copy(received.at[most], received.at[most], all_recv).wait()
    for c in range(3):
        sums = dot_plain(collect, received[:, c].reshape(4 * devices, NF)).astype(BF16)
        summed[c * rows : (c + 1) * rows, :NF] = sums[:rows]
        summed[c * rows : (c + 1) * rows, NF:] = sums[rows:]

    for c in range(3):
        for copy in halos[c]:
            copy.wait_send()
    pltpu.make_async_copy(list_out.at[others], list_out.at[others], list_send).wait()
    over.wait_send()
    pltpu.make_async_copy(labels.at[0, some], labels.at[0, some], y_send).wait()
    pltpu.make_async_copy(labels.at[some], labels.at[some], z_send).wait()
    pltpu.make_async_copy(outgoing.at[most], outgoing.at[most], all_send).wait()


def exchange(blks, subs, syn, obs, table, first, second, mask, weight, owner, element):
    devices = blks * subs
    samples, rows = syn.shape[2], syn.shape[1]
    in_hbm = pl.BlockSpec(memory_space=pltpu.HBM)
    dma = pltpu.SemaphoreType.DMA
    return pl.pallas_call(
        functools.partial(exchange_kernel, blks, subs),
        out_shape=pltpu.VMEM((3 * rows, 2 * NF), BF16),
        in_specs=[in_hbm] * 9,
        out_specs=pl.BlockSpec(memory_space=pltpu.VMEM),
        scratch_shapes=[
            pltpu.VMEM((3, 2 * rows, samples), BF16),
            pltpu.VMEM(table.shape, BF16),
            pltpu.VMEM(first.shape, jnp.int32),
            pltpu.VMEM(second.shape, jnp.int32),
            pltpu.VMEM(mask.shape, jnp.int32),
            pltpu.VMEM(weight.shape, F32),
            pltpu.VMEM(owner.shape, jnp.int32),
            pltpu.VMEM(element.shape, jnp.int32),
            pltpu.VMEM((6, rows, 2 * NF), BF16),
            pltpu.VMEM((6, 2 * BLOCK, 2 * NF), BF16),
            pltpu.VMEM((subs, 8, NF), F32),
            pltpu.VMEM((8, NF), F32),
            pltpu.VMEM((subs, 8, NF), F32),
            pltpu.VMEM((subs, 8, NF), F32),
            pltpu.VMEM((4, blks // 4, 2 * subs, NF), BF16),
            pltpu.VMEM((devices, 3, 4, NF), BF16),
            pltpu.VMEM((devices, 3, 4, NF), BF16),
            dma((13,)),
            dma,
            dma,
            dma,
            dma,
            dma((2, 3)),
            dma((2, 3)),
            pltpu.SemaphoreType.REGULAR,
            dma,
            dma,
            dma,
            dma,
            dma,
            dma,
        ],
        compiler_params=pltpu.CompilerParams(
            collective_id=0, has_side_effects=True, vmem_limit_bytes=60 * 2**20
        ),
        cost_estimate=pl.CostEstimate(
            flops=2 * 10**9, bytes_accessed=3 * 10**6, transcendentals=0
        ),
        name="exchange",
    )(syn, obs, table, first, second, mask, weight, owner, element)


def finish_kernel(summed, table, out, result, sems):
    samples = result.shape[1]
    chunk = samples // sems.shape[0]
    copies = []
    for n in range(sems.shape[0]):
        columns = pl.ds(n * chunk, chunk)
        result[:, columns] = dot_plain(summed[...], table[:, columns])
        copies.append(
            pltpu.make_async_copy(result.at[:, columns], out.at[:, columns], sems.at[n])
        )
        copies[-1].start()
    for copy in copies:
        copy.wait()


def finish(summed, table):
    count, samples = summed.shape[0], table.shape[1]
    in_vmem = pl.BlockSpec(memory_space=pltpu.VMEM)
    out = pl.pallas_call(
        finish_kernel,
        out_shape=jax.ShapeDtypeStruct((count, samples), F32),
        in_specs=[in_vmem] * 2,
        out_specs=pl.BlockSpec(memory_space=pl.ANY),
        scratch_shapes=[
            pltpu.VMEM((count, samples), F32),
            pltpu.SemaphoreType.DMA((4,)),
        ],
        compiler_params=pltpu.CompilerParams(vmem_limit_bytes=40 * 2**20),
        cost_estimate=pl.CostEstimate(
            flops=7 * 10**8, bytes_accessed=3 * 10**6, transcendentals=0
        ),
        name="finish",
    )(summed, table)
    return out.reshape(3, count // 3, samples)


def on_device(
    blks,
    subs,
    synthetic,
    observed,
    pair_first,
    pair_second,
    pair_mask,
    pair_weight,
    station_owner,
    station_element,
):
    rows, _, samples = synthetic.shape
    forward, inverse = dft_tables(samples, NF)
    summed = exchange(
        blks,
        subs,
        jnp.transpose(synthetic, (1, 0, 2)),
        jnp.transpose(observed, (1, 0, 2)),
        jnp.asarray(forward),
        pair_first,
        pair_second,
        pair_mask,
        pair_weight,
        station_owner.reshape(1, rows),
        station_element.reshape(1, rows),
    )
    out = finish(summed, jnp.asarray(inverse))
    return jnp.transpose(out, (1, 0, 2))


def solution(mesh):
    blks, subs = mesh.shape["blk"], mesh.shape["sub"]
    return jax.shard_map(
        functools.partial(on_device, blks, subs),
        mesh=mesh,
        in_specs=(
            P(("blk", "sub"), None, None),
            P(("blk", "sub"), None, None),
            P("blk", "sub"),
            P("blk", "sub"),
            P("blk", "sub"),
            P("blk", "sub"),
            P(("blk", "sub"), None),
            P(("blk", "sub")),
        ),
        out_specs=P(("blk", "sub"), None, None),
        check_vma=False,
    )
```

```python
import functools
import itertools
import math

import jax
import jax.numpy as jnp
import numpy as np
from jax import lax
from jax.experimental import pallas as pl
from jax.experimental.pallas import tpu as pltpu
from jax.sharding import PartitionSpec as P

MESH = pl.DeviceIdType.MESH
NF = 128
BLOCK = 64
F32 = jnp.float32
BF16 = jnp.bfloat16


def dft_tables(samples, freqs):
    phase = (np.arange(samples)[:, None] * np.arange(freqs)[None, :]) % samples
    angles = phase.astype(np.float64) * (2.0 * math.pi / samples)
    scale = 1.0 / math.sqrt(samples)
    cosine, sine = np.cos(angles) * scale, np.sin(angles) * scale
    forward = np.concatenate([cosine, -sine], axis=1).astype(np.float32)
    doubled = np.where(np.arange(freqs) == 0, 1.0, 2.0)[:, None]
    inverse = np.concatenate([cosine.T * doubled, -sine.T * doubled], axis=0)
    return forward.astype(jnp.bfloat16), inverse.astype(np.float32).astype(jnp.bfloat16)


def in_two(x):
    high = x.astype(BF16)
    return high, (x - high.astype(F32)).astype(BF16)


def dot_rows(a, b):
    return lax.dot_general(a, b, (((1,), (1,)), ((), ())), preferred_element_type=F32)


def dot_plain(a, b):
    return jnp.dot(a, b, preferred_element_type=F32)


def features(pair):
    xr, xi = pair[0][:, :NF].astype(F32), pair[0][:, NF:].astype(F32)
    o_r, o_i = pair[1][:, :NF].astype(F32), pair[1][:, NF:].astype(F32)
    dr, di = xr - o_r, xi - o_i
    parts = [dr * xr + di * xi, dr * xi - di * xr, o_r * xr + o_i * xi, o_r * xi - o_i * xr]
    both = [in_two(p) for p in parts]
    return jnp.concatenate(
        [jnp.concatenate([b[i] for b in both], axis=1) for i in range(2)], axis=0
    )


def for_features(links):
    high, low = in_two(links)
    return jnp.concatenate(
        [jnp.concatenate([high, high], axis=1), jnp.concatenate([low, low], axis=1)], axis=0
    )


def linked(links, values):
    rows = links.shape[0] // 2
    both = dot_plain(links, values)
    return both[:rows] + both[rows:]


def spread(rows, count, shift):
    index = lax.broadcasted_iota(jnp.int32, (count, NF), 0) + shift
    return jnp.concatenate(
        [(index == rows[s : s + 1]).astype(F32).astype(BF16) for s in range(rows.shape[0])], axis=1
    )


def spread_weights(rows, weights, count, shift):
    index = lax.broadcasted_iota(jnp.int32, (count, NF), 0) + shift
    parts = []
    for part in in_two(weights):
        wide = part.astype(F32)
        parts.append(
            jnp.concatenate(
                [
                    jnp.where(index == rows[s : s + 1], wide[s : s + 1], 0.0).astype(BF16)
                    for s in range(rows.shape[0])
                ],
                axis=1,
            )
        )
    return jnp.concatenate(parts, axis=0)


def spread_order(core):
    left = [step + (core,) for step in itertools.product(range(4), range(4), range(4))]
    ways = {0: (0.0, 0.0), 1: (1.0, 0.0), 2: (1.0, 1.0), 3: (0.0, 1.0)}

    def links(step):
        return np.array([way for axis in step[:3] for way in ways[axis]])

    used, order = np.zeros(6), []
    while left:
        step = min(left, key=lambda t: (np.max(used + links(t)), -np.sum(links(t)), t))
        left.remove(step)
        used = used + links(step)
        order.append(step)
    return order


def exchange_kernel(
    blks,
    subs,
    syn_hbm,
    obs_hbm,
    table_hbm,
    first_hbm,
    second_hbm,
    mask_hbm,
    weight_hbm,
    owner_hbm,
    element_hbm,
    summed,
    traces,
    table,
    first,
    second,
    mask,
    weight,
    owner,
    element,
    spec,
    halo,
    list_out,
    list_over,
    lists,
    lists_prev,
    labels,
    outgoing,
    received,
    load_sems,
    list_send,
    list_recv,
    over_send,
    over_recv,
    halo_send,
    halo_recv,
    joined,
    y_send,
    y_recv,
    z_send,
    z_recv,
    all_send,
    all_recv,
):
    devices = blks * subs
    blk, sub = lax.axis_index("blk"), lax.axis_index("sub")
    me = blk * subs + sub
    rows = spec.shape[1]
    blocks = first.shape[0]
    def around(at, step, size):
        there = at + step
        return jnp.where(there >= size, there - size, there)

    subs_there = [around(sub, step, subs) for step in range(1, subs)]
    blks_there = [around(blk, step, blks) for step in range(1, blks)]
    blk_after, blk_before = blks_there[0], blks_there[-1]
    after = (jnp.where(sub == subs - 1, blk_after, blk), subs_there[0])
    before = (jnp.where(sub == 0, blk_before, blk), subs_there[-1])

    pairs = [
        (owner_hbm, owner),
        (element_hbm, element),
        (first_hbm, first),
        (second_hbm, second),
        (mask_hbm, mask),
        (weight_hbm, weight),
        (table_hbm, table),
        (syn_hbm.at[0], traces.at[0, pl.ds(0, rows)]),
        (obs_hbm.at[0], traces.at[0, pl.ds(rows, rows)]),
        (syn_hbm.at[1], traces.at[1, pl.ds(0, rows)]),
        (obs_hbm.at[1], traces.at[1, pl.ds(rows, rows)]),
        (syn_hbm.at[2], traces.at[2, pl.ds(0, rows)]),
        (obs_hbm.at[2], traces.at[2, pl.ds(rows, rows)]),
    ]
    loads = [
        pltpu.make_async_copy(src, dst, load_sems.at[i]) for i, (src, dst) in enumerate(pairs)
    ]
    for load in loads:
        load.start()

    barrier = pltpu.get_barrier_semaphore()

    def greet(there):
        pl.semaphore_signal(barrier, inc=1, device_id=there, device_id_type=MESH)

    for there in subs_there:
        greet((blk, there))
    for there in blks_there:
        greet((there, sub))

    @pl.when(sub == 0)
    def _():
        for s in range(1, subs):
            greet((blk_before, s))

    @pl.when(sub == subs - 1)
    def _():
        greet((blk_after, 0))

    for i in range(2):
        loads[i].wait()
    lane = lax.broadcasted_iota(jnp.int32, (rows, rows), 1)
    line = lax.broadcasted_iota(jnp.int32, (rows, rows), 0)
    owner_row = owner[...]

    def column(row):
        return jnp.sum(jnp.where(lane == line, row, 0), axis=1, keepdims=True)

    owner_column, element_column = column(owner_row), column(element[...]).astype(F32)
    same = owner_column == owner_row
    rank_column = jnp.sum(jnp.where(same & (lane < line), 1, 0), axis=1, keepdims=True)
    label_rows = []
    for k in range(2):
        chosen = ((owner_column == lane) & (rank_column == k)).astype(F32)
        label_rows.append(
            jnp.sum(chosen * (element_column - rows), axis=0, keepdims=True) + float(rows)
        )

    for i in range(2, 6):
        loads[i].wait()
    base = (blk * blocks + lax.broadcasted_iota(jnp.int32, (blocks, NF), 0)) * BLOCK
    code = ((first[...] - base) * (2 * BLOCK) + (second[...] - base)).astype(F32)
    slot_weight = weight[...] * mask[...].astype(F32)
    zero_row = jnp.zeros((1, NF), F32)
    for s in range(subs):
        lines = [max(2 * s - 1, 0), 2 * s, 2 * s + 1]
        list_out[s] = jnp.concatenate(
            [code[i : i + 1] for i in lines]
            + [slot_weight[i : i + 1] for i in lines]
            + label_rows,
            axis=0,
        )
    list_over[...] = jnp.concatenate(
        [code[blocks - 1 : blocks]]
        + [zero_row] * 2
        + [slot_weight[blocks - 1 : blocks]]
        + [zero_row] * 4,
        axis=0,
    )
    lists[sub] = list_out[sub]

    pl.semaphore_wait(barrier, subs + blks - 1)
    for there in subs_there:
        pltpu.make_async_remote_copy(
            src_ref=list_out.at[there],
            dst_ref=lists.at[sub],
            send_sem=list_send,
            recv_sem=list_recv,
            device_id=(blk, there),
            device_id_type=MESH,
        ).start()
    over = pltpu.make_async_remote_copy(
        src_ref=list_over,
        dst_ref=lists_prev.at[sub],
        send_sem=over_send,
        recv_sem=over_recv,
        device_id=(blk_after, 0),
        device_id_type=MESH,
    )
    over.start()

    def transform(c):
        both = dot_plain(traces[c], table[...]).astype(BF16)
        spec[2 * c] = both[:rows]
        spec[2 * c + 1] = both[rows:]

    for i in range(6, 9):
        loads[i].wait()
    transform(0)

    def halo_copies(c):
        q = pl.ds(2 * c, 2)
        return [
            pltpu.make_async_remote_copy(
                src_ref=spec.at[q, pl.ds(0, BLOCK)],
                dst_ref=halo.at[q, pl.ds(BLOCK, BLOCK)],
                send_sem=halo_send.at[0, c],
                recv_sem=halo_recv.at[0, c],
                device_id=before,
                device_id_type=MESH,
            ),
            pltpu.make_async_remote_copy(
                src_ref=spec.at[q, pl.ds(rows - BLOCK, BLOCK)],
                dst_ref=halo.at[q, pl.ds(0, BLOCK)],
                send_sem=halo_send.at[1, c],
                recv_sem=halo_recv.at[1, c],
                device_id=after,
                device_id_type=MESH,
            ),
        ]

    halos = [halo_copies(c) for c in range(3)]
    for copy in halos[0]:
        copy.start()
    for c in (1, 2):
        loads[7 + 2 * c].wait()
        loads[8 + 2 * c].wait()
        transform(c)
        for copy in halos[c]:
            copy.start()

    for there in subs_there:
        pl.semaphore_signal(joined, inc=1, device_id=(blk, there), device_id_type=MESH)

    rank_row = jnp.sum(jnp.where(same & (line < lane), 1, 0), axis=0, keepdims=True)
    target = owner_row * 4 + rank_row * 2
    slot = lax.broadcasted_iota(jnp.int32, (4 * devices, 2 * rows), 0)
    placement = (slot == jnp.concatenate([target, target + 1], axis=1)).astype(F32).astype(BF16)

    def stations(c):
        return (spec[2 * c], spec[2 * c + 1])

    own = [features(stations(c)) for c in range(3)]

    others = pl.ds(0, subs - 1)
    pltpu.make_async_copy(lists.at[others], lists.at[others], list_recv).wait()

    z, y = lax.div(blk, 4), lax.rem(blk, 4)
    labels[z, y] = jnp.concatenate([lists[:, 6, :], lists[:, 7, :]], axis=0).astype(BF16)
    for step in range(1, 4):
        pltpu.make_async_remote_copy(
            src_ref=labels.at[z, y],
            dst_ref=labels.at[z, y],
            send_sem=y_send,
            recv_sem=y_recv,
            device_id=(z * 4 + around(y, step, 4), sub),
            device_id_type=MESH,
        ).start()

    @pl.when(sub == 0)
    def _():
        pltpu.make_async_copy(lists_prev, lists_prev, over_recv).wait()

    @pl.when(sub != 0)
    def _():
        lists_prev[...] = lists[...]

    def unpacked(ref, k):
        codes = ref[:, k, :].astype(jnp.int32)
        return codes >> 7, codes & 127, ref[:, 3 + k, :]

    first0, second0, weight0 = unpacked(lists_prev, 0)
    first1, second1, weight1 = unpacked(lists, 1)
    first2, second2, weight2 = unpacked(lists, 2)
    to_prev = dot_rows(spread_weights(second0, weight0, BLOCK, BLOCK), spread(first0, rows, 0))
    upper = dot_rows(spread_weights(first1, weight1, BLOCK, 0), spread(second1, rows, 0))
    lower = dot_rows(spread_weights(first2, weight2, BLOCK, 0), spread(second2, rows, 0))
    to_prev, upper, lower = (both[:BLOCK] + both[BLOCK:] for both in (to_prev, upper, lower))
    half = lax.broadcasted_iota(jnp.int32, (BLOCK, rows), 1) >= BLOCK
    inside = jnp.where(half, pltpu.roll(lower, BLOCK, 1), 0.0)
    one_way = jnp.concatenate([upper, inside], axis=0)
    link_own = for_features(one_way + one_way.T)
    link_halo = for_features(jnp.concatenate([to_prev, jnp.where(half, lower, 0.0)], axis=0))
    inner = [linked(link_own, own[c]) for c in range(3)]

    for c in range(3):
        for copy in halos[c]:
            copy.wait_recv()
        sums = inner[c] + linked(link_halo, features((halo[2 * c], halo[2 * c + 1])))
        g1r, g1i, g2r, g2i = (sums[:, i * NF : (i + 1) * NF] for i in range(4))
        x, o = stations(c)
        xr, xi = x[:, :NF].astype(F32), x[:, NF:].astype(F32)
        dr, di = xr - o[:, :NF].astype(F32), xi - o[:, NF:].astype(F32)
        real = (xr * g1r - xi * g1i) + (dr * g2r - di * g2i)
        imag = (xr * g1i + xi * g1r) + (dr * g2i + di * g2r)
        adjoint = jnp.concatenate([real, imag], axis=0).astype(BF16)
        outgoing[:, c] = dot_plain(placement, adjoint).astype(BF16).reshape(devices, 4, NF)

    pl.semaphore_wait(joined, subs - 1)

    core = lax.rem(sub, 2)

    def turns(at, size):
        up = [around(at, step, size) for step in range(1, size)]
        return [at] + [jnp.where(core == 0, up[i], up[-1 - i]) for i in range(size - 1)]

    chip = lax.div(me, 2)
    z_to, y_to, x_to = turns(z, 4), turns(y, 4), turns(lax.div(sub, 2), 4)
    core_to = [core, 1 - core]
    received[core, chip] = outgoing[me]

    def deliver(step):
        dz, dy, dx, other = step
        blk_to, sub_to = z_to[dz] * 4 + y_to[dy], x_to[dx] * 2 + core_to[other]
        pltpu.make_async_remote_copy(
            src_ref=outgoing.at[blk_to * subs + sub_to],
            dst_ref=received.at[core, chip],
            send_sem=all_send,
            recv_sem=all_recv.at[other],
            device_id=(blk_to, sub_to),
            device_id_type=MESH,
        ).start()

    order = spread_order(1) + spread_order(0)[1:]
    for step in order[:32]:
        deliver(step)
    some = pl.ds(0, 3)
    pltpu.make_async_copy(labels.at[0, some], labels.at[0, some], y_recv).wait()
    for step in range(1, 4):
        pltpu.make_async_remote_copy(
            src_ref=labels.at[z],
            dst_ref=labels.at[z],
            send_sem=z_send,
            recv_sem=z_recv,
            device_id=(around(z, step, 4) * 4 + y, sub),
            device_id_type=MESH,
        ).start()

    for step in order[32:]:
        deliver(step)

    pltpu.make_async_copy(labels.at[some], labels.at[some], z_recv).wait()
    by_owner = labels[...].reshape(2 * devices, NF)
    arrived = lax.broadcasted_iota(jnp.int32, (2 * devices, 2 * devices), 1)
    held = lax.broadcasted_iota(jnp.int32, (2 * devices, 2 * devices), 0)
    sub_bits = subs.bit_length() - 1
    wanted = (
        ((arrived >> (sub_bits + 1)) << (sub_bits + 1))
        + (((arrived >> 1) & 1) << sub_bits)
        + (((arrived >> 2) & (subs // 2 - 1)) << 1)
    )
    owner_line = lax.broadcasted_iota(jnp.int32, (rows, 2 * devices), 0)

    def collector(source_core):
        repeated = lax.dot_general(
            by_owner,
            (held == wanted + source_core).astype(F32).astype(BF16),
            (((0,), (0,)), ((), ())),
            preferred_element_type=F32,
        )
        label = jnp.sum(jnp.where(owner_line == me, repeated, 0.0), axis=0, keepdims=True)
        return jnp.concatenate(
            [
                ((label == owner_line.astype(F32)) & ((arrived[:rows] & 1) == i)).astype(F32)
                for i in range(2)
            ],
            axis=0,
        ).astype(BF16)

    collect_other, collect_same = collector(1 - core), collector(core)

    def sums(collect, source_core, c):
        return dot_plain(collect, received[source_core, :, c].reshape(2 * devices, NF))

    pltpu.make_async_copy(received.at[0], received.at[0], all_recv.at[1]).wait()
    first_sums = [sums(collect_other, 1 - core, c) for c in range(3)]
    most = pl.ds(0, devices // 2 - 1)
    pltpu.make_async_copy(received.at[0, most], received.at[0, most], all_recv.at[0]).wait()
    for c in range(3):
        total = (first_sums[c] + sums(collect_same, core, c)).astype(BF16)
        summed[c * rows : (c + 1) * rows, :NF] = total[:rows]
        summed[c * rows : (c + 1) * rows, NF:] = total[rows:]

    for c in range(3):
        for copy in halos[c]:
            copy.wait_send()
    pltpu.make_async_copy(list_out.at[others], list_out.at[others], list_send).wait()
    over.wait_send()
    pltpu.make_async_copy(labels.at[0, some], labels.at[0, some], y_send).wait()
    pltpu.make_async_copy(labels.at[some], labels.at[some], z_send).wait()
    most = pl.ds(0, devices - 1)
    pltpu.make_async_copy(outgoing.at[most], outgoing.at[most], all_send).wait()


def exchange(blks, subs, syn, obs, table, first, second, mask, weight, owner, element):
    devices = blks * subs
    samples, rows = syn.shape[2], syn.shape[1]
    in_hbm = pl.BlockSpec(memory_space=pltpu.HBM)
    dma = pltpu.SemaphoreType.DMA
    return pl.pallas_call(
        functools.partial(exchange_kernel, blks, subs),
        out_shape=pltpu.VMEM((3 * rows, 2 * NF), BF16),
        in_specs=[in_hbm] * 9,
        out_specs=pl.BlockSpec(memory_space=pltpu.VMEM),
        scratch_shapes=[
            pltpu.VMEM((3, 2 * rows, samples), BF16),
            pltpu.VMEM(table.shape, BF16),
            pltpu.VMEM(first.shape, jnp.int32),
            pltpu.VMEM(second.shape, jnp.int32),
            pltpu.VMEM(mask.shape, jnp.int32),
            pltpu.VMEM(weight.shape, F32),
            pltpu.VMEM(owner.shape, jnp.int32),
            pltpu.VMEM(element.shape, jnp.int32),
            pltpu.VMEM((6, rows, 2 * NF), BF16),
            pltpu.VMEM((6, 2 * BLOCK, 2 * NF), BF16),
            pltpu.VMEM((subs, 8, NF), F32),
            pltpu.VMEM((8, NF), F32),
            pltpu.VMEM((subs, 8, NF), F32),
            pltpu.VMEM((subs, 8, NF), F32),
            pltpu.VMEM((4, blks // 4, 2 * subs, NF), BF16),
            pltpu.VMEM((devices, 3, 4, NF), BF16),
            pltpu.VMEM((2, devices // 2, 3, 4, NF), BF16),
            dma((13,)),
            dma,
            dma,
            dma,
            dma,
            dma((2, 3)),
            dma((2, 3)),
            pltpu.SemaphoreType.REGULAR,
            dma,
            dma,
            dma,
            dma,
            dma,
            dma((2,)),
        ],
        compiler_params=pltpu.CompilerParams(
            collective_id=0, has_side_effects=True, vmem_limit_bytes=60 * 2**20
        ),
        cost_estimate=pl.CostEstimate(
            flops=2 * 10**9, bytes_accessed=3 * 10**6, transcendentals=0
        ),
        name="exchange",
    )(syn, obs, table, first, second, mask, weight, owner, element)


def finish_kernel(summed, table, out, result, sems):
    samples = result.shape[1]
    chunk = samples // sems.shape[0]
    copies = []
    for n in range(sems.shape[0]):
        columns = pl.ds(n * chunk, chunk)
        result[:, columns] = dot_plain(summed[...], table[:, columns])
        copies.append(
            pltpu.make_async_copy(result.at[:, columns], out.at[:, columns], sems.at[n])
        )
        copies[-1].start()
    for copy in copies:
        copy.wait()


def finish(summed, table):
    count, samples = summed.shape[0], table.shape[1]
    in_vmem = pl.BlockSpec(memory_space=pltpu.VMEM)
    out = pl.pallas_call(
        finish_kernel,
        out_shape=jax.ShapeDtypeStruct((count, samples), F32),
        in_specs=[in_vmem] * 2,
        out_specs=pl.BlockSpec(memory_space=pl.ANY),
        scratch_shapes=[
            pltpu.VMEM((count, samples), F32),
            pltpu.SemaphoreType.DMA((4,)),
        ],
        compiler_params=pltpu.CompilerParams(vmem_limit_bytes=40 * 2**20),
        cost_estimate=pl.CostEstimate(
            flops=7 * 10**8, bytes_accessed=3 * 10**6, transcendentals=0
        ),
        name="finish",
    )(summed, table)
    return out.reshape(3, count // 3, samples)


def on_device(
    blks,
    subs,
    synthetic,
    observed,
    pair_first,
    pair_second,
    pair_mask,
    pair_weight,
    station_owner,
    station_element,
):
    rows, _, samples = synthetic.shape
    forward, inverse = dft_tables(samples, NF)
    summed = exchange(
        blks,
        subs,
        jnp.transpose(synthetic, (1, 0, 2)),
        jnp.transpose(observed, (1, 0, 2)),
        jnp.asarray(forward),
        pair_first,
        pair_second,
        pair_mask,
        pair_weight,
        station_owner.reshape(1, rows),
        station_element.reshape(1, rows),
    )
    out = finish(summed, jnp.asarray(inverse))
    return jnp.transpose(out, (1, 0, 2))


def solution(mesh):
    blks, subs = mesh.shape["blk"], mesh.shape["sub"]
    return jax.shard_map(
        functools.partial(on_device, blks, subs),
        mesh=mesh,
        in_specs=(
            P(("blk", "sub"), None, None),
            P(("blk", "sub"), None, None),
            P("blk", "sub"),
            P("blk", "sub"),
            P("blk", "sub"),
            P("blk", "sub"),
            P(("blk", "sub"), None),
            P(("blk", "sub")),
        ),
        out_specs=P(("blk", "sub"), None, None),
        check_vma=False,
    )
```

```python
import functools
import itertools
import math

import jax
import jax.numpy as jnp
import numpy as np
from jax import lax
from jax.experimental import pallas as pl
from jax.experimental.pallas import tpu as pltpu
from jax.sharding import PartitionSpec as P

MESH = pl.DeviceIdType.MESH
NF = 128
BLOCK = 64
F32 = jnp.float32
BF16 = jnp.bfloat16


def dft_tables(samples, freqs):
    phase = (np.arange(samples)[:, None] * np.arange(freqs)[None, :]) % samples
    angles = phase.astype(np.float64) * (2.0 * math.pi / samples)
    scale = 1.0 / math.sqrt(samples)
    cosine, sine = np.cos(angles) * scale, np.sin(angles) * scale
    forward = np.concatenate([cosine, -sine], axis=1).astype(np.float32)
    doubled = np.where(np.arange(freqs) == 0, 1.0, 2.0)[:, None]
    inverse = np.concatenate([cosine.T * doubled, -sine.T * doubled], axis=0)
    return forward.astype(jnp.bfloat16), inverse.astype(np.float32).astype(jnp.bfloat16)


def in_two(x):
    high = x.astype(BF16)
    return high, (x - high.astype(F32)).astype(BF16)


def dot_rows(a, b):
    return lax.dot_general(a, b, (((1,), (1,)), ((), ())), preferred_element_type=F32)


def dot_plain(a, b):
    return jnp.dot(a, b, preferred_element_type=F32)


def features(pair):
    xr, xi = pair[0][:, :NF].astype(F32), pair[0][:, NF:].astype(F32)
    o_r, o_i = pair[1][:, :NF].astype(F32), pair[1][:, NF:].astype(F32)
    dr, di = xr - o_r, xi - o_i
    parts = [dr * xr + di * xi, dr * xi - di * xr, o_r * xr + o_i * xi, o_r * xi - o_i * xr]
    both = [in_two(p) for p in parts]
    return jnp.concatenate(
        [jnp.concatenate([b[i] for b in both], axis=1) for i in range(2)], axis=0
    )


def for_features(links):
    high, low = in_two(links)
    return jnp.concatenate(
        [jnp.concatenate([high, high], axis=1), jnp.concatenate([low, low], axis=1)], axis=0
    )


def linked(links, values):
    rows = links.shape[0] // 2
    both = dot_plain(links, values)
    return both[:rows] + both[rows:]


def spread(rows, count, shift):
    index = lax.broadcasted_iota(jnp.int32, (count, NF), 0) + shift
    return jnp.concatenate(
        [(index == rows[s : s + 1]).astype(F32).astype(BF16) for s in range(rows.shape[0])], axis=1
    )


def spread_weights(rows, weights, count, shift):
    index = lax.broadcasted_iota(jnp.int32, (count, NF), 0) + shift
    parts = []
    for part in in_two(weights):
        wide = part.astype(F32)
        parts.append(
            jnp.concatenate(
                [
                    jnp.where(index == rows[s : s + 1], wide[s : s + 1], 0.0).astype(BF16)
                    for s in range(rows.shape[0])
                ],
                axis=1,
            )
        )
    return jnp.concatenate(parts, axis=0)


def spread_order(core):
    left = [step + (core,) for step in itertools.product(range(4), range(4), range(4))]
    ways = {0: (0.0, 0.0), 1: (1.0, 0.0), 2: (1.0, 1.0), 3: (0.0, 1.0)}

    def links(step):
        return np.array([way for axis in step[:3] for way in ways[axis]])

    used, order = np.zeros(6), []
    while left:
        step = min(left, key=lambda t: (np.max(used + links(t)), -np.sum(links(t)), t))
        left.remove(step)
        used = used + links(step)
        order.append(step)
    return order


def exchange_kernel(
    blks,
    subs,
    syn_hbm,
    obs_hbm,
    table_hbm,
    first_hbm,
    second_hbm,
    mask_hbm,
    weight_hbm,
    owner_hbm,
    element_hbm,
    summed,
    traces,
    table,
    first,
    second,
    mask,
    weight,
    owner,
    element,
    spec,
    halo,
    list_out,
    list_over,
    lists,
    lists_prev,
    near_out,
    near_labels,
    labels,
    outgoing,
    received,
    load_sems,
    list_send,
    list_recv,
    over_send,
    over_recv,
    halo_send,
    halo_recv,
    joined,
    near_send,
    near_recv,
    y_send,
    y_recv,
    z_send,
    z_recv,
    all_send,
    all_recv,
):
    devices = blks * subs
    blk, sub = lax.axis_index("blk"), lax.axis_index("sub")
    me = blk * subs + sub
    rows = spec.shape[1]
    blocks = first.shape[0]
    def around(at, step, size):
        there = at + step
        return jnp.where(there >= size, there - size, there)

    subs_there = [around(sub, step, subs) for step in range(1, subs)]
    blks_there = [around(blk, step, blks) for step in range(1, blks)]
    blk_after, blk_before = blks_there[0], blks_there[-1]
    after = (jnp.where(sub == subs - 1, blk_after, blk), subs_there[0])
    before = (jnp.where(sub == 0, blk_before, blk), subs_there[-1])

    pairs = [
        (table_hbm, table),
        (syn_hbm.at[0], traces.at[0, pl.ds(0, rows)]),
        (obs_hbm.at[0], traces.at[0, pl.ds(rows, rows)]),
        (first_hbm, first),
        (second_hbm, second),
        (mask_hbm, mask),
        (weight_hbm, weight),
        (syn_hbm.at[1], traces.at[1, pl.ds(0, rows)]),
        (obs_hbm.at[1], traces.at[1, pl.ds(rows, rows)]),
        (syn_hbm.at[2], traces.at[2, pl.ds(0, rows)]),
        (obs_hbm.at[2], traces.at[2, pl.ds(rows, rows)]),
        (owner_hbm, owner),
        (element_hbm, element),
    ]
    loads = [
        pltpu.make_async_copy(src, dst, load_sems.at[i]) for i, (src, dst) in enumerate(pairs)
    ]
    for load in loads:
        load.start()

    barrier = pltpu.get_barrier_semaphore()

    def greet(there):
        pl.semaphore_signal(barrier, inc=1, device_id=there, device_id_type=MESH)

    for there in subs_there:
        greet((blk, there))
    for there in blks_there:
        greet((there, sub))

    @pl.when(sub == 0)
    def _():
        for s in range(1, subs):
            greet((blk_before, s))

    @pl.when(sub == subs - 1)
    def _():
        greet((blk_after, 0))

    def transform(c):
        both = dot_plain(traces[c], table[...]).astype(BF16)
        spec[2 * c] = both[:rows]
        spec[2 * c + 1] = both[rows:]

    for i in range(3):
        loads[i].wait()
    transform(0)

    pl.semaphore_wait(barrier, subs + blks - 1)

    def halo_copies(c):
        q = pl.ds(2 * c, 2)
        return [
            pltpu.make_async_remote_copy(
                src_ref=spec.at[q, pl.ds(0, BLOCK)],
                dst_ref=halo.at[q, pl.ds(BLOCK, BLOCK)],
                send_sem=halo_send.at[0, c],
                recv_sem=halo_recv.at[0, c],
                device_id=before,
                device_id_type=MESH,
            ),
            pltpu.make_async_remote_copy(
                src_ref=spec.at[q, pl.ds(rows - BLOCK, BLOCK)],
                dst_ref=halo.at[q, pl.ds(0, BLOCK)],
                send_sem=halo_send.at[1, c],
                recv_sem=halo_recv.at[1, c],
                device_id=after,
                device_id_type=MESH,
            ),
        ]

    halos = [halo_copies(c) for c in range(3)]
    for copy in halos[0]:
        copy.start()

    for i in range(3, 7):
        loads[i].wait()
    base = (blk * blocks + lax.broadcasted_iota(jnp.int32, (blocks, NF), 0)) * BLOCK
    code = ((first[...] - base) * (2 * BLOCK) + (second[...] - base)).astype(F32)
    slot_weight = weight[...] * mask[...].astype(F32)
    zero_row = jnp.zeros((1, NF), F32)
    for s in range(subs):
        lines = [max(2 * s - 1, 0), 2 * s, 2 * s + 1]
        list_out[s] = jnp.concatenate(
            [code[i : i + 1] for i in lines]
            + [slot_weight[i : i + 1] for i in lines]
            + [zero_row] * 2,
            axis=0,
        )
    list_over[...] = jnp.concatenate(
        [code[blocks - 1 : blocks]]
        + [zero_row] * 2
        + [slot_weight[blocks - 1 : blocks]]
        + [zero_row] * 4,
        axis=0,
    )
    lists[sub] = list_out[sub]

    for there in subs_there:
        pltpu.make_async_remote_copy(
            src_ref=list_out.at[there],
            dst_ref=lists.at[sub],
            send_sem=list_send,
            recv_sem=list_recv,
            device_id=(blk, there),
            device_id_type=MESH,
        ).start()
    over = pltpu.make_async_remote_copy(
        src_ref=list_over,
        dst_ref=lists_prev.at[sub],
        send_sem=over_send,
        recv_sem=over_recv,
        device_id=(blk_after, 0),
        device_id_type=MESH,
    )
    over.start()

    for c in (1, 2):
        loads[5 + 2 * c].wait()
        loads[6 + 2 * c].wait()
        transform(c)
        for copy in halos[c]:
            copy.start()

    for there in subs_there:
        pl.semaphore_signal(joined, inc=1, device_id=(blk, there), device_id_type=MESH)

    loads[11].wait()
    loads[12].wait()
    lane = lax.broadcasted_iota(jnp.int32, (rows, rows), 1)
    line = lax.broadcasted_iota(jnp.int32, (rows, rows), 0)
    owner_row = owner[...]

    def column(row):
        return jnp.sum(jnp.where(lane == line, row, 0), axis=1, keepdims=True)

    owner_column, element_column = column(owner_row), column(element[...]).astype(F32)
    same = owner_column == owner_row
    rank_column = jnp.sum(jnp.where(same & (lane < line), 1, 0), axis=1, keepdims=True)
    label_rows = []
    for k in range(2):
        chosen = ((owner_column == lane) & (rank_column == k)).astype(F32)
        label_rows.append(
            jnp.sum(chosen * (element_column - rows), axis=0, keepdims=True) + float(rows)
        )

    near_out[...] = jnp.concatenate(label_rows + [zero_row] * 6, axis=0)
    near_labels[sub] = near_out[...]
    for there in subs_there:
        pltpu.make_async_remote_copy(
            src_ref=near_out,
            dst_ref=near_labels.at[sub],
            send_sem=near_send,
            recv_sem=near_recv,
            device_id=(blk, there),
            device_id_type=MESH,
        ).start()

    rank_row = jnp.sum(jnp.where(same & (line < lane), 1, 0), axis=0, keepdims=True)
    target = owner_row * 4 + rank_row * 2
    slot = lax.broadcasted_iota(jnp.int32, (4 * devices, 2 * rows), 0)
    placement = (slot == jnp.concatenate([target, target + 1], axis=1)).astype(F32).astype(BF16)

    def stations(c):
        return (spec[2 * c], spec[2 * c + 1])

    own = [features(stations(c)) for c in range(3)]

    others = pl.ds(0, subs - 1)
    pltpu.make_async_copy(lists.at[others], lists.at[others], list_recv).wait()

    @pl.when(sub == 0)
    def _():
        pltpu.make_async_copy(lists_prev, lists_prev, over_recv).wait()

    @pl.when(sub != 0)
    def _():
        lists_prev[...] = lists[...]

    def unpacked(ref, k):
        codes = ref[:, k, :].astype(jnp.int32)
        return codes >> 7, codes & 127, ref[:, 3 + k, :]

    first0, second0, weight0 = unpacked(lists_prev, 0)
    first1, second1, weight1 = unpacked(lists, 1)
    first2, second2, weight2 = unpacked(lists, 2)
    to_prev = dot_rows(spread_weights(second0, weight0, BLOCK, BLOCK), spread(first0, rows, 0))
    upper = dot_rows(spread_weights(first1, weight1, BLOCK, 0), spread(second1, rows, 0))
    lower = dot_rows(spread_weights(first2, weight2, BLOCK, 0), spread(second2, rows, 0))
    to_prev, upper, lower = (both[:BLOCK] + both[BLOCK:] for both in (to_prev, upper, lower))
    half = lax.broadcasted_iota(jnp.int32, (BLOCK, rows), 1) >= BLOCK
    inside = jnp.where(half, pltpu.roll(lower, BLOCK, 1), 0.0)
    one_way = jnp.concatenate([upper, inside], axis=0)
    link_own = for_features(one_way + one_way.T)
    link_halo = for_features(jnp.concatenate([to_prev, jnp.where(half, lower, 0.0)], axis=0))
    inner = [linked(link_own, own[c]) for c in range(3)]

    z, y = lax.div(blk, 4), lax.rem(blk, 4)
    pltpu.make_async_copy(near_labels.at[others], near_labels.at[others], near_recv).wait()
    labels[z, y] = jnp.concatenate(
        [near_labels[:, 0, :], near_labels[:, 1, :]], axis=0
    ).astype(BF16)
    for step in range(1, 4):
        pltpu.make_async_remote_copy(
            src_ref=labels.at[z, y],
            dst_ref=labels.at[z, y],
            send_sem=y_send,
            recv_sem=y_recv,
            device_id=(z * 4 + around(y, step, 4), sub),
            device_id_type=MESH,
        ).start()

    for c in range(3):
        for copy in halos[c]:
            copy.wait_recv()
        sums = inner[c] + linked(link_halo, features((halo[2 * c], halo[2 * c + 1])))
        g1r, g1i, g2r, g2i = (sums[:, i * NF : (i + 1) * NF] for i in range(4))
        x, o = stations(c)
        xr, xi = x[:, :NF].astype(F32), x[:, NF:].astype(F32)
        dr, di = xr - o[:, :NF].astype(F32), xi - o[:, NF:].astype(F32)
        real = (xr * g1r - xi * g1i) + (dr * g2r - di * g2i)
        imag = (xr * g1i + xi * g1r) + (dr * g2i + di * g2r)
        adjoint = jnp.concatenate([real, imag], axis=0).astype(BF16)
        outgoing[:, c] = dot_plain(placement, adjoint).astype(BF16).reshape(devices, 4, NF)

    pl.semaphore_wait(joined, subs - 1)

    core = lax.rem(sub, 2)

    def turns(at, size):
        up = [around(at, step, size) for step in range(1, size)]
        return [at] + [jnp.where(core == 0, up[i], up[-1 - i]) for i in range(size - 1)]

    chip = lax.div(me, 2)
    z_to, y_to, x_to = turns(z, 4), turns(y, 4), turns(lax.div(sub, 2), 4)
    core_to = [core, 1 - core]
    received[core, chip] = outgoing[me]

    def deliver(step):
        dz, dy, dx, other = step
        blk_to, sub_to = z_to[dz] * 4 + y_to[dy], x_to[dx] * 2 + core_to[other]
        pltpu.make_async_remote_copy(
            src_ref=outgoing.at[blk_to * subs + sub_to],
            dst_ref=received.at[core, chip],
            send_sem=all_send,
            recv_sem=all_recv.at[other],
            device_id=(blk_to, sub_to),
            device_id_type=MESH,
        ).start()

    order = spread_order(1) + spread_order(0)[1:]
    for step in order[:32]:
        deliver(step)
    some = pl.ds(0, 3)
    pltpu.make_async_copy(labels.at[0, some], labels.at[0, some], y_recv).wait()
    for step in range(1, 4):
        pltpu.make_async_remote_copy(
            src_ref=labels.at[z],
            dst_ref=labels.at[z],
            send_sem=z_send,
            recv_sem=z_recv,
            device_id=(around(z, step, 4) * 4 + y, sub),
            device_id_type=MESH,
        ).start()

    for step in order[32:]:
        deliver(step)

    pltpu.make_async_copy(labels.at[some], labels.at[some], z_recv).wait()
    by_owner = labels[...].reshape(2 * devices, NF)
    arrived = lax.broadcasted_iota(jnp.int32, (2 * devices, 2 * devices), 1)
    held = lax.broadcasted_iota(jnp.int32, (2 * devices, 2 * devices), 0)
    sub_bits = subs.bit_length() - 1
    wanted = (
        ((arrived >> (sub_bits + 1)) << (sub_bits + 1))
        + (((arrived >> 1) & 1) << sub_bits)
        + (((arrived >> 2) & (subs // 2 - 1)) << 1)
    )
    owner_line = lax.broadcasted_iota(jnp.int32, (rows, 2 * devices), 0)

    def collector(source_core):
        repeated = lax.dot_general(
            by_owner,
            (held == wanted + source_core).astype(F32).astype(BF16),
            (((0,), (0,)), ((), ())),
            preferred_element_type=F32,
        )
        label = jnp.sum(jnp.where(owner_line == me, repeated, 0.0), axis=0, keepdims=True)
        return jnp.concatenate(
            [
                ((label == owner_line.astype(F32)) & ((arrived[:rows] & 1) == i)).astype(F32)
                for i in range(2)
            ],
            axis=0,
        ).astype(BF16)

    collect_other, collect_same = collector(1 - core), collector(core)

    def sums(collect, source_core, c):
        return dot_plain(collect, received[source_core, :, c].reshape(2 * devices, NF))

    pltpu.make_async_copy(received.at[0], received.at[0], all_recv.at[1]).wait()
    first_sums = [sums(collect_other, 1 - core, c) for c in range(3)]
    most = pl.ds(0, devices // 2 - 1)
    pltpu.make_async_copy(received.at[0, most], received.at[0, most], all_recv.at[0]).wait()
    for c in range(3):
        total = (first_sums[c] + sums(collect_same, core, c)).astype(BF16)
        summed[c * rows : (c + 1) * rows, :NF] = total[:rows]
        summed[c * rows : (c + 1) * rows, NF:] = total[rows:]

    for c in range(3):
        for copy in halos[c]:
            copy.wait_send()
    pltpu.make_async_copy(list_out.at[others], list_out.at[others], list_send).wait()
    over.wait_send()
    pltpu.make_async_copy(near_labels.at[others], near_labels.at[others], near_send).wait()
    pltpu.make_async_copy(labels.at[0, some], labels.at[0, some], y_send).wait()
    pltpu.make_async_copy(labels.at[some], labels.at[some], z_send).wait()
    most = pl.ds(0, devices - 1)
    pltpu.make_async_copy(outgoing.at[most], outgoing.at[most], all_send).wait()


def exchange(blks, subs, syn, obs, table, first, second, mask, weight, owner, element):
    devices = blks * subs
    samples, rows = syn.shape[2], syn.shape[1]
    in_hbm = pl.BlockSpec(memory_space=pltpu.HBM)
    dma = pltpu.SemaphoreType.DMA
    return pl.pallas_call(
        functools.partial(exchange_kernel, blks, subs),
        out_shape=pltpu.VMEM((3 * rows, 2 * NF), BF16),
        in_specs=[in_hbm] * 9,
        out_specs=pl.BlockSpec(memory_space=pltpu.VMEM),
        scratch_shapes=[
            pltpu.VMEM((3, 2 * rows, samples), BF16),
            pltpu.VMEM(table.shape, BF16),
            pltpu.VMEM(first.shape, jnp.int32),
            pltpu.VMEM(second.shape, jnp.int32),
            pltpu.VMEM(mask.shape, jnp.int32),
            pltpu.VMEM(weight.shape, F32),
            pltpu.VMEM(owner.shape, jnp.int32),
            pltpu.VMEM(element.shape, jnp.int32),
            pltpu.VMEM((6, rows, 2 * NF), BF16),
            pltpu.VMEM((6, 2 * BLOCK, 2 * NF), BF16),
            pltpu.VMEM((subs, 8, NF), F32),
            pltpu.VMEM((8, NF), F32),
            pltpu.VMEM((subs, 8, NF), F32),
            pltpu.VMEM((subs, 8, NF), F32),
            pltpu.VMEM((8, NF), F32),
            pltpu.VMEM((subs, 8, NF), F32),
            pltpu.VMEM((4, blks // 4, 2 * subs, NF), BF16),
            pltpu.VMEM((devices, 3, 4, NF), BF16),
            pltpu.VMEM((2, devices // 2, 3, 4, NF), BF16),
            dma((13,)),
            dma,
            dma,
            dma,
            dma,
            dma((2, 3)),
            dma((2, 3)),
            pltpu.SemaphoreType.REGULAR,
            dma,
            dma,
            dma,
            dma,
            dma,
            dma,
            dma,
            dma((2,)),
        ],
        compiler_params=pltpu.CompilerParams(
            collective_id=0, has_side_effects=True, vmem_limit_bytes=60 * 2**20
        ),
        cost_estimate=pl.CostEstimate(
            flops=2 * 10**9, bytes_accessed=3 * 10**6, transcendentals=0
        ),
        name="exchange",
    )(syn, obs, table, first, second, mask, weight, owner, element)


def finish_kernel(summed, table, out, result, sems):
    samples = result.shape[1]
    chunk = samples // sems.shape[0]
    copies = []
    for n in range(sems.shape[0]):
        columns = pl.ds(n * chunk, chunk)
        result[:, columns] = dot_plain(summed[...], table[:, columns])
        copies.append(
            pltpu.make_async_copy(result.at[:, columns], out.at[:, columns], sems.at[n])
        )
        copies[-1].start()
    for copy in copies:
        copy.wait()


def finish(summed, table):
    count, samples = summed.shape[0], table.shape[1]
    in_vmem = pl.BlockSpec(memory_space=pltpu.VMEM)
    out = pl.pallas_call(
        finish_kernel,
        out_shape=jax.ShapeDtypeStruct((count, samples), F32),
        in_specs=[in_vmem] * 2,
        out_specs=pl.BlockSpec(memory_space=pl.ANY),
        scratch_shapes=[
            pltpu.VMEM((count, samples), F32),
            pltpu.SemaphoreType.DMA((4,)),
        ],
        compiler_params=pltpu.CompilerParams(vmem_limit_bytes=40 * 2**20),
        cost_estimate=pl.CostEstimate(
            flops=7 * 10**8, bytes_accessed=3 * 10**6, transcendentals=0
        ),
        name="finish",
    )(summed, table)
    return out.reshape(3, count // 3, samples)


def on_device(
    blks,
    subs,
    synthetic,
    observed,
    pair_first,
    pair_second,
    pair_mask,
    pair_weight,
    station_owner,
    station_element,
):
    rows, _, samples = synthetic.shape
    forward, inverse = dft_tables(samples, NF)
    summed = exchange(
        blks,
        subs,
        jnp.transpose(synthetic, (1, 0, 2)),
        jnp.transpose(observed, (1, 0, 2)),
        jnp.asarray(forward),
        pair_first,
        pair_second,
        pair_mask,
        pair_weight,
        station_owner.reshape(1, rows),
        station_element.reshape(1, rows),
    )
    out = finish(summed, jnp.asarray(inverse))
    return jnp.transpose(out, (1, 0, 2))


def solution(mesh):
    blks, subs = mesh.shape["blk"], mesh.shape["sub"]
    return jax.shard_map(
        functools.partial(on_device, blks, subs),
        mesh=mesh,
        in_specs=(
            P(("blk", "sub"), None, None),
            P(("blk", "sub"), None, None),
            P("blk", "sub"),
            P("blk", "sub"),
            P("blk", "sub"),
            P("blk", "sub"),
            P(("blk", "sub"), None),
            P(("blk", "sub")),
        ),
        out_specs=P(("blk", "sub"), None, None),
        check_vma=False,
    )
```

```python
import functools
import itertools
import math

import jax
import jax.numpy as jnp
import numpy as np
from jax import lax
from jax.experimental import pallas as pl
from jax.experimental.pallas import tpu as pltpu
from jax.sharding import PartitionSpec as P

MESH = pl.DeviceIdType.MESH
NF = 128
BLOCK = 64
F32 = jnp.float32
BF16 = jnp.bfloat16


def dft_tables(samples, freqs):
    phase = (np.arange(samples)[:, None] * np.arange(freqs)[None, :]) % samples
    angles = phase.astype(np.float64) * (2.0 * math.pi / samples)
    scale = 1.0 / math.sqrt(samples)
    cosine, sine = np.cos(angles) * scale, np.sin(angles) * scale
    forward = np.concatenate([cosine, -sine], axis=1).astype(np.float32)
    doubled = np.where(np.arange(freqs) == 0, 1.0, 2.0)[:, None]
    inverse = np.concatenate([cosine.T * doubled, -sine.T * doubled], axis=0)
    return forward.astype(jnp.bfloat16), inverse.astype(np.float32).astype(jnp.bfloat16)


def in_two(x):
    high = x.astype(BF16)
    return high, (x - high.astype(F32)).astype(BF16)


def dot_rows(a, b):
    return lax.dot_general(a, b, (((1,), (1,)), ((), ())), preferred_element_type=F32)


def dot_plain(a, b):
    return jnp.dot(a, b, preferred_element_type=F32)


def features(pair):
    xr, xi = pair[0][:, :NF].astype(F32), pair[0][:, NF:].astype(F32)
    o_r, o_i = pair[1][:, :NF].astype(F32), pair[1][:, NF:].astype(F32)
    dr, di = xr - o_r, xi - o_i
    parts = [dr * xr + di * xi, dr * xi - di * xr, o_r * xr + o_i * xi, o_r * xi - o_i * xr]
    both = [in_two(p) for p in parts]
    return jnp.concatenate(
        [jnp.concatenate([b[i] for b in both], axis=1) for i in range(2)], axis=0
    )


def for_features(links):
    return jnp.concatenate([links.astype(BF16)] * 2, axis=1)


def spread(rows, count, shift):
    index = lax.broadcasted_iota(jnp.int32, (count, NF), 0) + shift
    return jnp.concatenate(
        [(index == rows[s : s + 1]).astype(F32).astype(BF16) for s in range(rows.shape[0])], axis=1
    )


def spread_weights(rows, weights, count, shift):
    index = lax.broadcasted_iota(jnp.int32, (count, NF), 0) + shift
    return jnp.concatenate(
        [
            jnp.where(index == rows[s : s + 1], weights[s : s + 1], 0.0).astype(BF16)
            for s in range(rows.shape[0])
        ],
        axis=1,
    )


def spread_order(core):
    left = [step + (core,) for step in itertools.product(range(4), range(4), range(4))]
    ways = {0: (0.0, 0.0), 1: (1.0, 0.0), 2: (1.0, 1.0), 3: (0.0, 1.0)}

    def links(step):
        return np.array([way for axis in step[:3] for way in ways[axis]])

    used, order = np.zeros(6), []
    while left:
        step = min(left, key=lambda t: (np.max(used + links(t)), -np.sum(links(t)), t))
        left.remove(step)
        used = used + links(step)
        order.append(step)
    return order


def exchange_kernel(
    blks,
    subs,
    syn_hbm,
    obs_hbm,
    table_hbm,
    first_hbm,
    second_hbm,
    mask_hbm,
    weight_hbm,
    owner_hbm,
    element_hbm,
    summed,
    traces,
    table,
    first,
    second,
    mask,
    weight,
    owner,
    element,
    spec,
    halo,
    list_out,
    list_over,
    lists,
    lists_prev,
    near_out,
    near_labels,
    labels,
    outgoing,
    received,
    load_sems,
    list_send,
    list_recv,
    over_send,
    over_recv,
    halo_send,
    halo_recv,
    joined,
    near_send,
    near_recv,
    y_send,
    y_recv,
    z_send,
    z_recv,
    all_send,
    all_recv,
):
    devices = blks * subs
    blk, sub = lax.axis_index("blk"), lax.axis_index("sub")
    me = blk * subs + sub
    rows = spec.shape[1]
    blocks = first.shape[0]
    def around(at, step, size):
        there = at + step
        return jnp.where(there >= size, there - size, there)

    subs_there = [around(sub, step, subs) for step in range(1, subs)]
    blks_there = [around(blk, step, blks) for step in range(1, blks)]
    blk_after, blk_before = blks_there[0], blks_there[-1]
    after = (jnp.where(sub == subs - 1, blk_after, blk), subs_there[0])
    before = (jnp.where(sub == 0, blk_before, blk), subs_there[-1])

    pairs = [
        (first_hbm, first),
        (second_hbm, second),
        (mask_hbm, mask),
        (weight_hbm, weight),
        (table_hbm, table),
        (syn_hbm.at[0], traces.at[0, pl.ds(0, rows)]),
        (obs_hbm.at[0], traces.at[0, pl.ds(rows, rows)]),
        (syn_hbm.at[1], traces.at[1, pl.ds(0, rows)]),
        (obs_hbm.at[1], traces.at[1, pl.ds(rows, rows)]),
        (syn_hbm.at[2], traces.at[2, pl.ds(0, rows)]),
        (obs_hbm.at[2], traces.at[2, pl.ds(rows, rows)]),
        (owner_hbm, owner),
        (element_hbm, element),
    ]
    loads = [
        pltpu.make_async_copy(src, dst, load_sems.at[i]) for i, (src, dst) in enumerate(pairs)
    ]
    for load in loads:
        load.start()

    barrier = pltpu.get_barrier_semaphore()

    def greet(there):
        pl.semaphore_signal(barrier, inc=1, device_id=there, device_id_type=MESH)

    for there in subs_there:
        greet((blk, there))
    for there in blks_there:
        greet((there, sub))

    @pl.when(sub == 0)
    def _():
        for s in range(1, subs):
            greet((blk_before, s))

    @pl.when(sub == subs - 1)
    def _():
        greet((blk_after, 0))

    for i in range(4):
        loads[i].wait()
    base = (blk * blocks + lax.broadcasted_iota(jnp.int32, (blocks, NF), 0)) * BLOCK
    code = ((first[...] - base) * (2 * BLOCK) + (second[...] - base)).astype(F32)
    slot_weight = weight[...] * mask[...].astype(F32)
    zero_row = jnp.zeros((1, NF), F32)
    for s in range(subs):
        lines = [max(2 * s - 1, 0), 2 * s, 2 * s + 1]
        list_out[s] = jnp.concatenate(
            [code[i : i + 1] for i in lines]
            + [slot_weight[i : i + 1] for i in lines]
            + [zero_row] * 2,
            axis=0,
        )
    list_over[...] = jnp.concatenate(
        [code[blocks - 1 : blocks]]
        + [zero_row] * 2
        + [slot_weight[blocks - 1 : blocks]]
        + [zero_row] * 4,
        axis=0,
    )
    lists[sub] = list_out[sub]

    pl.semaphore_wait(barrier, subs + blks - 1)
    for there in subs_there:
        pltpu.make_async_remote_copy(
            src_ref=list_out.at[there],
            dst_ref=lists.at[sub],
            send_sem=list_send,
            recv_sem=list_recv,
            device_id=(blk, there),
            device_id_type=MESH,
        ).start()
    over = pltpu.make_async_remote_copy(
        src_ref=list_over,
        dst_ref=lists_prev.at[sub],
        send_sem=over_send,
        recv_sem=over_recv,
        device_id=(blk_after, 0),
        device_id_type=MESH,
    )
    over.start()

    def transform(c):
        both = dot_plain(traces[c], table[...]).astype(BF16)
        spec[2 * c] = both[:rows]
        spec[2 * c + 1] = both[rows:]

    for i in range(4, 7):
        loads[i].wait()
    transform(0)

    def halo_copies(c):
        q = pl.ds(2 * c, 2)
        return [
            pltpu.make_async_remote_copy(
                src_ref=spec.at[q, pl.ds(0, BLOCK)],
                dst_ref=halo.at[q, pl.ds(BLOCK, BLOCK)],
                send_sem=halo_send.at[0, c],
                recv_sem=halo_recv.at[0, c],
                device_id=before,
                device_id_type=MESH,
            ),
            pltpu.make_async_remote_copy(
                src_ref=spec.at[q, pl.ds(rows - BLOCK, BLOCK)],
                dst_ref=halo.at[q, pl.ds(0, BLOCK)],
                send_sem=halo_send.at[1, c],
                recv_sem=halo_recv.at[1, c],
                device_id=after,
                device_id_type=MESH,
            ),
        ]

    halos = [halo_copies(c) for c in range(3)]
    for copy in halos[0]:
        copy.start()

    for c in (1, 2):
        loads[5 + 2 * c].wait()
        loads[6 + 2 * c].wait()
        transform(c)
        for copy in halos[c]:
            copy.start()

    for there in subs_there:
        pl.semaphore_signal(joined, inc=1, device_id=(blk, there), device_id_type=MESH)

    loads[11].wait()
    loads[12].wait()
    lane = lax.broadcasted_iota(jnp.int32, (rows, rows), 1)
    line = lax.broadcasted_iota(jnp.int32, (rows, rows), 0)
    owner_row = owner[...]

    def column(row):
        return jnp.sum(jnp.where(lane == line, row, 0), axis=1, keepdims=True)

    owner_column, element_column = column(owner_row), column(element[...]).astype(F32)
    same = owner_column == owner_row
    rank_column = jnp.sum(jnp.where(same & (lane < line), 1, 0), axis=1, keepdims=True)
    label_rows = []
    for k in range(2):
        chosen = ((owner_column == lane) & (rank_column == k)).astype(F32)
        label_rows.append(
            jnp.sum(chosen * (element_column - rows), axis=0, keepdims=True) + float(rows)
        )

    near_out[...] = jnp.concatenate(label_rows + [zero_row] * 6, axis=0)
    near_labels[sub] = near_out[...]
    for there in subs_there:
        pltpu.make_async_remote_copy(
            src_ref=near_out,
            dst_ref=near_labels.at[sub],
            send_sem=near_send,
            recv_sem=near_recv,
            device_id=(blk, there),
            device_id_type=MESH,
        ).start()

    rank_row = jnp.sum(jnp.where(same & (line < lane), 1, 0), axis=0, keepdims=True)
    target = owner_row * 4 + rank_row * 2
    slot = lax.broadcasted_iota(jnp.int32, (4 * devices, 2 * rows), 0)
    placement = (slot == jnp.concatenate([target, target + 1], axis=1)).astype(F32).astype(BF16)

    def stations(c):
        return (spec[2 * c], spec[2 * c + 1])

    own = [features(stations(c)) for c in range(3)]

    others = pl.ds(0, subs - 1)
    pltpu.make_async_copy(lists.at[others], lists.at[others], list_recv).wait()

    @pl.when(sub == 0)
    def _():
        pltpu.make_async_copy(lists_prev, lists_prev, over_recv).wait()

    @pl.when(sub != 0)
    def _():
        lists_prev[...] = lists[...]

    def unpacked(ref, k):
        codes = ref[:, k, :].astype(jnp.int32)
        return codes >> 7, codes & 127, ref[:, 3 + k, :]

    first0, second0, weight0 = unpacked(lists_prev, 0)
    first1, second1, weight1 = unpacked(lists, 1)
    first2, second2, weight2 = unpacked(lists, 2)
    to_prev = dot_rows(spread_weights(second0, weight0, BLOCK, BLOCK), spread(first0, rows, 0))
    upper = dot_rows(spread_weights(first1, weight1, BLOCK, 0), spread(second1, rows, 0))
    lower = dot_rows(spread_weights(first2, weight2, BLOCK, 0), spread(second2, rows, 0))
    half = lax.broadcasted_iota(jnp.int32, (BLOCK, rows), 1) >= BLOCK
    inside = jnp.where(half, pltpu.roll(lower, BLOCK, 1), 0.0)
    one_way = jnp.concatenate([upper, inside], axis=0)
    link_own = for_features(one_way + one_way.T)
    link_halo = for_features(jnp.concatenate([to_prev, jnp.where(half, lower, 0.0)], axis=0))
    inner = [dot_plain(link_own, own[c]) for c in range(3)]

    for c in range(3):
        for copy in halos[c]:
            copy.wait_recv()
        sums = inner[c] + dot_plain(link_halo, features((halo[2 * c], halo[2 * c + 1])))
        g1r, g1i, g2r, g2i = (sums[:, i * NF : (i + 1) * NF] for i in range(4))
        x, o = stations(c)
        xr, xi = x[:, :NF].astype(F32), x[:, NF:].astype(F32)
        dr, di = xr - o[:, :NF].astype(F32), xi - o[:, NF:].astype(F32)
        real = (xr * g1r - xi * g1i) + (dr * g2r - di * g2i)
        imag = (xr * g1i + xi * g1r) + (dr * g2i + di * g2r)
        adjoint = jnp.concatenate([real, imag], axis=0).astype(BF16)
        outgoing[:, c] = dot_plain(placement, adjoint).astype(BF16).reshape(devices, 4, NF)

    z, y = lax.div(blk, 4), lax.rem(blk, 4)
    pltpu.make_async_copy(near_labels.at[others], near_labels.at[others], near_recv).wait()
    labels[z, y] = jnp.concatenate(
        [near_labels[:, 0, :], near_labels[:, 1, :]], axis=0
    ).astype(BF16)
    for step in range(1, 4):
        pltpu.make_async_remote_copy(
            src_ref=labels.at[z, y],
            dst_ref=labels.at[z, y],
            send_sem=y_send,
            recv_sem=y_recv,
            device_id=(z * 4 + around(y, step, 4), sub),
            device_id_type=MESH,
        ).start()

    pl.semaphore_wait(joined, subs - 1)

    core = lax.rem(sub, 2)

    def turns(at, size):
        up = [around(at, step, size) for step in range(1, size)]
        return [at] + [jnp.where(core == 0, up[i], up[-1 - i]) for i in range(size - 1)]

    chip = lax.div(me, 2)
    z_to, y_to, x_to = turns(z, 4), turns(y, 4), turns(lax.div(sub, 2), 4)
    core_to = [core, 1 - core]
    received[core, chip] = outgoing[me]

    def deliver(step):
        dz, dy, dx, other = step
        blk_to, sub_to = z_to[dz] * 4 + y_to[dy], x_to[dx] * 2 + core_to[other]
        pltpu.make_async_remote_copy(
            src_ref=outgoing.at[blk_to * subs + sub_to],
            dst_ref=received.at[core, chip],
            send_sem=all_send,
            recv_sem=all_recv.at[other],
            device_id=(blk_to, sub_to),
            device_id_type=MESH,
        ).start()

    order = spread_order(1) + spread_order(0)[1:]
    for step in order[:56]:
        deliver(step)
    some = pl.ds(0, 3)
    pltpu.make_async_copy(labels.at[0, some], labels.at[0, some], y_recv).wait()
    for step in range(1, 4):
        pltpu.make_async_remote_copy(
            src_ref=labels.at[z],
            dst_ref=labels.at[z],
            send_sem=z_send,
            recv_sem=z_recv,
            device_id=(around(z, step, 4) * 4 + y, sub),
            device_id_type=MESH,
        ).start()

    for step in order[56:]:
        deliver(step)

    pltpu.make_async_copy(labels.at[some], labels.at[some], z_recv).wait()
    by_owner = labels[...].reshape(2 * devices, NF)
    arrived = lax.broadcasted_iota(jnp.int32, (2 * devices, 2 * devices), 1)
    held = lax.broadcasted_iota(jnp.int32, (2 * devices, 2 * devices), 0)
    sub_bits = subs.bit_length() - 1
    wanted = (
        ((arrived >> (sub_bits + 1)) << (sub_bits + 1))
        + (((arrived >> 1) & 1) << sub_bits)
        + (((arrived >> 2) & (subs // 2 - 1)) << 1)
    )
    owner_line = lax.broadcasted_iota(jnp.int32, (rows, 2 * devices), 0)

    def collector(source_core):
        repeated = lax.dot_general(
            by_owner,
            (held == wanted + source_core).astype(F32).astype(BF16),
            (((0,), (0,)), ((), ())),
            preferred_element_type=F32,
        )
        label = jnp.sum(jnp.where(owner_line == me, repeated, 0.0), axis=0, keepdims=True)
        return jnp.concatenate(
            [
                ((label == owner_line.astype(F32)) & ((arrived[:rows] & 1) == i)).astype(F32)
                for i in range(2)
            ],
            axis=0,
        ).astype(BF16)

    collect_other, collect_same = collector(1 - core), collector(core)

    def sums(collect, source_core, c):
        return dot_plain(collect, received[source_core, :, c].reshape(2 * devices, NF))

    pltpu.make_async_copy(received.at[0], received.at[0], all_recv.at[1]).wait()
    first_sums = [sums(collect_other, 1 - core, c) for c in range(3)]
    most = pl.ds(0, devices // 2 - 1)
    pltpu.make_async_copy(received.at[0, most], received.at[0, most], all_recv.at[0]).wait()
    for c in range(3):
        total = (first_sums[c] + sums(collect_same, core, c)).astype(BF16)
        summed[c * rows : (c + 1) * rows, :NF] = total[:rows]
        summed[c * rows : (c + 1) * rows, NF:] = total[rows:]

    for c in range(3):
        for copy in halos[c]:
            copy.wait_send()
    pltpu.make_async_copy(list_out.at[others], list_out.at[others], list_send).wait()
    over.wait_send()
    pltpu.make_async_copy(near_labels.at[others], near_labels.at[others], near_send).wait()
    pltpu.make_async_copy(labels.at[0, some], labels.at[0, some], y_send).wait()
    pltpu.make_async_copy(labels.at[some], labels.at[some], z_send).wait()
    most = pl.ds(0, devices - 1)
    pltpu.make_async_copy(outgoing.at[most], outgoing.at[most], all_send).wait()


def exchange(blks, subs, syn, obs, table, first, second, mask, weight, owner, element):
    devices = blks * subs
    samples, rows = syn.shape[2], syn.shape[1]
    in_hbm = pl.BlockSpec(memory_space=pltpu.HBM)
    dma = pltpu.SemaphoreType.DMA
    return pl.pallas_call(
        functools.partial(exchange_kernel, blks, subs),
        out_shape=pltpu.VMEM((3 * rows, 2 * NF), BF16),
        in_specs=[in_hbm] * 9,
        out_specs=pl.BlockSpec(memory_space=pltpu.VMEM),
        scratch_shapes=[
            pltpu.VMEM((3, 2 * rows, samples), BF16),
            pltpu.VMEM(table.shape, BF16),
            pltpu.VMEM(first.shape, jnp.int32),
            pltpu.VMEM(second.shape, jnp.int32),
            pltpu.VMEM(mask.shape, jnp.int32),
            pltpu.VMEM(weight.shape, F32),
            pltpu.VMEM(owner.shape, jnp.int32),
            pltpu.VMEM(element.shape, jnp.int32),
            pltpu.VMEM((6, rows, 2 * NF), BF16),
            pltpu.VMEM((6, 2 * BLOCK, 2 * NF), BF16),
            pltpu.VMEM((subs, 8, NF), F32),
            pltpu.VMEM((8, NF), F32),
            pltpu.VMEM((subs, 8, NF), F32),
            pltpu.VMEM((subs, 8, NF), F32),
            pltpu.VMEM((8, NF), F32),
            pltpu.VMEM((subs, 8, NF), F32),
            pltpu.VMEM((4, blks // 4, 2 * subs, NF), BF16),
            pltpu.VMEM((devices, 3, 4, NF), BF16),
            pltpu.VMEM((2, devices // 2, 3, 4, NF), BF16),
            dma((13,)),
            dma,
            dma,
            dma,
            dma,
            dma((2, 3)),
            dma((2, 3)),
            pltpu.SemaphoreType.REGULAR,
            dma,
            dma,
            dma,
            dma,
            dma,
            dma,
            dma,
            dma((2,)),
        ],
        compiler_params=pltpu.CompilerParams(
            collective_id=0, has_side_effects=True, vmem_limit_bytes=60 * 2**20
        ),
        cost_estimate=pl.CostEstimate(
            flops=2 * 10**9, bytes_accessed=3 * 10**6, transcendentals=0
        ),
        name="exchange",
    )(syn, obs, table, first, second, mask, weight, owner, element)


def finish_kernel(summed, table, out, result, sems):
    samples = result.shape[1]
    chunk = samples // sems.shape[0]
    copies = []
    for n in range(sems.shape[0]):
        columns = pl.ds(n * chunk, chunk)
        result[:, columns] = dot_plain(summed[...], table[:, columns])
        copies.append(
            pltpu.make_async_copy(result.at[:, columns], out.at[:, columns], sems.at[n])
        )
        copies[-1].start()
    for copy in copies:
        copy.wait()


def finish(summed, table):
    count, samples = summed.shape[0], table.shape[1]
    in_vmem = pl.BlockSpec(memory_space=pltpu.VMEM)
    out = pl.pallas_call(
        finish_kernel,
        out_shape=jax.ShapeDtypeStruct((count, samples), F32),
        in_specs=[in_vmem] * 2,
        out_specs=pl.BlockSpec(memory_space=pl.ANY),
        scratch_shapes=[
            pltpu.VMEM((count, samples), F32),
            pltpu.SemaphoreType.DMA((4,)),
        ],
        compiler_params=pltpu.CompilerParams(vmem_limit_bytes=40 * 2**20),
        cost_estimate=pl.CostEstimate(
            flops=7 * 10**8, bytes_accessed=3 * 10**6, transcendentals=0
        ),
        name="finish",
    )(summed, table)
    return out.reshape(3, count // 3, samples)


def on_device(
    blks,
    subs,
    synthetic,
    observed,
    pair_first,
    pair_second,
    pair_mask,
    pair_weight,
    station_owner,
    station_element,
):
    rows, _, samples = synthetic.shape
    forward, inverse = dft_tables(samples, NF)
    summed = exchange(
        blks,
        subs,
        jnp.transpose(synthetic, (1, 0, 2)),
        jnp.transpose(observed, (1, 0, 2)),
        jnp.asarray(forward),
        pair_first,
        pair_second,
        pair_mask,
        pair_weight,
        station_owner.reshape(1, rows),
        station_element.reshape(1, rows),
    )
    out = finish(summed, jnp.asarray(inverse))
    return jnp.transpose(out, (1, 0, 2))


def solution(mesh):
    blks, subs = mesh.shape["blk"], mesh.shape["sub"]
    return jax.shard_map(
        functools.partial(on_device, blks, subs),
        mesh=mesh,
        in_specs=(
            P(("blk", "sub"), None, None),
            P(("blk", "sub"), None, None),
            P("blk", "sub"),
            P("blk", "sub"),
            P("blk", "sub"),
            P("blk", "sub"),
            P(("blk", "sub"), None),
            P(("blk", "sub")),
        ),
        out_specs=P(("blk", "sub"), None, None),
        check_vma=False,
    )
```

```python
import functools
import itertools
import math

import jax
import jax.numpy as jnp
import numpy as np
from jax import lax
from jax.experimental import pallas as pl
from jax.experimental.pallas import tpu as pltpu
from jax.sharding import PartitionSpec as P

MESH = pl.DeviceIdType.MESH
NF = 128
BLOCK = 64
F32 = jnp.float32
BF16 = jnp.bfloat16


def dft_tables(samples, freqs):
    phase = (np.arange(samples)[:, None] * np.arange(freqs)[None, :]) % samples
    angles = phase.astype(np.float64) * (2.0 * math.pi / samples)
    scale = 1.0 / math.sqrt(samples)
    cosine, sine = np.cos(angles) * scale, np.sin(angles) * scale
    forward = np.concatenate([cosine, -sine], axis=1).astype(np.float32)
    doubled = np.where(np.arange(freqs) == 0, 1.0, 2.0)[:, None]
    inverse = np.concatenate([cosine.T * doubled, -sine.T * doubled], axis=0)
    return forward.astype(jnp.bfloat16), inverse.astype(np.float32).astype(jnp.bfloat16)


def in_two(x):
    high = x.astype(BF16)
    return high, (x - high.astype(F32)).astype(BF16)


def dot_rows(a, b):
    return lax.dot_general(a, b, (((1,), (1,)), ((), ())), preferred_element_type=F32)


def dot_plain(a, b):
    return jnp.dot(a, b, preferred_element_type=F32)


def features(pair):
    xr, xi = pair[0][:, :NF].astype(F32), pair[0][:, NF:].astype(F32)
    o_r, o_i = pair[1][:, :NF].astype(F32), pair[1][:, NF:].astype(F32)
    dr, di = xr - o_r, xi - o_i
    parts = [dr * xr + di * xi, dr * xi - di * xr, o_r * xr + o_i * xi, o_r * xi - o_i * xr]
    both = [in_two(p) for p in parts]
    return jnp.concatenate(
        [jnp.concatenate([b[i] for b in both], axis=1) for i in range(2)], axis=0
    )


def for_features(links):
    return jnp.concatenate([links.astype(BF16)] * 2, axis=1)


def spread(rows, count, shift):
    index = lax.broadcasted_iota(jnp.int32, (count, NF), 0) + shift
    return jnp.concatenate(
        [(index == rows[s : s + 1]).astype(F32).astype(BF16) for s in range(rows.shape[0])], axis=1
    )


def spread_weights(rows, weights, count, shift):
    index = lax.broadcasted_iota(jnp.int32, (count, NF), 0) + shift
    return jnp.concatenate(
        [
            jnp.where(index == rows[s : s + 1], weights[s : s + 1], 0.0).astype(BF16)
            for s in range(rows.shape[0])
        ],
        axis=1,
    )


def spread_order(core):
    left = [step + (core,) for step in itertools.product(range(4), range(4), range(4))]
    ways = {0: (0.0, 0.0), 1: (1.0, 0.0), 2: (1.0, 1.0), 3: (0.0, 1.0)}

    def links(step):
        return np.array([way for axis in step[:3] for way in ways[axis]])

    used, order = np.zeros(6), []
    while left:
        step = min(left, key=lambda t: (np.max(used + links(t)), -np.sum(links(t)), t))
        left.remove(step)
        used = used + links(step)
        order.append(step)
    return order


def exchange_kernel(
    blks,
    subs,
    syn_hbm,
    obs_hbm,
    table_hbm,
    first_hbm,
    second_hbm,
    mask_hbm,
    weight_hbm,
    owner_hbm,
    element_hbm,
    summed,
    traces,
    table,
    first,
    second,
    mask,
    weight,
    owner,
    element,
    spec,
    halo,
    list_out,
    list_over,
    lists,
    lists_prev,
    labels,
    outgoing,
    received,
    load_sems,
    list_send,
    list_recv,
    over_send,
    over_recv,
    halo_send,
    halo_recv,
    joined,
    y_send,
    y_recv,
    z_send,
    z_recv,
    all_send,
    all_recv,
):
    devices = blks * subs
    blk, sub = lax.axis_index("blk"), lax.axis_index("sub")
    me = blk * subs + sub
    rows = spec.shape[1]
    blocks = first.shape[0]
    def around(at, step, size):
        there = at + step
        return jnp.where(there >= size, there - size, there)

    subs_there = [around(sub, step, subs) for step in range(1, subs)]
    blks_there = [around(blk, step, blks) for step in range(1, blks)]
    blk_after, blk_before = blks_there[0], blks_there[-1]
    after = (jnp.where(sub == subs - 1, blk_after, blk), subs_there[0])
    before = (jnp.where(sub == 0, blk_before, blk), subs_there[-1])

    pairs = [
        (owner_hbm, owner),
        (element_hbm, element),
        (first_hbm, first),
        (second_hbm, second),
        (mask_hbm, mask),
        (weight_hbm, weight),
        (table_hbm, table),
        (syn_hbm.at[0], traces.at[0, pl.ds(0, rows)]),
        (obs_hbm.at[0], traces.at[0, pl.ds(rows, rows)]),
        (syn_hbm.at[1], traces.at[1, pl.ds(0, rows)]),
        (obs_hbm.at[1], traces.at[1, pl.ds(rows, rows)]),
        (syn_hbm.at[2], traces.at[2, pl.ds(0, rows)]),
        (obs_hbm.at[2], traces.at[2, pl.ds(rows, rows)]),
    ]
    loads = [
        pltpu.make_async_copy(src, dst, load_sems.at[i]) for i, (src, dst) in enumerate(pairs)
    ]
    for load in loads:
        load.start()

    barrier = pltpu.get_barrier_semaphore()

    def greet(there):
        pl.semaphore_signal(barrier, inc=1, device_id=there, device_id_type=MESH)

    for there in subs_there:
        greet((blk, there))
    for there in blks_there:
        greet((there, sub))

    @pl.when(sub == 0)
    def _():
        for s in range(1, subs):
            greet((blk_before, s))

    @pl.when(sub == subs - 1)
    def _():
        greet((blk_after, 0))

    for i in range(2):
        loads[i].wait()
    lane = lax.broadcasted_iota(jnp.int32, (rows, rows), 1)
    line = lax.broadcasted_iota(jnp.int32, (rows, rows), 0)
    owner_row = owner[...]

    def column(row):
        return jnp.sum(jnp.where(lane == line, row, 0), axis=1, keepdims=True)

    owner_column, element_column = column(owner_row), column(element[...]).astype(F32)
    same = owner_column == owner_row
    rank_column = jnp.sum(jnp.where(same & (lane < line), 1, 0), axis=1, keepdims=True)
    label_rows = []
    for k in range(2):
        chosen = ((owner_column == lane) & (rank_column == k)).astype(F32)
        label_rows.append(
            jnp.sum(chosen * (element_column - rows), axis=0, keepdims=True) + float(rows)
        )

    for i in range(2, 6):
        loads[i].wait()
    base = (blk * blocks + lax.broadcasted_iota(jnp.int32, (blocks, NF), 0)) * BLOCK
    code = ((first[...] - base) * (2 * BLOCK) + (second[...] - base)).astype(F32)
    slot_weight = weight[...] * mask[...].astype(F32)
    zero_row = jnp.zeros((1, NF), F32)
    for s in range(subs):
        lines = [max(2 * s - 1, 0), 2 * s, 2 * s + 1]
        list_out[s] = jnp.concatenate(
            [code[i : i + 1] for i in lines]
            + [slot_weight[i : i + 1] for i in lines]
            + label_rows,
            axis=0,
        )
    list_over[...] = jnp.concatenate(
        [code[blocks - 1 : blocks]]
        + [zero_row] * 2
        + [slot_weight[blocks - 1 : blocks]]
        + [zero_row] * 4,
        axis=0,
    )
    lists[sub] = list_out[sub]

    pl.semaphore_wait(barrier, subs + blks - 1)
    for there in subs_there:
        pltpu.make_async_remote_copy(
            src_ref=list_out.at[there],
            dst_ref=lists.at[sub],
            send_sem=list_send,
            recv_sem=list_recv,
            device_id=(blk, there),
            device_id_type=MESH,
        ).start()
    over = pltpu.make_async_remote_copy(
        src_ref=list_over,
        dst_ref=lists_prev.at[sub],
        send_sem=over_send,
        recv_sem=over_recv,
        device_id=(blk_after, 0),
        device_id_type=MESH,
    )
    over.start()

    def transform(c):
        both = dot_plain(traces[c], table[...]).astype(BF16)
        spec[2 * c] = both[:rows]
        spec[2 * c + 1] = both[rows:]

    for i in range(6, 9):
        loads[i].wait()
    transform(0)

    def halo_copies(c):
        q = pl.ds(2 * c, 2)
        return [
            pltpu.make_async_remote_copy(
                src_ref=spec.at[q, pl.ds(0, BLOCK)],
                dst_ref=halo.at[q, pl.ds(BLOCK, BLOCK)],
                send_sem=halo_send.at[0, c],
                recv_sem=halo_recv.at[0, c],
                device_id=before,
                device_id_type=MESH,
            ),
            pltpu.make_async_remote_copy(
                src_ref=spec.at[q, pl.ds(rows - BLOCK, BLOCK)],
                dst_ref=halo.at[q, pl.ds(0, BLOCK)],
                send_sem=halo_send.at[1, c],
                recv_sem=halo_recv.at[1, c],
                device_id=after,
                device_id_type=MESH,
            ),
        ]

    halos = [halo_copies(c) for c in range(3)]
    for copy in halos[0]:
        copy.start()
    for c in (1, 2):
        loads[7 + 2 * c].wait()
        loads[8 + 2 * c].wait()
        transform(c)
        for copy in halos[c]:
            copy.start()

    for there in subs_there:
        pl.semaphore_signal(joined, inc=1, device_id=(blk, there), device_id_type=MESH)

    rank_row = jnp.sum(jnp.where(same & (line < lane), 1, 0), axis=0, keepdims=True)
    target = owner_row * 4 + rank_row * 2
    slot = lax.broadcasted_iota(jnp.int32, (4 * devices, 2 * rows), 0)
    placement = (slot == jnp.concatenate([target, target + 1], axis=1)).astype(F32).astype(BF16)

    def stations(c):
        return (spec[2 * c], spec[2 * c + 1])

    own = [features(stations(c)) for c in range(3)]

    others = pl.ds(0, subs - 1)
    pltpu.make_async_copy(lists.at[others], lists.at[others], list_recv).wait()

    z, y = lax.div(blk, 4), lax.rem(blk, 4)
    labels[z, y] = jnp.concatenate([lists[:, 6, :], lists[:, 7, :]], axis=0).astype(BF16)
    for step in range(1, 4):
        pltpu.make_async_remote_copy(
            src_ref=labels.at[z, y],
            dst_ref=labels.at[z, y],
            send_sem=y_send,
            recv_sem=y_recv,
            device_id=(z * 4 + around(y, step, 4), sub),
            device_id_type=MESH,
        ).start()

    @pl.when(sub == 0)
    def _():
        pltpu.make_async_copy(lists_prev, lists_prev, over_recv).wait()

    @pl.when(sub != 0)
    def _():
        lists_prev[...] = lists[...]

    def unpacked(ref, k):
        codes = ref[:, k, :].astype(jnp.int32)
        return codes >> 7, codes & 127, ref[:, 3 + k, :]

    first0, second0, weight0 = unpacked(lists_prev, 0)
    first1, second1, weight1 = unpacked(lists, 1)
    first2, second2, weight2 = unpacked(lists, 2)
    to_prev = dot_rows(spread_weights(second0, weight0, BLOCK, BLOCK), spread(first0, rows, 0))
    upper = dot_rows(spread_weights(first1, weight1, BLOCK, 0), spread(second1, rows, 0))
    lower = dot_rows(spread_weights(first2, weight2, BLOCK, 0), spread(second2, rows, 0))
    half = lax.broadcasted_iota(jnp.int32, (BLOCK, rows), 1) >= BLOCK
    inside = jnp.where(half, pltpu.roll(lower, BLOCK, 1), 0.0)
    one_way = jnp.concatenate([upper, inside], axis=0)
    link_own = for_features(one_way + one_way.T)
    link_halo = for_features(jnp.concatenate([to_prev, jnp.where(half, lower, 0.0)], axis=0))
    inner = [dot_plain(link_own, own[c]) for c in range(3)]

    for c in range(3):
        for copy in halos[c]:
            copy.wait_recv()
        sums = inner[c] + dot_plain(link_halo, features((halo[2 * c], halo[2 * c + 1])))
        g1r, g1i, g2r, g2i = (sums[:, i * NF : (i + 1) * NF] for i in range(4))
        x, o = stations(c)
        xr, xi = x[:, :NF].astype(F32), x[:, NF:].astype(F32)
        dr, di = xr - o[:, :NF].astype(F32), xi - o[:, NF:].astype(F32)
        real = (xr * g1r - xi * g1i) + (dr * g2r - di * g2i)
        imag = (xr * g1i + xi * g1r) + (dr * g2i + di * g2r)
        adjoint = jnp.concatenate([real, imag], axis=0).astype(BF16)
        outgoing[:, c] = dot_plain(placement, adjoint).astype(BF16).reshape(devices, 4, NF)

    pl.semaphore_wait(joined, subs - 1)

    core = lax.rem(sub, 2)

    def turns(at, size):
        up = [around(at, step, size) for step in range(1, size)]
        return [at] + [jnp.where(core == 0, up[i], up[-1 - i]) for i in range(size - 1)]

    chip = lax.div(me, 2)
    z_to, y_to, x_to = turns(z, 4), turns(y, 4), turns(lax.div(sub, 2), 4)
    core_to = [core, 1 - core]
    received[core, chip] = outgoing[me]

    def deliver(step):
        dz, dy, dx, other = step
        blk_to, sub_to = z_to[dz] * 4 + y_to[dy], x_to[dx] * 2 + core_to[other]
        pltpu.make_async_remote_copy(
            src_ref=outgoing.at[blk_to * subs + sub_to],
            dst_ref=received.at[core, chip],
            send_sem=all_send,
            recv_sem=all_recv.at[other],
            device_id=(blk_to, sub_to),
            device_id_type=MESH,
        ).start()

    order = spread_order(1) + spread_order(0)[1:]
    for step in order[:48]:
        deliver(step)
    some = pl.ds(0, 3)
    pltpu.make_async_copy(labels.at[0, some], labels.at[0, some], y_recv).wait()
    for step in range(1, 4):
        pltpu.make_async_remote_copy(
            src_ref=labels.at[z],
            dst_ref=labels.at[z],
            send_sem=z_send,
            recv_sem=z_recv,
            device_id=(around(z, step, 4) * 4 + y, sub),
            device_id_type=MESH,
        ).start()

    for step in order[48:]:
        deliver(step)

    pltpu.make_async_copy(labels.at[some], labels.at[some], z_recv).wait()
    by_owner = labels[...].reshape(2 * devices, NF)
    arrived = lax.broadcasted_iota(jnp.int32, (2 * devices, 2 * devices), 1)
    held = lax.broadcasted_iota(jnp.int32, (2 * devices, 2 * devices), 0)
    sub_bits = subs.bit_length() - 1
    wanted = (
        ((arrived >> (sub_bits + 1)) << (sub_bits + 1))
        + (((arrived >> 1) & 1) << sub_bits)
        + (((arrived >> 2) & (subs // 2 - 1)) << 1)
    )
    owner_line = lax.broadcasted_iota(jnp.int32, (rows, 2 * devices), 0)

    def collector(source_core):
        repeated = lax.dot_general(
            by_owner,
            (held == wanted + source_core).astype(F32).astype(BF16),
            (((0,), (0,)), ((), ())),
            preferred_element_type=F32,
        )
        label = jnp.sum(jnp.where(owner_line == me, repeated, 0.0), axis=0, keepdims=True)
        return jnp.concatenate(
            [
                ((label == owner_line.astype(F32)) & ((arrived[:rows] & 1) == i)).astype(F32)
                for i in range(2)
            ],
            axis=0,
        ).astype(BF16)

    collect_other, collect_same = collector(1 - core), collector(core)

    def sums(collect, source_core, c):
        return dot_plain(collect, received[source_core, :, c].reshape(2 * devices, NF))

    pltpu.make_async_copy(received.at[0], received.at[0], all_recv.at[1]).wait()
    first_sums = [sums(collect_other, 1 - core, c) for c in range(3)]
    most = pl.ds(0, devices // 2 - 1)
    pltpu.make_async_copy(received.at[0, most], received.at[0, most], all_recv.at[0]).wait()
    for c in range(3):
        total = (first_sums[c] + sums(collect_same, core, c)).astype(BF16)
        summed[c * rows : (c + 1) * rows, :NF] = total[:rows]
        summed[c * rows : (c + 1) * rows, NF:] = total[rows:]

    for c in range(3):
        for copy in halos[c]:
            copy.wait_send()
    pltpu.make_async_copy(list_out.at[others], list_out.at[others], list_send).wait()
    over.wait_send()
    pltpu.make_async_copy(labels.at[0, some], labels.at[0, some], y_send).wait()
    pltpu.make_async_copy(labels.at[some], labels.at[some], z_send).wait()
    most = pl.ds(0, devices - 1)
    pltpu.make_async_copy(outgoing.at[most], outgoing.at[most], all_send).wait()


def exchange(blks, subs, syn, obs, table, first, second, mask, weight, owner, element):
    devices = blks * subs
    samples, rows = syn.shape[2], syn.shape[1]
    in_hbm = pl.BlockSpec(memory_space=pltpu.HBM)
    dma = pltpu.SemaphoreType.DMA
    return pl.pallas_call(
        functools.partial(exchange_kernel, blks, subs),
        out_shape=pltpu.VMEM((3 * rows, 2 * NF), BF16),
        in_specs=[in_hbm] * 9,
        out_specs=pl.BlockSpec(memory_space=pltpu.VMEM),
        scratch_shapes=[
            pltpu.VMEM((3, 2 * rows, samples), BF16),
            pltpu.VMEM(table.shape, BF16),
            pltpu.VMEM(first.shape, jnp.int32),
            pltpu.VMEM(second.shape, jnp.int32),
            pltpu.VMEM(mask.shape, jnp.int32),
            pltpu.VMEM(weight.shape, F32),
            pltpu.VMEM(owner.shape, jnp.int32),
            pltpu.VMEM(element.shape, jnp.int32),
            pltpu.VMEM((6, rows, 2 * NF), BF16),
            pltpu.VMEM((6, 2 * BLOCK, 2 * NF), BF16),
            pltpu.VMEM((subs, 8, NF), F32),
            pltpu.VMEM((8, NF), F32),
            pltpu.VMEM((subs, 8, NF), F32),
            pltpu.VMEM((subs, 8, NF), F32),
            pltpu.VMEM((4, blks // 4, 2 * subs, NF), BF16),
            pltpu.VMEM((devices, 3, 4, NF), BF16),
            pltpu.VMEM((2, devices // 2, 3, 4, NF), BF16),
            dma((13,)),
            dma,
            dma,
            dma,
            dma,
            dma((2, 3)),
            dma((2, 3)),
            pltpu.SemaphoreType.REGULAR,
            dma,
            dma,
            dma,
            dma,
            dma,
            dma((2,)),
        ],
        compiler_params=pltpu.CompilerParams(
            collective_id=0, has_side_effects=True, vmem_limit_bytes=60 * 2**20
        ),
        cost_estimate=pl.CostEstimate(
            flops=2 * 10**9, bytes_accessed=3 * 10**6, transcendentals=0
        ),
        name="exchange",
    )(syn, obs, table, first, second, mask, weight, owner, element)


def finish_kernel(summed, table, out, result, sems):
    samples = result.shape[1]
    chunk = samples // sems.shape[0]
    copies = []
    for n in range(sems.shape[0]):
        columns = pl.ds(n * chunk, chunk)
        result[:, columns] = dot_plain(summed[...], table[:, columns])
        copies.append(
            pltpu.make_async_copy(result.at[:, columns], out.at[:, columns], sems.at[n])
        )
        copies[-1].start()
    for copy in copies:
        copy.wait()


def finish(summed, table):
    count, samples = summed.shape[0], table.shape[1]
    in_vmem = pl.BlockSpec(memory_space=pltpu.VMEM)
    out = pl.pallas_call(
        finish_kernel,
        out_shape=jax.ShapeDtypeStruct((count, samples), F32),
        in_specs=[in_vmem] * 2,
        out_specs=pl.BlockSpec(memory_space=pl.ANY),
        scratch_shapes=[
            pltpu.VMEM((count, samples), F32),
            pltpu.SemaphoreType.DMA((4,)),
        ],
        compiler_params=pltpu.CompilerParams(vmem_limit_bytes=40 * 2**20),
        cost_estimate=pl.CostEstimate(
            flops=7 * 10**8, bytes_accessed=3 * 10**6, transcendentals=0
        ),
        name="finish",
    )(summed, table)
    return out.reshape(3, count // 3, samples)


def on_device(
    blks,
    subs,
    synthetic,
    observed,
    pair_first,
    pair_second,
    pair_mask,
    pair_weight,
    station_owner,
    station_element,
):
    rows, _, samples = synthetic.shape
    forward, inverse = dft_tables(samples, NF)
    summed = exchange(
        blks,
        subs,
        jnp.transpose(synthetic, (1, 0, 2)),
        jnp.transpose(observed, (1, 0, 2)),
        jnp.asarray(forward),
        pair_first,
        pair_second,
        pair_mask,
        pair_weight,
        station_owner.reshape(1, rows),
        station_element.reshape(1, rows),
    )
    out = finish(summed, jnp.asarray(inverse))
    return jnp.transpose(out, (1, 0, 2))


def solution(mesh):
    blks, subs = mesh.shape["blk"], mesh.shape["sub"]
    return jax.shard_map(
        functools.partial(on_device, blks, subs),
        mesh=mesh,
        in_specs=(
            P(("blk", "sub"), None, None),
            P(("blk", "sub"), None, None),
            P("blk", "sub"),
            P("blk", "sub"),
            P("blk", "sub"),
            P("blk", "sub"),
            P(("blk", "sub"), None),
            P(("blk", "sub")),
        ),
        out_specs=P(("blk", "sub"), None, None),
        check_vma=False,
    )
```

```python
import functools
import itertools
import math

import jax
import jax.numpy as jnp
import numpy as np
from jax import lax
from jax.experimental import pallas as pl
from jax.experimental.pallas import tpu as pltpu
from jax.sharding import PartitionSpec as P

MESH = pl.DeviceIdType.MESH
NF = 128
BLOCK = 64
F32 = jnp.float32
BF16 = jnp.bfloat16


def dft_tables(samples, freqs):
    phase = (np.arange(samples)[:, None] * np.arange(freqs)[None, :]) % samples
    angles = phase.astype(np.float64) * (2.0 * math.pi / samples)
    scale = 1.0 / math.sqrt(samples)
    cosine, sine = np.cos(angles) * scale, np.sin(angles) * scale
    forward = np.concatenate([cosine, -sine], axis=1).astype(np.float32)
    doubled = np.where(np.arange(freqs) == 0, 1.0, 2.0)[:, None]
    inverse = np.concatenate([cosine.T * doubled, -sine.T * doubled], axis=0)
    return forward.astype(jnp.bfloat16), inverse.astype(np.float32).astype(jnp.bfloat16)


def in_two(x):
    high = x.astype(BF16)
    return high, (x - high.astype(F32)).astype(BF16)


def dot_rows(a, b):
    return lax.dot_general(a, b, (((1,), (1,)), ((), ())), preferred_element_type=F32)


def dot_plain(a, b):
    return jnp.dot(a, b, preferred_element_type=F32)


def features(pair):
    xr, xi = pair[0][:, :NF].astype(F32), pair[0][:, NF:].astype(F32)
    o_r, o_i = pair[1][:, :NF].astype(F32), pair[1][:, NF:].astype(F32)
    dr, di = xr - o_r, xi - o_i
    parts = [dr * xr + di * xi, dr * xi - di * xr, o_r * xr + o_i * xi, o_r * xi - o_i * xr]
    both = [in_two(p) for p in parts]
    return jnp.concatenate(
        [jnp.concatenate([b[i] for b in both], axis=1) for i in range(2)], axis=0
    )


def for_features(links):
    return jnp.concatenate([links.astype(BF16)] * 2, axis=1)


def spread(rows, count, shift):
    index = lax.broadcasted_iota(jnp.int32, (count, NF), 0) + shift
    return jnp.concatenate(
        [(index == rows[s : s + 1]).astype(F32).astype(BF16) for s in range(rows.shape[0])], axis=1
    )


def spread_weights(rows, weights, count, shift):
    index = lax.broadcasted_iota(jnp.int32, (count, NF), 0) + shift
    return jnp.concatenate(
        [
            jnp.where(index == rows[s : s + 1], weights[s : s + 1], 0.0).astype(BF16)
            for s in range(rows.shape[0])
        ],
        axis=1,
    )


def spread_order(core):
    left = [step + (core,) for step in itertools.product(range(4), range(4), range(4))]
    ways = {0: (0.0, 0.0), 1: (1.0, 0.0), 2: (1.0, 1.0), 3: (0.0, 1.0)}

    def links(step):
        return np.array([way for axis in step[:3] for way in ways[axis]])

    used, order = np.zeros(6), []
    while left:
        step = min(left, key=lambda t: (np.max(used + links(t)), -np.sum(links(t)), t))
        left.remove(step)
        used = used + links(step)
        order.append(step)
    return order


def exchange_kernel(
    blks,
    subs,
    syn_hbm,
    obs_hbm,
    table_hbm,
    first_hbm,
    second_hbm,
    mask_hbm,
    weight_hbm,
    owner_hbm,
    element_hbm,
    summed,
    traces,
    table,
    first,
    second,
    mask,
    weight,
    owner,
    element,
    spec,
    halo,
    list_out,
    list_over,
    lists,
    lists_prev,
    labels,
    outgoing,
    received,
    load_sems,
    list_send,
    list_recv,
    over_send,
    over_recv,
    halo_send,
    halo_recv,
    joined,
    y_send,
    y_recv,
    z_send,
    z_recv,
    all_send,
    all_recv,
):
    devices = blks * subs
    blk, sub = lax.axis_index("blk"), lax.axis_index("sub")
    me = blk * subs + sub
    rows = spec.shape[1]
    blocks = first.shape[0]
    def around(at, step, size):
        there = at + step
        return jnp.where(there >= size, there - size, there)

    subs_there = [around(sub, step, subs) for step in range(1, subs)]
    blks_there = [around(blk, step, blks) for step in range(1, blks)]
    blk_after, blk_before = blks_there[0], blks_there[-1]
    after = (jnp.where(sub == subs - 1, blk_after, blk), subs_there[0])
    before = (jnp.where(sub == 0, blk_before, blk), subs_there[-1])

    pairs = [
        (table_hbm, table),
        (syn_hbm.at[0], traces.at[0, pl.ds(0, rows)]),
        (obs_hbm.at[0], traces.at[0, pl.ds(rows, rows)]),
        (owner_hbm, owner),
        (element_hbm, element),
        (first_hbm, first),
        (second_hbm, second),
        (mask_hbm, mask),
        (weight_hbm, weight),
        (syn_hbm.at[1], traces.at[1, pl.ds(0, rows)]),
        (obs_hbm.at[1], traces.at[1, pl.ds(rows, rows)]),
        (syn_hbm.at[2], traces.at[2, pl.ds(0, rows)]),
        (obs_hbm.at[2], traces.at[2, pl.ds(rows, rows)]),
    ]
    loads = [
        pltpu.make_async_copy(src, dst, load_sems.at[i]) for i, (src, dst) in enumerate(pairs)
    ]
    for load in loads:
        load.start()

    barrier = pltpu.get_barrier_semaphore()

    def greet(there):
        pl.semaphore_signal(barrier, inc=1, device_id=there, device_id_type=MESH)

    for there in subs_there:
        greet((blk, there))
    for there in blks_there:
        greet((there, sub))

    @pl.when(sub == 0)
    def _():
        for s in range(1, subs):
            greet((blk_before, s))

    @pl.when(sub == subs - 1)
    def _():
        greet((blk_after, 0))

    def transform(c):
        both = dot_plain(traces[c], table[...]).astype(BF16)
        spec[2 * c] = both[:rows]
        spec[2 * c + 1] = both[rows:]

    for i in range(3):
        loads[i].wait()
    transform(0)

    pl.semaphore_wait(barrier, subs + blks - 1)

    def halo_copies(c):
        q = pl.ds(2 * c, 2)
        return [
            pltpu.make_async_remote_copy(
                src_ref=spec.at[q, pl.ds(0, BLOCK)],
                dst_ref=halo.at[q, pl.ds(BLOCK, BLOCK)],
                send_sem=halo_send.at[0, c],
                recv_sem=halo_recv.at[0, c],
                device_id=before,
                device_id_type=MESH,
            ),
            pltpu.make_async_remote_copy(
                src_ref=spec.at[q, pl.ds(rows - BLOCK, BLOCK)],
                dst_ref=halo.at[q, pl.ds(0, BLOCK)],
                send_sem=halo_send.at[1, c],
                recv_sem=halo_recv.at[1, c],
                device_id=after,
                device_id_type=MESH,
            ),
        ]

    halos = [halo_copies(c) for c in range(3)]
    for copy in halos[0]:
        copy.start()

    for i in range(3, 5):
        loads[i].wait()
    lane = lax.broadcasted_iota(jnp.int32, (rows, rows), 1)
    line = lax.broadcasted_iota(jnp.int32, (rows, rows), 0)
    owner_row = owner[...]

    def column(row):
        return jnp.sum(jnp.where(lane == line, row, 0), axis=1, keepdims=True)

    owner_column, element_column = column(owner_row), column(element[...]).astype(F32)
    same = owner_column == owner_row
    rank_column = jnp.sum(jnp.where(same & (lane < line), 1, 0), axis=1, keepdims=True)
    label_rows = []
    for k in range(2):
        chosen = ((owner_column == lane) & (rank_column == k)).astype(F32)
        label_rows.append(
            jnp.sum(chosen * (element_column - rows), axis=0, keepdims=True) + float(rows)
        )

    for i in range(5, 9):
        loads[i].wait()
    base = (blk * blocks + lax.broadcasted_iota(jnp.int32, (blocks, NF), 0)) * BLOCK
    code = ((first[...] - base) * (2 * BLOCK) + (second[...] - base)).astype(F32)
    slot_weight = weight[...] * mask[...].astype(F32)
    zero_row = jnp.zeros((1, NF), F32)
    for s in range(subs):
        lines = [max(2 * s - 1, 0), 2 * s, 2 * s + 1]
        list_out[s] = jnp.concatenate(
            [code[i : i + 1] for i in lines]
            + [slot_weight[i : i + 1] for i in lines]
            + label_rows,
            axis=0,
        )
    list_over[...] = jnp.concatenate(
        [code[blocks - 1 : blocks]]
        + [zero_row] * 2
        + [slot_weight[blocks - 1 : blocks]]
        + [zero_row] * 4,
        axis=0,
    )
    lists[sub] = list_out[sub]

    for there in subs_there:
        pltpu.make_async_remote_copy(
            src_ref=list_out.at[there],
            dst_ref=lists.at[sub],
            send_sem=list_send,
            recv_sem=list_recv,
            device_id=(blk, there),
            device_id_type=MESH,
        ).start()
    over = pltpu.make_async_remote_copy(
        src_ref=list_over,
        dst_ref=lists_prev.at[sub],
        send_sem=over_send,
        recv_sem=over_recv,
        device_id=(blk_after, 0),
        device_id_type=MESH,
    )
    over.start()

    for c in (1, 2):
        loads[7 + 2 * c].wait()
        loads[8 + 2 * c].wait()
        transform(c)
        for copy in halos[c]:
            copy.start()

    for there in subs_there:
        pl.semaphore_signal(joined, inc=1, device_id=(blk, there), device_id_type=MESH)

    rank_row = jnp.sum(jnp.where(same & (line < lane), 1, 0), axis=0, keepdims=True)
    target = owner_row * 4 + rank_row * 2
    slot = lax.broadcasted_iota(jnp.int32, (4 * devices, 2 * rows), 0)
    placement = (slot == jnp.concatenate([target, target + 1], axis=1)).astype(F32).astype(BF16)

    def stations(c):
        return (spec[2 * c], spec[2 * c + 1])

    own = [features(stations(c)) for c in range(3)]

    others = pl.ds(0, subs - 1)
    pltpu.make_async_copy(lists.at[others], lists.at[others], list_recv).wait()

    z, y = lax.div(blk, 4), lax.rem(blk, 4)
    labels[z, y] = jnp.concatenate([lists[:, 6, :], lists[:, 7, :]], axis=0).astype(BF16)
    for step in range(1, 4):
        pltpu.make_async_remote_copy(
            src_ref=labels.at[z, y],
            dst_ref=labels.at[z, y],
            send_sem=y_send,
            recv_sem=y_recv,
            device_id=(z * 4 + around(y, step, 4), sub),
            device_id_type=MESH,
        ).start()

    @pl.when(sub == 0)
    def _():
        pltpu.make_async_copy(lists_prev, lists_prev, over_recv).wait()

    @pl.when(sub != 0)
    def _():
        lists_prev[...] = lists[...]

    def unpacked(ref, k):
        codes = ref[:, k, :].astype(jnp.int32)
        return codes >> 7, codes & 127, ref[:, 3 + k, :]

    first0, second0, weight0 = unpacked(lists_prev, 0)
    first1, second1, weight1 = unpacked(lists, 1)
    first2, second2, weight2 = unpacked(lists, 2)
    to_prev = dot_rows(spread_weights(second0, weight0, BLOCK, BLOCK), spread(first0, rows, 0))
    upper = dot_rows(spread_weights(first1, weight1, BLOCK, 0), spread(second1, rows, 0))
    lower = dot_rows(spread_weights(first2, weight2, BLOCK, 0), spread(second2, rows, 0))
    half = lax.broadcasted_iota(jnp.int32, (BLOCK, rows), 1) >= BLOCK
    inside = jnp.where(half, pltpu.roll(lower, BLOCK, 1), 0.0)
    one_way = jnp.concatenate([upper, inside], axis=0)
    link_own = for_features(one_way + one_way.T)
    link_halo = for_features(jnp.concatenate([to_prev, jnp.where(half, lower, 0.0)], axis=0))
    inner = [dot_plain(link_own, own[c]) for c in range(3)]

    for c in range(3):
        for copy in halos[c]:
            copy.wait_recv()
        sums = inner[c] + dot_plain(link_halo, features((halo[2 * c], halo[2 * c + 1])))
        g1r, g1i, g2r, g2i = (sums[:, i * NF : (i + 1) * NF] for i in range(4))
        x, o = stations(c)
        xr, xi = x[:, :NF].astype(F32), x[:, NF:].astype(F32)
        dr, di = xr - o[:, :NF].astype(F32), xi - o[:, NF:].astype(F32)
        real = (xr * g1r - xi * g1i) + (dr * g2r - di * g2i)
        imag = (xr * g1i + xi * g1r) + (dr * g2i + di * g2r)
        adjoint = jnp.concatenate([real, imag], axis=0).astype(BF16)
        outgoing[:, c] = dot_plain(placement, adjoint).astype(BF16).reshape(devices, 4, NF)

    pl.semaphore_wait(joined, subs - 1)

    core = lax.rem(sub, 2)

    def turns(at, size):
        up = [around(at, step, size) for step in range(1, size)]
        return [at] + [jnp.where(core == 0, up[i], up[-1 - i]) for i in range(size - 1)]

    chip = lax.div(me, 2)
    z_to, y_to, x_to = turns(z, 4), turns(y, 4), turns(lax.div(sub, 2), 4)
    core_to = [core, 1 - core]
    received[core, chip] = outgoing[me]

    def deliver(step):
        dz, dy, dx, other = step
        blk_to, sub_to = z_to[dz] * 4 + y_to[dy], x_to[dx] * 2 + core_to[other]
        pltpu.make_async_remote_copy(
            src_ref=outgoing.at[blk_to * subs + sub_to],
            dst_ref=received.at[core, chip],
            send_sem=all_send,
            recv_sem=all_recv.at[other],
            device_id=(blk_to, sub_to),
            device_id_type=MESH,
        ).start()

    order = spread_order(1) + spread_order(0)[1:]
    for step in order[:48]:
        deliver(step)
    some = pl.ds(0, 3)
    pltpu.make_async_copy(labels.at[0, some], labels.at[0, some], y_recv).wait()
    for step in range(1, 4):
        pltpu.make_async_remote_copy(
            src_ref=labels.at[z],
            dst_ref=labels.at[z],
            send_sem=z_send,
            recv_sem=z_recv,
            device_id=(around(z, step, 4) * 4 + y, sub),
            device_id_type=MESH,
        ).start()

    for step in order[48:]:
        deliver(step)

    pltpu.make_async_copy(labels.at[some], labels.at[some], z_recv).wait()
    by_owner = labels[...].reshape(2 * devices, NF)
    arrived = lax.broadcasted_iota(jnp.int32, (2 * devices, 2 * devices), 1)
    held = lax.broadcasted_iota(jnp.int32, (2 * devices, 2 * devices), 0)
    sub_bits = subs.bit_length() - 1
    wanted = (
        ((arrived >> (sub_bits + 1)) << (sub_bits + 1))
        + (((arrived >> 1) & 1) << sub_bits)
        + (((arrived >> 2) & (subs // 2 - 1)) << 1)
    )
    owner_line = lax.broadcasted_iota(jnp.int32, (rows, 2 * devices), 0)

    def collector(source_core):
        repeated = lax.dot_general(
            by_owner,
            (held == wanted + source_core).astype(F32).astype(BF16),
            (((0,), (0,)), ((), ())),
            preferred_element_type=F32,
        )
        label = jnp.sum(jnp.where(owner_line == me, repeated, 0.0), axis=0, keepdims=True)
        return jnp.concatenate(
            [
                ((label == owner_line.astype(F32)) & ((arrived[:rows] & 1) == i)).astype(F32)
                for i in range(2)
            ],
            axis=0,
        ).astype(BF16)

    collect_other, collect_same = collector(1 - core), collector(core)

    def sums(collect, source_core, c):
        return dot_plain(collect, received[source_core, :, c].reshape(2 * devices, NF))

    pltpu.make_async_copy(received.at[0], received.at[0], all_recv.at[1]).wait()
    first_sums = [sums(collect_other, 1 - core, c) for c in range(3)]
    most = pl.ds(0, devices // 2 - 1)
    pltpu.make_async_copy(received.at[0, most], received.at[0, most], all_recv.at[0]).wait()
    for c in range(3):
        total = (first_sums[c] + sums(collect_same, core, c)).astype(BF16)
        summed[c * rows : (c + 1) * rows, :NF] = total[:rows]
        summed[c * rows : (c + 1) * rows, NF:] = total[rows:]

    for c in range(3):
        for copy in halos[c]:
            copy.wait_send()
    pltpu.make_async_copy(list_out.at[others], list_out.at[others], list_send).wait()
    over.wait_send()
    pltpu.make_async_copy(labels.at[0, some], labels.at[0, some], y_send).wait()
    pltpu.make_async_copy(labels.at[some], labels.at[some], z_send).wait()
    most = pl.ds(0, devices - 1)
    pltpu.make_async_copy(outgoing.at[most], outgoing.at[most], all_send).wait()


def exchange(blks, subs, syn, obs, table, first, second, mask, weight, owner, element):
    devices = blks * subs
    samples, rows = syn.shape[2], syn.shape[1]
    in_hbm = pl.BlockSpec(memory_space=pltpu.HBM)
    dma = pltpu.SemaphoreType.DMA
    return pl.pallas_call(
        functools.partial(exchange_kernel, blks, subs),
        out_shape=pltpu.VMEM((3 * rows, 2 * NF), BF16),
        in_specs=[in_hbm] * 9,
        out_specs=pl.BlockSpec(memory_space=pltpu.VMEM),
        scratch_shapes=[
            pltpu.VMEM((3, 2 * rows, samples), BF16),
            pltpu.VMEM(table.shape, BF16),
            pltpu.VMEM(first.shape, jnp.int32),
            pltpu.VMEM(second.shape, jnp.int32),
            pltpu.VMEM(mask.shape, jnp.int32),
            pltpu.VMEM(weight.shape, F32),
            pltpu.VMEM(owner.shape, jnp.int32),
            pltpu.VMEM(element.shape, jnp.int32),
            pltpu.VMEM((6, rows, 2 * NF), BF16),
            pltpu.VMEM((6, 2 * BLOCK, 2 * NF), BF16),
            pltpu.VMEM((subs, 8, NF), F32),
            pltpu.VMEM((8, NF), F32),
            pltpu.VMEM((subs, 8, NF), F32),
            pltpu.VMEM((subs, 8, NF), F32),
            pltpu.VMEM((4, blks // 4, 2 * subs, NF), BF16),
            pltpu.VMEM((devices, 3, 4, NF), BF16),
            pltpu.VMEM((2, devices // 2, 3, 4, NF), BF16),
            dma((13,)),
            dma,
            dma,
            dma,
            dma,
            dma((2, 3)),
            dma((2, 3)),
            pltpu.SemaphoreType.REGULAR,
            dma,
            dma,
            dma,
            dma,
            dma,
            dma((2,)),
        ],
        compiler_params=pltpu.CompilerParams(
            collective_id=0, has_side_effects=True, vmem_limit_bytes=60 * 2**20
        ),
        cost_estimate=pl.CostEstimate(
            flops=2 * 10**9, bytes_accessed=3 * 10**6, transcendentals=0
        ),
        name="exchange",
    )(syn, obs, table, first, second, mask, weight, owner, element)


def finish_kernel(summed, table, out, result, sems):
    samples = result.shape[1]
    chunk = samples // sems.shape[0]
    copies = []
    for n in range(sems.shape[0]):
        columns = pl.ds(n * chunk, chunk)
        result[:, columns] = dot_plain(summed[...], table[:, columns])
        copies.append(
            pltpu.make_async_copy(result.at[:, columns], out.at[:, columns], sems.at[n])
        )
        copies[-1].start()
    for copy in copies:
        copy.wait()


def finish(summed, table):
    count, samples = summed.shape[0], table.shape[1]
    in_vmem = pl.BlockSpec(memory_space=pltpu.VMEM)
    out = pl.pallas_call(
        finish_kernel,
        out_shape=jax.ShapeDtypeStruct((count, samples), F32),
        in_specs=[in_vmem] * 2,
        out_specs=pl.BlockSpec(memory_space=pl.ANY),
        scratch_shapes=[
            pltpu.VMEM((count, samples), F32),
            pltpu.SemaphoreType.DMA((4,)),
        ],
        compiler_params=pltpu.CompilerParams(vmem_limit_bytes=40 * 2**20),
        cost_estimate=pl.CostEstimate(
            flops=7 * 10**8, bytes_accessed=3 * 10**6, transcendentals=0
        ),
        name="finish",
    )(summed, table)
    return out.reshape(3, count // 3, samples)


def on_device(
    blks,
    subs,
    synthetic,
    observed,
    pair_first,
    pair_second,
    pair_mask,
    pair_weight,
    station_owner,
    station_element,
):
    rows, _, samples = synthetic.shape
    forward, inverse = dft_tables(samples, NF)
    summed = exchange(
        blks,
        subs,
        jnp.transpose(synthetic, (1, 0, 2)),
        jnp.transpose(observed, (1, 0, 2)),
        jnp.asarray(forward),
        pair_first,
        pair_second,
        pair_mask,
        pair_weight,
        station_owner.reshape(1, rows),
        station_element.reshape(1, rows),
    )
    out = finish(summed, jnp.asarray(inverse))
    return jnp.transpose(out, (1, 0, 2))


def solution(mesh):
    blks, subs = mesh.shape["blk"], mesh.shape["sub"]
    return jax.shard_map(
        functools.partial(on_device, blks, subs),
        mesh=mesh,
        in_specs=(
            P(("blk", "sub"), None, None),
            P(("blk", "sub"), None, None),
            P("blk", "sub"),
            P("blk", "sub"),
            P("blk", "sub"),
            P("blk", "sub"),
            P(("blk", "sub"), None),
            P(("blk", "sub")),
        ),
        out_specs=P(("blk", "sub"), None, None),
        check_vma=False,
    )
```

```python
import functools
import itertools
import math

import jax
import jax.numpy as jnp
import numpy as np
from jax import lax
from jax.experimental import pallas as pl
from jax.experimental.pallas import tpu as pltpu
from jax.sharding import PartitionSpec as P

MESH = pl.DeviceIdType.MESH
NF = 128
BLOCK = 64
F32 = jnp.float32
BF16 = jnp.bfloat16


def dft_tables(samples, freqs):
    phase = (np.arange(samples)[:, None] * np.arange(freqs)[None, :]) % samples
    angles = phase.astype(np.float64) * (2.0 * math.pi / samples)
    scale = 1.0 / math.sqrt(samples)
    cosine, sine = np.cos(angles) * scale, np.sin(angles) * scale
    forward = np.concatenate([cosine, -sine], axis=1).astype(np.float32)
    doubled = np.where(np.arange(freqs) == 0, 1.0, 2.0)[:, None]
    inverse = np.concatenate([cosine.T * doubled, -sine.T * doubled], axis=0)
    return forward.astype(jnp.bfloat16), inverse.astype(np.float32).astype(jnp.bfloat16)


def in_two(x):
    high = x.astype(BF16)
    return high, (x - high.astype(F32)).astype(BF16)


def dot_rows(a, b):
    return lax.dot_general(a, b, (((1,), (1,)), ((), ())), preferred_element_type=F32)


def dot_plain(a, b):
    return jnp.dot(a, b, preferred_element_type=F32)


def features(pair):
    xr, xi = pair[0][:, :NF].astype(F32), pair[0][:, NF:].astype(F32)
    o_r, o_i = pair[1][:, :NF].astype(F32), pair[1][:, NF:].astype(F32)
    dr, di = xr - o_r, xi - o_i
    parts = [dr * xr + di * xi, dr * xi - di * xr, o_r * xr + o_i * xi, o_r * xi - o_i * xr]
    both = [in_two(p) for p in parts]
    return jnp.concatenate(
        [jnp.concatenate([b[i] for b in both], axis=1) for i in range(2)], axis=0
    )


def for_features(links):
    return jnp.concatenate([links.astype(BF16)] * 2, axis=1)


def spread(rows, count, shift):
    index = lax.broadcasted_iota(jnp.int32, (count, NF), 0) + shift
    return jnp.concatenate(
        [(index == rows[s : s + 1]).astype(F32).astype(BF16) for s in range(rows.shape[0])], axis=1
    )


def spread_weights(rows, weights, count, shift):
    index = lax.broadcasted_iota(jnp.int32, (count, NF), 0) + shift
    return jnp.concatenate(
        [
            jnp.where(index == rows[s : s + 1], weights[s : s + 1], 0.0).astype(BF16)
            for s in range(rows.shape[0])
        ],
        axis=1,
    )


def spread_order(core):
    left = [step + (core,) for step in itertools.product(range(4), range(4), range(4))]
    ways = {0: (0.0, 0.0), 1: (1.0, 0.0), 2: (1.0, 1.0), 3: (0.0, 1.0)}

    def links(step):
        return np.array([way for axis in step[:3] for way in ways[axis]])

    used, order = np.zeros(6), []
    while left:
        step = min(left, key=lambda t: (np.max(used + links(t)), -np.sum(links(t)), t))
        left.remove(step)
        used = used + links(step)
        order.append(step)
    return order


def exchange_kernel(
    blks,
    subs,
    syn_hbm,
    obs_hbm,
    table_hbm,
    first_hbm,
    second_hbm,
    mask_hbm,
    weight_hbm,
    owner_hbm,
    element_hbm,
    summed,
    traces,
    table,
    first,
    second,
    mask,
    weight,
    owner,
    element,
    spec,
    halo,
    list_out,
    list_over,
    lists,
    lists_prev,
    labels,
    outgoing,
    received,
    load_sems,
    list_send,
    list_recv,
    over_send,
    over_recv,
    halo_send,
    halo_recv,
    joined,
    y_send,
    y_recv,
    z_send,
    z_recv,
    all_send,
    all_recv,
):
    devices = blks * subs
    blk, sub = lax.axis_index("blk"), lax.axis_index("sub")
    me = blk * subs + sub
    rows = spec.shape[1]
    blocks = first.shape[0]
    def around(at, step, size):
        there = at + step
        return jnp.where(there >= size, there - size, there)

    subs_there = [around(sub, step, subs) for step in range(1, subs)]
    blks_there = [around(blk, step, blks) for step in range(1, blks)]
    blk_after, blk_before = blks_there[0], blks_there[-1]
    after = (jnp.where(sub == subs - 1, blk_after, blk), subs_there[0])
    before = (jnp.where(sub == 0, blk_before, blk), subs_there[-1])

    pairs = [
        (table_hbm, table),
        (syn_hbm.at[0], traces.at[0, pl.ds(0, rows)]),
        (obs_hbm.at[0], traces.at[0, pl.ds(rows, rows)]),
        (owner_hbm, owner),
        (element_hbm, element),
        (first_hbm, first),
        (second_hbm, second),
        (mask_hbm, mask),
        (weight_hbm, weight),
        (syn_hbm.at[1], traces.at[1, pl.ds(0, rows)]),
        (obs_hbm.at[1], traces.at[1, pl.ds(rows, rows)]),
        (syn_hbm.at[2], traces.at[2, pl.ds(0, rows)]),
        (obs_hbm.at[2], traces.at[2, pl.ds(rows, rows)]),
    ]
    loads = [
        pltpu.make_async_copy(src, dst, load_sems.at[i]) for i, (src, dst) in enumerate(pairs)
    ]
    for load in loads:
        load.start()

    barrier = pltpu.get_barrier_semaphore()

    def greet(there):
        pl.semaphore_signal(barrier, inc=1, device_id=there, device_id_type=MESH)

    for there in subs_there:
        greet((blk, there))
    for there in blks_there:
        greet((there, sub))

    @pl.when(sub == 0)
    def _():
        for s in range(1, subs):
            greet((blk_before, s))

    @pl.when(sub == subs - 1)
    def _():
        greet((blk_after, 0))

    def transform(c):
        both = dot_plain(traces[c], table[...]).astype(BF16)
        spec[2 * c] = both[:rows]
        spec[2 * c + 1] = both[rows:]

    for i in range(3):
        loads[i].wait()
    transform(0)

    pl.semaphore_wait(barrier, subs + blks - 1)

    def halo_copies(c):
        q = pl.ds(2 * c, 2)
        return [
            pltpu.make_async_remote_copy(
                src_ref=spec.at[q, pl.ds(0, BLOCK)],
                dst_ref=halo.at[q, pl.ds(BLOCK, BLOCK)],
                send_sem=halo_send.at[0, c],
                recv_sem=halo_recv.at[0, c],
                device_id=before,
                device_id_type=MESH,
            ),
            pltpu.make_async_remote_copy(
                src_ref=spec.at[q, pl.ds(rows - BLOCK, BLOCK)],
                dst_ref=halo.at[q, pl.ds(0, BLOCK)],
                send_sem=halo_send.at[1, c],
                recv_sem=halo_recv.at[1, c],
                device_id=after,
                device_id_type=MESH,
            ),
        ]

    halos = [halo_copies(c) for c in range(3)]
    for copy in halos[0]:
        copy.start()

    for i in range(3, 5):
        loads[i].wait()
    lane = lax.broadcasted_iota(jnp.int32, (rows, rows), 1)
    line = lax.broadcasted_iota(jnp.int32, (rows, rows), 0)
    owner_row = owner[...]

    def column(row):
        return jnp.sum(jnp.where(lane == line, row, 0), axis=1, keepdims=True)

    owner_column, element_column = column(owner_row), column(element[...]).astype(F32)
    same = owner_column == owner_row
    rank_column = jnp.sum(jnp.where(same & (lane < line), 1, 0), axis=1, keepdims=True)
    label_rows = []
    for k in range(2):
        chosen = ((owner_column == lane) & (rank_column == k)).astype(F32)
        label_rows.append(
            jnp.sum(chosen * (element_column - rows), axis=0, keepdims=True) + float(rows)
        )

    for i in range(5, 9):
        loads[i].wait()
    base = (blk * blocks + lax.broadcasted_iota(jnp.int32, (blocks, NF), 0)) * BLOCK
    code = ((first[...] - base) * (2 * BLOCK) + (second[...] - base)).astype(F32)
    slot_weight = weight[...] * mask[...].astype(F32)
    zero_row = jnp.zeros((1, NF), F32)
    for s in range(subs):
        lines = [max(2 * s - 1, 0), 2 * s, 2 * s + 1]
        list_out[s] = jnp.concatenate(
            [code[i : i + 1] for i in lines]
            + [slot_weight[i : i + 1] for i in lines]
            + label_rows,
            axis=0,
        )
    list_over[...] = jnp.concatenate(
        [code[blocks - 1 : blocks]]
        + [zero_row] * 2
        + [slot_weight[blocks - 1 : blocks]]
        + [zero_row] * 4,
        axis=0,
    )
    lists[sub] = list_out[sub]

    for there in subs_there:
        pltpu.make_async_remote_copy(
            src_ref=list_out.at[there],
            dst_ref=lists.at[sub],
            send_sem=list_send,
            recv_sem=list_recv,
            device_id=(blk, there),
            device_id_type=MESH,
        ).start()
    over = pltpu.make_async_remote_copy(
        src_ref=list_over,
        dst_ref=lists_prev.at[sub],
        send_sem=over_send,
        recv_sem=over_recv,
        device_id=(blk_after, 0),
        device_id_type=MESH,
    )
    over.start()

    for c in (1, 2):
        loads[7 + 2 * c].wait()
        loads[8 + 2 * c].wait()
        transform(c)
        for copy in halos[c]:
            copy.start()

    for there in subs_there:
        pl.semaphore_signal(joined, inc=1, device_id=(blk, there), device_id_type=MESH)

    rank_row = jnp.sum(jnp.where(same & (line < lane), 1, 0), axis=0, keepdims=True)
    target = owner_row * 4 + rank_row * 2
    slot = lax.broadcasted_iota(jnp.int32, (4 * devices, 2 * rows), 0)
    placement = (slot == jnp.concatenate([target, target + 1], axis=1)).astype(F32).astype(BF16)

    def stations(c):
        return (spec[2 * c], spec[2 * c + 1])

    own = [features(stations(c)) for c in range(3)]

    others = pl.ds(0, subs - 1)
    pltpu.make_async_copy(lists.at[others], lists.at[others], list_recv).wait()

    z, y = lax.div(blk, 4), lax.rem(blk, 4)
    labels[z, y] = jnp.concatenate([lists[:, 6, :], lists[:, 7, :]], axis=0).astype(BF16)
    for step in range(1, 4):
        pltpu.make_async_remote_copy(
            src_ref=labels.at[z, y],
            dst_ref=labels.at[z, y],
            send_sem=y_send,
            recv_sem=y_recv,
            device_id=(z * 4 + around(y, step, 4), sub),
            device_id_type=MESH,
        ).start()

    @pl.when(sub == 0)
    def _():
        pltpu.make_async_copy(lists_prev, lists_prev, over_recv).wait()

    @pl.when(sub != 0)
    def _():
        lists_prev[...] = lists[...]

    def unpacked(ref, k):
        codes = ref[:, k, :].astype(jnp.int32)
        return codes >> 7, codes & 127, ref[:, 3 + k, :]

    first0, second0, weight0 = unpacked(lists_prev, 0)
    first1, second1, weight1 = unpacked(lists, 1)
    first2, second2, weight2 = unpacked(lists, 2)
    to_prev = dot_rows(spread_weights(second0, weight0, BLOCK, BLOCK), spread(first0, rows, 0))
    upper = dot_rows(spread_weights(first1, weight1, BLOCK, 0), spread(second1, rows, 0))
    lower = dot_rows(spread_weights(first2, weight2, BLOCK, 0), spread(second2, rows, 0))
    half = lax.broadcasted_iota(jnp.int32, (BLOCK, rows), 1) >= BLOCK
    inside = jnp.where(half, pltpu.roll(lower, BLOCK, 1), 0.0)
    one_way = jnp.concatenate([upper, inside], axis=0)
    link_own = for_features(one_way + one_way.T)
    link_halo = for_features(jnp.concatenate([to_prev, jnp.where(half, lower, 0.0)], axis=0))
    inner = [dot_plain(link_own, own[c]) for c in range(3)]

    for c in range(3):
        for copy in halos[c]:
            copy.wait_recv()
        sums = inner[c] + dot_plain(link_halo, features((halo[2 * c], halo[2 * c + 1])))
        g1r, g1i, g2r, g2i = (sums[:, i * NF : (i + 1) * NF] for i in range(4))
        x, o = stations(c)
        xr, xi = x[:, :NF].astype(F32), x[:, NF:].astype(F32)
        dr, di = xr - o[:, :NF].astype(F32), xi - o[:, NF:].astype(F32)
        real = (xr * g1r - xi * g1i) + (dr * g2r - di * g2i)
        imag = (xr * g1i + xi * g1r) + (dr * g2i + di * g2r)
        adjoint = jnp.concatenate([real, imag], axis=0).astype(BF16)
        outgoing[:, c] = dot_plain(placement, adjoint).astype(BF16).reshape(devices, 4, NF)

    some = pl.ds(0, 3)
    pltpu.make_async_copy(labels.at[0, some], labels.at[0, some], y_recv).wait()
    for step in range(1, 4):
        pltpu.make_async_remote_copy(
            src_ref=labels.at[z],
            dst_ref=labels.at[z],
            send_sem=z_send,
            recv_sem=z_recv,
            device_id=(around(z, step, 4) * 4 + y, sub),
            device_id_type=MESH,
        ).start()

    pl.semaphore_wait(joined, subs - 1)

    core = lax.rem(sub, 2)

    def turns(at, size):
        up = [around(at, step, size) for step in range(1, size)]
        return [at] + [jnp.where(core == 0, up[i], up[-1 - i]) for i in range(size - 1)]

    chip = lax.div(me, 2)
    z_to, y_to, x_to = turns(z, 4), turns(y, 4), turns(lax.div(sub, 2), 4)
    core_to = [core, 1 - core]
    received[core, chip] = outgoing[me]

    def deliver(step):
        dz, dy, dx, other = step
        blk_to, sub_to = z_to[dz] * 4 + y_to[dy], x_to[dx] * 2 + core_to[other]
        pltpu.make_async_remote_copy(
            src_ref=outgoing.at[blk_to * subs + sub_to],
            dst_ref=received.at[core, chip],
            send_sem=all_send,
            recv_sem=all_recv.at[other],
            device_id=(blk_to, sub_to),
            device_id_type=MESH,
        ).start()

    for step in spread_order(1) + spread_order(0)[1:]:
        deliver(step)

    pltpu.make_async_copy(labels.at[some], labels.at[some], z_recv).wait()
    by_owner = labels[...].reshape(2 * devices, NF)
    arrived = lax.broadcasted_iota(jnp.int32, (2 * devices, 2 * devices), 1)
    held = lax.broadcasted_iota(jnp.int32, (2 * devices, 2 * devices), 0)
    sub_bits = subs.bit_length() - 1
    wanted = (
        ((arrived >> (sub_bits + 1)) << (sub_bits + 1))
        + (((arrived >> 1) & 1) << sub_bits)
        + (((arrived >> 2) & (subs // 2 - 1)) << 1)
    )
    owner_line = lax.broadcasted_iota(jnp.int32, (rows, 2 * devices), 0)

    def collector(source_core):
        repeated = lax.dot_general(
            by_owner,
            (held == wanted + source_core).astype(F32).astype(BF16),
            (((0,), (0,)), ((), ())),
            preferred_element_type=F32,
        )
        label = jnp.sum(jnp.where(owner_line == me, repeated, 0.0), axis=0, keepdims=True)
        return jnp.concatenate(
            [
                ((label == owner_line.astype(F32)) & ((arrived[:rows] & 1) == i)).astype(F32)
                for i in range(2)
            ],
            axis=0,
        ).astype(BF16)

    collect_other, collect_same = collector(1 - core), collector(core)

    def sums(collect, source_core, c):
        return dot_plain(collect, received[source_core, :, c].reshape(2 * devices, NF))

    pltpu.make_async_copy(received.at[0], received.at[0], all_recv.at[1]).wait()
    first_sums = [sums(collect_other, 1 - core, c) for c in range(3)]
    most = pl.ds(0, devices // 2 - 1)
    pltpu.make_async_copy(received.at[0, most], received.at[0, most], all_recv.at[0]).wait()
    for c in range(3):
        total = (first_sums[c] + sums(collect_same, core, c)).astype(BF16)
        summed[c * rows : (c + 1) * rows, :NF] = total[:rows]
        summed[c * rows : (c + 1) * rows, NF:] = total[rows:]

    for c in range(3):
        for copy in halos[c]:
            copy.wait_send()
    pltpu.make_async_copy(list_out.at[others], list_out.at[others], list_send).wait()
    over.wait_send()
    pltpu.make_async_copy(labels.at[0, some], labels.at[0, some], y_send).wait()
    pltpu.make_async_copy(labels.at[some], labels.at[some], z_send).wait()
    most = pl.ds(0, devices - 1)
    pltpu.make_async_copy(outgoing.at[most], outgoing.at[most], all_send).wait()


def exchange(blks, subs, syn, obs, table, first, second, mask, weight, owner, element):
    devices = blks * subs
    samples, rows = syn.shape[2], syn.shape[1]
    in_hbm = pl.BlockSpec(memory_space=pltpu.HBM)
    dma = pltpu.SemaphoreType.DMA
    return pl.pallas_call(
        functools.partial(exchange_kernel, blks, subs),
        out_shape=pltpu.VMEM((3 * rows, 2 * NF), BF16),
        in_specs=[in_hbm] * 9,
        out_specs=pl.BlockSpec(memory_space=pltpu.VMEM),
        scratch_shapes=[
            pltpu.VMEM((3, 2 * rows, samples), BF16),
            pltpu.VMEM(table.shape, BF16),
            pltpu.VMEM(first.shape, jnp.int32),
            pltpu.VMEM(second.shape, jnp.int32),
            pltpu.VMEM(mask.shape, jnp.int32),
            pltpu.VMEM(weight.shape, F32),
            pltpu.VMEM(owner.shape, jnp.int32),
            pltpu.VMEM(element.shape, jnp.int32),
            pltpu.VMEM((6, rows, 2 * NF), BF16),
            pltpu.VMEM((6, 2 * BLOCK, 2 * NF), BF16),
            pltpu.VMEM((subs, 8, NF), F32),
            pltpu.VMEM((8, NF), F32),
            pltpu.VMEM((subs, 8, NF), F32),
            pltpu.VMEM((subs, 8, NF), F32),
            pltpu.VMEM((4, blks // 4, 2 * subs, NF), BF16),
            pltpu.VMEM((devices, 3, 4, NF), BF16),
            pltpu.VMEM((2, devices // 2, 3, 4, NF), BF16),
            dma((13,)),
            dma,
            dma,
            dma,
            dma,
            dma((2, 3)),
            dma((2, 3)),
            pltpu.SemaphoreType.REGULAR,
            dma,
            dma,
            dma,
            dma,
            dma,
            dma((2,)),
        ],
        compiler_params=pltpu.CompilerParams(
            collective_id=0, has_side_effects=True, vmem_limit_bytes=60 * 2**20
        ),
        cost_estimate=pl.CostEstimate(
            flops=2 * 10**9, bytes_accessed=3 * 10**6, transcendentals=0
        ),
        name="exchange",
    )(syn, obs, table, first, second, mask, weight, owner, element)


def finish_kernel(summed, table, out, result, sems):
    samples = result.shape[1]
    chunk = samples // sems.shape[0]
    copies = []
    for n in range(sems.shape[0]):
        columns = pl.ds(n * chunk, chunk)
        result[:, columns] = dot_plain(summed[...], table[:, columns])
        copies.append(
            pltpu.make_async_copy(result.at[:, columns], out.at[:, columns], sems.at[n])
        )
        copies[-1].start()
    for copy in copies:
        copy.wait()


def finish(summed, table):
    count, samples = summed.shape[0], table.shape[1]
    in_vmem = pl.BlockSpec(memory_space=pltpu.VMEM)
    out = pl.pallas_call(
        finish_kernel,
        out_shape=jax.ShapeDtypeStruct((count, samples), F32),
        in_specs=[in_vmem] * 2,
        out_specs=pl.BlockSpec(memory_space=pl.ANY),
        scratch_shapes=[
            pltpu.VMEM((count, samples), F32),
            pltpu.SemaphoreType.DMA((4,)),
        ],
        compiler_params=pltpu.CompilerParams(vmem_limit_bytes=40 * 2**20),
        cost_estimate=pl.CostEstimate(
            flops=7 * 10**8, bytes_accessed=3 * 10**6, transcendentals=0
        ),
        name="finish",
    )(summed, table)
    return out.reshape(3, count // 3, samples)


def on_device(
    blks,
    subs,
    synthetic,
    observed,
    pair_first,
    pair_second,
    pair_mask,
    pair_weight,
    station_owner,
    station_element,
):
    rows, _, samples = synthetic.shape
    forward, inverse = dft_tables(samples, NF)
    summed = exchange(
        blks,
        subs,
        jnp.transpose(synthetic, (1, 0, 2)),
        jnp.transpose(observed, (1, 0, 2)),
        jnp.asarray(forward),
        pair_first,
        pair_second,
        pair_mask,
        pair_weight,
        station_owner.reshape(1, rows),
        station_element.reshape(1, rows),
    )
    out = finish(summed, jnp.asarray(inverse))
    return jnp.transpose(out, (1, 0, 2))


def solution(mesh):
    blks, subs = mesh.shape["blk"], mesh.shape["sub"]
    return jax.shard_map(
        functools.partial(on_device, blks, subs),
        mesh=mesh,
        in_specs=(
            P(("blk", "sub"), None, None),
            P(("blk", "sub"), None, None),
            P("blk", "sub"),
            P("blk", "sub"),
            P("blk", "sub"),
            P("blk", "sub"),
            P(("blk", "sub"), None),
            P(("blk", "sub")),
        ),
        out_specs=P(("blk", "sub"), None, None),
        check_vma=False,
    )
```

```python
import functools
import math

import jax
import jax.numpy as jnp
import numpy as np
from jax import lax
from jax.experimental import pallas as pl
from jax.experimental.pallas import tpu as pltpu
from jax.sharding import PartitionSpec as P

MESH = pl.DeviceIdType.MESH
NF = 128
BLOCK = 64
F32 = jnp.float32
BF16 = jnp.bfloat16


def dft_tables(samples, freqs):
    phase = (np.arange(samples)[:, None] * np.arange(freqs)[None, :]) % samples
    angles = phase.astype(np.float64) * (2.0 * math.pi / samples)
    scale = 1.0 / math.sqrt(samples)
    cosine, sine = np.cos(angles) * scale, np.sin(angles) * scale
    forward = np.concatenate([cosine, -sine], axis=1).astype(np.float32)
    doubled = np.where(np.arange(freqs) == 0, 1.0, 2.0)[:, None]
    inverse = np.concatenate([cosine.T * doubled, -sine.T * doubled], axis=0)
    return forward.astype(jnp.bfloat16), inverse.astype(np.float32).astype(jnp.bfloat16)


def in_two(x):
    high = x.astype(BF16)
    return high, (x - high.astype(F32)).astype(BF16)


def dot_rows(a, b):
    return lax.dot_general(a, b, (((1,), (1,)), ((), ())), preferred_element_type=F32)


def dot_plain(a, b):
    return jnp.dot(a, b, preferred_element_type=F32)


def features(pair):
    xr, xi = pair[0][:, :NF].astype(F32), pair[0][:, NF:].astype(F32)
    o_r, o_i = pair[1][:, :NF].astype(F32), pair[1][:, NF:].astype(F32)
    dr, di = xr - o_r, xi - o_i
    parts = [dr * xr + di * xi, dr * xi - di * xr, o_r * xr + o_i * xi, o_r * xi - o_i * xr]
    both = [in_two(p) for p in parts]
    return jnp.concatenate(
        [jnp.concatenate([b[i] for b in both], axis=1) for i in range(2)], axis=0
    )


def for_features(links):
    return jnp.concatenate([links.astype(BF16)] * 2, axis=1)


def spread(rows, count, shift):
    index = lax.broadcasted_iota(jnp.int32, (count, NF), 0) + shift
    return jnp.concatenate(
        [(index == rows[s : s + 1]).astype(F32).astype(BF16) for s in range(rows.shape[0])], axis=1
    )


def spread_weights(rows, weights, count, shift):
    index = lax.broadcasted_iota(jnp.int32, (count, NF), 0) + shift
    return jnp.concatenate(
        [
            jnp.where(index == rows[s : s + 1], weights[s : s + 1], 0.0).astype(BF16)
            for s in range(rows.shape[0])
        ],
        axis=1,
    )


def exchange_kernel(
    blks,
    subs,
    syn_hbm,
    obs_hbm,
    table_hbm,
    first_hbm,
    second_hbm,
    mask_hbm,
    weight_hbm,
    owner_hbm,
    element_hbm,
    summed,
    traces,
    table,
    first,
    second,
    mask,
    weight,
    owner,
    element,
    spec,
    halo,
    list_out,
    list_over,
    lists,
    lists_prev,
    labels,
    outgoing,
    received,
    load_sems,
    list_send,
    list_recv,
    over_send,
    over_recv,
    halo_send,
    halo_recv,
    joined,
    y_send,
    y_recv,
    z_send,
    z_recv,
    all_send,
    all_recv,
):
    devices = blks * subs
    blk, sub = lax.axis_index("blk"), lax.axis_index("sub")
    me = blk * subs + sub
    rows = spec.shape[1]
    blocks = first.shape[0]
    def around(at, step, size):
        there = at + step
        return jnp.where(there >= size, there - size, there)

    subs_there = [around(sub, step, subs) for step in range(1, subs)]
    blks_there = [around(blk, step, blks) for step in range(1, blks)]
    blk_after, blk_before = blks_there[0], blks_there[-1]
    after = (jnp.where(sub == subs - 1, blk_after, blk), subs_there[0])
    before = (jnp.where(sub == 0, blk_before, blk), subs_there[-1])

    pairs = [
        (table_hbm, table),
        (syn_hbm.at[0], traces.at[0, pl.ds(0, rows)]),
        (obs_hbm.at[0], traces.at[0, pl.ds(rows, rows)]),
        (owner_hbm, owner),
        (element_hbm, element),
        (first_hbm, first),
        (second_hbm, second),
        (mask_hbm, mask),
        (weight_hbm, weight),
        (syn_hbm.at[1], traces.at[1, pl.ds(0, rows)]),
        (obs_hbm.at[1], traces.at[1, pl.ds(rows, rows)]),
        (syn_hbm.at[2], traces.at[2, pl.ds(0, rows)]),
        (obs_hbm.at[2], traces.at[2, pl.ds(rows, rows)]),
    ]
    loads = [
        pltpu.make_async_copy(src, dst, load_sems.at[i]) for i, (src, dst) in enumerate(pairs)
    ]
    for load in loads:
        load.start()

    barrier = pltpu.get_barrier_semaphore()

    def greet(there):
        pl.semaphore_signal(barrier, inc=1, device_id=there, device_id_type=MESH)

    for there in subs_there:
        greet((blk, there))
    for there in blks_there:
        greet((there, sub))

    @pl.when(sub == 0)
    def _():
        for s in range(1, subs):
            greet((blk_before, s))

    @pl.when(sub == subs - 1)
    def _():
        greet((blk_after, 0))

    def transform(c):
        both = dot_plain(traces[c], table[...]).astype(BF16)
        spec[2 * c] = both[:rows]
        spec[2 * c + 1] = both[rows:]

    for i in range(3):
        loads[i].wait()
    transform(0)

    pl.semaphore_wait(barrier, subs + blks - 1)

    def halo_copies(c):
        q = pl.ds(2 * c, 2)
        return [
            pltpu.make_async_remote_copy(
                src_ref=spec.at[q, pl.ds(0, BLOCK)],
                dst_ref=halo.at[q, pl.ds(BLOCK, BLOCK)],
                send_sem=halo_send.at[0, c],
                recv_sem=halo_recv.at[0, c],
                device_id=before,
                device_id_type=MESH,
            ),
            pltpu.make_async_remote_copy(
                src_ref=spec.at[q, pl.ds(rows - BLOCK, BLOCK)],
                dst_ref=halo.at[q, pl.ds(0, BLOCK)],
                send_sem=halo_send.at[1, c],
                recv_sem=halo_recv.at[1, c],
                device_id=after,
                device_id_type=MESH,
            ),
        ]

    halos = [halo_copies(c) for c in range(3)]
    for copy in halos[0]:
        copy.start()

    for i in range(3, 5):
        loads[i].wait()
    lane = lax.broadcasted_iota(jnp.int32, (rows, rows), 1)
    line = lax.broadcasted_iota(jnp.int32, (rows, rows), 0)
    owner_row = owner[...]

    def column(row):
        return jnp.sum(jnp.where(lane == line, row, 0), axis=1, keepdims=True)

    owner_column, element_column = column(owner_row), column(element[...]).astype(F32)
    same = owner_column == owner_row
    rank_column = jnp.sum(jnp.where(same & (lane < line), 1, 0), axis=1, keepdims=True)
    label_rows = []
    for k in range(2):
        chosen = ((owner_column == lane) & (rank_column == k)).astype(F32)
        label_rows.append(
            jnp.sum(chosen * (element_column - rows), axis=0, keepdims=True) + float(rows)
        )

    for i in range(5, 9):
        loads[i].wait()
    base = (blk * blocks + lax.broadcasted_iota(jnp.int32, (blocks, NF), 0)) * BLOCK
    code = ((first[...] - base) * (2 * BLOCK) + (second[...] - base)).astype(F32)
    slot_weight = weight[...] * mask[...].astype(F32)
    zero_row = jnp.zeros((1, NF), F32)
    for s in range(subs):
        lines = [max(2 * s - 1, 0), 2 * s, 2 * s + 1]
        list_out[s] = jnp.concatenate(
            [code[i : i + 1] for i in lines]
            + [slot_weight[i : i + 1] for i in lines]
            + label_rows,
            axis=0,
        )
    list_over[...] = jnp.concatenate(
        [code[blocks - 1 : blocks]]
        + [zero_row] * 2
        + [slot_weight[blocks - 1 : blocks]]
        + [zero_row] * 4,
        axis=0,
    )
    lists[sub] = list_out[sub]

    for there in subs_there:
        pltpu.make_async_remote_copy(
            src_ref=list_out.at[there],
            dst_ref=lists.at[sub],
            send_sem=list_send,
            recv_sem=list_recv,
            device_id=(blk, there),
            device_id_type=MESH,
        ).start()
    over = pltpu.make_async_remote_copy(
        src_ref=list_over,
        dst_ref=lists_prev.at[sub],
        send_sem=over_send,
        recv_sem=over_recv,
        device_id=(blk_after, 0),
        device_id_type=MESH,
    )
    over.start()

    for c in (1, 2):
        loads[7 + 2 * c].wait()
        loads[8 + 2 * c].wait()
        transform(c)
        for copy in halos[c]:
            copy.start()

    for there in subs_there:
        pl.semaphore_signal(joined, inc=1, device_id=(blk, there), device_id_type=MESH)

    rank_row = jnp.sum(jnp.where(same & (line < lane), 1, 0), axis=0, keepdims=True)
    target = owner_row * 4 + rank_row * 2
    slot = lax.broadcasted_iota(jnp.int32, (4 * devices, 2 * rows), 0)
    placement = (slot == jnp.concatenate([target, target + 1], axis=1)).astype(F32).astype(BF16)

    def stations(c):
        return (spec[2 * c], spec[2 * c + 1])

    own = [features(stations(c)) for c in range(3)]

    others = pl.ds(0, subs - 1)
    pltpu.make_async_copy(lists.at[others], lists.at[others], list_recv).wait()

    z, y = lax.div(blk, 4), lax.rem(blk, 4)
    labels[z, y] = jnp.concatenate([lists[:, 6, :], lists[:, 7, :]], axis=0).astype(BF16)
    for step in range(1, 4):
        pltpu.make_async_remote_copy(
            src_ref=labels.at[z, y],
            dst_ref=labels.at[z, y],
            send_sem=y_send,
            recv_sem=y_recv,
            device_id=(z * 4 + around(y, step, 4), sub),
            device_id_type=MESH,
        ).start()

    @pl.when(sub == 0)
    def _():
        pltpu.make_async_copy(lists_prev, lists_prev, over_recv).wait()

    @pl.when(sub != 0)
    def _():
        lists_prev[...] = lists[...]

    def unpacked(ref, k):
        codes = ref[:, k, :].astype(jnp.int32)
        return codes >> 7, codes & 127, ref[:, 3 + k, :]

    first0, second0, weight0 = unpacked(lists_prev, 0)
    first1, second1, weight1 = unpacked(lists, 1)
    first2, second2, weight2 = unpacked(lists, 2)
    to_prev = dot_rows(spread_weights(second0, weight0, BLOCK, BLOCK), spread(first0, rows, 0))
    upper = dot_rows(spread_weights(first1, weight1, BLOCK, 0), spread(second1, rows, 0))
    lower = dot_rows(spread_weights(first2, weight2, BLOCK, 0), spread(second2, rows, 0))
    half = lax.broadcasted_iota(jnp.int32, (BLOCK, rows), 1) >= BLOCK
    inside = jnp.where(half, pltpu.roll(lower, BLOCK, 1), 0.0)
    one_way = jnp.concatenate([upper, inside], axis=0)
    link_own = for_features(one_way + one_way.T)
    link_halo = for_features(jnp.concatenate([to_prev, jnp.where(half, lower, 0.0)], axis=0))
    inner = [dot_plain(link_own, own[c]) for c in range(3)]

    for c in range(3):
        for copy in halos[c]:
            copy.wait_recv()
        sums = inner[c] + dot_plain(link_halo, features((halo[2 * c], halo[2 * c + 1])))
        g1r, g1i, g2r, g2i = (sums[:, i * NF : (i + 1) * NF] for i in range(4))
        x, o = stations(c)
        xr, xi = x[:, :NF].astype(F32), x[:, NF:].astype(F32)
        dr, di = xr - o[:, :NF].astype(F32), xi - o[:, NF:].astype(F32)
        real = (xr * g1r - xi * g1i) + (dr * g2r - di * g2i)
        imag = (xr * g1i + xi * g1r) + (dr * g2i + di * g2r)
        adjoint = jnp.concatenate([real, imag], axis=0).astype(BF16)
        outgoing[:, c] = dot_plain(placement, adjoint).astype(BF16).reshape(devices, 4, NF)

    pl.semaphore_wait(joined, subs - 1)

    core, chip, x = lax.rem(sub, 2), lax.div(me, 2), lax.div(sub, 2)
    received[core, chip] = outgoing[me]

    def stepped(at, step):
        step = jnp.where(step >= 4, step - 4, step)
        step = jnp.where((core == 1) & (step > 0), 4 - step, step)
        return around(at, step, 4)

    def deliver(a, b, j, other):
        blk_to = stepped(z, j) * 4 + stepped(y, a + j)
        sub_to = stepped(x, b + j) * 2 + (1 - core if other else core)
        pltpu.make_async_remote_copy(
            src_ref=outgoing.at[blk_to * subs + sub_to],
            dst_ref=received.at[core, chip],
            send_sem=all_send,
            recv_sem=all_recv.at[other],
            device_id=(blk_to, sub_to),
            device_id_type=MESH,
        ).start()

    def turn(other, i, carry):
        for j in (2, 1, 3, 0):
            deliver(lax.div(i, 4), lax.rem(i, 4), j, other)
        return carry

    lax.fori_loop(0, blks, functools.partial(turn, 1), 0)
    some = pl.ds(0, 3)
    pltpu.make_async_copy(labels.at[0, some], labels.at[0, some], y_recv).wait()
    for step in range(1, 4):
        pltpu.make_async_remote_copy(
            src_ref=labels.at[z],
            dst_ref=labels.at[z],
            send_sem=z_send,
            recv_sem=z_recv,
            device_id=(around(z, step, 4) * 4 + y, sub),
            device_id_type=MESH,
        ).start()

    for j in (2, 1, 3):
        deliver(0, 0, j, 0)
    lax.fori_loop(1, blks, functools.partial(turn, 0), 0)

    pltpu.make_async_copy(labels.at[some], labels.at[some], z_recv).wait()
    by_owner = labels[...].reshape(2 * devices, NF)
    arrived = lax.broadcasted_iota(jnp.int32, (2 * devices, 2 * devices), 1)
    held = lax.broadcasted_iota(jnp.int32, (2 * devices, 2 * devices), 0)
    sub_bits = subs.bit_length() - 1
    wanted = (
        ((arrived >> (sub_bits + 1)) << (sub_bits + 1))
        + (((arrived >> 1) & 1) << sub_bits)
        + (((arrived >> 2) & (subs // 2 - 1)) << 1)
    )
    owner_line = lax.broadcasted_iota(jnp.int32, (rows, 2 * devices), 0)

    def collector(source_core):
        repeated = lax.dot_general(
            by_owner,
            (held == wanted + source_core).astype(F32).astype(BF16),
            (((0,), (0,)), ((), ())),
            preferred_element_type=F32,
        )
        label = jnp.sum(jnp.where(owner_line == me, repeated, 0.0), axis=0, keepdims=True)
        return jnp.concatenate(
            [
                ((label == owner_line.astype(F32)) & ((arrived[:rows] & 1) == i)).astype(F32)
                for i in range(2)
            ],
            axis=0,
        ).astype(BF16)

    collect_other, collect_same = collector(1 - core), collector(core)

    def sums(collect, source_core, c):
        return dot_plain(collect, received[source_core, :, c].reshape(2 * devices, NF))

    pltpu.make_async_copy(received.at[0], received.at[0], all_recv.at[1]).wait()
    first_sums = [sums(collect_other, 1 - core, c) for c in range(3)]
    most = pl.ds(0, devices // 2 - 1)
    pltpu.make_async_copy(received.at[0, most], received.at[0, most], all_recv.at[0]).wait()
    for c in range(3):
        total = (first_sums[c] + sums(collect_same, core, c)).astype(BF16)
        summed[c * rows : (c + 1) * rows, :NF] = total[:rows]
        summed[c * rows : (c + 1) * rows, NF:] = total[rows:]

    for c in range(3):
        for copy in halos[c]:
            copy.wait_send()
    pltpu.make_async_copy(list_out.at[others], list_out.at[others], list_send).wait()
    over.wait_send()
    pltpu.make_async_copy(labels.at[0, some], labels.at[0, some], y_send).wait()
    pltpu.make_async_copy(labels.at[some], labels.at[some], z_send).wait()
    most = pl.ds(0, devices - 1)
    pltpu.make_async_copy(outgoing.at[most], outgoing.at[most], all_send).wait()


def exchange(blks, subs, syn, obs, table, first, second, mask, weight, owner, element):
    devices = blks * subs
    samples, rows = syn.shape[2], syn.shape[1]
    in_hbm = pl.BlockSpec(memory_space=pltpu.HBM)
    dma = pltpu.SemaphoreType.DMA
    return pl.pallas_call(
        functools.partial(exchange_kernel, blks, subs),
        out_shape=pltpu.VMEM((3 * rows, 2 * NF), BF16),
        in_specs=[in_hbm] * 9,
        out_specs=pl.BlockSpec(memory_space=pltpu.VMEM),
        scratch_shapes=[
            pltpu.VMEM((3, 2 * rows, samples), BF16),
            pltpu.VMEM(table.shape, BF16),
            pltpu.VMEM(first.shape, jnp.int32),
            pltpu.VMEM(second.shape, jnp.int32),
            pltpu.VMEM(mask.shape, jnp.int32),
            pltpu.VMEM(weight.shape, F32),
            pltpu.VMEM(owner.shape, jnp.int32),
            pltpu.VMEM(element.shape, jnp.int32),
            pltpu.VMEM((6, rows, 2 * NF), BF16),
            pltpu.VMEM((6, 2 * BLOCK, 2 * NF), BF16),
            pltpu.VMEM((subs, 8, NF), F32),
            pltpu.VMEM((8, NF), F32),
            pltpu.VMEM((subs, 8, NF), F32),
            pltpu.VMEM((subs, 8, NF), F32),
            pltpu.VMEM((4, blks // 4, 2 * subs, NF), BF16),
            pltpu.VMEM((devices, 3, 4, NF), BF16),
            pltpu.VMEM((2, devices // 2, 3, 4, NF), BF16),
            dma((13,)),
            dma,
            dma,
            dma,
            dma,
            dma((2, 3)),
            dma((2, 3)),
            pltpu.SemaphoreType.REGULAR,
            dma,
            dma,
            dma,
            dma,
            dma,
            dma((2,)),
        ],
        compiler_params=pltpu.CompilerParams(
            collective_id=0, has_side_effects=True, vmem_limit_bytes=60 * 2**20
        ),
        cost_estimate=pl.CostEstimate(
            flops=2 * 10**9, bytes_accessed=3 * 10**6, transcendentals=0
        ),
        name="exchange",
    )(syn, obs, table, first, second, mask, weight, owner, element)


def finish_kernel(summed, table, out, result, sems):
    samples = result.shape[1]
    chunk = samples // sems.shape[0]
    copies = []
    for n in range(sems.shape[0]):
        columns = pl.ds(n * chunk, chunk)
        result[:, columns] = dot_plain(summed[...], table[:, columns])
        copies.append(
            pltpu.make_async_copy(result.at[:, columns], out.at[:, columns], sems.at[n])
        )
        copies[-1].start()
    for copy in copies:
        copy.wait()


def finish(summed, table):
    count, samples = summed.shape[0], table.shape[1]
    in_vmem = pl.BlockSpec(memory_space=pltpu.VMEM)
    out = pl.pallas_call(
        finish_kernel,
        out_shape=jax.ShapeDtypeStruct((count, samples), F32),
        in_specs=[in_vmem] * 2,
        out_specs=pl.BlockSpec(memory_space=pl.ANY),
        scratch_shapes=[
            pltpu.VMEM((count, samples), F32),
            pltpu.SemaphoreType.DMA((4,)),
        ],
        compiler_params=pltpu.CompilerParams(vmem_limit_bytes=40 * 2**20),
        cost_estimate=pl.CostEstimate(
            flops=7 * 10**8, bytes_accessed=3 * 10**6, transcendentals=0
        ),
        name="finish",
    )(summed, table)
    return out.reshape(3, count // 3, samples)


def on_device(
    blks,
    subs,
    synthetic,
    observed,
    pair_first,
    pair_second,
    pair_mask,
    pair_weight,
    station_owner,
    station_element,
):
    rows, _, samples = synthetic.shape
    forward, inverse = dft_tables(samples, NF)
    summed = exchange(
        blks,
        subs,
        jnp.transpose(synthetic, (1, 0, 2)),
        jnp.transpose(observed, (1, 0, 2)),
        jnp.asarray(forward),
        pair_first,
        pair_second,
        pair_mask,
        pair_weight,
        station_owner.reshape(1, rows),
        station_element.reshape(1, rows),
    )
    out = finish(summed, jnp.asarray(inverse))
    return jnp.transpose(out, (1, 0, 2))


def solution(mesh):
    blks, subs = mesh.shape["blk"], mesh.shape["sub"]
    return jax.shard_map(
        functools.partial(on_device, blks, subs),
        mesh=mesh,
        in_specs=(
            P(("blk", "sub"), None, None),
            P(("blk", "sub"), None, None),
            P("blk", "sub"),
            P("blk", "sub"),
            P("blk", "sub"),
            P("blk", "sub"),
            P(("blk", "sub"), None),
            P(("blk", "sub")),
        ),
        out_specs=P(("blk", "sub"), None, None),
        check_vma=False,
    )
```

```python
import functools
import itertools
import math

import jax
import jax.numpy as jnp
import numpy as np
from jax import lax
from jax.experimental import pallas as pl
from jax.experimental.pallas import tpu as pltpu
from jax.sharding import PartitionSpec as P

MESH = pl.DeviceIdType.MESH
NF = 128
BLOCK = 64
F32 = jnp.float32
BF16 = jnp.bfloat16


def dft_tables(samples, freqs):
    phase = (np.arange(samples)[:, None] * np.arange(freqs)[None, :]) % samples
    angles = phase.astype(np.float64) * (2.0 * math.pi / samples)
    scale = 1.0 / math.sqrt(samples)
    cosine, sine = np.cos(angles) * scale, np.sin(angles) * scale
    forward = np.concatenate([cosine, -sine], axis=1).astype(np.float32)
    doubled = np.where(np.arange(freqs) == 0, 1.0, 2.0)[:, None]
    inverse = np.concatenate([cosine.T * doubled, -sine.T * doubled], axis=0)
    return forward.astype(jnp.bfloat16), inverse.astype(np.float32).astype(jnp.bfloat16)


def in_two(x):
    high = x.astype(BF16)
    return high, (x - high.astype(F32)).astype(BF16)


def dot_rows(a, b):
    return lax.dot_general(a, b, (((1,), (1,)), ((), ())), preferred_element_type=F32)


def dot_plain(a, b):
    return jnp.dot(a, b, preferred_element_type=F32)


def features(pair):
    xr, xi = pair[0][:, :NF].astype(F32), pair[0][:, NF:].astype(F32)
    o_r, o_i = pair[1][:, :NF].astype(F32), pair[1][:, NF:].astype(F32)
    dr, di = xr - o_r, xi - o_i
    parts = [dr * xr + di * xi, dr * xi - di * xr, o_r * xr + o_i * xi, o_r * xi - o_i * xr]
    both = [in_two(p) for p in parts]
    return jnp.concatenate(
        [jnp.concatenate([b[i] for b in both], axis=1) for i in range(2)], axis=0
    )


def for_features(links):
    return jnp.concatenate([links.astype(BF16)] * 2, axis=1)


def spread(rows, count, shift):
    index = lax.broadcasted_iota(jnp.int32, (count, NF), 0) + shift
    return jnp.concatenate(
        [(index == rows[s : s + 1]).astype(F32).astype(BF16) for s in range(rows.shape[0])], axis=1
    )


def spread_weights(rows, weights, count, shift):
    index = lax.broadcasted_iota(jnp.int32, (count, NF), 0) + shift
    return jnp.concatenate(
        [
            jnp.where(index == rows[s : s + 1], weights[s : s + 1], 0.0).astype(BF16)
            for s in range(rows.shape[0])
        ],
        axis=1,
    )


def spread_order():
    left = list(itertools.product(range(4), range(4), range(4), range(2)))[1:]
    ways = {0: (0.0, 0.0), 1: (1.0, 0.0), 2: (1.0, 1.0), 3: (0.0, 1.0)}

    def links(step):
        return np.array([way for axis in step[:3] for way in ways[axis]])

    used, order = np.zeros(6), []
    while left:
        step = min(left, key=lambda t: (-np.sum(links(t)), np.max(used + links(t)), t))
        left.remove(step)
        used = used + links(step)
        order.append(step)
    return order


def exchange_kernel(
    blks,
    subs,
    syn_hbm,
    obs_hbm,
    table_hbm,
    first_hbm,
    second_hbm,
    mask_hbm,
    weight_hbm,
    owner_hbm,
    element_hbm,
    summed,
    traces,
    table,
    first,
    second,
    mask,
    weight,
    owner,
    element,
    spec,
    halo,
    list_out,
    list_over,
    lists,
    lists_prev,
    labels,
    outgoing,
    received,
    load_sems,
    list_send,
    list_recv,
    over_send,
    over_recv,
    halo_send,
    halo_recv,
    joined,
    y_send,
    y_recv,
    z_send,
    z_recv,
    all_send,
    all_recv,
):
    devices = blks * subs
    blk, sub = lax.axis_index("blk"), lax.axis_index("sub")
    me = blk * subs + sub
    rows = spec.shape[1]
    blocks = first.shape[0]
    def around(at, step, size):
        there = at + step
        return jnp.where(there >= size, there - size, there)

    subs_there = [around(sub, step, subs) for step in range(1, subs)]
    blks_there = [around(blk, step, blks) for step in range(1, blks)]
    blk_after, blk_before = blks_there[0], blks_there[-1]
    after = (jnp.where(sub == subs - 1, blk_after, blk), subs_there[0])
    before = (jnp.where(sub == 0, blk_before, blk), subs_there[-1])

    pairs = [
        (table_hbm, table),
        (syn_hbm.at[0], traces.at[0, pl.ds(0, rows)]),
        (obs_hbm.at[0], traces.at[0, pl.ds(rows, rows)]),
        (owner_hbm, owner),
        (element_hbm, element),
        (first_hbm, first),
        (second_hbm, second),
        (mask_hbm, mask),
        (weight_hbm, weight),
        (syn_hbm.at[1], traces.at[1, pl.ds(0, rows)]),
        (obs_hbm.at[1], traces.at[1, pl.ds(rows, rows)]),
        (syn_hbm.at[2], traces.at[2, pl.ds(0, rows)]),
        (obs_hbm.at[2], traces.at[2, pl.ds(rows, rows)]),
    ]
    loads = [
        pltpu.make_async_copy(src, dst, load_sems.at[i]) for i, (src, dst) in enumerate(pairs)
    ]
    for load in loads:
        load.start()

    barrier = pltpu.get_barrier_semaphore()

    def greet(there):
        pl.semaphore_signal(barrier, inc=1, device_id=there, device_id_type=MESH)

    for there in subs_there:
        greet((blk, there))
    for there in blks_there:
        greet((there, sub))

    @pl.when(sub == 0)
    def _():
        for s in range(1, subs):
            greet((blk_before, s))

    @pl.when(sub == subs - 1)
    def _():
        greet((blk_after, 0))

    def transform(c):
        both = dot_plain(traces[c], table[...]).astype(BF16)
        spec[2 * c] = both[:rows]
        spec[2 * c + 1] = both[rows:]

    for i in range(3):
        loads[i].wait()
    transform(0)

    pl.semaphore_wait(barrier, subs + blks - 1)

    def halo_copies(c):
        q = pl.ds(2 * c, 2)
        return [
            pltpu.make_async_remote_copy(
                src_ref=spec.at[q, pl.ds(0, BLOCK)],
                dst_ref=halo.at[q, pl.ds(BLOCK, BLOCK)],
                send_sem=halo_send.at[0, c],
                recv_sem=halo_recv.at[0, c],
                device_id=before,
                device_id_type=MESH,
            ),
            pltpu.make_async_remote_copy(
                src_ref=spec.at[q, pl.ds(rows - BLOCK, BLOCK)],
                dst_ref=halo.at[q, pl.ds(0, BLOCK)],
                send_sem=halo_send.at[1, c],
                recv_sem=halo_recv.at[1, c],
                device_id=after,
                device_id_type=MESH,
            ),
        ]

    halos = [halo_copies(c) for c in range(3)]
    for copy in halos[0]:
        copy.start()

    for i in range(3, 5):
        loads[i].wait()
    lane = lax.broadcasted_iota(jnp.int32, (rows, rows), 1)
    line = lax.broadcasted_iota(jnp.int32, (rows, rows), 0)
    owner_row = owner[...]

    def column(row):
        return jnp.sum(jnp.where(lane == line, row, 0), axis=1, keepdims=True)

    owner_column, element_column = column(owner_row), column(element[...]).astype(F32)
    same = owner_column == owner_row
    rank_column = jnp.sum(jnp.where(same & (lane < line), 1, 0), axis=1, keepdims=True)
    label_rows = []
    for k in range(2):
        chosen = ((owner_column == lane) & (rank_column == k)).astype(F32)
        label_rows.append(
            jnp.sum(chosen * (element_column - rows), axis=0, keepdims=True) + float(rows)
        )

    for i in range(5, 9):
        loads[i].wait()
    base = (blk * blocks + lax.broadcasted_iota(jnp.int32, (blocks, NF), 0)) * BLOCK
    code = ((first[...] - base) * (2 * BLOCK) + (second[...] - base)).astype(F32)
    slot_weight = weight[...] * mask[...].astype(F32)
    zero_row = jnp.zeros((1, NF), F32)
    for s in range(subs):
        lines = [max(2 * s - 1, 0), 2 * s, 2 * s + 1]
        list_out[s] = jnp.concatenate(
            [code[i : i + 1] for i in lines]
            + [slot_weight[i : i + 1] for i in lines]
            + label_rows,
            axis=0,
        )
    list_over[...] = jnp.concatenate(
        [code[blocks - 1 : blocks]]
        + [zero_row] * 2
        + [slot_weight[blocks - 1 : blocks]]
        + [zero_row] * 4,
        axis=0,
    )
    lists[sub] = list_out[sub]

    for there in subs_there:
        pltpu.make_async_remote_copy(
            src_ref=list_out.at[there],
            dst_ref=lists.at[sub],
            send_sem=list_send,
            recv_sem=list_recv,
            device_id=(blk, there),
            device_id_type=MESH,
        ).start()
    over = pltpu.make_async_remote_copy(
        src_ref=list_over,
        dst_ref=lists_prev.at[sub],
        send_sem=over_send,
        recv_sem=over_recv,
        device_id=(blk_after, 0),
        device_id_type=MESH,
    )
    over.start()

    for c in (1, 2):
        loads[7 + 2 * c].wait()
        loads[8 + 2 * c].wait()
        transform(c)
        for copy in halos[c]:
            copy.start()

    for there in subs_there:
        pl.semaphore_signal(joined, inc=1, device_id=(blk, there), device_id_type=MESH)

    rank_row = jnp.sum(jnp.where(same & (line < lane), 1, 0), axis=0, keepdims=True)
    target = owner_row * 4 + rank_row * 2
    slot = lax.broadcasted_iota(jnp.int32, (4 * devices, 2 * rows), 0)
    placement = (slot == jnp.concatenate([target, target + 1], axis=1)).astype(F32).astype(BF16)

    def stations(c):
        return (spec[2 * c], spec[2 * c + 1])

    own = [features(stations(c)) for c in range(3)]

    others = pl.ds(0, subs - 1)
    pltpu.make_async_copy(lists.at[others], lists.at[others], list_recv).wait()

    z, y = lax.div(blk, 4), lax.rem(blk, 4)
    labels[z, y] = jnp.concatenate([lists[:, 6, :], lists[:, 7, :]], axis=0).astype(BF16)
    for step in range(1, 4):
        pltpu.make_async_remote_copy(
            src_ref=labels.at[z, y],
            dst_ref=labels.at[z, y],
            send_sem=y_send,
            recv_sem=y_recv,
            device_id=(z * 4 + around(y, step, 4), sub),
            device_id_type=MESH,
        ).start()

    @pl.when(sub == 0)
    def _():
        pltpu.make_async_copy(lists_prev, lists_prev, over_recv).wait()

    @pl.when(sub != 0)
    def _():
        lists_prev[...] = lists[...]

    def unpacked(ref, k):
        codes = ref[:, k, :].astype(jnp.int32)
        return codes >> 7, codes & 127, ref[:, 3 + k, :]

    first0, second0, weight0 = unpacked(lists_prev, 0)
    first1, second1, weight1 = unpacked(lists, 1)
    first2, second2, weight2 = unpacked(lists, 2)
    to_prev = dot_rows(spread_weights(second0, weight0, BLOCK, BLOCK), spread(first0, rows, 0))
    upper = dot_rows(spread_weights(first1, weight1, BLOCK, 0), spread(second1, rows, 0))
    lower = dot_rows(spread_weights(first2, weight2, BLOCK, 0), spread(second2, rows, 0))
    half = lax.broadcasted_iota(jnp.int32, (BLOCK, rows), 1) >= BLOCK
    inside = jnp.where(half, pltpu.roll(lower, BLOCK, 1), 0.0)
    one_way = jnp.concatenate([upper, inside], axis=0)
    link_own = for_features(one_way + one_way.T)
    link_halo = for_features(jnp.concatenate([to_prev, jnp.where(half, lower, 0.0)], axis=0))
    inner = [dot_plain(link_own, own[c]) for c in range(3)]

    for c in range(3):
        for copy in halos[c]:
            copy.wait_recv()
        sums = inner[c] + dot_plain(link_halo, features((halo[2 * c], halo[2 * c + 1])))
        g1r, g1i, g2r, g2i = (sums[:, i * NF : (i + 1) * NF] for i in range(4))
        x, o = stations(c)
        xr, xi = x[:, :NF].astype(F32), x[:, NF:].astype(F32)
        dr, di = xr - o[:, :NF].astype(F32), xi - o[:, NF:].astype(F32)
        real = (xr * g1r - xi * g1i) + (dr * g2r - di * g2i)
        imag = (xr * g1i + xi * g1r) + (dr * g2i + di * g2r)
        adjoint = jnp.concatenate([real, imag], axis=0).astype(BF16)
        outgoing[:, c] = dot_plain(placement, adjoint).astype(BF16).reshape(devices, 4, NF)

    pl.semaphore_wait(joined, subs - 1)

    core = lax.rem(sub, 2)

    def turns(at, size):
        up = [around(at, step, size) for step in range(1, size)]
        return [at] + [jnp.where(core == 0, up[i], up[-1 - i]) for i in range(size - 1)]

    chip = lax.div(me, 2)
    z_to, y_to, x_to = turns(z, 4), turns(y, 4), turns(lax.div(sub, 2), 4)
    core_to = [core, 1 - core]
    received[core, chip] = outgoing[me]

    def deliver(step):
        dz, dy, dx, other = step
        blk_to, sub_to = z_to[dz] * 4 + y_to[dy], x_to[dx] * 2 + core_to[other]
        pltpu.make_async_remote_copy(
            src_ref=outgoing.at[blk_to * subs + sub_to],
            dst_ref=received.at[core, chip],
            send_sem=all_send,
            recv_sem=all_recv.at[other],
            device_id=(blk_to, sub_to),
            device_id_type=MESH,
        ).start()

    order = spread_order()
    for step in order[:48]:
        deliver(step)
    some = pl.ds(0, 3)
    pltpu.make_async_copy(labels.at[0, some], labels.at[0, some], y_recv).wait()
    for step in range(1, 4):
        pltpu.make_async_remote_copy(
            src_ref=labels.at[z],
            dst_ref=labels.at[z],
            send_sem=z_send,
            recv_sem=z_recv,
            device_id=(around(z, step, 4) * 4 + y, sub),
            device_id_type=MESH,
        ).start()

    for step in order[48:]:
        deliver(step)

    pltpu.make_async_copy(labels.at[some], labels.at[some], z_recv).wait()
    by_owner = labels[...].reshape(2 * devices, NF)
    arrived = lax.broadcasted_iota(jnp.int32, (2 * devices, 2 * devices), 1)
    held = lax.broadcasted_iota(jnp.int32, (2 * devices, 2 * devices), 0)
    sub_bits = subs.bit_length() - 1
    wanted = (
        ((arrived >> (sub_bits + 1)) << (sub_bits + 1))
        + (((arrived >> 1) & 1) << sub_bits)
        + (((arrived >> 2) & (subs // 2 - 1)) << 1)
    )
    owner_line = lax.broadcasted_iota(jnp.int32, (rows, 2 * devices), 0)

    def collector(source_core):
        repeated = lax.dot_general(
            by_owner,
            (held == wanted + source_core).astype(F32).astype(BF16),
            (((0,), (0,)), ((), ())),
            preferred_element_type=F32,
        )
        label = jnp.sum(jnp.where(owner_line == me, repeated, 0.0), axis=0, keepdims=True)
        return jnp.concatenate(
            [
                ((label == owner_line.astype(F32)) & ((arrived[:rows] & 1) == i)).astype(F32)
                for i in range(2)
            ],
            axis=0,
        ).astype(BF16)

    collect_other, collect_same = collector(1 - core), collector(core)

    def sums(collect, source_core, c):
        return dot_plain(collect, received[source_core, :, c].reshape(2 * devices, NF))

    pltpu.make_async_copy(received.at[0], received.at[0], all_recv.at[1]).wait()
    first_sums = [sums(collect_other, 1 - core, c) for c in range(3)]
    most = pl.ds(0, devices // 2 - 1)
    pltpu.make_async_copy(received.at[0, most], received.at[0, most], all_recv.at[0]).wait()
    for c in range(3):
        total = (first_sums[c] + sums(collect_same, core, c)).astype(BF16)
        summed[c * rows : (c + 1) * rows, :NF] = total[:rows]
        summed[c * rows : (c + 1) * rows, NF:] = total[rows:]

    for c in range(3):
        for copy in halos[c]:
            copy.wait_send()
    pltpu.make_async_copy(list_out.at[others], list_out.at[others], list_send).wait()
    over.wait_send()
    pltpu.make_async_copy(labels.at[0, some], labels.at[0, some], y_send).wait()
    pltpu.make_async_copy(labels.at[some], labels.at[some], z_send).wait()
    most = pl.ds(0, devices - 1)
    pltpu.make_async_copy(outgoing.at[most], outgoing.at[most], all_send).wait()


def exchange(blks, subs, syn, obs, table, first, second, mask, weight, owner, element):
    devices = blks * subs
    samples, rows = syn.shape[2], syn.shape[1]
    in_hbm = pl.BlockSpec(memory_space=pltpu.HBM)
    dma = pltpu.SemaphoreType.DMA
    return pl.pallas_call(
        functools.partial(exchange_kernel, blks, subs),
        out_shape=pltpu.VMEM((3 * rows, 2 * NF), BF16),
        in_specs=[in_hbm] * 9,
        out_specs=pl.BlockSpec(memory_space=pltpu.VMEM),
        scratch_shapes=[
            pltpu.VMEM((3, 2 * rows, samples), BF16),
            pltpu.VMEM(table.shape, BF16),
            pltpu.VMEM(first.shape, jnp.int32),
            pltpu.VMEM(second.shape, jnp.int32),
            pltpu.VMEM(mask.shape, jnp.int32),
            pltpu.VMEM(weight.shape, F32),
            pltpu.VMEM(owner.shape, jnp.int32),
            pltpu.VMEM(element.shape, jnp.int32),
            pltpu.VMEM((6, rows, 2 * NF), BF16),
            pltpu.VMEM((6, 2 * BLOCK, 2 * NF), BF16),
            pltpu.VMEM((subs, 8, NF), F32),
            pltpu.VMEM((8, NF), F32),
            pltpu.VMEM((subs, 8, NF), F32),
            pltpu.VMEM((subs, 8, NF), F32),
            pltpu.VMEM((4, blks // 4, 2 * subs, NF), BF16),
            pltpu.VMEM((devices, 3, 4, NF), BF16),
            pltpu.VMEM((2, devices // 2, 3, 4, NF), BF16),
            dma((13,)),
            dma,
            dma,
            dma,
            dma,
            dma((2, 3)),
            dma((2, 3)),
            pltpu.SemaphoreType.REGULAR,
            dma,
            dma,
            dma,
            dma,
            dma,
            dma((2,)),
        ],
        compiler_params=pltpu.CompilerParams(
            collective_id=0, has_side_effects=True, vmem_limit_bytes=60 * 2**20
        ),
        cost_estimate=pl.CostEstimate(
            flops=2 * 10**9, bytes_accessed=3 * 10**6, transcendentals=0
        ),
        name="exchange",
    )(syn, obs, table, first, second, mask, weight, owner, element)


def finish_kernel(summed, table, out, result, sems):
    samples = result.shape[1]
    chunk = samples // sems.shape[0]
    copies = []
    for n in range(sems.shape[0]):
        columns = pl.ds(n * chunk, chunk)
        result[:, columns] = dot_plain(summed[...], table[:, columns])
        copies.append(
            pltpu.make_async_copy(result.at[:, columns], out.at[:, columns], sems.at[n])
        )
        copies[-1].start()
    for copy in copies:
        copy.wait()


def finish(summed, table):
    count, samples = summed.shape[0], table.shape[1]
    in_vmem = pl.BlockSpec(memory_space=pltpu.VMEM)
    out = pl.pallas_call(
        finish_kernel,
        out_shape=jax.ShapeDtypeStruct((count, samples), F32),
        in_specs=[in_vmem] * 2,
        out_specs=pl.BlockSpec(memory_space=pl.ANY),
        scratch_shapes=[
            pltpu.VMEM((count, samples), F32),
            pltpu.SemaphoreType.DMA((4,)),
        ],
        compiler_params=pltpu.CompilerParams(vmem_limit_bytes=40 * 2**20),
        cost_estimate=pl.CostEstimate(
            flops=7 * 10**8, bytes_accessed=3 * 10**6, transcendentals=0
        ),
        name="finish",
    )(summed, table)
    return out.reshape(3, count // 3, samples)


def on_device(
    blks,
    subs,
    synthetic,
    observed,
    pair_first,
    pair_second,
    pair_mask,
    pair_weight,
    station_owner,
    station_element,
):
    rows, _, samples = synthetic.shape
    forward, inverse = dft_tables(samples, NF)
    summed = exchange(
        blks,
        subs,
        jnp.transpose(synthetic, (1, 0, 2)),
        jnp.transpose(observed, (1, 0, 2)),
        jnp.asarray(forward),
        pair_first,
        pair_second,
        pair_mask,
        pair_weight,
        station_owner.reshape(1, rows),
        station_element.reshape(1, rows),
    )
    out = finish(summed, jnp.asarray(inverse))
    return jnp.transpose(out, (1, 0, 2))


def solution(mesh):
    blks, subs = mesh.shape["blk"], mesh.shape["sub"]
    return jax.shard_map(
        functools.partial(on_device, blks, subs),
        mesh=mesh,
        in_specs=(
            P(("blk", "sub"), None, None),
            P(("blk", "sub"), None, None),
            P("blk", "sub"),
            P("blk", "sub"),
            P("blk", "sub"),
            P("blk", "sub"),
            P(("blk", "sub"), None),
            P(("blk", "sub")),
        ),
        out_specs=P(("blk", "sub"), None, None),
        check_vma=False,
    )
```

```python
import functools
import itertools
import math

import jax
import jax.numpy as jnp
import numpy as np
from jax import lax
from jax.experimental import pallas as pl
from jax.experimental.pallas import tpu as pltpu
from jax.sharding import PartitionSpec as P

MESH = pl.DeviceIdType.MESH
NF = 128
BLOCK = 64
F32 = jnp.float32
BF16 = jnp.bfloat16


def dft_tables(samples, freqs):
    phase = (np.arange(samples)[:, None] * np.arange(freqs)[None, :]) % samples
    angles = phase.astype(np.float64) * (2.0 * math.pi / samples)
    scale = 1.0 / math.sqrt(samples)
    cosine, sine = np.cos(angles) * scale, np.sin(angles) * scale
    forward = np.concatenate([cosine, -sine], axis=1).astype(np.float32)
    doubled = np.where(np.arange(freqs) == 0, 1.0, 2.0)[:, None]
    inverse = np.concatenate([cosine.T * doubled, -sine.T * doubled], axis=0)
    return forward.astype(jnp.bfloat16), inverse.astype(np.float32).astype(jnp.bfloat16)


def in_two(x):
    high = x.astype(BF16)
    return high, (x - high.astype(F32)).astype(BF16)


def dot_rows(a, b):
    return lax.dot_general(a, b, (((1,), (1,)), ((), ())), preferred_element_type=F32)


def dot_plain(a, b):
    return jnp.dot(a, b, preferred_element_type=F32)


def features(pair):
    xr, xi = pair[0][:, :NF].astype(F32), pair[0][:, NF:].astype(F32)
    o_r, o_i = pair[1][:, :NF].astype(F32), pair[1][:, NF:].astype(F32)
    dr, di = xr - o_r, xi - o_i
    parts = [dr * xr + di * xi, dr * xi - di * xr, o_r * xr + o_i * xi, o_r * xi - o_i * xr]
    both = [in_two(p) for p in parts]
    return jnp.concatenate(
        [jnp.concatenate([b[i] for b in both], axis=1) for i in range(2)], axis=0
    )


def for_features(links):
    return jnp.concatenate([links.astype(BF16)] * 2, axis=1)


def spread(rows, count, shift):
    index = lax.broadcasted_iota(jnp.int32, (count, NF), 0) + shift
    return jnp.concatenate(
        [(index == rows[s : s + 1]).astype(F32).astype(BF16) for s in range(rows.shape[0])], axis=1
    )


def spread_weights(rows, weights, count, shift):
    index = lax.broadcasted_iota(jnp.int32, (count, NF), 0) + shift
    return jnp.concatenate(
        [
            jnp.where(index == rows[s : s + 1], weights[s : s + 1], 0.0).astype(BF16)
            for s in range(rows.shape[0])
        ],
        axis=1,
    )


def spread_order():
    left = list(itertools.product(range(4), range(4), range(4), range(2)))[1:]
    ways = {0: (0.0, 0.0), 1: (1.0, 0.0), 2: (1.0, 1.0), 3: (0.0, 1.0)}
    entered = ((0.0, 1.1, 2.0, 2.5), (0.0, 0.65, 1.1, 1.5), (0.0, 0.8, 1.2, 1.25))

    def links(step):
        return np.array([way for axis in step[:3] for way in ways[axis]])

    def lead(step):
        return sum(
            max(at[source] - at[(source + by) % 4] for source in range(4))
            for at, by in zip(entered, step)
        )

    used, order = np.zeros(6), []
    while left:
        if len(order) % 2 == 0:
            step = max(left, key=lambda t: (lead(t), t))
        else:
            step = min(left, key=lambda t: (np.max(used + links(t)), -lead(t), t))
        left.remove(step)
        used = used + links(step)
        order.append(step)
    return order


def exchange_kernel(
    blks,
    subs,
    syn_hbm,
    obs_hbm,
    table_hbm,
    first_hbm,
    second_hbm,
    mask_hbm,
    weight_hbm,
    owner_hbm,
    element_hbm,
    summed,
    traces,
    table,
    first,
    second,
    mask,
    weight,
    owner,
    element,
    spec,
    halo,
    list_out,
    list_over,
    lists,
    lists_prev,
    labels,
    outgoing,
    received,
    load_sems,
    list_send,
    list_recv,
    over_send,
    over_recv,
    halo_send,
    halo_recv,
    joined,
    y_send,
    y_recv,
    z_send,
    z_recv,
    all_send,
    all_recv,
):
    devices = blks * subs
    blk, sub = lax.axis_index("blk"), lax.axis_index("sub")
    me = blk * subs + sub
    rows = spec.shape[1]
    blocks = first.shape[0]
    def around(at, step, size):
        there = at + step
        return jnp.where(there >= size, there - size, there)

    subs_there = [around(sub, step, subs) for step in range(1, subs)]
    blks_there = [around(blk, step, blks) for step in range(1, blks)]
    blk_after, blk_before = blks_there[0], blks_there[-1]
    after = (jnp.where(sub == subs - 1, blk_after, blk), subs_there[0])
    before = (jnp.where(sub == 0, blk_before, blk), subs_there[-1])

    pairs = [
        (table_hbm, table),
        (syn_hbm.at[0], traces.at[0, pl.ds(0, rows)]),
        (obs_hbm.at[0], traces.at[0, pl.ds(rows, rows)]),
        (owner_hbm, owner),
        (element_hbm, element),
        (first_hbm, first),
        (second_hbm, second),
        (mask_hbm, mask),
        (weight_hbm, weight),
        (syn_hbm.at[1], traces.at[1, pl.ds(0, rows)]),
        (obs_hbm.at[1], traces.at[1, pl.ds(rows, rows)]),
        (syn_hbm.at[2], traces.at[2, pl.ds(0, rows)]),
        (obs_hbm.at[2], traces.at[2, pl.ds(rows, rows)]),
    ]
    loads = [
        pltpu.make_async_copy(src, dst, load_sems.at[i]) for i, (src, dst) in enumerate(pairs)
    ]
    for load in loads:
        load.start()

    barrier = pltpu.get_barrier_semaphore()

    def greet(there):
        pl.semaphore_signal(barrier, inc=1, device_id=there, device_id_type=MESH)

    for there in subs_there:
        greet((blk, there))
    for there in blks_there:
        greet((there, sub))

    @pl.when(sub == 0)
    def _():
        for s in range(1, subs):
            greet((blk_before, s))

    @pl.when(sub == subs - 1)
    def _():
        greet((blk_after, 0))

    def transform(c):
        both = dot_plain(traces[c], table[...]).astype(BF16)
        spec[2 * c] = both[:rows]
        spec[2 * c + 1] = both[rows:]

    for i in range(3):
        loads[i].wait()
    transform(0)

    pl.semaphore_wait(barrier, subs + blks - 1)

    def halo_copies(c):
        q = pl.ds(2 * c, 2)
        return [
            pltpu.make_async_remote_copy(
                src_ref=spec.at[q, pl.ds(0, BLOCK)],
                dst_ref=halo.at[q, pl.ds(BLOCK, BLOCK)],
                send_sem=halo_send.at[0, c],
                recv_sem=halo_recv.at[0, c],
                device_id=before,
                device_id_type=MESH,
            ),
            pltpu.make_async_remote_copy(
                src_ref=spec.at[q, pl.ds(rows - BLOCK, BLOCK)],
                dst_ref=halo.at[q, pl.ds(0, BLOCK)],
                send_sem=halo_send.at[1, c],
                recv_sem=halo_recv.at[1, c],
                device_id=after,
                device_id_type=MESH,
            ),
        ]

    halos = [halo_copies(c) for c in range(3)]
    for copy in halos[0]:
        copy.start()

    for i in range(3, 5):
        loads[i].wait()
    lane = lax.broadcasted_iota(jnp.int32, (rows, rows), 1)
    line = lax.broadcasted_iota(jnp.int32, (rows, rows), 0)
    owner_row = owner[...]

    def column(row):
        return jnp.sum(jnp.where(lane == line, row, 0), axis=1, keepdims=True)

    owner_column, element_column = column(owner_row), column(element[...]).astype(F32)
    same = owner_column == owner_row
    rank_column = jnp.sum(jnp.where(same & (lane < line), 1, 0), axis=1, keepdims=True)
    label_rows = []
    for k in range(2):
        chosen = ((owner_column == lane) & (rank_column == k)).astype(F32)
        label_rows.append(
            jnp.sum(chosen * (element_column - rows), axis=0, keepdims=True) + float(rows)
        )

    for i in range(5, 9):
        loads[i].wait()
    base = (blk * blocks + lax.broadcasted_iota(jnp.int32, (blocks, NF), 0)) * BLOCK
    code = ((first[...] - base) * (2 * BLOCK) + (second[...] - base)).astype(F32)
    slot_weight = weight[...] * mask[...].astype(F32)
    zero_row = jnp.zeros((1, NF), F32)
    for s in range(subs):
        lines = [max(2 * s - 1, 0), 2 * s, 2 * s + 1]
        list_out[s] = jnp.concatenate(
            [code[i : i + 1] for i in lines]
            + [slot_weight[i : i + 1] for i in lines]
            + label_rows,
            axis=0,
        )
    list_over[...] = jnp.concatenate(
        [code[blocks - 1 : blocks]]
        + [zero_row] * 2
        + [slot_weight[blocks - 1 : blocks]]
        + [zero_row] * 4,
        axis=0,
    )
    lists[sub] = list_out[sub]

    for there in subs_there:
        pltpu.make_async_remote_copy(
            src_ref=list_out.at[there],
            dst_ref=lists.at[sub],
            send_sem=list_send,
            recv_sem=list_recv,
            device_id=(blk, there),
            device_id_type=MESH,
        ).start()
    over = pltpu.make_async_remote_copy(
        src_ref=list_over,
        dst_ref=lists_prev.at[sub],
        send_sem=over_send,
        recv_sem=over_recv,
        device_id=(blk_after, 0),
        device_id_type=MESH,
    )
    over.start()

    for c in (1, 2):
        loads[7 + 2 * c].wait()
        loads[8 + 2 * c].wait()
        transform(c)
        for copy in halos[c]:
            copy.start()

    for there in subs_there:
        pl.semaphore_signal(joined, inc=1, device_id=(blk, there), device_id_type=MESH)

    rank_row = jnp.sum(jnp.where(same & (line < lane), 1, 0), axis=0, keepdims=True)
    target = owner_row * 4 + rank_row * 2
    slot = lax.broadcasted_iota(jnp.int32, (4 * devices, 2 * rows), 0)
    placement = (slot == jnp.concatenate([target, target + 1], axis=1)).astype(F32).astype(BF16)

    def stations(c):
        return (spec[2 * c], spec[2 * c + 1])

    own = [features(stations(c)) for c in range(3)]

    others = pl.ds(0, subs - 1)
    pltpu.make_async_copy(lists.at[others], lists.at[others], list_recv).wait()

    z, y = lax.div(blk, 4), lax.rem(blk, 4)
    labels[z, y] = jnp.concatenate([lists[:, 6, :], lists[:, 7, :]], axis=0).astype(BF16)
    for step in range(1, 4):
        pltpu.make_async_remote_copy(
            src_ref=labels.at[z, y],
            dst_ref=labels.at[z, y],
            send_sem=y_send,
            recv_sem=y_recv,
            device_id=(z * 4 + around(y, step, 4), sub),
            device_id_type=MESH,
        ).start()

    @pl.when(sub == 0)
    def _():
        pltpu.make_async_copy(lists_prev, lists_prev, over_recv).wait()

    @pl.when(sub != 0)
    def _():
        lists_prev[...] = lists[...]

    def unpacked(ref, k):
        codes = ref[:, k, :].astype(jnp.int32)
        return codes >> 7, codes & 127, ref[:, 3 + k, :]

    first0, second0, weight0 = unpacked(lists_prev, 0)
    first1, second1, weight1 = unpacked(lists, 1)
    first2, second2, weight2 = unpacked(lists, 2)
    to_prev = dot_rows(spread_weights(second0, weight0, BLOCK, BLOCK), spread(first0, rows, 0))
    upper = dot_rows(spread_weights(first1, weight1, BLOCK, 0), spread(second1, rows, 0))
    lower = dot_rows(spread_weights(first2, weight2, BLOCK, 0), spread(second2, rows, 0))
    half = lax.broadcasted_iota(jnp.int32, (BLOCK, rows), 1) >= BLOCK
    inside = jnp.where(half, pltpu.roll(lower, BLOCK, 1), 0.0)
    one_way = jnp.concatenate([upper, inside], axis=0)
    link_own = for_features(one_way + one_way.T)
    link_halo = for_features(jnp.concatenate([to_prev, jnp.where(half, lower, 0.0)], axis=0))
    inner = [dot_plain(link_own, own[c]) for c in range(3)]

    for c in range(3):
        for copy in halos[c]:
            copy.wait_recv()
        sums = inner[c] + dot_plain(link_halo, features((halo[2 * c], halo[2 * c + 1])))
        g1r, g1i, g2r, g2i = (sums[:, i * NF : (i + 1) * NF] for i in range(4))
        x, o = stations(c)
        xr, xi = x[:, :NF].astype(F32), x[:, NF:].astype(F32)
        dr, di = xr - o[:, :NF].astype(F32), xi - o[:, NF:].astype(F32)
        real = (xr * g1r - xi * g1i) + (dr * g2r - di * g2i)
        imag = (xr * g1i + xi * g1r) + (dr * g2i + di * g2r)
        adjoint = jnp.concatenate([real, imag], axis=0).astype(BF16)
        outgoing[:, c] = dot_plain(placement, adjoint).astype(BF16).reshape(devices, 4, NF)

    pl.semaphore_wait(joined, subs - 1)

    def turns(at, size):
        return [at] + [around(at, step, size) for step in range(1, size)]

    core, chip = lax.rem(sub, 2), lax.div(me, 2)
    z_to, y_to, x_to = turns(z, 4), turns(y, 4), turns(lax.div(sub, 2), 4)
    core_to = [core, 1 - core]
    received[core, chip] = outgoing[me]

    def deliver(step):
        dz, dy, dx, other = step
        blk_to, sub_to = z_to[dz] * 4 + y_to[dy], x_to[dx] * 2 + core_to[other]
        pltpu.make_async_remote_copy(
            src_ref=outgoing.at[blk_to * subs + sub_to],
            dst_ref=received.at[core, chip],
            send_sem=all_send,
            recv_sem=all_recv.at[other],
            device_id=(blk_to, sub_to),
            device_id_type=MESH,
        ).start()

    order = spread_order()
    for step in order[:48]:
        deliver(step)
    some = pl.ds(0, 3)
    pltpu.make_async_copy(labels.at[0, some], labels.at[0, some], y_recv).wait()
    for step in range(1, 4):
        pltpu.make_async_remote_copy(
            src_ref=labels.at[z],
            dst_ref=labels.at[z],
            send_sem=z_send,
            recv_sem=z_recv,
            device_id=(around(z, step, 4) * 4 + y, sub),
            device_id_type=MESH,
        ).start()

    for step in order[48:]:
        deliver(step)

    pltpu.make_async_copy(labels.at[some], labels.at[some], z_recv).wait()
    by_owner = labels[...].reshape(2 * devices, NF)
    arrived = lax.broadcasted_iota(jnp.int32, (2 * devices, 2 * devices), 1)
    held = lax.broadcasted_iota(jnp.int32, (2 * devices, 2 * devices), 0)
    sub_bits = subs.bit_length() - 1
    wanted = (
        ((arrived >> (sub_bits + 1)) << (sub_bits + 1))
        + (((arrived >> 1) & 1) << sub_bits)
        + (((arrived >> 2) & (subs // 2 - 1)) << 1)
    )
    owner_line = lax.broadcasted_iota(jnp.int32, (rows, 2 * devices), 0)

    def collector(source_core):
        repeated = lax.dot_general(
            by_owner,
            (held == wanted + source_core).astype(F32).astype(BF16),
            (((0,), (0,)), ((), ())),
            preferred_element_type=F32,
        )
        label = jnp.sum(jnp.where(owner_line == me, repeated, 0.0), axis=0, keepdims=True)
        return jnp.concatenate(
            [
                ((label == owner_line.astype(F32)) & ((arrived[:rows] & 1) == i)).astype(F32)
                for i in range(2)
            ],
            axis=0,
        ).astype(BF16)

    collect_other, collect_same = collector(1 - core), collector(core)

    def sums(collect, source_core, c):
        return dot_plain(collect, received[source_core, :, c].reshape(2 * devices, NF))

    pltpu.make_async_copy(received.at[0], received.at[0], all_recv.at[1]).wait()
    first_sums = [sums(collect_other, 1 - core, c) for c in range(3)]
    most = pl.ds(0, devices // 2 - 1)
    pltpu.make_async_copy(received.at[0, most], received.at[0, most], all_recv.at[0]).wait()
    for c in range(3):
        total = (first_sums[c] + sums(collect_same, core, c)).astype(BF16)
        summed[c * rows : (c + 1) * rows, :NF] = total[:rows]
        summed[c * rows : (c + 1) * rows, NF:] = total[rows:]

    for c in range(3):
        for copy in halos[c]:
            copy.wait_send()
    pltpu.make_async_copy(list_out.at[others], list_out.at[others], list_send).wait()
    over.wait_send()
    pltpu.make_async_copy(labels.at[0, some], labels.at[0, some], y_send).wait()
    pltpu.make_async_copy(labels.at[some], labels.at[some], z_send).wait()
    most = pl.ds(0, devices - 1)
    pltpu.make_async_copy(outgoing.at[most], outgoing.at[most], all_send).wait()


def exchange(blks, subs, syn, obs, table, first, second, mask, weight, owner, element):
    devices = blks * subs
    samples, rows = syn.shape[2], syn.shape[1]
    in_hbm = pl.BlockSpec(memory_space=pltpu.HBM)
    dma = pltpu.SemaphoreType.DMA
    return pl.pallas_call(
        functools.partial(exchange_kernel, blks, subs),
        out_shape=pltpu.VMEM((3 * rows, 2 * NF), BF16),
        in_specs=[in_hbm] * 9,
        out_specs=pl.BlockSpec(memory_space=pltpu.VMEM),
        scratch_shapes=[
            pltpu.VMEM((3, 2 * rows, samples), BF16),
            pltpu.VMEM(table.shape, BF16),
            pltpu.VMEM(first.shape, jnp.int32),
            pltpu.VMEM(second.shape, jnp.int32),
            pltpu.VMEM(mask.shape, jnp.int32),
            pltpu.VMEM(weight.shape, F32),
            pltpu.VMEM(owner.shape, jnp.int32),
            pltpu.VMEM(element.shape, jnp.int32),
            pltpu.VMEM((6, rows, 2 * NF), BF16),
            pltpu.VMEM((6, 2 * BLOCK, 2 * NF), BF16),
            pltpu.VMEM((subs, 8, NF), F32),
            pltpu.VMEM((8, NF), F32),
            pltpu.VMEM((subs, 8, NF), F32),
            pltpu.VMEM((subs, 8, NF), F32),
            pltpu.VMEM((4, blks // 4, 2 * subs, NF), BF16),
            pltpu.VMEM((devices, 3, 4, NF), BF16),
            pltpu.VMEM((2, devices // 2, 3, 4, NF), BF16),
            dma((13,)),
            dma,
            dma,
            dma,
            dma,
            dma((2, 3)),
            dma((2, 3)),
            pltpu.SemaphoreType.REGULAR,
            dma,
            dma,
            dma,
            dma,
            dma,
            dma((2,)),
        ],
        compiler_params=pltpu.CompilerParams(
            collective_id=0, has_side_effects=True, vmem_limit_bytes=60 * 2**20
        ),
        cost_estimate=pl.CostEstimate(
            flops=2 * 10**9, bytes_accessed=3 * 10**6, transcendentals=0
        ),
        name="exchange",
    )(syn, obs, table, first, second, mask, weight, owner, element)


def finish_kernel(summed, table, out, result, sems):
    samples = result.shape[1]
    chunk = samples // sems.shape[0]
    copies = []
    for n in range(sems.shape[0]):
        columns = pl.ds(n * chunk, chunk)
        result[:, columns] = dot_plain(summed[...], table[:, columns])
        copies.append(
            pltpu.make_async_copy(result.at[:, columns], out.at[:, columns], sems.at[n])
        )
        copies[-1].start()
    for copy in copies:
        copy.wait()


def finish(summed, table):
    count, samples = summed.shape[0], table.shape[1]
    in_vmem = pl.BlockSpec(memory_space=pltpu.VMEM)
    out = pl.pallas_call(
        finish_kernel,
        out_shape=jax.ShapeDtypeStruct((count, samples), F32),
        in_specs=[in_vmem] * 2,
        out_specs=pl.BlockSpec(memory_space=pl.ANY),
        scratch_shapes=[
            pltpu.VMEM((count, samples), F32),
            pltpu.SemaphoreType.DMA((4,)),
        ],
        compiler_params=pltpu.CompilerParams(vmem_limit_bytes=40 * 2**20),
        cost_estimate=pl.CostEstimate(
            flops=7 * 10**8, bytes_accessed=3 * 10**6, transcendentals=0
        ),
        name="finish",
    )(summed, table)
    return out.reshape(3, count // 3, samples)


def on_device(
    blks,
    subs,
    synthetic,
    observed,
    pair_first,
    pair_second,
    pair_mask,
    pair_weight,
    station_owner,
    station_element,
):
    rows, _, samples = synthetic.shape
    forward, inverse = dft_tables(samples, NF)
    summed = exchange(
        blks,
        subs,
        jnp.transpose(synthetic, (1, 0, 2)),
        jnp.transpose(observed, (1, 0, 2)),
        jnp.asarray(forward),
        pair_first,
        pair_second,
        pair_mask,
        pair_weight,
        station_owner.reshape(1, rows),
        station_element.reshape(1, rows),
    )
    out = finish(summed, jnp.asarray(inverse))
    return jnp.transpose(out, (1, 0, 2))


def solution(mesh):
    blks, subs = mesh.shape["blk"], mesh.shape["sub"]
    return jax.shard_map(
        functools.partial(on_device, blks, subs),
        mesh=mesh,
        in_specs=(
            P(("blk", "sub"), None, None),
            P(("blk", "sub"), None, None),
            P("blk", "sub"),
            P("blk", "sub"),
            P("blk", "sub"),
            P("blk", "sub"),
            P(("blk", "sub"), None),
            P(("blk", "sub")),
        ),
        out_specs=P(("blk", "sub"), None, None),
        check_vma=False,
    )
```

```python
import functools
import itertools
import math

import jax
import jax.numpy as jnp
import numpy as np
from jax import lax
from jax.experimental import pallas as pl
from jax.experimental.pallas import tpu as pltpu
from jax.sharding import PartitionSpec as P

MESH = pl.DeviceIdType.MESH
NF = 128
BLOCK = 64
F32 = jnp.float32
BF16 = jnp.bfloat16


def dft_tables(samples, freqs):
    phase = (np.arange(samples)[:, None] * np.arange(freqs)[None, :]) % samples
    angles = phase.astype(np.float64) * (2.0 * math.pi / samples)
    scale = 1.0 / math.sqrt(samples)
    cosine, sine = np.cos(angles) * scale, np.sin(angles) * scale
    forward = np.concatenate([cosine, -sine], axis=1).astype(np.float32)
    doubled = np.where(np.arange(freqs) == 0, 1.0, 2.0)[:, None]
    inverse = np.concatenate([cosine.T * doubled, -sine.T * doubled], axis=0)
    return forward.astype(jnp.bfloat16), inverse.astype(np.float32).astype(jnp.bfloat16)


def in_two(x):
    high = x.astype(BF16)
    return high, (x - high.astype(F32)).astype(BF16)


def dot_rows(a, b):
    return lax.dot_general(a, b, (((1,), (1,)), ((), ())), preferred_element_type=F32)


def dot_plain(a, b):
    return jnp.dot(a, b, preferred_element_type=F32)


def features(pair):
    xr, xi = pair[0][:, :NF].astype(F32), pair[0][:, NF:].astype(F32)
    o_r, o_i = pair[1][:, :NF].astype(F32), pair[1][:, NF:].astype(F32)
    dr, di = xr - o_r, xi - o_i
    parts = [dr * xr + di * xi, dr * xi - di * xr, o_r * xr + o_i * xi, o_r * xi - o_i * xr]
    both = [in_two(p) for p in parts]
    return jnp.concatenate(
        [jnp.concatenate([b[i] for b in both], axis=1) for i in range(2)], axis=0
    )


def for_features(links):
    return jnp.concatenate([links.astype(BF16)] * 2, axis=1)


def spread(rows, count, shift):
    index = lax.broadcasted_iota(jnp.int32, (count, NF), 0) + shift
    return jnp.concatenate(
        [(index == rows[s : s + 1]).astype(F32).astype(BF16) for s in range(rows.shape[0])], axis=1
    )


def spread_weights(rows, weights, count, shift):
    index = lax.broadcasted_iota(jnp.int32, (count, NF), 0) + shift
    return jnp.concatenate(
        [
            jnp.where(index == rows[s : s + 1], weights[s : s + 1], 0.0).astype(BF16)
            for s in range(rows.shape[0])
        ],
        axis=1,
    )


def spread_order(core):
    left = [step + (core,) for step in itertools.product(range(4), range(4), range(4))]
    ways = {0: (0.0, 0.0), 1: (1.0, 0.0), 2: (1.0, 1.0), 3: (0.0, 1.0)}

    def links(step):
        return np.array([way for axis in step[:3] for way in ways[axis]])

    used, order = np.zeros(6), []
    while left:
        step = min(left, key=lambda t: (np.max(used + links(t)), -np.sum(links(t)), t))
        left.remove(step)
        used = used + links(step)
        order.append(step)
    return order


def exchange_kernel(
    blks,
    subs,
    syn_hbm,
    obs_hbm,
    table_hbm,
    first_hbm,
    second_hbm,
    mask_hbm,
    weight_hbm,
    owner_hbm,
    element_hbm,
    summed,
    traces,
    table,
    first,
    second,
    mask,
    weight,
    owner,
    element,
    spec,
    halo,
    list_out,
    list_over,
    lists,
    lists_prev,
    labels,
    outgoing,
    received,
    load_sems,
    list_send,
    list_recv,
    over_send,
    over_recv,
    halo_send,
    halo_recv,
    joined,
    y_send,
    y_recv,
    z_send,
    z_recv,
    all_send,
    all_recv,
):
    devices = blks * subs
    blk, sub = lax.axis_index("blk"), lax.axis_index("sub")
    me = blk * subs + sub
    rows = spec.shape[1]
    blocks = first.shape[0]
    def around(at, step, size):
        there = at + step
        return jnp.where(there >= size, there - size, there)

    subs_there = [around(sub, step, subs) for step in range(1, subs)]
    blks_there = [around(blk, step, blks) for step in range(1, blks)]
    blk_after, blk_before = blks_there[0], blks_there[-1]
    after = (jnp.where(sub == subs - 1, blk_after, blk), subs_there[0])
    before = (jnp.where(sub == 0, blk_before, blk), subs_there[-1])

    pairs = [
        (table_hbm, table),
        (syn_hbm.at[0], traces.at[0, pl.ds(0, rows)]),
        (obs_hbm.at[0], traces.at[0, pl.ds(rows, rows)]),
        (owner_hbm, owner),
        (element_hbm, element),
        (first_hbm, first),
        (second_hbm, second),
        (mask_hbm, mask),
        (weight_hbm, weight),
        (syn_hbm.at[1], traces.at[1, pl.ds(0, rows)]),
        (obs_hbm.at[1], traces.at[1, pl.ds(rows, rows)]),
        (syn_hbm.at[2], traces.at[2, pl.ds(0, rows)]),
        (obs_hbm.at[2], traces.at[2, pl.ds(rows, rows)]),
    ]
    loads = [
        pltpu.make_async_copy(src, dst, load_sems.at[i]) for i, (src, dst) in enumerate(pairs)
    ]
    for load in loads:
        load.start()

    barrier = pltpu.get_barrier_semaphore()

    def greet(there):
        pl.semaphore_signal(barrier, inc=1, device_id=there, device_id_type=MESH)

    for there in subs_there:
        greet((blk, there))
    for there in blks_there:
        greet((there, sub))

    @pl.when(sub == 0)
    def _():
        for s in range(1, subs):
            greet((blk_before, s))

    @pl.when(sub == subs - 1)
    def _():
        greet((blk_after, 0))

    def transform(c):
        both = dot_plain(traces[c], table[...]).astype(BF16)
        spec[2 * c] = both[:rows]
        spec[2 * c + 1] = both[rows:]

    for i in range(3):
        loads[i].wait()
    transform(0)

    pl.semaphore_wait(barrier, subs + blks - 1)

    def halo_copies(c):
        q = pl.ds(2 * c, 2)
        return [
            pltpu.make_async_remote_copy(
                src_ref=spec.at[q, pl.ds(0, BLOCK)],
                dst_ref=halo.at[q, pl.ds(BLOCK, BLOCK)],
                send_sem=halo_send.at[0, c],
                recv_sem=halo_recv.at[0, c],
                device_id=before,
                device_id_type=MESH,
            ),
            pltpu.make_async_remote_copy(
                src_ref=spec.at[q, pl.ds(rows - BLOCK, BLOCK)],
                dst_ref=halo.at[q, pl.ds(0, BLOCK)],
                send_sem=halo_send.at[1, c],
                recv_sem=halo_recv.at[1, c],
                device_id=after,
                device_id_type=MESH,
            ),
        ]

    halos = [halo_copies(c) for c in range(3)]
    for copy in halos[0]:
        copy.start()

    for i in range(3, 5):
        loads[i].wait()
    lane = lax.broadcasted_iota(jnp.int32, (rows, rows), 1)
    line = lax.broadcasted_iota(jnp.int32, (rows, rows), 0)
    owner_row = owner[...]

    def column(row):
        return jnp.sum(jnp.where(lane == line, row, 0), axis=1, keepdims=True)

    owner_column, element_column = column(owner_row), column(element[...]).astype(F32)
    same = owner_column == owner_row
    rank_column = jnp.sum(jnp.where(same & (lane < line), 1, 0), axis=1, keepdims=True)
    label_rows = []
    for k in range(2):
        chosen = ((owner_column == lane) & (rank_column == k)).astype(F32)
        label_rows.append(
            jnp.sum(chosen * (element_column - rows), axis=0, keepdims=True) + float(rows)
        )

    for i in range(5, 9):
        loads[i].wait()
    base = (blk * blocks + lax.broadcasted_iota(jnp.int32, (blocks, NF), 0)) * BLOCK
    code = ((first[...] - base) * (2 * BLOCK) + (second[...] - base)).astype(F32)
    slot_weight = weight[...] * mask[...].astype(F32)
    zero_row = jnp.zeros((1, NF), F32)
    for s in range(subs):
        lines = [max(2 * s - 1, 0), 2 * s, 2 * s + 1]
        list_out[s] = jnp.concatenate(
            [code[i : i + 1] for i in lines]
            + [slot_weight[i : i + 1] for i in lines]
            + label_rows,
            axis=0,
        )
    list_over[...] = jnp.concatenate(
        [code[blocks - 1 : blocks]]
        + [zero_row] * 2
        + [slot_weight[blocks - 1 : blocks]]
        + [zero_row] * 4,
        axis=0,
    )
    lists[sub] = list_out[sub]

    for there in subs_there:
        pltpu.make_async_remote_copy(
            src_ref=list_out.at[there],
            dst_ref=lists.at[sub],
            send_sem=list_send,
            recv_sem=list_recv,
            device_id=(blk, there),
            device_id_type=MESH,
        ).start()
    over = pltpu.make_async_remote_copy(
        src_ref=list_over,
        dst_ref=lists_prev.at[sub],
        send_sem=over_send,
        recv_sem=over_recv,
        device_id=(blk_after, 0),
        device_id_type=MESH,
    )
    over.start()

    for c in (1, 2):
        loads[7 + 2 * c].wait()
        loads[8 + 2 * c].wait()
        transform(c)
        for copy in halos[c]:
            copy.start()

    for there in subs_there:
        pl.semaphore_signal(joined, inc=1, device_id=(blk, there), device_id_type=MESH)

    rank_row = jnp.sum(jnp.where(same & (line < lane), 1, 0), axis=0, keepdims=True)
    target = owner_row * 4 + rank_row * 2
    slot = lax.broadcasted_iota(jnp.int32, (4 * devices, 2 * rows), 0)
    placement = (slot == jnp.concatenate([target, target + 1], axis=1)).astype(F32).astype(BF16)

    def stations(c):
        return (spec[2 * c], spec[2 * c + 1])

    own = [features(stations(c)) for c in range(3)]

    others = pl.ds(0, subs - 1)
    pltpu.make_async_copy(lists.at[others], lists.at[others], list_recv).wait()

    z, y = lax.div(blk, 4), lax.rem(blk, 4)
    labels[z, y] = jnp.concatenate([lists[:, 6, :], lists[:, 7, :]], axis=0).astype(BF16)
    for step in range(1, 4):
        pltpu.make_async_remote_copy(
            src_ref=labels.at[z, y],
            dst_ref=labels.at[z, y],
            send_sem=y_send,
            recv_sem=y_recv,
            device_id=(z * 4 + around(y, step, 4), sub),
            device_id_type=MESH,
        ).start()

    @pl.when(sub == 0)
    def _():
        pltpu.make_async_copy(lists_prev, lists_prev, over_recv).wait()

    @pl.when(sub != 0)
    def _():
        lists_prev[...] = lists[...]

    def unpacked(ref, k):
        codes = ref[:, k, :].astype(jnp.int32)
        return codes >> 7, codes & 127, ref[:, 3 + k, :]

    first0, second0, weight0 = unpacked(lists_prev, 0)
    first1, second1, weight1 = unpacked(lists, 1)
    first2, second2, weight2 = unpacked(lists, 2)
    to_prev = dot_rows(spread_weights(second0, weight0, BLOCK, BLOCK), spread(first0, rows, 0))
    upper = dot_rows(spread_weights(first1, weight1, BLOCK, 0), spread(second1, rows, 0))
    lower = dot_rows(spread_weights(first2, weight2, BLOCK, 0), spread(second2, rows, 0))
    half = lax.broadcasted_iota(jnp.int32, (BLOCK, rows), 1) >= BLOCK
    inside = jnp.where(half, pltpu.roll(lower, BLOCK, 1), 0.0)
    one_way = jnp.concatenate([upper, inside], axis=0)
    link_own = for_features(one_way + one_way.T)
    link_halo = for_features(jnp.concatenate([to_prev, jnp.where(half, lower, 0.0)], axis=0))
    inner = [dot_plain(link_own, own[c]) for c in range(3)]

    def adjoint(c):
        sums = inner[c] + dot_plain(link_halo, features((halo[2 * c], halo[2 * c + 1])))
        g1r, g1i, g2r, g2i = (sums[:, i * NF : (i + 1) * NF] for i in range(4))
        x, o = stations(c)
        xr, xi = x[:, :NF].astype(F32), x[:, NF:].astype(F32)
        dr, di = xr - o[:, :NF].astype(F32), xi - o[:, NF:].astype(F32)
        real = (xr * g1r - xi * g1i) + (dr * g2r - di * g2i)
        imag = (xr * g1i + xi * g1r) + (dr * g2i + di * g2r)
        return jnp.concatenate([real, imag], axis=0).astype(BF16)

    for together in ((0, 1), (2,)):
        for c in together:
            for copy in halos[c]:
                copy.wait_recv()
        placed = dot_plain(placement, jnp.concatenate([adjoint(c) for c in together], axis=1))
        for i, c in enumerate(together):
            outgoing[:, c] = (
                placed[:, i * NF : (i + 1) * NF].astype(BF16).reshape(devices, 4, NF)
            )

    pl.semaphore_wait(joined, subs - 1)

    core = lax.rem(sub, 2)

    def turns(at, size):
        up = [around(at, step, size) for step in range(1, size)]
        return [at] + [jnp.where(core == 0, up[i], up[-1 - i]) for i in range(size - 1)]

    chip = lax.div(me, 2)
    z_to, y_to, x_to = turns(z, 4), turns(y, 4), turns(lax.div(sub, 2), 4)
    core_to = [core, 1 - core]
    received[core, chip] = outgoing[me]

    def deliver(step):
        dz, dy, dx, other = step
        blk_to, sub_to = z_to[dz] * 4 + y_to[dy], x_to[dx] * 2 + core_to[other]
        pltpu.make_async_remote_copy(
            src_ref=outgoing.at[blk_to * subs + sub_to],
            dst_ref=received.at[core, chip],
            send_sem=all_send,
            recv_sem=all_recv.at[other],
            device_id=(blk_to, sub_to),
            device_id_type=MESH,
        ).start()

    order = spread_order(1) + spread_order(0)[1:]
    for step in order[:48]:
        deliver(step)
    some = pl.ds(0, 3)
    pltpu.make_async_copy(labels.at[0, some], labels.at[0, some], y_recv).wait()
    for step in range(1, 4):
        pltpu.make_async_remote_copy(
            src_ref=labels.at[z],
            dst_ref=labels.at[z],
            send_sem=z_send,
            recv_sem=z_recv,
            device_id=(around(z, step, 4) * 4 + y, sub),
            device_id_type=MESH,
        ).start()

    for step in order[48:]:
        deliver(step)

    pltpu.make_async_copy(labels.at[some], labels.at[some], z_recv).wait()
    by_owner = labels[...].reshape(2 * devices, NF)
    arrived = lax.broadcasted_iota(jnp.int32, (2 * devices, 2 * devices), 1)
    held = lax.broadcasted_iota(jnp.int32, (2 * devices, 2 * devices), 0)
    sub_bits = subs.bit_length() - 1
    wanted = (
        ((arrived >> (sub_bits + 1)) << (sub_bits + 1))
        + (((arrived >> 1) & 1) << sub_bits)
        + (((arrived >> 2) & (subs // 2 - 1)) << 1)
    )
    owner_line = lax.broadcasted_iota(jnp.int32, (rows, 2 * devices), 0)

    def collector(source_core):
        repeated = lax.dot_general(
            by_owner,
            (held == wanted + source_core).astype(F32).astype(BF16),
            (((0,), (0,)), ((), ())),
            preferred_element_type=F32,
        )
        label = jnp.sum(jnp.where(owner_line == me, repeated, 0.0), axis=0, keepdims=True)
        return jnp.concatenate(
            [
                ((label == owner_line.astype(F32)) & ((arrived[:rows] & 1) == i)).astype(F32)
                for i in range(2)
            ],
            axis=0,
        ).astype(BF16)

    collect_other, collect_same = collector(1 - core), collector(core)

    def sums(collect, source_core):
        values = [received[source_core, :, c].reshape(2 * devices, NF) for c in range(3)]
        return dot_plain(collect, jnp.concatenate(values, axis=1))

    pltpu.make_async_copy(received.at[0], received.at[0], all_recv.at[1]).wait()
    first_sums = sums(collect_other, 1 - core)
    most = pl.ds(0, devices // 2 - 1)
    pltpu.make_async_copy(received.at[0, most], received.at[0, most], all_recv.at[0]).wait()
    total = (first_sums + sums(collect_same, core)).astype(BF16)
    for c in range(3):
        summed[c * rows : (c + 1) * rows, :NF] = total[:rows, c * NF : (c + 1) * NF]
        summed[c * rows : (c + 1) * rows, NF:] = total[rows:, c * NF : (c + 1) * NF]

    for c in range(3):
        for copy in halos[c]:
            copy.wait_send()
    pltpu.make_async_copy(list_out.at[others], list_out.at[others], list_send).wait()
    over.wait_send()
    pltpu.make_async_copy(labels.at[0, some], labels.at[0, some], y_send).wait()
    pltpu.make_async_copy(labels.at[some], labels.at[some], z_send).wait()
    most = pl.ds(0, devices - 1)
    pltpu.make_async_copy(outgoing.at[most], outgoing.at[most], all_send).wait()


def exchange(blks, subs, syn, obs, table, first, second, mask, weight, owner, element):
    devices = blks * subs
    samples, rows = syn.shape[2], syn.shape[1]
    in_hbm = pl.BlockSpec(memory_space=pltpu.HBM)
    dma = pltpu.SemaphoreType.DMA
    return pl.pallas_call(
        functools.partial(exchange_kernel, blks, subs),
        out_shape=pltpu.VMEM((3 * rows, 2 * NF), BF16),
        in_specs=[in_hbm] * 9,
        out_specs=pl.BlockSpec(memory_space=pltpu.VMEM),
        scratch_shapes=[
            pltpu.VMEM((3, 2 * rows, samples), BF16),
            pltpu.VMEM(table.shape, BF16),
            pltpu.VMEM(first.shape, jnp.int32),
            pltpu.VMEM(second.shape, jnp.int32),
            pltpu.VMEM(mask.shape, jnp.int32),
            pltpu.VMEM(weight.shape, F32),
            pltpu.VMEM(owner.shape, jnp.int32),
            pltpu.VMEM(element.shape, jnp.int32),
            pltpu.VMEM((6, rows, 2 * NF), BF16),
            pltpu.VMEM((6, 2 * BLOCK, 2 * NF), BF16),
            pltpu.VMEM((subs, 8, NF), F32),
            pltpu.VMEM((8, NF), F32),
            pltpu.VMEM((subs, 8, NF), F32),
            pltpu.VMEM((subs, 8, NF), F32),
            pltpu.VMEM((4, blks // 4, 2 * subs, NF), BF16),
            pltpu.VMEM((devices, 3, 4, NF), BF16),
            pltpu.VMEM((2, devices // 2, 3, 4, NF), BF16),
            dma((13,)),
            dma,
            dma,
            dma,
            dma,
            dma((2, 3)),
            dma((2, 3)),
            pltpu.SemaphoreType.REGULAR,
            dma,
            dma,
            dma,
            dma,
            dma,
            dma((2,)),
        ],
        compiler_params=pltpu.CompilerParams(
            collective_id=0, has_side_effects=True, vmem_limit_bytes=60 * 2**20
        ),
        cost_estimate=pl.CostEstimate(
            flops=2 * 10**9, bytes_accessed=3 * 10**6, transcendentals=0
        ),
        name="exchange",
    )(syn, obs, table, first, second, mask, weight, owner, element)


def finish_kernel(summed, table, out, result, sems):
    samples = result.shape[1]
    chunk = samples // sems.shape[0]
    copies = []
    for n in range(sems.shape[0]):
        columns = pl.ds(n * chunk, chunk)
        result[:, columns] = dot_plain(summed[...], table[:, columns])
        copies.append(
            pltpu.make_async_copy(result.at[:, columns], out.at[:, columns], sems.at[n])
        )
        copies[-1].start()
    for copy in copies:
        copy.wait()


def finish(summed, table):
    count, samples = summed.shape[0], table.shape[1]
    in_vmem = pl.BlockSpec(memory_space=pltpu.VMEM)
    out = pl.pallas_call(
        finish_kernel,
        out_shape=jax.ShapeDtypeStruct((count, samples), F32),
        in_specs=[in_vmem] * 2,
        out_specs=pl.BlockSpec(memory_space=pl.ANY),
        scratch_shapes=[
            pltpu.VMEM((count, samples), F32),
            pltpu.SemaphoreType.DMA((4,)),
        ],
        compiler_params=pltpu.CompilerParams(vmem_limit_bytes=40 * 2**20),
        cost_estimate=pl.CostEstimate(
            flops=7 * 10**8, bytes_accessed=3 * 10**6, transcendentals=0
        ),
        name="finish",
    )(summed, table)
    return out.reshape(3, count // 3, samples)


def on_device(
    blks,
    subs,
    synthetic,
    observed,
    pair_first,
    pair_second,
    pair_mask,
    pair_weight,
    station_owner,
    station_element,
):
    rows, _, samples = synthetic.shape
    forward, inverse = dft_tables(samples, NF)
    summed = exchange(
        blks,
        subs,
        jnp.transpose(synthetic, (1, 0, 2)),
        jnp.transpose(observed, (1, 0, 2)),
        jnp.asarray(forward),
        pair_first,
        pair_second,
        pair_mask,
        pair_weight,
        station_owner.reshape(1, rows),
        station_element.reshape(1, rows),
    )
    out = finish(summed, jnp.asarray(inverse))
    return jnp.transpose(out, (1, 0, 2))


def solution(mesh):
    blks, subs = mesh.shape["blk"], mesh.shape["sub"]
    return jax.shard_map(
        functools.partial(on_device, blks, subs),
        mesh=mesh,
        in_specs=(
            P(("blk", "sub"), None, None),
            P(("blk", "sub"), None, None),
            P("blk", "sub"),
            P("blk", "sub"),
            P("blk", "sub"),
            P("blk", "sub"),
            P(("blk", "sub"), None),
            P(("blk", "sub")),
        ),
        out_specs=P(("blk", "sub"), None, None),
        check_vma=False,
    )
```

```python
import functools
import itertools
import math

import jax
import jax.numpy as jnp
import numpy as np
from jax import lax
from jax.experimental import pallas as pl
from jax.experimental.pallas import tpu as pltpu
from jax.sharding import PartitionSpec as P

MESH = pl.DeviceIdType.MESH
NF = 128
BLOCK = 64
F32 = jnp.float32
BF16 = jnp.bfloat16


def dft_tables(samples, freqs):
    phase = (np.arange(samples)[:, None] * np.arange(freqs)[None, :]) % samples
    angles = phase.astype(np.float64) * (2.0 * math.pi / samples)
    scale = 1.0 / math.sqrt(samples)
    cosine, sine = np.cos(angles) * scale, np.sin(angles) * scale
    forward = np.concatenate([cosine, -sine], axis=1).astype(np.float32)
    doubled = np.where(np.arange(freqs) == 0, 1.0, 2.0)[:, None]
    inverse = np.concatenate([cosine.T * doubled, -sine.T * doubled], axis=0)
    return forward.astype(jnp.bfloat16), inverse.astype(np.float32).astype(jnp.bfloat16)


def in_two(x):
    high = x.astype(BF16)
    return high, (x - high.astype(F32)).astype(BF16)


def dot_rows(a, b):
    return lax.dot_general(a, b, (((1,), (1,)), ((), ())), preferred_element_type=F32)


def dot_plain(a, b):
    return jnp.dot(a, b, preferred_element_type=F32)


def features(pair):
    xr, xi = pair[0][:, :NF].astype(F32), pair[0][:, NF:].astype(F32)
    o_r, o_i = pair[1][:, :NF].astype(F32), pair[1][:, NF:].astype(F32)
    dr, di = xr - o_r, xi - o_i
    parts = [dr * xr + di * xi, dr * xi - di * xr, o_r * xr + o_i * xi, o_r * xi - o_i * xr]
    both = [in_two(p) for p in parts]
    return jnp.concatenate(
        [jnp.concatenate([b[i] for b in both], axis=1) for i in range(2)], axis=0
    )


def for_features(links):
    return jnp.concatenate([links.astype(BF16)] * 2, axis=1)


def spread(rows, count, shift):
    index = lax.broadcasted_iota(jnp.int32, (count, NF), 0) + shift
    return jnp.concatenate(
        [(index == rows[s : s + 1]).astype(F32).astype(BF16) for s in range(rows.shape[0])], axis=1
    )


def spread_weights(rows, weights, count, shift):
    index = lax.broadcasted_iota(jnp.int32, (count, NF), 0) + shift
    return jnp.concatenate(
        [
            jnp.where(index == rows[s : s + 1], weights[s : s + 1], 0.0).astype(BF16)
            for s in range(rows.shape[0])
        ],
        axis=1,
    )


def spread_order():
    left = list(itertools.product(range(4), range(4), range(2)))[1:]
    ways = {0: (0.0, 0.0), 1: (1.0, 0.0), 2: (1.0, 1.0), 3: (0.0, 1.0)}

    def links(step):
        return np.array([way for axis in step[:2] for way in ways[axis]])

    used, order = np.zeros(4), []
    while left:
        step = min(left, key=lambda t: (np.max(used + links(t)), -np.sum(links(t)), t))
        left.remove(step)
        used = used + links(step)
        order.append(step)
    return order


def exchange_kernel(
    blks,
    subs,
    syn_hbm,
    obs_hbm,
    table_hbm,
    first_hbm,
    second_hbm,
    mask_hbm,
    weight_hbm,
    owner_hbm,
    element_hbm,
    summed,
    traces,
    table,
    first,
    second,
    mask,
    weight,
    owner,
    element,
    spec,
    halo,
    list_out,
    list_over,
    lists,
    lists_prev,
    labels,
    outgoing,
    received,
    load_sems,
    list_send,
    list_recv,
    over_send,
    over_recv,
    halo_send,
    halo_recv,
    entered,
    joined,
    y_send,
    y_recv,
    z_send,
    z_recv,
    all_send,
    all_recv,
):
    devices = blks * subs
    blk, sub = lax.axis_index("blk"), lax.axis_index("sub")
    me = blk * subs + sub
    rows = spec.shape[1]
    blocks = first.shape[0]
    def around(at, step, size):
        there = at + step
        return jnp.where(there >= size, there - size, there)

    subs_there = [around(sub, step, subs) for step in range(1, subs)]
    blks_there = [around(blk, step, blks) for step in range(1, blks)]
    blk_after, blk_before = blks_there[0], blks_there[-1]
    after = (jnp.where(sub == subs - 1, blk_after, blk), subs_there[0])
    before = (jnp.where(sub == 0, blk_before, blk), subs_there[-1])

    pairs = [
        (table_hbm, table),
        (syn_hbm.at[0], traces.at[0, pl.ds(0, rows)]),
        (obs_hbm.at[0], traces.at[0, pl.ds(rows, rows)]),
        (owner_hbm, owner),
        (element_hbm, element),
        (first_hbm, first),
        (second_hbm, second),
        (mask_hbm, mask),
        (weight_hbm, weight),
        (syn_hbm.at[1], traces.at[1, pl.ds(0, rows)]),
        (obs_hbm.at[1], traces.at[1, pl.ds(rows, rows)]),
        (syn_hbm.at[2], traces.at[2, pl.ds(0, rows)]),
        (obs_hbm.at[2], traces.at[2, pl.ds(rows, rows)]),
    ]
    loads = [
        pltpu.make_async_copy(src, dst, load_sems.at[i]) for i, (src, dst) in enumerate(pairs)
    ]
    for load in loads:
        load.start()

    z, y = lax.div(blk, 4), lax.rem(blk, 4)
    has_before, has_after = me > 0, me < devices - 1
    row_before, row_after = blk > 0, blk < blks - 1
    barrier = pltpu.get_barrier_semaphore()

    def greet(there):
        pl.semaphore_signal(barrier, inc=1, device_id=there, device_id_type=MESH)

    def greet_column(there, carry):
        greet((there, sub))
        return carry

    for there in subs_there:
        greet((blk, there))
    lax.fori_loop(blk + 1, blks, greet_column, 0)

    @pl.when((sub == 0) & row_before)
    def _():
        for s in range(subs):
            greet((blk_before, s))

    @pl.when((sub == subs - 1) & row_after)
    def _():
        greet((blk_after, 0))

    for i in range(3):
        pl.semaphore_signal(entered.at[i], inc=1)
    greetings = (
        (subs - 1)
        + jnp.where(row_after, 1, 0)
        + jnp.where((sub == 0) & row_before, 1, 0)
        + blk
    )

    def transform(c):
        both = dot_plain(traces[c], table[...]).astype(BF16)
        spec[2 * c] = both[:rows]
        spec[2 * c + 1] = both[rows:]

    for i in range(3):
        loads[i].wait()
    transform(0)

    pl.semaphore_wait(barrier, greetings)

    def halo_copies(c):
        q = pl.ds(2 * c, 2)
        return [
            pltpu.make_async_remote_copy(
                src_ref=spec.at[q, pl.ds(0, BLOCK)],
                dst_ref=halo.at[q, pl.ds(BLOCK, BLOCK)],
                send_sem=halo_send.at[0, c],
                recv_sem=halo_recv.at[0, c],
                device_id=before,
                device_id_type=MESH,
            ),
            pltpu.make_async_remote_copy(
                src_ref=spec.at[q, pl.ds(rows - BLOCK, BLOCK)],
                dst_ref=halo.at[q, pl.ds(0, BLOCK)],
                send_sem=halo_send.at[1, c],
                recv_sem=halo_recv.at[1, c],
                device_id=after,
                device_id_type=MESH,
            ),
        ]

    halos = [halo_copies(c) for c in range(3)]

    def start_halos(c):
        @pl.when(has_before)
        def _():
            halos[c][0].start()

        @pl.when(has_after)
        def _():
            halos[c][1].start()

    start_halos(0)

    for i in range(3, 5):
        loads[i].wait()
    lane = lax.broadcasted_iota(jnp.int32, (rows, rows), 1)
    line = lax.broadcasted_iota(jnp.int32, (rows, rows), 0)
    owner_row = owner[...]

    def column(row):
        return jnp.sum(jnp.where(lane == line, row, 0), axis=1, keepdims=True)

    owner_column, element_column = column(owner_row), column(element[...]).astype(F32)
    same = owner_column == owner_row
    rank_column = jnp.sum(jnp.where(same & (lane < line), 1, 0), axis=1, keepdims=True)
    label_rows = []
    for k in range(2):
        chosen = ((owner_column == lane) & (rank_column == k)).astype(F32)
        label_rows.append(
            jnp.sum(chosen * (element_column - rows), axis=0, keepdims=True) + float(rows)
        )

    for i in range(5, 9):
        loads[i].wait()
    base = (blk * blocks + lax.broadcasted_iota(jnp.int32, (blocks, NF), 0)) * BLOCK
    code = ((first[...] - base) * (2 * BLOCK) + (second[...] - base)).astype(F32)
    slot_weight = weight[...] * mask[...].astype(F32)
    zero_row = jnp.zeros((1, NF), F32)
    for s in range(subs):
        lines = [max(2 * s - 1, 0), 2 * s, 2 * s + 1]
        list_out[s] = jnp.concatenate(
            [code[i : i + 1] for i in lines]
            + [slot_weight[i : i + 1] for i in lines]
            + label_rows,
            axis=0,
        )
    list_over[...] = jnp.concatenate(
        [code[blocks - 1 : blocks]]
        + [zero_row] * 2
        + [slot_weight[blocks - 1 : blocks]]
        + [zero_row] * 4,
        axis=0,
    )
    lists[sub] = list_out[sub]

    for there in subs_there:
        pltpu.make_async_remote_copy(
            src_ref=list_out.at[there],
            dst_ref=lists.at[sub],
            send_sem=list_send,
            recv_sem=list_recv,
            device_id=(blk, there),
            device_id_type=MESH,
        ).start()
    over = pltpu.make_async_remote_copy(
        src_ref=list_over,
        dst_ref=lists_prev.at[sub],
        send_sem=over_send,
        recv_sem=over_recv,
        device_id=(blk_after, 0),
        device_id_type=MESH,
    )

    @pl.when(row_after)
    def _():
        over.start()


    for c in (1, 2):
        loads[7 + 2 * c].wait()
        loads[8 + 2 * c].wait()
        transform(c)
        start_halos(c)

    @pl.when(jnp.logical_not(has_before))
    def _():
        halo[:, :BLOCK] = jnp.zeros((6, BLOCK, 2 * NF), BF16)

    @pl.when(jnp.logical_not(has_after))
    def _():
        halo[:, BLOCK:] = jnp.zeros((6, BLOCK, 2 * NF), BF16)

    def answer(there, carry):
        kind = jnp.where(lax.div(there, 4) == z, 0, jnp.where(z == 1, 1, 2))
        pl.semaphore_signal(
            entered.at[kind], inc=1, device_id=(there, sub), device_id_type=MESH
        )
        return carry

    lax.fori_loop(0, blk, answer, 0)

    def tell_row(which):
        for there in subs_there:
            pl.semaphore_signal(
                joined.at[which], inc=1, device_id=(blk, there), device_id_type=MESH
            )

    @pl.when(z >= 2)
    def _():
        tell_row(0)

    rank_row = jnp.sum(jnp.where(same & (line < lane), 1, 0), axis=0, keepdims=True)
    target = owner_row * 4 + rank_row * 2
    slot = lax.broadcasted_iota(jnp.int32, (4 * devices, 2 * rows), 0)
    placement = (slot == jnp.concatenate([target, target + 1], axis=1)).astype(F32).astype(BF16)

    def stations(c):
        return (spec[2 * c], spec[2 * c + 1])

    own = [features(stations(c)) for c in range(3)]

    others = pl.ds(0, subs - 1)
    pltpu.make_async_copy(lists.at[others], lists.at[others], list_recv).wait()

    @pl.when((sub == 0) & row_before)
    def _():
        pltpu.make_async_copy(lists_prev, lists_prev, over_recv).wait()

    @pl.when((sub == 0) & jnp.logical_not(row_before))
    def _():
        lists_prev[...] = jnp.zeros(lists_prev.shape, F32)

    @pl.when(sub != 0)
    def _():
        lists_prev[...] = lists[...]

    def unpacked(ref, k):
        codes = ref[:, k, :].astype(jnp.int32)
        return codes >> 7, codes & 127, ref[:, 3 + k, :]

    first0, second0, weight0 = unpacked(lists_prev, 0)
    first1, second1, weight1 = unpacked(lists, 1)
    first2, second2, weight2 = unpacked(lists, 2)
    to_prev = dot_rows(spread_weights(second0, weight0, BLOCK, BLOCK), spread(first0, rows, 0))
    upper = dot_rows(spread_weights(first1, weight1, BLOCK, 0), spread(second1, rows, 0))
    lower = dot_rows(spread_weights(first2, weight2, BLOCK, 0), spread(second2, rows, 0))
    half = lax.broadcasted_iota(jnp.int32, (BLOCK, rows), 1) >= BLOCK
    inside = jnp.where(half, pltpu.roll(lower, BLOCK, 1), 0.0)
    one_way = jnp.concatenate([upper, inside], axis=0)
    link_own = for_features(one_way + one_way.T)
    link_halo = for_features(jnp.concatenate([to_prev, jnp.where(half, lower, 0.0)], axis=0))
    inner = [dot_plain(link_own, own[c]) for c in range(3)]

    def adjoint(c):
        sums = inner[c] + dot_plain(link_halo, features((halo[2 * c], halo[2 * c + 1])))
        g1r, g1i, g2r, g2i = (sums[:, i * NF : (i + 1) * NF] for i in range(4))
        x, o = stations(c)
        xr, xi = x[:, :NF].astype(F32), x[:, NF:].astype(F32)
        dr, di = xr - o[:, :NF].astype(F32), xi - o[:, NF:].astype(F32)
        real = (xr * g1r - xi * g1i) + (dr * g2r - di * g2i)
        imag = (xr * g1i + xi * g1r) + (dr * g2i + di * g2r)
        return jnp.concatenate([real, imag], axis=0).astype(BF16)

    def handle(together):
        for c in together:

            @pl.when(has_after)
            def _():
                halos[c][0].wait_recv()

            @pl.when(has_before)
            def _():
                halos[c][1].wait_recv()

        placed = dot_plain(placement, jnp.concatenate([adjoint(c) for c in together], axis=1))
        for i, c in enumerate(together):
            outgoing[:, c] = (
                placed[:, i * NF : (i + 1) * NF].astype(BF16).reshape(devices, 4, NF)
            )

    handle((0, 1))

    pl.semaphore_wait(entered.at[0], 4 - y)
    labels[z, y] = jnp.concatenate([lists[:, 6, :], lists[:, 7, :]], axis=0).astype(BF16)
    for step in range(1, 4):
        pltpu.make_async_remote_copy(
            src_ref=labels.at[z, y],
            dst_ref=labels.at[z, y],
            send_sem=y_send,
            recv_sem=y_recv,
            device_id=(z * 4 + around(y, step, 4), sub),
            device_id_type=MESH,
        ).start()

    pl.semaphore_wait(entered.at[1], 1 + jnp.where(z == 0, 4, 0))

    @pl.when(z < 2)
    def _():
        tell_row(0)

    handle((2,))

    pl.semaphore_wait(entered.at[2], 1 + jnp.where(z < 2, 8, jnp.where(z == 2, 4, 0)))
    tell_row(1)

    def turns(at, size):
        return [at] + [around(at, step, size) for step in range(1, size)]

    core, chip = lax.rem(sub, 2), lax.div(me, 2)
    y_to, x_to = turns(y, 4), turns(lax.div(sub, 2), 4)
    core_to = [core, 1 - core]
    received[core, chip] = outgoing[me]

    def deliver(plane, step):
        dy, dx, other = step
        blk_to, sub_to = plane * 4 + y_to[dy], x_to[dx] * 2 + core_to[other]
        pltpu.make_async_remote_copy(
            src_ref=outgoing.at[blk_to * subs + sub_to],
            dst_ref=received.at[core, chip],
            send_sem=all_send,
            recv_sem=all_recv.at[other],
            device_id=(blk_to, sub_to),
            device_id_type=MESH,
        ).start()

    def deliver_plane(plane):
        for step in spread_order():
            deliver(plane, step)

        @pl.when(z != plane)
        def _():
            deliver(plane, (0, 0, 0))

    pl.semaphore_wait(joined.at[0], subs - 1)
    deliver_plane(0)
    some = pl.ds(0, 3)
    pltpu.make_async_copy(labels.at[0, some], labels.at[0, some], y_recv).wait()
    for step in range(1, 4):
        pltpu.make_async_remote_copy(
            src_ref=labels.at[z],
            dst_ref=labels.at[z],
            send_sem=z_send,
            recv_sem=z_recv,
            device_id=(around(z, step, 4) * 4 + y, sub),
            device_id_type=MESH,
        ).start()

    deliver_plane(1)
    pl.semaphore_wait(joined.at[1], subs - 1)
    deliver_plane(2)
    deliver_plane(3)

    pltpu.make_async_copy(labels.at[some], labels.at[some], z_recv).wait()
    by_owner = labels[...].reshape(2 * devices, NF)
    arrived = lax.broadcasted_iota(jnp.int32, (2 * devices, 2 * devices), 1)
    held = lax.broadcasted_iota(jnp.int32, (2 * devices, 2 * devices), 0)
    sub_bits = subs.bit_length() - 1
    wanted = (
        ((arrived >> (sub_bits + 1)) << (sub_bits + 1))
        + (((arrived >> 1) & 1) << sub_bits)
        + (((arrived >> 2) & (subs // 2 - 1)) << 1)
    )
    owner_line = lax.broadcasted_iota(jnp.int32, (rows, 2 * devices), 0)

    def collector(source_core):
        repeated = lax.dot_general(
            by_owner,
            (held == wanted + source_core).astype(F32).astype(BF16),
            (((0,), (0,)), ((), ())),
            preferred_element_type=F32,
        )
        label = jnp.sum(jnp.where(owner_line == me, repeated, 0.0), axis=0, keepdims=True)
        return jnp.concatenate(
            [
                ((label == owner_line.astype(F32)) & ((arrived[:rows] & 1) == i)).astype(F32)
                for i in range(2)
            ],
            axis=0,
        ).astype(BF16)

    collect_other, collect_same = collector(1 - core), collector(core)

    def sums(collect, source_core):
        values = [received[source_core, :, c].reshape(2 * devices, NF) for c in range(3)]
        return dot_plain(collect, jnp.concatenate(values, axis=1))

    pltpu.make_async_copy(received.at[0], received.at[0], all_recv.at[1]).wait()
    first_sums = sums(collect_other, 1 - core)
    most = pl.ds(0, devices // 2 - 1)
    pltpu.make_async_copy(received.at[0, most], received.at[0, most], all_recv.at[0]).wait()
    total = (first_sums + sums(collect_same, core)).astype(BF16)
    for c in range(3):
        summed[c * rows : (c + 1) * rows, :NF] = total[:rows, c * NF : (c + 1) * NF]
        summed[c * rows : (c + 1) * rows, NF:] = total[rows:, c * NF : (c + 1) * NF]

    for c in range(3):

        @pl.when(has_before)
        def _():
            halos[c][0].wait_send()

        @pl.when(has_after)
        def _():
            halos[c][1].wait_send()

    pltpu.make_async_copy(list_out.at[others], list_out.at[others], list_send).wait()

    @pl.when(row_after)
    def _():
        over.wait_send()

    pltpu.make_async_copy(labels.at[0, some], labels.at[0, some], y_send).wait()
    pltpu.make_async_copy(labels.at[some], labels.at[some], z_send).wait()
    most = pl.ds(0, devices - 1)
    pltpu.make_async_copy(outgoing.at[most], outgoing.at[most], all_send).wait()


def exchange(blks, subs, syn, obs, table, first, second, mask, weight, owner, element):
    devices = blks * subs
    samples, rows = syn.shape[2], syn.shape[1]
    in_hbm = pl.BlockSpec(memory_space=pltpu.HBM)
    dma = pltpu.SemaphoreType.DMA
    return pl.pallas_call(
        functools.partial(exchange_kernel, blks, subs),
        out_shape=pltpu.VMEM((3 * rows, 2 * NF), BF16),
        in_specs=[in_hbm] * 9,
        out_specs=pl.BlockSpec(memory_space=pltpu.VMEM),
        scratch_shapes=[
            pltpu.VMEM((3, 2 * rows, samples), BF16),
            pltpu.VMEM(table.shape, BF16),
            pltpu.VMEM(first.shape, jnp.int32),
            pltpu.VMEM(second.shape, jnp.int32),
            pltpu.VMEM(mask.shape, jnp.int32),
            pltpu.VMEM(weight.shape, F32),
            pltpu.VMEM(owner.shape, jnp.int32),
            pltpu.VMEM(element.shape, jnp.int32),
            pltpu.VMEM((6, rows, 2 * NF), BF16),
            pltpu.VMEM((6, 2 * BLOCK, 2 * NF), BF16),
            pltpu.VMEM((subs, 8, NF), F32),
            pltpu.VMEM((8, NF), F32),
            pltpu.VMEM((subs, 8, NF), F32),
            pltpu.VMEM((subs, 8, NF), F32),
            pltpu.VMEM((4, blks // 4, 2 * subs, NF), BF16),
            pltpu.VMEM((devices, 3, 4, NF), BF16),
            pltpu.VMEM((2, devices // 2, 3, 4, NF), BF16),
            dma((13,)),
            dma,
            dma,
            dma,
            dma,
            dma((2, 3)),
            dma((2, 3)),
            pltpu.SemaphoreType.REGULAR((3,)),
            pltpu.SemaphoreType.REGULAR((2,)),
            dma,
            dma,
            dma,
            dma,
            dma,
            dma((2,)),
        ],
        compiler_params=pltpu.CompilerParams(
            collective_id=0, has_side_effects=True, vmem_limit_bytes=60 * 2**20
        ),
        cost_estimate=pl.CostEstimate(
            flops=2 * 10**9, bytes_accessed=3 * 10**6, transcendentals=0
        ),
        name="exchange",
    )(syn, obs, table, first, second, mask, weight, owner, element)


def finish_kernel(summed, table, out, result, sems):
    samples = result.shape[1]
    chunk = samples // sems.shape[0]
    copies = []
    for n in range(sems.shape[0]):
        columns = pl.ds(n * chunk, chunk)
        result[:, columns] = dot_plain(summed[...], table[:, columns])
        copies.append(
            pltpu.make_async_copy(result.at[:, columns], out.at[:, columns], sems.at[n])
        )
        copies[-1].start()
    for copy in copies:
        copy.wait()


def finish(summed, table):
    count, samples = summed.shape[0], table.shape[1]
    in_vmem = pl.BlockSpec(memory_space=pltpu.VMEM)
    out = pl.pallas_call(
        finish_kernel,
        out_shape=jax.ShapeDtypeStruct((count, samples), F32),
        in_specs=[in_vmem] * 2,
        out_specs=pl.BlockSpec(memory_space=pl.ANY),
        scratch_shapes=[
            pltpu.VMEM((count, samples), F32),
            pltpu.SemaphoreType.DMA((4,)),
        ],
        compiler_params=pltpu.CompilerParams(vmem_limit_bytes=40 * 2**20),
        cost_estimate=pl.CostEstimate(
            flops=7 * 10**8, bytes_accessed=3 * 10**6, transcendentals=0
        ),
        name="finish",
    )(summed, table)
    return out.reshape(3, count // 3, samples)


def on_device(
    blks,
    subs,
    synthetic,
    observed,
    pair_first,
    pair_second,
    pair_mask,
    pair_weight,
    station_owner,
    station_element,
):
    rows, _, samples = synthetic.shape
    forward, inverse = dft_tables(samples, NF)
    summed = exchange(
        blks,
        subs,
        jnp.transpose(synthetic, (1, 0, 2)),
        jnp.transpose(observed, (1, 0, 2)),
        jnp.asarray(forward),
        pair_first,
        pair_second,
        pair_mask,
        pair_weight,
        station_owner.reshape(1, rows),
        station_element.reshape(1, rows),
    )
    out = finish(summed, jnp.asarray(inverse))
    return jnp.transpose(out, (1, 0, 2))


def solution(mesh):
    blks, subs = mesh.shape["blk"], mesh.shape["sub"]
    return jax.shard_map(
        functools.partial(on_device, blks, subs),
        mesh=mesh,
        in_specs=(
            P(("blk", "sub"), None, None),
            P(("blk", "sub"), None, None),
            P("blk", "sub"),
            P("blk", "sub"),
            P("blk", "sub"),
            P("blk", "sub"),
            P(("blk", "sub"), None),
            P(("blk", "sub")),
        ),
        out_specs=P(("blk", "sub"), None, None),
        check_vma=False,
    )
```

```python
import functools
import itertools
import math

import jax
import jax.numpy as jnp
import numpy as np
from jax import lax
from jax.experimental import pallas as pl
from jax.experimental.pallas import tpu as pltpu
from jax.sharding import PartitionSpec as P

MESH = pl.DeviceIdType.MESH
NF = 128
BLOCK = 64
F32 = jnp.float32
BF16 = jnp.bfloat16


def dft_tables(samples, freqs):
    phase = (np.arange(samples)[:, None] * np.arange(freqs)[None, :]) % samples
    angles = phase.astype(np.float64) * (2.0 * math.pi / samples)
    scale = 1.0 / math.sqrt(samples)
    cosine, sine = np.cos(angles) * scale, np.sin(angles) * scale
    forward = np.concatenate([cosine, -sine], axis=1).astype(np.float32)
    doubled = np.where(np.arange(freqs) == 0, 1.0, 2.0)[:, None]
    inverse = np.concatenate([cosine.T * doubled, -sine.T * doubled], axis=0)
    return forward.astype(jnp.bfloat16), inverse.astype(np.float32).astype(jnp.bfloat16)


def in_two(x):
    high = x.astype(BF16)
    return high, (x - high.astype(F32)).astype(BF16)


def dot_rows(a, b):
    return lax.dot_general(a, b, (((1,), (1,)), ((), ())), preferred_element_type=F32)


def dot_plain(a, b):
    return jnp.dot(a, b, preferred_element_type=F32)


def features(pair):
    xr, xi = pair[0][:, :NF].astype(F32), pair[0][:, NF:].astype(F32)
    o_r, o_i = pair[1][:, :NF].astype(F32), pair[1][:, NF:].astype(F32)
    dr, di = xr - o_r, xi - o_i
    parts = [dr * xr + di * xi, dr * xi - di * xr, o_r * xr + o_i * xi, o_r * xi - o_i * xr]
    both = [in_two(p) for p in parts]
    return jnp.concatenate(
        [jnp.concatenate([b[i] for b in both], axis=1) for i in range(2)], axis=0
    )


def for_features(links):
    return jnp.concatenate([links.astype(BF16)] * 2, axis=1)


def spread(rows, count, shift):
    index = lax.broadcasted_iota(jnp.int32, (count, NF), 0) + shift
    return jnp.concatenate(
        [(index == rows[s : s + 1]).astype(F32).astype(BF16) for s in range(rows.shape[0])], axis=1
    )


def spread_weights(rows, weights, count, shift):
    index = lax.broadcasted_iota(jnp.int32, (count, NF), 0) + shift
    return jnp.concatenate(
        [
            jnp.where(index == rows[s : s + 1], weights[s : s + 1], 0.0).astype(BF16)
            for s in range(rows.shape[0])
        ],
        axis=1,
    )


def spread_order():
    left = list(itertools.product(range(4), range(4), range(2)))[1:]
    ways = {0: (0.0, 0.0), 1: (1.0, 0.0), 2: (1.0, 1.0), 3: (0.0, 1.0)}

    def links(step):
        return np.array([way for axis in step[:2] for way in ways[axis]])

    used, order = np.zeros(4), []
    while left:
        step = min(left, key=lambda t: (np.max(used + links(t)), -np.sum(links(t)), t))
        left.remove(step)
        used = used + links(step)
        order.append(step)
    return order


def exchange_kernel(
    blks,
    subs,
    syn_hbm,
    obs_hbm,
    table_hbm,
    first_hbm,
    second_hbm,
    mask_hbm,
    weight_hbm,
    owner_hbm,
    element_hbm,
    summed,
    traces,
    table,
    first,
    second,
    mask,
    weight,
    owner,
    element,
    spec,
    halo,
    list_out,
    list_over,
    lists,
    lists_prev,
    labels,
    outgoing,
    received,
    load_sems,
    list_send,
    list_recv,
    over_send,
    over_recv,
    halo_send,
    halo_recv,
    entered,
    joined,
    y_send,
    y_recv,
    z_send,
    z_recv,
    all_send,
    all_recv,
):
    devices = blks * subs
    blk, sub = lax.axis_index("blk"), lax.axis_index("sub")
    me = blk * subs + sub
    rows = spec.shape[1]
    blocks = first.shape[0]
    def around(at, step, size):
        there = at + step
        return jnp.where(there >= size, there - size, there)

    subs_there = [around(sub, step, subs) for step in range(1, subs)]
    blks_there = [around(blk, step, blks) for step in range(1, blks)]
    blk_after, blk_before = blks_there[0], blks_there[-1]
    after = (jnp.where(sub == subs - 1, blk_after, blk), subs_there[0])
    before = (jnp.where(sub == 0, blk_before, blk), subs_there[-1])

    pairs = [
        (table_hbm, table),
        (syn_hbm.at[0], traces.at[0, pl.ds(0, rows)]),
        (obs_hbm.at[0], traces.at[0, pl.ds(rows, rows)]),
        (owner_hbm, owner),
        (element_hbm, element),
        (first_hbm, first),
        (second_hbm, second),
        (mask_hbm, mask),
        (weight_hbm, weight),
        (syn_hbm.at[1], traces.at[1, pl.ds(0, rows)]),
        (obs_hbm.at[1], traces.at[1, pl.ds(rows, rows)]),
        (syn_hbm.at[2], traces.at[2, pl.ds(0, rows)]),
        (obs_hbm.at[2], traces.at[2, pl.ds(rows, rows)]),
    ]
    loads = [
        pltpu.make_async_copy(src, dst, load_sems.at[i]) for i, (src, dst) in enumerate(pairs)
    ]
    for load in loads:
        load.start()

    z, y = lax.div(blk, 4), lax.rem(blk, 4)
    has_before, has_after = me > 0, me < devices - 1
    row_before, row_after = blk > 0, blk < blks - 1
    barrier = pltpu.get_barrier_semaphore()

    def greet(there):
        pl.semaphore_signal(barrier, inc=1, device_id=there, device_id_type=MESH)

    def greet_column(there, carry):
        greet((there, sub))
        return carry

    for there in subs_there:
        greet((blk, there))
    lax.fori_loop(blk + 1, blks, greet_column, 0)

    @pl.when((sub == 0) & row_before)
    def _():
        for s in range(subs):
            greet((blk_before, s))

    @pl.when((sub == subs - 1) & row_after)
    def _():
        greet((blk_after, 0))

    for i in range(3):
        pl.semaphore_signal(entered.at[i], inc=1)
    greetings = (
        (subs - 1)
        + jnp.where(row_after, 1, 0)
        + jnp.where((sub == 0) & row_before, 1, 0)
        + blk
    )

    def transform(c):
        both = dot_plain(traces[c], table[...]).astype(BF16)
        spec[2 * c] = both[:rows]
        spec[2 * c + 1] = both[rows:]

    for i in range(3):
        loads[i].wait()
    transform(0)

    pl.semaphore_wait(barrier, greetings)

    def halo_copies(c):
        q = pl.ds(2 * c, 2)
        return [
            pltpu.make_async_remote_copy(
                src_ref=spec.at[q, pl.ds(0, BLOCK)],
                dst_ref=halo.at[q, pl.ds(BLOCK, BLOCK)],
                send_sem=halo_send.at[0, c],
                recv_sem=halo_recv.at[0, c],
                device_id=before,
                device_id_type=MESH,
            ),
            pltpu.make_async_remote_copy(
                src_ref=spec.at[q, pl.ds(rows - BLOCK, BLOCK)],
                dst_ref=halo.at[q, pl.ds(0, BLOCK)],
                send_sem=halo_send.at[1, c],
                recv_sem=halo_recv.at[1, c],
                device_id=after,
                device_id_type=MESH,
            ),
        ]

    halos = [halo_copies(c) for c in range(3)]

    def start_halos(c):
        @pl.when(has_before)
        def _():
            halos[c][0].start()

        @pl.when(has_after)
        def _():
            halos[c][1].start()

    start_halos(0)

    def answer(there, carry):
        kind = jnp.where(lax.div(there, 4) == z, 0, jnp.where(z == 1, 1, 2))
        pl.semaphore_signal(
            entered.at[kind], inc=1, device_id=(there, sub), device_id_type=MESH
        )
        return carry

    @pl.when(z < 3)
    def _():
        lax.fori_loop(0, blk, answer, 0)


    for i in range(3, 5):
        loads[i].wait()
    lane = lax.broadcasted_iota(jnp.int32, (rows, rows), 1)
    line = lax.broadcasted_iota(jnp.int32, (rows, rows), 0)
    owner_row = owner[...]

    def column(row):
        return jnp.sum(jnp.where(lane == line, row, 0), axis=1, keepdims=True)

    owner_column, element_column = column(owner_row), column(element[...]).astype(F32)
    same = owner_column == owner_row
    rank_column = jnp.sum(jnp.where(same & (lane < line), 1, 0), axis=1, keepdims=True)
    label_rows = []
    for k in range(2):
        chosen = ((owner_column == lane) & (rank_column == k)).astype(F32)
        label_rows.append(
            jnp.sum(chosen * (element_column - rows), axis=0, keepdims=True) + float(rows)
        )

    for i in range(5, 9):
        loads[i].wait()
    base = (blk * blocks + lax.broadcasted_iota(jnp.int32, (blocks, NF), 0)) * BLOCK
    code = ((first[...] - base) * (2 * BLOCK) + (second[...] - base)).astype(F32)
    slot_weight = weight[...] * mask[...].astype(F32)
    zero_row = jnp.zeros((1, NF), F32)
    for s in range(subs):
        lines = [max(2 * s - 1, 0), 2 * s, 2 * s + 1]
        list_out[s] = jnp.concatenate(
            [code[i : i + 1] for i in lines]
            + [slot_weight[i : i + 1] for i in lines]
            + label_rows,
            axis=0,
        )
    list_over[...] = jnp.concatenate(
        [code[blocks - 1 : blocks]]
        + [zero_row] * 2
        + [slot_weight[blocks - 1 : blocks]]
        + [zero_row] * 4,
        axis=0,
    )
    lists[sub] = list_out[sub]

    for there in subs_there:
        pltpu.make_async_remote_copy(
            src_ref=list_out.at[there],
            dst_ref=lists.at[sub],
            send_sem=list_send,
            recv_sem=list_recv,
            device_id=(blk, there),
            device_id_type=MESH,
        ).start()
    over = pltpu.make_async_remote_copy(
        src_ref=list_over,
        dst_ref=lists_prev.at[sub],
        send_sem=over_send,
        recv_sem=over_recv,
        device_id=(blk_after, 0),
        device_id_type=MESH,
    )

    @pl.when(row_after)
    def _():
        over.start()


    for c in (1, 2):
        loads[7 + 2 * c].wait()
        loads[8 + 2 * c].wait()
        transform(c)
        start_halos(c)

    @pl.when(jnp.logical_not(has_before))
    def _():
        halo[:, :BLOCK] = jnp.zeros((6, BLOCK, 2 * NF), BF16)

    @pl.when(jnp.logical_not(has_after))
    def _():
        halo[:, BLOCK:] = jnp.zeros((6, BLOCK, 2 * NF), BF16)

    @pl.when(z == 3)
    def _():
        lax.fori_loop(0, blk, answer, 0)

    def tell_row(which):
        for there in subs_there:
            pl.semaphore_signal(
                joined.at[which], inc=1, device_id=(blk, there), device_id_type=MESH
            )

    @pl.when(z >= 2)
    def _():
        tell_row(0)

    rank_row = jnp.sum(jnp.where(same & (line < lane), 1, 0), axis=0, keepdims=True)
    target = owner_row * 4 + rank_row * 2
    slot = lax.broadcasted_iota(jnp.int32, (4 * devices, 2 * rows), 0)
    placement = (slot == jnp.concatenate([target, target + 1], axis=1)).astype(F32).astype(BF16)

    def stations(c):
        return (spec[2 * c], spec[2 * c + 1])

    own = [features(stations(c)) for c in range(3)]

    others = pl.ds(0, subs - 1)
    pltpu.make_async_copy(lists.at[others], lists.at[others], list_recv).wait()

    @pl.when((sub == 0) & row_before)
    def _():
        pltpu.make_async_copy(lists_prev, lists_prev, over_recv).wait()

    @pl.when((sub == 0) & jnp.logical_not(row_before))
    def _():
        lists_prev[...] = jnp.zeros(lists_prev.shape, F32)

    @pl.when(sub != 0)
    def _():
        lists_prev[...] = lists[...]

    def unpacked(ref, k):
        codes = ref[:, k, :].astype(jnp.int32)
        return codes >> 7, codes & 127, ref[:, 3 + k, :]

    first0, second0, weight0 = unpacked(lists_prev, 0)
    first1, second1, weight1 = unpacked(lists, 1)
    first2, second2, weight2 = unpacked(lists, 2)
    to_prev = dot_rows(spread_weights(second0, weight0, BLOCK, BLOCK), spread(first0, rows, 0))
    upper = dot_rows(spread_weights(first1, weight1, BLOCK, 0), spread(second1, rows, 0))
    lower = dot_rows(spread_weights(first2, weight2, BLOCK, 0), spread(second2, rows, 0))
    half = lax.broadcasted_iota(jnp.int32, (BLOCK, rows), 1) >= BLOCK
    inside = jnp.where(half, pltpu.roll(lower, BLOCK, 1), 0.0)
    one_way = jnp.concatenate([upper, inside], axis=0)
    link_own = for_features(one_way + one_way.T)
    link_halo = for_features(jnp.concatenate([to_prev, jnp.where(half, lower, 0.0)], axis=0))
    inner = [dot_plain(link_own, own[c]) for c in range(3)]

    def adjoint(c):
        sums = inner[c] + dot_plain(link_halo, features((halo[2 * c], halo[2 * c + 1])))
        g1r, g1i, g2r, g2i = (sums[:, i * NF : (i + 1) * NF] for i in range(4))
        x, o = stations(c)
        xr, xi = x[:, :NF].astype(F32), x[:, NF:].astype(F32)
        dr, di = xr - o[:, :NF].astype(F32), xi - o[:, NF:].astype(F32)
        real = (xr * g1r - xi * g1i) + (dr * g2r - di * g2i)
        imag = (xr * g1i + xi * g1r) + (dr * g2i + di * g2r)
        return jnp.concatenate([real, imag], axis=0).astype(BF16)

    def handle(together):
        for c in together:

            @pl.when(has_after)
            def _():
                halos[c][0].wait_recv()

            @pl.when(has_before)
            def _():
                halos[c][1].wait_recv()

        placed = dot_plain(placement, jnp.concatenate([adjoint(c) for c in together], axis=1))
        for i, c in enumerate(together):
            outgoing[:, c] = (
                placed[:, i * NF : (i + 1) * NF].astype(BF16).reshape(devices, 4, NF)
            )

    handle((0, 1))

    pl.semaphore_wait(entered.at[0], 4 - y)
    labels[z, y] = jnp.concatenate([lists[:, 6, :], lists[:, 7, :]], axis=0).astype(BF16)
    for step in range(1, 4):
        pltpu.make_async_remote_copy(
            src_ref=labels.at[z, y],
            dst_ref=labels.at[z, y],
            send_sem=y_send,
            recv_sem=y_recv,
            device_id=(z * 4 + around(y, step, 4), sub),
            device_id_type=MESH,
        ).start()

    pl.semaphore_wait(entered.at[1], 1 + jnp.where(z == 0, 4, 0))

    @pl.when(z < 2)
    def _():
        tell_row(0)

    handle((2,))

    def rest_entered(answers):
        pl.semaphore_wait(entered.at[2], 1 + answers)
        tell_row(1)

    @pl.when(z >= 2)
    def _():
        rest_entered(jnp.where(z == 2, 4, 0))

    def turns(at, size):
        return [at] + [around(at, step, size) for step in range(1, size)]

    core, chip = lax.rem(sub, 2), lax.div(me, 2)
    y_to, x_to = turns(y, 4), turns(lax.div(sub, 2), 4)
    core_to = [core, 1 - core]
    received[core, chip] = outgoing[me]

    def deliver(plane, step):
        dy, dx, other = step
        blk_to, sub_to = plane * 4 + y_to[dy], x_to[dx] * 2 + core_to[other]
        pltpu.make_async_remote_copy(
            src_ref=outgoing.at[blk_to * subs + sub_to],
            dst_ref=received.at[core, chip],
            send_sem=all_send,
            recv_sem=all_recv.at[other],
            device_id=(blk_to, sub_to),
            device_id_type=MESH,
        ).start()

    def deliver_plane(plane):
        for step in spread_order():
            deliver(plane, step)

        @pl.when(z != plane)
        def _():
            deliver(plane, (0, 0, 0))

    pl.semaphore_wait(joined.at[0], subs - 1)
    deliver_plane(0)

    @pl.when(z < 2)
    def _():
        rest_entered(8)

    some = pl.ds(0, 3)
    pltpu.make_async_copy(labels.at[0, some], labels.at[0, some], y_recv).wait()
    for step in range(1, 4):
        pltpu.make_async_remote_copy(
            src_ref=labels.at[z],
            dst_ref=labels.at[z],
            send_sem=z_send,
            recv_sem=z_recv,
            device_id=(around(z, step, 4) * 4 + y, sub),
            device_id_type=MESH,
        ).start()

    deliver_plane(1)
    pl.semaphore_wait(joined.at[1], subs - 1)
    deliver_plane(2)
    deliver_plane(3)

    pltpu.make_async_copy(labels.at[some], labels.at[some], z_recv).wait()
    by_owner = labels[...].reshape(2 * devices, NF)
    arrived = lax.broadcasted_iota(jnp.int32, (2 * devices, 2 * devices), 1)
    held = lax.broadcasted_iota(jnp.int32, (2 * devices, 2 * devices), 0)
    sub_bits = subs.bit_length() - 1
    wanted = (
        ((arrived >> (sub_bits + 1)) << (sub_bits + 1))
        + (((arrived >> 1) & 1) << sub_bits)
        + (((arrived >> 2) & (subs // 2 - 1)) << 1)
    )
    owner_line = lax.broadcasted_iota(jnp.int32, (rows, 2 * devices), 0)

    def collector(source_core):
        repeated = lax.dot_general(
            by_owner,
            (held == wanted + source_core).astype(F32).astype(BF16),
            (((0,), (0,)), ((), ())),
            preferred_element_type=F32,
        )
        label = jnp.sum(jnp.where(owner_line == me, repeated, 0.0), axis=0, keepdims=True)
        return jnp.concatenate(
            [
                ((label == owner_line.astype(F32)) & ((arrived[:rows] & 1) == i)).astype(F32)
                for i in range(2)
            ],
            axis=0,
        ).astype(BF16)

    collect_other, collect_same = collector(1 - core), collector(core)

    def sums(collect, source_core):
        values = [received[source_core, :, c].reshape(2 * devices, NF) for c in range(3)]
        return dot_plain(collect, jnp.concatenate(values, axis=1))

    pltpu.make_async_copy(received.at[0], received.at[0], all_recv.at[1]).wait()
    first_sums = sums(collect_other, 1 - core)
    most = pl.ds(0, devices // 2 - 1)
    pltpu.make_async_copy(received.at[0, most], received.at[0, most], all_recv.at[0]).wait()
    total = (first_sums + sums(collect_same, core)).astype(BF16)
    for c in range(3):
        summed[c * rows : (c + 1) * rows, :NF] = total[:rows, c * NF : (c + 1) * NF]
        summed[c * rows : (c + 1) * rows, NF:] = total[rows:, c * NF : (c + 1) * NF]

    for c in range(3):

        @pl.when(has_before)
        def _():
            halos[c][0].wait_send()

        @pl.when(has_after)
        def _():
            halos[c][1].wait_send()

    pltpu.make_async_copy(list_out.at[others], list_out.at[others], list_send).wait()

    @pl.when(row_after)
    def _():
        over.wait_send()

    pltpu.make_async_copy(labels.at[0, some], labels.at[0, some], y_send).wait()
    pltpu.make_async_copy(labels.at[some], labels.at[some], z_send).wait()
    most = pl.ds(0, devices - 1)
    pltpu.make_async_copy(outgoing.at[most], outgoing.at[most], all_send).wait()


def exchange(blks, subs, syn, obs, table, first, second, mask, weight, owner, element):
    devices = blks * subs
    samples, rows = syn.shape[2], syn.shape[1]
    in_hbm = pl.BlockSpec(memory_space=pltpu.HBM)
    dma = pltpu.SemaphoreType.DMA
    return pl.pallas_call(
        functools.partial(exchange_kernel, blks, subs),
        out_shape=pltpu.VMEM((3 * rows, 2 * NF), BF16),
        in_specs=[in_hbm] * 9,
        out_specs=pl.BlockSpec(memory_space=pltpu.VMEM),
        scratch_shapes=[
            pltpu.VMEM((3, 2 * rows, samples), BF16),
            pltpu.VMEM(table.shape, BF16),
            pltpu.VMEM(first.shape, jnp.int32),
            pltpu.VMEM(second.shape, jnp.int32),
            pltpu.VMEM(mask.shape, jnp.int32),
            pltpu.VMEM(weight.shape, F32),
            pltpu.VMEM(owner.shape, jnp.int32),
            pltpu.VMEM(element.shape, jnp.int32),
            pltpu.VMEM((6, rows, 2 * NF), BF16),
            pltpu.VMEM((6, 2 * BLOCK, 2 * NF), BF16),
            pltpu.VMEM((subs, 8, NF), F32),
            pltpu.VMEM((8, NF), F32),
            pltpu.VMEM((subs, 8, NF), F32),
            pltpu.VMEM((subs, 8, NF), F32),
            pltpu.VMEM((4, blks // 4, 2 * subs, NF), BF16),
            pltpu.VMEM((devices, 3, 4, NF), BF16),
            pltpu.VMEM((2, devices // 2, 3, 4, NF), BF16),
            dma((13,)),
            dma,
            dma,
            dma,
            dma,
            dma((2, 3)),
            dma((2, 3)),
            pltpu.SemaphoreType.REGULAR((3,)),
            pltpu.SemaphoreType.REGULAR((2,)),
            dma,
            dma,
            dma,
            dma,
            dma,
            dma((2,)),
        ],
        compiler_params=pltpu.CompilerParams(
            collective_id=0, has_side_effects=True, vmem_limit_bytes=60 * 2**20
        ),
        cost_estimate=pl.CostEstimate(
            flops=2 * 10**9, bytes_accessed=3 * 10**6, transcendentals=0
        ),
        name="exchange",
    )(syn, obs, table, first, second, mask, weight, owner, element)


def finish_kernel(summed, table, out, result, sems):
    samples = result.shape[1]
    chunk = samples // sems.shape[0]
    copies = []
    for n in range(sems.shape[0]):
        columns = pl.ds(n * chunk, chunk)
        result[:, columns] = dot_plain(summed[...], table[:, columns])
        copies.append(
            pltpu.make_async_copy(result.at[:, columns], out.at[:, columns], sems.at[n])
        )
        copies[-1].start()
    for copy in copies:
        copy.wait()


def finish(summed, table):
    count, samples = summed.shape[0], table.shape[1]
    in_vmem = pl.BlockSpec(memory_space=pltpu.VMEM)
    out = pl.pallas_call(
        finish_kernel,
        out_shape=jax.ShapeDtypeStruct((count, samples), F32),
        in_specs=[in_vmem] * 2,
        out_specs=pl.BlockSpec(memory_space=pl.ANY),
        scratch_shapes=[
            pltpu.VMEM((count, samples), F32),
            pltpu.SemaphoreType.DMA((4,)),
        ],
        compiler_params=pltpu.CompilerParams(vmem_limit_bytes=40 * 2**20),
        cost_estimate=pl.CostEstimate(
            flops=7 * 10**8, bytes_accessed=3 * 10**6, transcendentals=0
        ),
        name="finish",
    )(summed, table)
    return out.reshape(3, count // 3, samples)


def on_device(
    blks,
    subs,
    synthetic,
    observed,
    pair_first,
    pair_second,
    pair_mask,
    pair_weight,
    station_owner,
    station_element,
):
    rows, _, samples = synthetic.shape
    forward, inverse = dft_tables(samples, NF)
    summed = exchange(
        blks,
        subs,
        jnp.transpose(synthetic, (1, 0, 2)),
        jnp.transpose(observed, (1, 0, 2)),
        jnp.asarray(forward),
        pair_first,
        pair_second,
        pair_mask,
        pair_weight,
        station_owner.reshape(1, rows),
        station_element.reshape(1, rows),
    )
    out = finish(summed, jnp.asarray(inverse))
    return jnp.transpose(out, (1, 0, 2))


def solution(mesh):
    blks, subs = mesh.shape["blk"], mesh.shape["sub"]
    return jax.shard_map(
        functools.partial(on_device, blks, subs),
        mesh=mesh,
        in_specs=(
            P(("blk", "sub"), None, None),
            P(("blk", "sub"), None, None),
            P("blk", "sub"),
            P("blk", "sub"),
            P("blk", "sub"),
            P("blk", "sub"),
            P(("blk", "sub"), None),
            P(("blk", "sub")),
        ),
        out_specs=P(("blk", "sub"), None, None),
        check_vma=False,
    )
```

```python
import functools
import itertools
import math

import jax
import jax.numpy as jnp
import numpy as np
from jax import lax
from jax.experimental import pallas as pl
from jax.experimental.pallas import tpu as pltpu
from jax.sharding import PartitionSpec as P

MESH = pl.DeviceIdType.MESH
NF = 128
BLOCK = 64
F32 = jnp.float32
BF16 = jnp.bfloat16


def dft_tables(samples, freqs):
    phase = (np.arange(samples)[:, None] * np.arange(freqs)[None, :]) % samples
    angles = phase.astype(np.float64) * (2.0 * math.pi / samples)
    scale = 1.0 / math.sqrt(samples)
    cosine, sine = np.cos(angles) * scale, np.sin(angles) * scale
    forward = np.concatenate([cosine, -sine], axis=1).astype(np.float32)
    doubled = np.where(np.arange(freqs) == 0, 1.0, 2.0)[:, None]
    inverse = np.concatenate([cosine.T * doubled, -sine.T * doubled], axis=0)
    return forward.astype(jnp.bfloat16), inverse.astype(np.float32).astype(jnp.bfloat16)


def in_two(x):
    high = x.astype(BF16)
    return high, (x - high.astype(F32)).astype(BF16)


def dot_rows(a, b):
    return lax.dot_general(a, b, (((1,), (1,)), ((), ())), preferred_element_type=F32)


def dot_plain(a, b):
    return jnp.dot(a, b, preferred_element_type=F32)


def features(pair):
    xr, xi = pair[0][:, :NF].astype(F32), pair[0][:, NF:].astype(F32)
    o_r, o_i = pair[1][:, :NF].astype(F32), pair[1][:, NF:].astype(F32)
    dr, di = xr - o_r, xi - o_i
    parts = [dr * xr + di * xi, dr * xi - di * xr, o_r * xr + o_i * xi, o_r * xi - o_i * xr]
    both = [in_two(p) for p in parts]
    return jnp.concatenate(
        [jnp.concatenate([b[i] for b in both], axis=1) for i in range(2)], axis=0
    )


def for_features(links):
    return jnp.concatenate([links.astype(BF16)] * 2, axis=1)


def spread(rows, count, shift):
    index = lax.broadcasted_iota(jnp.int32, (count, NF), 0) + shift
    return jnp.concatenate(
        [(index == rows[s : s + 1]).astype(F32).astype(BF16) for s in range(rows.shape[0])], axis=1
    )


def spread_weights(rows, weights, count, shift):
    index = lax.broadcasted_iota(jnp.int32, (count, NF), 0) + shift
    return jnp.concatenate(
        [
            jnp.where(index == rows[s : s + 1], weights[s : s + 1], 0.0).astype(BF16)
            for s in range(rows.shape[0])
        ],
        axis=1,
    )


def spread_order():
    left = list(itertools.product(range(4), range(4), range(2)))[1:]
    ways = {0: (0.0, 0.0), 1: (1.0, 0.0), 2: (1.0, 1.0), 3: (0.0, 1.0)}

    def links(step):
        return np.array([way for axis in step[:2] for way in ways[axis]])

    used, order = np.zeros(4), []
    while left:
        step = min(left, key=lambda t: (np.max(used + links(t)), -np.sum(links(t)), t))
        left.remove(step)
        used = used + links(step)
        order.append(step)
    return order


def exchange_kernel(
    blks,
    subs,
    syn_hbm,
    obs_hbm,
    table_hbm,
    first_hbm,
    second_hbm,
    mask_hbm,
    weight_hbm,
    owner_hbm,
    element_hbm,
    summed,
    traces,
    table,
    first,
    second,
    mask,
    weight,
    owner,
    element,
    spec,
    halo,
    list_out,
    list_over,
    lists,
    lists_prev,
    labels,
    outgoing,
    received,
    load_sems,
    list_send,
    list_recv,
    over_send,
    over_recv,
    halo_send,
    halo_recv,
    entered,
    joined,
    y_send,
    y_recv,
    z_send,
    z_recv,
    all_send,
    all_recv,
):
    devices = blks * subs
    blk, sub = lax.axis_index("blk"), lax.axis_index("sub")
    me = blk * subs + sub
    rows = spec.shape[1]
    blocks = first.shape[0]
    def around(at, step, size):
        there = at + step
        return jnp.where(there >= size, there - size, there)

    subs_there = [around(sub, step, subs) for step in range(1, subs)]
    blks_there = [around(blk, step, blks) for step in range(1, blks)]
    blk_after, blk_before = blks_there[0], blks_there[-1]
    after = (jnp.where(sub == subs - 1, blk_after, blk), subs_there[0])
    before = (jnp.where(sub == 0, blk_before, blk), subs_there[-1])

    pairs = [
        (table_hbm, table),
        (syn_hbm.at[0], traces.at[0, pl.ds(0, rows)]),
        (obs_hbm.at[0], traces.at[0, pl.ds(rows, rows)]),
        (owner_hbm, owner),
        (element_hbm, element),
        (first_hbm, first),
        (second_hbm, second),
        (mask_hbm, mask),
        (weight_hbm, weight),
        (syn_hbm.at[1], traces.at[1, pl.ds(0, rows)]),
        (obs_hbm.at[1], traces.at[1, pl.ds(rows, rows)]),
        (syn_hbm.at[2], traces.at[2, pl.ds(0, rows)]),
        (obs_hbm.at[2], traces.at[2, pl.ds(rows, rows)]),
    ]
    loads = [
        pltpu.make_async_copy(src, dst, load_sems.at[i]) for i, (src, dst) in enumerate(pairs)
    ]
    for load in loads:
        load.start()

    z, y = lax.div(blk, 4), lax.rem(blk, 4)
    has_before, has_after = me > 0, me < devices - 1
    row_before, row_after = blk > 0, blk < blks - 1
    barrier = pltpu.get_barrier_semaphore()

    def greet(there):
        pl.semaphore_signal(barrier, inc=1, device_id=there, device_id_type=MESH)

    def greet_column(there, carry):
        greet((there, sub))
        return carry

    for there in subs_there:
        greet((blk, there))
    lax.fori_loop(blk + 1, blks, greet_column, 0)

    @pl.when((sub == 0) & row_before)
    def _():
        for s in range(subs):
            greet((blk_before, s))

    @pl.when((sub == subs - 1) & row_after)
    def _():
        greet((blk_after, 0))

    for i in (0, 2):
        pl.semaphore_signal(entered.at[i], inc=1)
    greetings = (
        (subs - 1)
        + jnp.where(row_after, 1, 0)
        + jnp.where((sub == 0) & row_before, 1, 0)
        + blk
    )

    pl.semaphore_wait(barrier, greetings)

    def answer(there, carry):
        kind = jnp.where(lax.div(there, 4) == z, 0, jnp.where(z == 1, 1, 2))
        pl.semaphore_signal(
            entered.at[kind], inc=1, device_id=(there, sub), device_id_type=MESH
        )
        return carry

    @pl.when(z < 3)
    def _():
        lax.fori_loop(0, blk, answer, 0)


    def transform(c):
        both = dot_plain(traces[c], table[...]).astype(BF16)
        spec[2 * c] = both[:rows]
        spec[2 * c + 1] = both[rows:]

    for i in range(3):
        loads[i].wait()
    transform(0)


    def halo_copies(c):
        q = pl.ds(2 * c, 2)
        return [
            pltpu.make_async_remote_copy(
                src_ref=spec.at[q, pl.ds(0, BLOCK)],
                dst_ref=halo.at[q, pl.ds(BLOCK, BLOCK)],
                send_sem=halo_send.at[0, c],
                recv_sem=halo_recv.at[0, c],
                device_id=before,
                device_id_type=MESH,
            ),
            pltpu.make_async_remote_copy(
                src_ref=spec.at[q, pl.ds(rows - BLOCK, BLOCK)],
                dst_ref=halo.at[q, pl.ds(0, BLOCK)],
                send_sem=halo_send.at[1, c],
                recv_sem=halo_recv.at[1, c],
                device_id=after,
                device_id_type=MESH,
            ),
        ]

    halos = [halo_copies(c) for c in range(3)]

    def start_halos(c):
        @pl.when(has_before)
        def _():
            halos[c][0].start()

        @pl.when(has_after)
        def _():
            halos[c][1].start()

    start_halos(0)

    for i in range(3, 5):
        loads[i].wait()
    lane = lax.broadcasted_iota(jnp.int32, (rows, rows), 1)
    line = lax.broadcasted_iota(jnp.int32, (rows, rows), 0)
    owner_row = owner[...]

    def column(row):
        return jnp.sum(jnp.where(lane == line, row, 0), axis=1, keepdims=True)

    owner_column, element_column = column(owner_row), column(element[...]).astype(F32)
    same = owner_column == owner_row
    rank_column = jnp.sum(jnp.where(same & (lane < line), 1, 0), axis=1, keepdims=True)
    label_rows = []
    for k in range(2):
        chosen = ((owner_column == lane) & (rank_column == k)).astype(F32)
        label_rows.append(
            jnp.sum(chosen * (element_column - rows), axis=0, keepdims=True) + float(rows)
        )

    for i in range(5, 9):
        loads[i].wait()
    base = (blk * blocks + lax.broadcasted_iota(jnp.int32, (blocks, NF), 0)) * BLOCK
    code = ((first[...] - base) * (2 * BLOCK) + (second[...] - base)).astype(F32)
    slot_weight = weight[...] * mask[...].astype(F32)
    zero_row = jnp.zeros((1, NF), F32)
    for s in range(subs):
        lines = [max(2 * s - 1, 0), 2 * s, 2 * s + 1]
        list_out[s] = jnp.concatenate(
            [code[i : i + 1] for i in lines]
            + [slot_weight[i : i + 1] for i in lines]
            + label_rows,
            axis=0,
        )
    list_over[...] = jnp.concatenate(
        [code[blocks - 1 : blocks]]
        + [zero_row] * 2
        + [slot_weight[blocks - 1 : blocks]]
        + [zero_row] * 4,
        axis=0,
    )
    lists[sub] = list_out[sub]

    for there in subs_there:
        pltpu.make_async_remote_copy(
            src_ref=list_out.at[there],
            dst_ref=lists.at[sub],
            send_sem=list_send,
            recv_sem=list_recv,
            device_id=(blk, there),
            device_id_type=MESH,
        ).start()
    over = pltpu.make_async_remote_copy(
        src_ref=list_over,
        dst_ref=lists_prev.at[sub],
        send_sem=over_send,
        recv_sem=over_recv,
        device_id=(blk_after, 0),
        device_id_type=MESH,
    )

    @pl.when(row_after)
    def _():
        over.start()


    for c in (1, 2):
        loads[7 + 2 * c].wait()
        loads[8 + 2 * c].wait()
        transform(c)
        start_halos(c)

    @pl.when(jnp.logical_not(has_before))
    def _():
        halo[:, :BLOCK] = jnp.zeros((6, BLOCK, 2 * NF), BF16)

    @pl.when(jnp.logical_not(has_after))
    def _():
        halo[:, BLOCK:] = jnp.zeros((6, BLOCK, 2 * NF), BF16)

    @pl.when(z == 3)
    def _():
        lax.fori_loop(0, blk, answer, 0)

    def tell_row(which):
        for there in subs_there:
            pl.semaphore_signal(
                joined.at[which], inc=1, device_id=(blk, there), device_id_type=MESH
            )

    @pl.when(z >= 1)
    def _():
        tell_row(0)

    @pl.when(z >= 2)
    def _():
        tell_row(1)

    rank_row = jnp.sum(jnp.where(same & (line < lane), 1, 0), axis=0, keepdims=True)
    target = owner_row * 4 + rank_row * 2
    slot = lax.broadcasted_iota(jnp.int32, (4 * devices, 2 * rows), 0)
    placement = (slot == jnp.concatenate([target, target + 1], axis=1)).astype(F32).astype(BF16)

    def stations(c):
        return (spec[2 * c], spec[2 * c + 1])

    own = [features(stations(c)) for c in range(3)]

    others = pl.ds(0, subs - 1)
    pltpu.make_async_copy(lists.at[others], lists.at[others], list_recv).wait()

    @pl.when(z < 2)
    def _():
        pl.semaphore_wait(entered.at[0], 4 - y)
        tell_row(z)

    @pl.when((sub == 0) & row_before)
    def _():
        pltpu.make_async_copy(lists_prev, lists_prev, over_recv).wait()

    @pl.when((sub == 0) & jnp.logical_not(row_before))
    def _():
        lists_prev[...] = jnp.zeros(lists_prev.shape, F32)

    @pl.when(sub != 0)
    def _():
        lists_prev[...] = lists[...]

    def unpacked(ref, k):
        codes = ref[:, k, :].astype(jnp.int32)
        return codes >> 7, codes & 127, ref[:, 3 + k, :]

    first0, second0, weight0 = unpacked(lists_prev, 0)
    first1, second1, weight1 = unpacked(lists, 1)
    first2, second2, weight2 = unpacked(lists, 2)
    to_prev = dot_rows(spread_weights(second0, weight0, BLOCK, BLOCK), spread(first0, rows, 0))
    upper = dot_rows(spread_weights(first1, weight1, BLOCK, 0), spread(second1, rows, 0))
    lower = dot_rows(spread_weights(first2, weight2, BLOCK, 0), spread(second2, rows, 0))
    half = lax.broadcasted_iota(jnp.int32, (BLOCK, rows), 1) >= BLOCK
    inside = jnp.where(half, pltpu.roll(lower, BLOCK, 1), 0.0)
    one_way = jnp.concatenate([upper, inside], axis=0)
    link_own = for_features(one_way + one_way.T)
    link_halo = for_features(jnp.concatenate([to_prev, jnp.where(half, lower, 0.0)], axis=0))
    inner = [dot_plain(link_own, own[c]) for c in range(3)]

    def adjoint(c):
        sums = inner[c] + dot_plain(link_halo, features((halo[2 * c], halo[2 * c + 1])))
        g1r, g1i, g2r, g2i = (sums[:, i * NF : (i + 1) * NF] for i in range(4))
        x, o = stations(c)
        xr, xi = x[:, :NF].astype(F32), x[:, NF:].astype(F32)
        dr, di = xr - o[:, :NF].astype(F32), xi - o[:, NF:].astype(F32)
        real = (xr * g1r - xi * g1i) + (dr * g2r - di * g2i)
        imag = (xr * g1i + xi * g1r) + (dr * g2i + di * g2r)
        return jnp.concatenate([real, imag], axis=0).astype(BF16)

    def handle(together):
        for c in together:

            @pl.when(has_after)
            def _():
                halos[c][0].wait_recv()

            @pl.when(has_before)
            def _():
                halos[c][1].wait_recv()

        placed = dot_plain(placement, jnp.concatenate([adjoint(c) for c in together], axis=1))
        for i, c in enumerate(together):
            outgoing[:, c] = (
                placed[:, i * NF : (i + 1) * NF].astype(BF16).reshape(devices, 4, NF)
            )

    handle((0, 1))

    @pl.when(z >= 2)
    def _():
        pl.semaphore_wait(entered.at[0], 4 - y)

    labels[z, y] = jnp.concatenate([lists[:, 6, :], lists[:, 7, :]], axis=0).astype(BF16)
    for step in range(1, 4):
        pltpu.make_async_remote_copy(
            src_ref=labels.at[z, y],
            dst_ref=labels.at[z, y],
            send_sem=y_send,
            recv_sem=y_recv,
            device_id=(z * 4 + around(y, step, 4), sub),
            device_id_type=MESH,
        ).start()

    @pl.when(z == 0)
    def _():
        pl.semaphore_wait(entered.at[1], 4)
        tell_row(1)

    handle((2,))

    def rest_entered(answers):
        pl.semaphore_wait(entered.at[2], 1 + answers)
        tell_row(2)

    @pl.when(z >= 2)
    def _():
        rest_entered(jnp.where(z == 2, 4, 0))

    def turns(at, size):
        return [at] + [around(at, step, size) for step in range(1, size)]

    core, chip = lax.rem(sub, 2), lax.div(me, 2)
    y_to, x_to = turns(y, 4), turns(lax.div(sub, 2), 4)
    core_to = [core, 1 - core]
    received[core, chip] = outgoing[me]

    def deliver(plane, step):
        dy, dx, other = step
        blk_to, sub_to = plane * 4 + y_to[dy], x_to[dx] * 2 + core_to[other]
        pltpu.make_async_remote_copy(
            src_ref=outgoing.at[blk_to * subs + sub_to],
            dst_ref=received.at[core, chip],
            send_sem=all_send,
            recv_sem=all_recv.at[other],
            device_id=(blk_to, sub_to),
            device_id_type=MESH,
        ).start()

    def deliver_plane(plane):
        for step in spread_order():
            deliver(plane, step)

        @pl.when(z != plane)
        def _():
            deliver(plane, (0, 0, 0))

    pl.semaphore_wait(joined.at[0], subs - 1)
    deliver_plane(0)

    @pl.when(z < 2)
    def _():
        rest_entered(8)

    some = pl.ds(0, 3)
    pltpu.make_async_copy(labels.at[0, some], labels.at[0, some], y_recv).wait()
    for step in range(1, 4):
        pltpu.make_async_remote_copy(
            src_ref=labels.at[z],
            dst_ref=labels.at[z],
            send_sem=z_send,
            recv_sem=z_recv,
            device_id=(around(z, step, 4) * 4 + y, sub),
            device_id_type=MESH,
        ).start()

    pl.semaphore_wait(joined.at[1], subs - 1)
    deliver_plane(1)
    pl.semaphore_wait(joined.at[2], subs - 1)
    deliver_plane(2)
    deliver_plane(3)

    pltpu.make_async_copy(labels.at[some], labels.at[some], z_recv).wait()
    by_owner = labels[...].reshape(2 * devices, NF)
    arrived = lax.broadcasted_iota(jnp.int32, (2 * devices, 2 * devices), 1)
    held = lax.broadcasted_iota(jnp.int32, (2 * devices, 2 * devices), 0)
    sub_bits = subs.bit_length() - 1
    wanted = (
        ((arrived >> (sub_bits + 1)) << (sub_bits + 1))
        + (((arrived >> 1) & 1) << sub_bits)
        + (((arrived >> 2) & (subs // 2 - 1)) << 1)
    )
    owner_line = lax.broadcasted_iota(jnp.int32, (rows, 2 * devices), 0)

    def collector(source_core):
        repeated = lax.dot_general(
            by_owner,
            (held == wanted + source_core).astype(F32).astype(BF16),
            (((0,), (0,)), ((), ())),
            preferred_element_type=F32,
        )
        label = jnp.sum(jnp.where(owner_line == me, repeated, 0.0), axis=0, keepdims=True)
        return jnp.concatenate(
            [
                ((label == owner_line.astype(F32)) & ((arrived[:rows] & 1) == i)).astype(F32)
                for i in range(2)
            ],
            axis=0,
        ).astype(BF16)

    collect_other, collect_same = collector(1 - core), collector(core)

    def sums(collect, source_core):
        values = [received[source_core, :, c].reshape(2 * devices, NF) for c in range(3)]
        return dot_plain(collect, jnp.concatenate(values, axis=1))

    pltpu.make_async_copy(received.at[0], received.at[0], all_recv.at[1]).wait()
    first_sums = sums(collect_other, 1 - core)
    most = pl.ds(0, devices // 2 - 1)
    pltpu.make_async_copy(received.at[0, most], received.at[0, most], all_recv.at[0]).wait()
    total = (first_sums + sums(collect_same, core)).astype(BF16)
    for c in range(3):
        summed[c * rows : (c + 1) * rows, :NF] = total[:rows, c * NF : (c + 1) * NF]
        summed[c * rows : (c + 1) * rows, NF:] = total[rows:, c * NF : (c + 1) * NF]

    for c in range(3):

        @pl.when(has_before)
        def _():
            halos[c][0].wait_send()

        @pl.when(has_after)
        def _():
            halos[c][1].wait_send()

    pltpu.make_async_copy(list_out.at[others], list_out.at[others], list_send).wait()

    @pl.when(row_after)
    def _():
        over.wait_send()

    pltpu.make_async_copy(labels.at[0, some], labels.at[0, some], y_send).wait()
    pltpu.make_async_copy(labels.at[some], labels.at[some], z_send).wait()
    most = pl.ds(0, devices - 1)
    pltpu.make_async_copy(outgoing.at[most], outgoing.at[most], all_send).wait()


def exchange(blks, subs, syn, obs, table, first, second, mask, weight, owner, element):
    devices = blks * subs
    samples, rows = syn.shape[2], syn.shape[1]
    in_hbm = pl.BlockSpec(memory_space=pltpu.HBM)
    dma = pltpu.SemaphoreType.DMA
    return pl.pallas_call(
        functools.partial(exchange_kernel, blks, subs),
        out_shape=pltpu.VMEM((3 * rows, 2 * NF), BF16),
        in_specs=[in_hbm] * 9,
        out_specs=pl.BlockSpec(memory_space=pltpu.VMEM),
        scratch_shapes=[
            pltpu.VMEM((3, 2 * rows, samples), BF16),
            pltpu.VMEM(table.shape, BF16),
            pltpu.VMEM(first.shape, jnp.int32),
            pltpu.VMEM(second.shape, jnp.int32),
            pltpu.VMEM(mask.shape, jnp.int32),
            pltpu.VMEM(weight.shape, F32),
            pltpu.VMEM(owner.shape, jnp.int32),
            pltpu.VMEM(element.shape, jnp.int32),
            pltpu.VMEM((6, rows, 2 * NF), BF16),
            pltpu.VMEM((6, 2 * BLOCK, 2 * NF), BF16),
            pltpu.VMEM((subs, 8, NF), F32),
            pltpu.VMEM((8, NF), F32),
            pltpu.VMEM((subs, 8, NF), F32),
            pltpu.VMEM((subs, 8, NF), F32),
            pltpu.VMEM((4, blks // 4, 2 * subs, NF), BF16),
            pltpu.VMEM((devices, 3, 4, NF), BF16),
            pltpu.VMEM((2, devices // 2, 3, 4, NF), BF16),
            dma((13,)),
            dma,
            dma,
            dma,
            dma,
            dma((2, 3)),
            dma((2, 3)),
            pltpu.SemaphoreType.REGULAR((3,)),
            pltpu.SemaphoreType.REGULAR((3,)),
            dma,
            dma,
            dma,
            dma,
            dma,
            dma((2,)),
        ],
        compiler_params=pltpu.CompilerParams(
            collective_id=0, has_side_effects=True, vmem_limit_bytes=60 * 2**20
        ),
        cost_estimate=pl.CostEstimate(
            flops=2 * 10**9, bytes_accessed=3 * 10**6, transcendentals=0
        ),
        name="exchange",
    )(syn, obs, table, first, second, mask, weight, owner, element)


def finish_kernel(summed, table, out, result, sems):
    samples = result.shape[1]
    chunk = samples // sems.shape[0]
    copies = []
    for n in range(sems.shape[0]):
        columns = pl.ds(n * chunk, chunk)
        result[:, columns] = dot_plain(summed[...], table[:, columns])
        copies.append(
            pltpu.make_async_copy(result.at[:, columns], out.at[:, columns], sems.at[n])
        )
        copies[-1].start()
    for copy in copies:
        copy.wait()


def finish(summed, table):
    count, samples = summed.shape[0], table.shape[1]
    in_vmem = pl.BlockSpec(memory_space=pltpu.VMEM)
    out = pl.pallas_call(
        finish_kernel,
        out_shape=jax.ShapeDtypeStruct((count, samples), F32),
        in_specs=[in_vmem] * 2,
        out_specs=pl.BlockSpec(memory_space=pl.ANY),
        scratch_shapes=[
            pltpu.VMEM((count, samples), F32),
            pltpu.SemaphoreType.DMA((4,)),
        ],
        compiler_params=pltpu.CompilerParams(vmem_limit_bytes=40 * 2**20),
        cost_estimate=pl.CostEstimate(
            flops=7 * 10**8, bytes_accessed=3 * 10**6, transcendentals=0
        ),
        name="finish",
    )(summed, table)
    return out.reshape(3, count // 3, samples)


def on_device(
    blks,
    subs,
    synthetic,
    observed,
    pair_first,
    pair_second,
    pair_mask,
    pair_weight,
    station_owner,
    station_element,
):
    rows, _, samples = synthetic.shape
    forward, inverse = dft_tables(samples, NF)
    summed = exchange(
        blks,
        subs,
        jnp.transpose(synthetic, (1, 0, 2)),
        jnp.transpose(observed, (1, 0, 2)),
        jnp.asarray(forward),
        pair_first,
        pair_second,
        pair_mask,
        pair_weight,
        station_owner.reshape(1, rows),
        station_element.reshape(1, rows),
    )
    out = finish(summed, jnp.asarray(inverse))
    return jnp.transpose(out, (1, 0, 2))


def solution(mesh):
    blks, subs = mesh.shape["blk"], mesh.shape["sub"]
    return jax.shard_map(
        functools.partial(on_device, blks, subs),
        mesh=mesh,
        in_specs=(
            P(("blk", "sub"), None, None),
            P(("blk", "sub"), None, None),
            P("blk", "sub"),
            P("blk", "sub"),
            P("blk", "sub"),
            P("blk", "sub"),
            P(("blk", "sub"), None),
            P(("blk", "sub")),
        ),
        out_specs=P(("blk", "sub"), None, None),
        check_vma=False,
    )
```

```python
import functools
import itertools
import math

import jax
import jax.numpy as jnp
import numpy as np
from jax import lax
from jax.experimental import pallas as pl
from jax.experimental.pallas import tpu as pltpu
from jax.sharding import PartitionSpec as P

MESH = pl.DeviceIdType.MESH
NF = 128
BLOCK = 64
F32 = jnp.float32
BF16 = jnp.bfloat16


def dft_tables(samples, freqs):
    phase = (np.arange(samples)[:, None] * np.arange(freqs)[None, :]) % samples
    angles = phase.astype(np.float64) * (2.0 * math.pi / samples)
    scale = 1.0 / math.sqrt(samples)
    cosine, sine = np.cos(angles) * scale, np.sin(angles) * scale
    forward = np.concatenate([cosine, -sine], axis=1).astype(np.float32)
    doubled = np.where(np.arange(freqs) == 0, 1.0, 2.0)[:, None]
    inverse = np.concatenate([cosine.T * doubled, -sine.T * doubled], axis=0)
    return forward.astype(jnp.bfloat16), inverse.astype(np.float32).astype(jnp.bfloat16)


def in_two(x):
    high = x.astype(BF16)
    return high, (x - high.astype(F32)).astype(BF16)


def dot_rows(a, b):
    return lax.dot_general(a, b, (((1,), (1,)), ((), ())), preferred_element_type=F32)


def dot_plain(a, b):
    return jnp.dot(a, b, preferred_element_type=F32)


def features(pair):
    xr, xi = pair[0][:, :NF].astype(F32), pair[0][:, NF:].astype(F32)
    o_r, o_i = pair[1][:, :NF].astype(F32), pair[1][:, NF:].astype(F32)
    dr, di = xr - o_r, xi - o_i
    parts = [dr * xr + di * xi, dr * xi - di * xr, o_r * xr + o_i * xi, o_r * xi - o_i * xr]
    both = [in_two(p) for p in parts]
    return jnp.concatenate(
        [jnp.concatenate([b[i] for b in both], axis=1) for i in range(2)], axis=0
    )


def for_features(links):
    return jnp.concatenate([links.astype(BF16)] * 2, axis=1)


def spread(rows, count, shift):
    index = lax.broadcasted_iota(jnp.int32, (count, NF), 0) + shift
    return jnp.concatenate(
        [(index == rows[s : s + 1]).astype(F32).astype(BF16) for s in range(rows.shape[0])], axis=1
    )


def spread_weights(rows, weights, count, shift):
    index = lax.broadcasted_iota(jnp.int32, (count, NF), 0) + shift
    return jnp.concatenate(
        [
            jnp.where(index == rows[s : s + 1], weights[s : s + 1], 0.0).astype(BF16)
            for s in range(rows.shape[0])
        ],
        axis=1,
    )


def spread_order():
    left = list(itertools.product(range(4), range(4), range(2)))[1:]
    ways = {0: (0.0, 0.0), 1: (1.0, 0.0), 2: (1.0, 1.0), 3: (0.0, 1.0)}

    def links(step):
        return np.array([way for axis in step[:2] for way in ways[axis]])

    used, order = np.zeros(4), []
    while left:
        step = min(left, key=lambda t: (np.max(used + links(t)), -np.sum(links(t)), t))
        left.remove(step)
        used = used + links(step)
        order.append(step)
    return order


def exchange_kernel(
    blks,
    subs,
    syn_hbm,
    obs_hbm,
    table_hbm,
    first_hbm,
    second_hbm,
    mask_hbm,
    weight_hbm,
    owner_hbm,
    element_hbm,
    summed,
    traces,
    table,
    first,
    second,
    mask,
    weight,
    owner,
    element,
    spec,
    halo,
    list_out,
    list_over,
    lists,
    lists_prev,
    labels,
    outgoing,
    received,
    load_sems,
    list_send,
    list_recv,
    over_send,
    over_recv,
    halo_send,
    halo_recv,
    entered,
    joined,
    y_send,
    y_recv,
    z_send,
    z_recv,
    all_send,
    all_recv,
):
    devices = blks * subs
    blk, sub = lax.axis_index("blk"), lax.axis_index("sub")
    me = blk * subs + sub
    rows = spec.shape[1]
    blocks = first.shape[0]
    def around(at, step, size):
        there = at + step
        return jnp.where(there >= size, there - size, there)

    subs_there = [around(sub, step, subs) for step in range(1, subs)]
    blks_there = [around(blk, step, blks) for step in range(1, blks)]
    blk_after, blk_before = blks_there[0], blks_there[-1]
    after = (jnp.where(sub == subs - 1, blk_after, blk), subs_there[0])
    before = (jnp.where(sub == 0, blk_before, blk), subs_there[-1])

    pairs = [
        (table_hbm, table),
        (syn_hbm.at[0], traces.at[0, pl.ds(0, rows)]),
        (obs_hbm.at[0], traces.at[0, pl.ds(rows, rows)]),
        (owner_hbm, owner),
        (element_hbm, element),
        (first_hbm, first),
        (second_hbm, second),
        (mask_hbm, mask),
        (weight_hbm, weight),
        (syn_hbm.at[1], traces.at[1, pl.ds(0, rows)]),
        (obs_hbm.at[1], traces.at[1, pl.ds(rows, rows)]),
        (syn_hbm.at[2], traces.at[2, pl.ds(0, rows)]),
        (obs_hbm.at[2], traces.at[2, pl.ds(rows, rows)]),
    ]
    loads = [
        pltpu.make_async_copy(src, dst, load_sems.at[i]) for i, (src, dst) in enumerate(pairs)
    ]
    for load in loads:
        load.start()

    z, y = lax.div(blk, 4), lax.rem(blk, 4)
    has_before, has_after = me > 0, me < devices - 1
    row_before, row_after = blk > 0, blk < blks - 1
    barrier = pltpu.get_barrier_semaphore()

    def greet(there):
        pl.semaphore_signal(barrier, inc=1, device_id=there, device_id_type=MESH)

    def greet_column(there, carry):
        greet((there, sub))
        return carry

    for there in subs_there:
        greet((blk, there))
    lax.fori_loop(blk + 1, blks, greet_column, 0)

    @pl.when((sub == 0) & row_before)
    def _():
        for s in range(subs):
            greet((blk_before, s))

    @pl.when((sub == subs - 1) & row_after)
    def _():
        greet((blk_after, 0))

    for i in range(3):
        pl.semaphore_signal(entered.at[i], inc=1)
    greetings = (
        (subs - 1)
        + jnp.where(row_after, 1, 0)
        + jnp.where((sub == 0) & row_before, 1, 0)
        + blk
    )

    def transform(c):
        both = dot_plain(traces[c], table[...]).astype(BF16)
        spec[2 * c] = both[:rows]
        spec[2 * c + 1] = both[rows:]

    for i in range(3):
        loads[i].wait()
    transform(0)

    pl.semaphore_wait(barrier, greetings)

    def halo_copies(c):
        q = pl.ds(2 * c, 2)
        return [
            pltpu.make_async_remote_copy(
                src_ref=spec.at[q, pl.ds(0, BLOCK)],
                dst_ref=halo.at[q, pl.ds(BLOCK, BLOCK)],
                send_sem=halo_send.at[0, c],
                recv_sem=halo_recv.at[0, c],
                device_id=before,
                device_id_type=MESH,
            ),
            pltpu.make_async_remote_copy(
                src_ref=spec.at[q, pl.ds(rows - BLOCK, BLOCK)],
                dst_ref=halo.at[q, pl.ds(0, BLOCK)],
                send_sem=halo_send.at[1, c],
                recv_sem=halo_recv.at[1, c],
                device_id=after,
                device_id_type=MESH,
            ),
        ]

    halos = [halo_copies(c) for c in range(3)]

    def start_halos(c):
        @pl.when(has_before)
        def _():
            halos[c][0].start()

        @pl.when(has_after)
        def _():
            halos[c][1].start()

    start_halos(0)

    def answer(there, carry):
        kind = jnp.where(lax.div(there, 4) == z, 0, jnp.where(z == 1, 1, 2))
        pl.semaphore_signal(
            entered.at[kind], inc=1, device_id=(there, sub), device_id_type=MESH
        )
        return carry

    @pl.when(z < 3)
    def _():
        lax.fori_loop(0, blk, answer, 0)


    for i in range(3, 5):
        loads[i].wait()
    lane = lax.broadcasted_iota(jnp.int32, (rows, rows), 1)
    line = lax.broadcasted_iota(jnp.int32, (rows, rows), 0)
    owner_row = owner[...]

    def column(row):
        return jnp.sum(jnp.where(lane == line, row, 0), axis=1, keepdims=True)

    owner_column, element_column = column(owner_row), column(element[...]).astype(F32)
    same = owner_column == owner_row
    rank_column = jnp.sum(jnp.where(same & (lane < line), 1, 0), axis=1, keepdims=True)
    label_rows = []
    for k in range(2):
        chosen = ((owner_column == lane) & (rank_column == k)).astype(F32)
        label_rows.append(
            jnp.sum(chosen * (element_column - rows), axis=0, keepdims=True) + float(rows)
        )

    for i in range(5, 9):
        loads[i].wait()
    base = (blk * blocks + lax.broadcasted_iota(jnp.int32, (blocks, NF), 0)) * BLOCK
    code = ((first[...] - base) * (2 * BLOCK) + (second[...] - base)).astype(F32)
    slot_weight = weight[...] * mask[...].astype(F32)
    zero_row = jnp.zeros((1, NF), F32)
    for s in range(subs):
        lines = [max(2 * s - 1, 0), 2 * s, 2 * s + 1]
        list_out[s] = jnp.concatenate(
            [code[i : i + 1] for i in lines]
            + [slot_weight[i : i + 1] for i in lines]
            + label_rows,
            axis=0,
        )
    list_over[...] = jnp.concatenate(
        [code[blocks - 1 : blocks]]
        + [zero_row] * 2
        + [slot_weight[blocks - 1 : blocks]]
        + [zero_row] * 4,
        axis=0,
    )
    lists[sub] = list_out[sub]

    for there in subs_there:
        pltpu.make_async_remote_copy(
            src_ref=list_out.at[there],
            dst_ref=lists.at[sub],
            send_sem=list_send,
            recv_sem=list_recv,
            device_id=(blk, there),
            device_id_type=MESH,
        ).start()
    over = pltpu.make_async_remote_copy(
        src_ref=list_over,
        dst_ref=lists_prev.at[sub],
        send_sem=over_send,
        recv_sem=over_recv,
        device_id=(blk_after, 0),
        device_id_type=MESH,
    )

    @pl.when(row_after)
    def _():
        over.start()


    for c in (1, 2):
        loads[7 + 2 * c].wait()
        loads[8 + 2 * c].wait()
        transform(c)
        start_halos(c)

    @pl.when(jnp.logical_not(has_before))
    def _():
        halo[:, :BLOCK] = jnp.zeros((6, BLOCK, 2 * NF), BF16)

    @pl.when(jnp.logical_not(has_after))
    def _():
        halo[:, BLOCK:] = jnp.zeros((6, BLOCK, 2 * NF), BF16)

    @pl.when(z == 3)
    def _():
        lax.fori_loop(0, blk, answer, 0)

    def tell_row(which):
        for there in subs_there:
            pl.semaphore_signal(
                joined.at[which], inc=1, device_id=(blk, there), device_id_type=MESH
            )

    @pl.when(z >= 2)
    def _():
        tell_row(0)

    rank_row = jnp.sum(jnp.where(same & (line < lane), 1, 0), axis=0, keepdims=True)
    target = owner_row * 4 + rank_row * 2
    slot = lax.broadcasted_iota(jnp.int32, (4 * devices, 2 * rows), 0)
    placement = (slot == jnp.concatenate([target, target + 1], axis=1)).astype(F32).astype(BF16)

    def stations(c):
        return (spec[2 * c], spec[2 * c + 1])

    own = [features(stations(c)) for c in range(3)]

    others = pl.ds(0, subs - 1)
    pltpu.make_async_copy(lists.at[others], lists.at[others], list_recv).wait()

    @pl.when((sub == 0) & row_before)
    def _():
        pltpu.make_async_copy(lists_prev, lists_prev, over_recv).wait()

    @pl.when((sub == 0) & jnp.logical_not(row_before))
    def _():
        lists_prev[...] = jnp.zeros(lists_prev.shape, F32)

    @pl.when(sub != 0)
    def _():
        lists_prev[...] = lists[...]

    def unpacked(ref, k):
        codes = ref[:, k, :].astype(jnp.int32)
        return codes >> 7, codes & 127, ref[:, 3 + k, :]

    first0, second0, weight0 = unpacked(lists_prev, 0)
    first1, second1, weight1 = unpacked(lists, 1)
    first2, second2, weight2 = unpacked(lists, 2)
    to_prev = dot_rows(spread_weights(second0, weight0, BLOCK, BLOCK), spread(first0, rows, 0))
    upper = dot_rows(spread_weights(first1, weight1, BLOCK, 0), spread(second1, rows, 0))
    lower = dot_rows(spread_weights(first2, weight2, BLOCK, 0), spread(second2, rows, 0))
    half = lax.broadcasted_iota(jnp.int32, (BLOCK, rows), 1) >= BLOCK
    inside = jnp.where(half, pltpu.roll(lower, BLOCK, 1), 0.0)
    one_way = jnp.concatenate([upper, inside], axis=0)
    link_own = for_features(one_way + one_way.T)
    link_halo = for_features(jnp.concatenate([to_prev, jnp.where(half, lower, 0.0)], axis=0))
    inner = [dot_plain(link_own, own[c]) for c in range(3)]

    def adjoint(c):
        sums = inner[c] + dot_plain(link_halo, features((halo[2 * c], halo[2 * c + 1])))
        g1r, g1i, g2r, g2i = (sums[:, i * NF : (i + 1) * NF] for i in range(4))
        x, o = stations(c)
        xr, xi = x[:, :NF].astype(F32), x[:, NF:].astype(F32)
        dr, di = xr - o[:, :NF].astype(F32), xi - o[:, NF:].astype(F32)
        real = (xr * g1r - xi * g1i) + (dr * g2r - di * g2i)
        imag = (xr * g1i + xi * g1r) + (dr * g2i + di * g2r)
        return jnp.concatenate([real, imag], axis=0).astype(BF16)

    def handle(together):
        for c in together:

            @pl.when(has_after)
            def _():
                halos[c][0].wait_recv()

            @pl.when(has_before)
            def _():
                halos[c][1].wait_recv()

        placed = dot_plain(placement, jnp.concatenate([adjoint(c) for c in together], axis=1))
        for i, c in enumerate(together):
            outgoing[:, c] = (
                placed[:, i * NF : (i + 1) * NF].astype(BF16).reshape(devices, 4, NF)
            )

    handle((0, 1))

    pl.semaphore_wait(entered.at[0], 4 - y)
    labels[z, y] = jnp.concatenate([lists[:, 6, :], lists[:, 7, :]], axis=0).astype(BF16)
    for step in range(1, 4):
        pltpu.make_async_remote_copy(
            src_ref=labels.at[z, y],
            dst_ref=labels.at[z, y],
            send_sem=y_send,
            recv_sem=y_recv,
            device_id=(z * 4 + around(y, step, 4), sub),
            device_id_type=MESH,
        ).start()

    pl.semaphore_wait(entered.at[1], 1 + jnp.where(z == 0, 4, 0))

    @pl.when(z < 2)
    def _():
        tell_row(0)

    handle((2,))

    def rest_entered(answers):
        pl.semaphore_wait(entered.at[2], 1 + answers)
        tell_row(1)

    @pl.when(z >= 2)
    def _():
        rest_entered(jnp.where(z == 2, 4, 0))

    def turns(at, size):
        return [at] + [around(at, step, size) for step in range(1, size)]

    core, chip = lax.rem(sub, 2), lax.div(me, 2)
    y_to, x_to = turns(y, 4), turns(lax.div(sub, 2), 4)
    core_to = [core, 1 - core]
    received[core, chip] = outgoing[me]

    def deliver(plane, step):
        dy, dx, other = step
        blk_to, sub_to = plane * 4 + y_to[dy], x_to[dx] * 2 + core_to[other]
        pltpu.make_async_remote_copy(
            src_ref=outgoing.at[blk_to * subs + sub_to],
            dst_ref=received.at[core, chip],
            send_sem=all_send,
            recv_sem=all_recv.at[other],
            device_id=(blk_to, sub_to),
            device_id_type=MESH,
        ).start()

    def deliver_planes(planes, steps):
        for step in steps:
            for plane in planes:
                if step != (0, 0, 0):
                    deliver(plane, step)
                    continue

                @pl.when(z != plane)
                def _():
                    deliver(plane, step)

    order = spread_order() + [(0, 0, 0)]
    pl.semaphore_wait(joined.at[0], subs - 1)
    deliver_planes((0, 1), order[:16])

    @pl.when(z < 2)
    def _():
        rest_entered(8)

    some = pl.ds(0, 3)
    pltpu.make_async_copy(labels.at[0, some], labels.at[0, some], y_recv).wait()
    for step in range(1, 4):
        pltpu.make_async_remote_copy(
            src_ref=labels.at[z],
            dst_ref=labels.at[z],
            send_sem=z_send,
            recv_sem=z_recv,
            device_id=(around(z, step, 4) * 4 + y, sub),
            device_id_type=MESH,
        ).start()

    deliver_planes((0, 1), order[16:])
    pl.semaphore_wait(joined.at[1], subs - 1)
    deliver_planes((2, 3), order)

    pltpu.make_async_copy(labels.at[some], labels.at[some], z_recv).wait()
    by_owner = labels[...].reshape(2 * devices, NF)
    arrived = lax.broadcasted_iota(jnp.int32, (2 * devices, 2 * devices), 1)
    held = lax.broadcasted_iota(jnp.int32, (2 * devices, 2 * devices), 0)
    sub_bits = subs.bit_length() - 1
    wanted = (
        ((arrived >> (sub_bits + 1)) << (sub_bits + 1))
        + (((arrived >> 1) & 1) << sub_bits)
        + (((arrived >> 2) & (subs // 2 - 1)) << 1)
    )
    owner_line = lax.broadcasted_iota(jnp.int32, (rows, 2 * devices), 0)

    def collector(source_core):
        repeated = lax.dot_general(
            by_owner,
            (held == wanted + source_core).astype(F32).astype(BF16),
            (((0,), (0,)), ((), ())),
            preferred_element_type=F32,
        )
        label = jnp.sum(jnp.where(owner_line == me, repeated, 0.0), axis=0, keepdims=True)
        return jnp.concatenate(
            [
                ((label == owner_line.astype(F32)) & ((arrived[:rows] & 1) == i)).astype(F32)
                for i in range(2)
            ],
            axis=0,
        ).astype(BF16)

    collect_other, collect_same = collector(1 - core), collector(core)

    def sums(collect, source_core):
        values = [received[source_core, :, c].reshape(2 * devices, NF) for c in range(3)]
        return dot_plain(collect, jnp.concatenate(values, axis=1))

    pltpu.make_async_copy(received.at[0], received.at[0], all_recv.at[1]).wait()
    first_sums = sums(collect_other, 1 - core)
    most = pl.ds(0, devices // 2 - 1)
    pltpu.make_async_copy(received.at[0, most], received.at[0, most], all_recv.at[0]).wait()
    total = (first_sums + sums(collect_same, core)).astype(BF16)
    for c in range(3):
        summed[c * rows : (c + 1) * rows, :NF] = total[:rows, c * NF : (c + 1) * NF]
        summed[c * rows : (c + 1) * rows, NF:] = total[rows:, c * NF : (c + 1) * NF]

    for c in range(3):

        @pl.when(has_before)
        def _():
            halos[c][0].wait_send()

        @pl.when(has_after)
        def _():
            halos[c][1].wait_send()

    pltpu.make_async_copy(list_out.at[others], list_out.at[others], list_send).wait()

    @pl.when(row_after)
    def _():
        over.wait_send()

    pltpu.make_async_copy(labels.at[0, some], labels.at[0, some], y_send).wait()
    pltpu.make_async_copy(labels.at[some], labels.at[some], z_send).wait()
    most = pl.ds(0, devices - 1)
    pltpu.make_async_copy(outgoing.at[most], outgoing.at[most], all_send).wait()


def exchange(blks, subs, syn, obs, table, first, second, mask, weight, owner, element):
    devices = blks * subs
    samples, rows = syn.shape[2], syn.shape[1]
    in_hbm = pl.BlockSpec(memory_space=pltpu.HBM)
    dma = pltpu.SemaphoreType.DMA
    return pl.pallas_call(
        functools.partial(exchange_kernel, blks, subs),
        out_shape=pltpu.VMEM((3 * rows, 2 * NF), BF16),
        in_specs=[in_hbm] * 9,
        out_specs=pl.BlockSpec(memory_space=pltpu.VMEM),
        scratch_shapes=[
            pltpu.VMEM((3, 2 * rows, samples), BF16),
            pltpu.VMEM(table.shape, BF16),
            pltpu.VMEM(first.shape, jnp.int32),
            pltpu.VMEM(second.shape, jnp.int32),
            pltpu.VMEM(mask.shape, jnp.int32),
            pltpu.VMEM(weight.shape, F32),
            pltpu.VMEM(owner.shape, jnp.int32),
            pltpu.VMEM(element.shape, jnp.int32),
            pltpu.VMEM((6, rows, 2 * NF), BF16),
            pltpu.VMEM((6, 2 * BLOCK, 2 * NF), BF16),
            pltpu.VMEM((subs, 8, NF), F32),
            pltpu.VMEM((8, NF), F32),
            pltpu.VMEM((subs, 8, NF), F32),
            pltpu.VMEM((subs, 8, NF), F32),
            pltpu.VMEM((4, blks // 4, 2 * subs, NF), BF16),
            pltpu.VMEM((devices, 3, 4, NF), BF16),
            pltpu.VMEM((2, devices // 2, 3, 4, NF), BF16),
            dma((13,)),
            dma,
            dma,
            dma,
            dma,
            dma((2, 3)),
            dma((2, 3)),
            pltpu.SemaphoreType.REGULAR((3,)),
            pltpu.SemaphoreType.REGULAR((2,)),
            dma,
            dma,
            dma,
            dma,
            dma,
            dma((2,)),
        ],
        compiler_params=pltpu.CompilerParams(
            collective_id=0, has_side_effects=True, vmem_limit_bytes=60 * 2**20
        ),
        cost_estimate=pl.CostEstimate(
            flops=2 * 10**9, bytes_accessed=3 * 10**6, transcendentals=0
        ),
        name="exchange",
    )(syn, obs, table, first, second, mask, weight, owner, element)


def finish_kernel(summed, table, out, result, sems):
    samples = result.shape[1]
    chunk = samples // sems.shape[0]
    copies = []
    for n in range(sems.shape[0]):
        columns = pl.ds(n * chunk, chunk)
        result[:, columns] = dot_plain(summed[...], table[:, columns])
        copies.append(
            pltpu.make_async_copy(result.at[:, columns], out.at[:, columns], sems.at[n])
        )
        copies[-1].start()
    for copy in copies:
        copy.wait()


def finish(summed, table):
    count, samples = summed.shape[0], table.shape[1]
    in_vmem = pl.BlockSpec(memory_space=pltpu.VMEM)
    out = pl.pallas_call(
        finish_kernel,
        out_shape=jax.ShapeDtypeStruct((count, samples), F32),
        in_specs=[in_vmem] * 2,
        out_specs=pl.BlockSpec(memory_space=pl.ANY),
        scratch_shapes=[
            pltpu.VMEM((count, samples), F32),
            pltpu.SemaphoreType.DMA((4,)),
        ],
        compiler_params=pltpu.CompilerParams(vmem_limit_bytes=40 * 2**20),
        cost_estimate=pl.CostEstimate(
            flops=7 * 10**8, bytes_accessed=3 * 10**6, transcendentals=0
        ),
        name="finish",
    )(summed, table)
    return out.reshape(3, count // 3, samples)


def on_device(
    blks,
    subs,
    synthetic,
    observed,
    pair_first,
    pair_second,
    pair_mask,
    pair_weight,
    station_owner,
    station_element,
):
    rows, _, samples = synthetic.shape
    forward, inverse = dft_tables(samples, NF)
    summed = exchange(
        blks,
        subs,
        jnp.transpose(synthetic, (1, 0, 2)),
        jnp.transpose(observed, (1, 0, 2)),
        jnp.asarray(forward),
        pair_first,
        pair_second,
        pair_mask,
        pair_weight,
        station_owner.reshape(1, rows),
        station_element.reshape(1, rows),
    )
    out = finish(summed, jnp.asarray(inverse))
    return jnp.transpose(out, (1, 0, 2))


def solution(mesh):
    blks, subs = mesh.shape["blk"], mesh.shape["sub"]
    return jax.shard_map(
        functools.partial(on_device, blks, subs),
        mesh=mesh,
        in_specs=(
            P(("blk", "sub"), None, None),
            P(("blk", "sub"), None, None),
            P("blk", "sub"),
            P("blk", "sub"),
            P("blk", "sub"),
            P("blk", "sub"),
            P(("blk", "sub"), None),
            P(("blk", "sub")),
        ),
        out_specs=P(("blk", "sub"), None, None),
        check_vma=False,
    )
```

```python
import functools
import itertools
import math

import jax
import jax.numpy as jnp
import numpy as np
from jax import lax
from jax.experimental import pallas as pl
from jax.experimental.pallas import tpu as pltpu
from jax.sharding import PartitionSpec as P

MESH = pl.DeviceIdType.MESH
NF = 128
BLOCK = 64
F32 = jnp.float32
BF16 = jnp.bfloat16


def dft_tables(samples, freqs):
    phase = (np.arange(samples)[:, None] * np.arange(freqs)[None, :]) % samples
    angles = phase.astype(np.float64) * (2.0 * math.pi / samples)
    scale = 1.0 / math.sqrt(samples)
    cosine, sine = np.cos(angles) * scale, np.sin(angles) * scale
    forward = np.concatenate([cosine, -sine], axis=1).astype(np.float32)
    doubled = np.where(np.arange(freqs) == 0, 1.0, 2.0)[:, None]
    inverse = np.concatenate([cosine.T * doubled, -sine.T * doubled], axis=0)
    return forward.astype(jnp.bfloat16), inverse.astype(np.float32).astype(jnp.bfloat16)


def in_two(x):
    high = x.astype(BF16)
    return high, (x - high.astype(F32)).astype(BF16)


def dot_rows(a, b):
    return lax.dot_general(a, b, (((1,), (1,)), ((), ())), preferred_element_type=F32)


def dot_plain(a, b):
    return jnp.dot(a, b, preferred_element_type=F32)


def features(pair):
    xr, xi = pair[0][:, :NF].astype(F32), pair[0][:, NF:].astype(F32)
    o_r, o_i = pair[1][:, :NF].astype(F32), pair[1][:, NF:].astype(F32)
    dr, di = xr - o_r, xi - o_i
    parts = [dr * xr + di * xi, dr * xi - di * xr, o_r * xr + o_i * xi, o_r * xi - o_i * xr]
    both = [in_two(p) for p in parts]
    return jnp.concatenate(
        [jnp.concatenate([b[i] for b in both], axis=1) for i in range(2)], axis=0
    )


def for_features(links):
    return jnp.concatenate([links.astype(BF16)] * 2, axis=1)


def spread(rows, count, shift):
    index = lax.broadcasted_iota(jnp.int32, (count, NF), 0) + shift
    return jnp.concatenate(
        [(index == rows[s : s + 1]).astype(F32).astype(BF16) for s in range(rows.shape[0])], axis=1
    )


def spread_weights(rows, weights, count, shift):
    index = lax.broadcasted_iota(jnp.int32, (count, NF), 0) + shift
    return jnp.concatenate(
        [
            jnp.where(index == rows[s : s + 1], weights[s : s + 1], 0.0).astype(BF16)
            for s in range(rows.shape[0])
        ],
        axis=1,
    )


def spread_order():
    entered = ((0.0, 0.65, 1.1, 1.5), (0.0, 0.8, 1.2, 1.25))

    def lead(step):
        return sum(
            max(at[source] - at[(source + by) % 4] for source in range(4))
            for at, by in zip(entered, step)
        )

    steps = list(itertools.product(range(4), range(4), range(2)))[1:]
    return sorted(steps, key=lambda step: (-lead(step), step))


def exchange_kernel(
    blks,
    subs,
    syn_hbm,
    obs_hbm,
    table_hbm,
    first_hbm,
    second_hbm,
    mask_hbm,
    weight_hbm,
    owner_hbm,
    element_hbm,
    summed,
    traces,
    table,
    first,
    second,
    mask,
    weight,
    owner,
    element,
    spec,
    halo,
    list_out,
    list_over,
    lists,
    lists_prev,
    labels,
    outgoing,
    received,
    load_sems,
    list_send,
    list_recv,
    over_send,
    over_recv,
    halo_send,
    halo_recv,
    entered,
    joined,
    y_send,
    y_recv,
    z_send,
    z_recv,
    all_send,
    all_recv,
):
    devices = blks * subs
    blk, sub = lax.axis_index("blk"), lax.axis_index("sub")
    me = blk * subs + sub
    rows = spec.shape[1]
    blocks = first.shape[0]
    def around(at, step, size):
        there = at + step
        return jnp.where(there >= size, there - size, there)

    subs_there = [around(sub, step, subs) for step in range(1, subs)]
    blks_there = [around(blk, step, blks) for step in range(1, blks)]
    blk_after, blk_before = blks_there[0], blks_there[-1]
    after = (jnp.where(sub == subs - 1, blk_after, blk), subs_there[0])
    before = (jnp.where(sub == 0, blk_before, blk), subs_there[-1])

    pairs = [
        (table_hbm, table),
        (syn_hbm.at[0], traces.at[0, pl.ds(0, rows)]),
        (obs_hbm.at[0], traces.at[0, pl.ds(rows, rows)]),
        (owner_hbm, owner),
        (element_hbm, element),
        (first_hbm, first),
        (second_hbm, second),
        (mask_hbm, mask),
        (weight_hbm, weight),
        (syn_hbm.at[1], traces.at[1, pl.ds(0, rows)]),
        (obs_hbm.at[1], traces.at[1, pl.ds(rows, rows)]),
        (syn_hbm.at[2], traces.at[2, pl.ds(0, rows)]),
        (obs_hbm.at[2], traces.at[2, pl.ds(rows, rows)]),
    ]
    loads = [
        pltpu.make_async_copy(src, dst, load_sems.at[i]) for i, (src, dst) in enumerate(pairs)
    ]
    for load in loads:
        load.start()

    z, y = lax.div(blk, 4), lax.rem(blk, 4)
    has_before, has_after = me > 0, me < devices - 1
    row_before, row_after = blk > 0, blk < blks - 1
    barrier = pltpu.get_barrier_semaphore()

    def greet(there):
        pl.semaphore_signal(barrier, inc=1, device_id=there, device_id_type=MESH)

    def greet_column(there, carry):
        greet((there, sub))
        return carry

    for there in subs_there:
        greet((blk, there))
    lax.fori_loop(blk + 1, blks, greet_column, 0)

    @pl.when((sub == 0) & row_before)
    def _():
        for s in range(subs):
            greet((blk_before, s))

    @pl.when((sub == subs - 1) & row_after)
    def _():
        greet((blk_after, 0))

    for i in range(3):
        pl.semaphore_signal(entered.at[i], inc=1)
    greetings = (
        (subs - 1)
        + jnp.where(row_after, 1, 0)
        + jnp.where((sub == 0) & row_before, 1, 0)
        + blk
    )

    def transform(c):
        both = dot_plain(traces[c], table[...]).astype(BF16)
        spec[2 * c] = both[:rows]
        spec[2 * c + 1] = both[rows:]

    for i in range(3):
        loads[i].wait()
    transform(0)

    pl.semaphore_wait(barrier, greetings)

    def halo_copies(c):
        q = pl.ds(2 * c, 2)
        return [
            pltpu.make_async_remote_copy(
                src_ref=spec.at[q, pl.ds(0, BLOCK)],
                dst_ref=halo.at[q, pl.ds(BLOCK, BLOCK)],
                send_sem=halo_send.at[0, c],
                recv_sem=halo_recv.at[0, c],
                device_id=before,
                device_id_type=MESH,
            ),
            pltpu.make_async_remote_copy(
                src_ref=spec.at[q, pl.ds(rows - BLOCK, BLOCK)],
                dst_ref=halo.at[q, pl.ds(0, BLOCK)],
                send_sem=halo_send.at[1, c],
                recv_sem=halo_recv.at[1, c],
                device_id=after,
                device_id_type=MESH,
            ),
        ]

    halos = [halo_copies(c) for c in range(3)]

    def start_halos(c):
        @pl.when(has_before)
        def _():
            halos[c][0].start()

        @pl.when(has_after)
        def _():
            halos[c][1].start()

    start_halos(0)

    def answer(there, carry):
        kind = jnp.where(lax.div(there, 4) == z, 0, jnp.where(z == 1, 1, 2))
        pl.semaphore_signal(
            entered.at[kind], inc=1, device_id=(there, sub), device_id_type=MESH
        )
        return carry

    @pl.when(z < 3)
    def _():
        lax.fori_loop(0, blk, answer, 0)


    for i in range(3, 5):
        loads[i].wait()
    lane = lax.broadcasted_iota(jnp.int32, (rows, rows), 1)
    line = lax.broadcasted_iota(jnp.int32, (rows, rows), 0)
    owner_row = owner[...]

    def column(row):
        return jnp.sum(jnp.where(lane == line, row, 0), axis=1, keepdims=True)

    owner_column, element_column = column(owner_row), column(element[...]).astype(F32)
    same = owner_column == owner_row
    rank_column = jnp.sum(jnp.where(same & (lane < line), 1, 0), axis=1, keepdims=True)
    label_rows = []
    for k in range(2):
        chosen = ((owner_column == lane) & (rank_column == k)).astype(F32)
        label_rows.append(
            jnp.sum(chosen * (element_column - rows), axis=0, keepdims=True) + float(rows)
        )

    for i in range(5, 9):
        loads[i].wait()
    base = (blk * blocks + lax.broadcasted_iota(jnp.int32, (blocks, NF), 0)) * BLOCK
    code = ((first[...] - base) * (2 * BLOCK) + (second[...] - base)).astype(F32)
    slot_weight = weight[...] * mask[...].astype(F32)
    zero_row = jnp.zeros((1, NF), F32)
    for s in range(subs):
        lines = [max(2 * s - 1, 0), 2 * s, 2 * s + 1]
        list_out[s] = jnp.concatenate(
            [code[i : i + 1] for i in lines]
            + [slot_weight[i : i + 1] for i in lines]
            + label_rows,
            axis=0,
        )
    list_over[...] = jnp.concatenate(
        [code[blocks - 1 : blocks]]
        + [zero_row] * 2
        + [slot_weight[blocks - 1 : blocks]]
        + [zero_row] * 4,
        axis=0,
    )
    lists[sub] = list_out[sub]

    for there in subs_there:
        pltpu.make_async_remote_copy(
            src_ref=list_out.at[there],
            dst_ref=lists.at[sub],
            send_sem=list_send,
            recv_sem=list_recv,
            device_id=(blk, there),
            device_id_type=MESH,
        ).start()
    over = pltpu.make_async_remote_copy(
        src_ref=list_over,
        dst_ref=lists_prev.at[sub],
        send_sem=over_send,
        recv_sem=over_recv,
        device_id=(blk_after, 0),
        device_id_type=MESH,
    )

    @pl.when(row_after)
    def _():
        over.start()


    for c in (1, 2):
        loads[7 + 2 * c].wait()
        loads[8 + 2 * c].wait()
        transform(c)
        start_halos(c)

    @pl.when(jnp.logical_not(has_before))
    def _():
        halo[:, :BLOCK] = jnp.zeros((6, BLOCK, 2 * NF), BF16)

    @pl.when(jnp.logical_not(has_after))
    def _():
        halo[:, BLOCK:] = jnp.zeros((6, BLOCK, 2 * NF), BF16)

    @pl.when(z == 3)
    def _():
        lax.fori_loop(0, blk, answer, 0)

    def tell_row(which):
        for there in subs_there:
            pl.semaphore_signal(
                joined.at[which], inc=1, device_id=(blk, there), device_id_type=MESH
            )

    @pl.when(z >= 2)
    def _():
        tell_row(0)

    rank_row = jnp.sum(jnp.where(same & (line < lane), 1, 0), axis=0, keepdims=True)
    target = owner_row * 4 + rank_row * 2
    slot = lax.broadcasted_iota(jnp.int32, (4 * devices, 2 * rows), 0)
    placement = (slot == jnp.concatenate([target, target + 1], axis=1)).astype(F32).astype(BF16)

    def stations(c):
        return (spec[2 * c], spec[2 * c + 1])

    own = [features(stations(c)) for c in range(3)]

    others = pl.ds(0, subs - 1)
    pltpu.make_async_copy(lists.at[others], lists.at[others], list_recv).wait()

    @pl.when((sub == 0) & row_before)
    def _():
        pltpu.make_async_copy(lists_prev, lists_prev, over_recv).wait()

    @pl.when((sub == 0) & jnp.logical_not(row_before))
    def _():
        lists_prev[...] = jnp.zeros(lists_prev.shape, F32)

    @pl.when(sub != 0)
    def _():
        lists_prev[...] = lists[...]

    def unpacked(ref, k):
        codes = ref[:, k, :].astype(jnp.int32)
        return codes >> 7, codes & 127, ref[:, 3 + k, :]

    first0, second0, weight0 = unpacked(lists_prev, 0)
    first1, second1, weight1 = unpacked(lists, 1)
    first2, second2, weight2 = unpacked(lists, 2)
    to_prev = dot_rows(spread_weights(second0, weight0, BLOCK, BLOCK), spread(first0, rows, 0))
    upper = dot_rows(spread_weights(first1, weight1, BLOCK, 0), spread(second1, rows, 0))
    lower = dot_rows(spread_weights(first2, weight2, BLOCK, 0), spread(second2, rows, 0))
    half = lax.broadcasted_iota(jnp.int32, (BLOCK, rows), 1) >= BLOCK
    inside = jnp.where(half, pltpu.roll(lower, BLOCK, 1), 0.0)
    one_way = jnp.concatenate([upper, inside], axis=0)
    link_own = for_features(one_way + one_way.T)
    link_halo = for_features(jnp.concatenate([to_prev, jnp.where(half, lower, 0.0)], axis=0))
    inner = [dot_plain(link_own, own[c]) for c in range(3)]

    def adjoint(c):
        sums = inner[c] + dot_plain(link_halo, features((halo[2 * c], halo[2 * c + 1])))
        g1r, g1i, g2r, g2i = (sums[:, i * NF : (i + 1) * NF] for i in range(4))
        x, o = stations(c)
        xr, xi = x[:, :NF].astype(F32), x[:, NF:].astype(F32)
        dr, di = xr - o[:, :NF].astype(F32), xi - o[:, NF:].astype(F32)
        real = (xr * g1r - xi * g1i) + (dr * g2r - di * g2i)
        imag = (xr * g1i + xi * g1r) + (dr * g2i + di * g2r)
        return jnp.concatenate([real, imag], axis=0).astype(BF16)

    def handle(together):
        for c in together:

            @pl.when(has_after)
            def _():
                halos[c][0].wait_recv()

            @pl.when(has_before)
            def _():
                halos[c][1].wait_recv()

        placed = dot_plain(placement, jnp.concatenate([adjoint(c) for c in together], axis=1))
        for i, c in enumerate(together):
            outgoing[:, c] = (
                placed[:, i * NF : (i + 1) * NF].astype(BF16).reshape(devices, 4, NF)
            )

    handle((0, 1))

    pl.semaphore_wait(entered.at[0], 4 - y)
    labels[z, y] = jnp.concatenate([lists[:, 6, :], lists[:, 7, :]], axis=0).astype(BF16)
    for step in range(1, 4):
        pltpu.make_async_remote_copy(
            src_ref=labels.at[z, y],
            dst_ref=labels.at[z, y],
            send_sem=y_send,
            recv_sem=y_recv,
            device_id=(z * 4 + around(y, step, 4), sub),
            device_id_type=MESH,
        ).start()

    pl.semaphore_wait(entered.at[1], 1 + jnp.where(z == 0, 4, 0))

    @pl.when(z < 2)
    def _():
        tell_row(0)

    handle((2,))

    def rest_entered(answers):
        pl.semaphore_wait(entered.at[2], 1 + answers)
        tell_row(1)

    @pl.when(z >= 2)
    def _():
        rest_entered(jnp.where(z == 2, 4, 0))

    def turns(at, size):
        return [at] + [around(at, step, size) for step in range(1, size)]

    core, chip = lax.rem(sub, 2), lax.div(me, 2)
    y_to, x_to = turns(y, 4), turns(lax.div(sub, 2), 4)
    core_to = [core, 1 - core]
    received[core, chip] = outgoing[me]

    def deliver(plane, step):
        dy, dx, other = step
        blk_to, sub_to = plane * 4 + y_to[dy], x_to[dx] * 2 + core_to[other]
        pltpu.make_async_remote_copy(
            src_ref=outgoing.at[blk_to * subs + sub_to],
            dst_ref=received.at[core, chip],
            send_sem=all_send,
            recv_sem=all_recv.at[other],
            device_id=(blk_to, sub_to),
            device_id_type=MESH,
        ).start()

    def deliver_plane(plane):
        for step in spread_order():
            deliver(plane, step)

        @pl.when(z != plane)
        def _():
            deliver(plane, (0, 0, 0))

    pl.semaphore_wait(joined.at[0], subs - 1)
    deliver_plane(0)

    @pl.when(z < 2)
    def _():
        rest_entered(8)

    some = pl.ds(0, 3)
    pltpu.make_async_copy(labels.at[0, some], labels.at[0, some], y_recv).wait()
    for step in range(1, 4):
        pltpu.make_async_remote_copy(
            src_ref=labels.at[z],
            dst_ref=labels.at[z],
            send_sem=z_send,
            recv_sem=z_recv,
            device_id=(around(z, step, 4) * 4 + y, sub),
            device_id_type=MESH,
        ).start()

    deliver_plane(1)
    pl.semaphore_wait(joined.at[1], subs - 1)
    deliver_plane(2)
    deliver_plane(3)

    pltpu.make_async_copy(labels.at[some], labels.at[some], z_recv).wait()
    by_owner = labels[...].reshape(2 * devices, NF)
    arrived = lax.broadcasted_iota(jnp.int32, (2 * devices, 2 * devices), 1)
    held = lax.broadcasted_iota(jnp.int32, (2 * devices, 2 * devices), 0)
    sub_bits = subs.bit_length() - 1
    wanted = (
        ((arrived >> (sub_bits + 1)) << (sub_bits + 1))
        + (((arrived >> 1) & 1) << sub_bits)
        + (((arrived >> 2) & (subs // 2 - 1)) << 1)
    )
    owner_line = lax.broadcasted_iota(jnp.int32, (rows, 2 * devices), 0)

    def collector(source_core):
        repeated = lax.dot_general(
            by_owner,
            (held == wanted + source_core).astype(F32).astype(BF16),
            (((0,), (0,)), ((), ())),
            preferred_element_type=F32,
        )
        label = jnp.sum(jnp.where(owner_line == me, repeated, 0.0), axis=0, keepdims=True)
        return jnp.concatenate(
            [
                ((label == owner_line.astype(F32)) & ((arrived[:rows] & 1) == i)).astype(F32)
                for i in range(2)
            ],
            axis=0,
        ).astype(BF16)

    collect_other, collect_same = collector(1 - core), collector(core)

    def sums(collect, source_core):
        values = [received[source_core, :, c].reshape(2 * devices, NF) for c in range(3)]
        return dot_plain(collect, jnp.concatenate(values, axis=1))

    pltpu.make_async_copy(received.at[0], received.at[0], all_recv.at[1]).wait()
    first_sums = sums(collect_other, 1 - core)
    most = pl.ds(0, devices // 2 - 1)
    pltpu.make_async_copy(received.at[0, most], received.at[0, most], all_recv.at[0]).wait()
    total = (first_sums + sums(collect_same, core)).astype(BF16)
    for c in range(3):
        summed[c * rows : (c + 1) * rows, :NF] = total[:rows, c * NF : (c + 1) * NF]
        summed[c * rows : (c + 1) * rows, NF:] = total[rows:, c * NF : (c + 1) * NF]

    for c in range(3):

        @pl.when(has_before)
        def _():
            halos[c][0].wait_send()

        @pl.when(has_after)
        def _():
            halos[c][1].wait_send()

    pltpu.make_async_copy(list_out.at[others], list_out.at[others], list_send).wait()

    @pl.when(row_after)
    def _():
        over.wait_send()

    pltpu.make_async_copy(labels.at[0, some], labels.at[0, some], y_send).wait()
    pltpu.make_async_copy(labels.at[some], labels.at[some], z_send).wait()
    most = pl.ds(0, devices - 1)
    pltpu.make_async_copy(outgoing.at[most], outgoing.at[most], all_send).wait()


def exchange(blks, subs, syn, obs, table, first, second, mask, weight, owner, element):
    devices = blks * subs
    samples, rows = syn.shape[2], syn.shape[1]
    in_hbm = pl.BlockSpec(memory_space=pltpu.HBM)
    dma = pltpu.SemaphoreType.DMA
    return pl.pallas_call(
        functools.partial(exchange_kernel, blks, subs),
        out_shape=pltpu.VMEM((3 * rows, 2 * NF), BF16),
        in_specs=[in_hbm] * 9,
        out_specs=pl.BlockSpec(memory_space=pltpu.VMEM),
        scratch_shapes=[
            pltpu.VMEM((3, 2 * rows, samples), BF16),
            pltpu.VMEM(table.shape, BF16),
            pltpu.VMEM(first.shape, jnp.int32),
            pltpu.VMEM(second.shape, jnp.int32),
            pltpu.VMEM(mask.shape, jnp.int32),
            pltpu.VMEM(weight.shape, F32),
            pltpu.VMEM(owner.shape, jnp.int32),
            pltpu.VMEM(element.shape, jnp.int32),
            pltpu.VMEM((6, rows, 2 * NF), BF16),
            pltpu.VMEM((6, 2 * BLOCK, 2 * NF), BF16),
            pltpu.VMEM((subs, 8, NF), F32),
            pltpu.VMEM((8, NF), F32),
            pltpu.VMEM((subs, 8, NF), F32),
            pltpu.VMEM((subs, 8, NF), F32),
            pltpu.VMEM((4, blks // 4, 2 * subs, NF), BF16),
            pltpu.VMEM((devices, 3, 4, NF), BF16),
            pltpu.VMEM((2, devices // 2, 3, 4, NF), BF16),
            dma((13,)),
            dma,
            dma,
            dma,
            dma,
            dma((2, 3)),
            dma((2, 3)),
            pltpu.SemaphoreType.REGULAR((3,)),
            pltpu.SemaphoreType.REGULAR((2,)),
            dma,
            dma,
            dma,
            dma,
            dma,
            dma((2,)),
        ],
        compiler_params=pltpu.CompilerParams(
            collective_id=0, has_side_effects=True, vmem_limit_bytes=60 * 2**20
        ),
        cost_estimate=pl.CostEstimate(
            flops=2 * 10**9, bytes_accessed=3 * 10**6, transcendentals=0
        ),
        name="exchange",
    )(syn, obs, table, first, second, mask, weight, owner, element)


def finish_kernel(summed, table, out, result, sems):
    samples = result.shape[1]
    chunk = samples // sems.shape[0]
    copies = []
    for n in range(sems.shape[0]):
        columns = pl.ds(n * chunk, chunk)
        result[:, columns] = dot_plain(summed[...], table[:, columns])
        copies.append(
            pltpu.make_async_copy(result.at[:, columns], out.at[:, columns], sems.at[n])
        )
        copies[-1].start()
    for copy in copies:
        copy.wait()


def finish(summed, table):
    count, samples = summed.shape[0], table.shape[1]
    in_vmem = pl.BlockSpec(memory_space=pltpu.VMEM)
    out = pl.pallas_call(
        finish_kernel,
        out_shape=jax.ShapeDtypeStruct((count, samples), F32),
        in_specs=[in_vmem] * 2,
        out_specs=pl.BlockSpec(memory_space=pl.ANY),
        scratch_shapes=[
            pltpu.VMEM((count, samples), F32),
            pltpu.SemaphoreType.DMA((4,)),
        ],
        compiler_params=pltpu.CompilerParams(vmem_limit_bytes=40 * 2**20),
        cost_estimate=pl.CostEstimate(
            flops=7 * 10**8, bytes_accessed=3 * 10**6, transcendentals=0
        ),
        name="finish",
    )(summed, table)
    return out.reshape(3, count // 3, samples)


def on_device(
    blks,
    subs,
    synthetic,
    observed,
    pair_first,
    pair_second,
    pair_mask,
    pair_weight,
    station_owner,
    station_element,
):
    rows, _, samples = synthetic.shape
    forward, inverse = dft_tables(samples, NF)
    summed = exchange(
        blks,
        subs,
        jnp.transpose(synthetic, (1, 0, 2)),
        jnp.transpose(observed, (1, 0, 2)),
        jnp.asarray(forward),
        pair_first,
        pair_second,
        pair_mask,
        pair_weight,
        station_owner.reshape(1, rows),
        station_element.reshape(1, rows),
    )
    out = finish(summed, jnp.asarray(inverse))
    return jnp.transpose(out, (1, 0, 2))


def solution(mesh):
    blks, subs = mesh.shape["blk"], mesh.shape["sub"]
    return jax.shard_map(
        functools.partial(on_device, blks, subs),
        mesh=mesh,
        in_specs=(
            P(("blk", "sub"), None, None),
            P(("blk", "sub"), None, None),
            P("blk", "sub"),
            P("blk", "sub"),
            P("blk", "sub"),
            P("blk", "sub"),
            P(("blk", "sub"), None),
            P(("blk", "sub")),
        ),
        out_specs=P(("blk", "sub"), None, None),
        check_vma=False,
    )
```

```python
import functools
import itertools
import math

import jax
import jax.numpy as jnp
import numpy as np
from jax import lax
from jax.experimental import pallas as pl
from jax.experimental.pallas import tpu as pltpu
from jax.sharding import PartitionSpec as P

MESH = pl.DeviceIdType.MESH
NF = 128
BLOCK = 64
F32 = jnp.float32
BF16 = jnp.bfloat16


def dft_tables(samples, freqs):
    phase = (np.arange(samples)[:, None] * np.arange(freqs)[None, :]) % samples
    angles = phase.astype(np.float64) * (2.0 * math.pi / samples)
    scale = 1.0 / math.sqrt(samples)
    cosine, sine = np.cos(angles) * scale, np.sin(angles) * scale
    forward = np.concatenate([cosine, -sine], axis=1).astype(np.float32)
    doubled = np.where(np.arange(freqs) == 0, 1.0, 2.0)[:, None]
    inverse = np.concatenate([cosine.T * doubled, -sine.T * doubled], axis=0)
    return forward.astype(jnp.bfloat16), inverse.astype(np.float32).astype(jnp.bfloat16)


def in_two(x):
    high = x.astype(BF16)
    return high, (x - high.astype(F32)).astype(BF16)


def dot_rows(a, b):
    return lax.dot_general(a, b, (((1,), (1,)), ((), ())), preferred_element_type=F32)


def dot_plain(a, b):
    return jnp.dot(a, b, preferred_element_type=F32)


def features(pair):
    xr, xi = pair[0][:, :NF].astype(F32), pair[0][:, NF:].astype(F32)
    o_r, o_i = pair[1][:, :NF].astype(F32), pair[1][:, NF:].astype(F32)
    dr, di = xr - o_r, xi - o_i
    parts = [dr * xr + di * xi, dr * xi - di * xr, o_r * xr + o_i * xi, o_r * xi - o_i * xr]
    both = [in_two(p) for p in parts]
    return jnp.concatenate(
        [jnp.concatenate([b[i] for b in both], axis=1) for i in range(2)], axis=0
    )


def for_features(links):
    return jnp.concatenate([links.astype(BF16)] * 2, axis=1)


def spread(rows, count, shift):
    index = lax.broadcasted_iota(jnp.int32, (count, NF), 0) + shift
    return jnp.concatenate(
        [(index == rows[s : s + 1]).astype(F32).astype(BF16) for s in range(rows.shape[0])], axis=1
    )


def spread_weights(rows, weights, count, shift):
    index = lax.broadcasted_iota(jnp.int32, (count, NF), 0) + shift
    return jnp.concatenate(
        [
            jnp.where(index == rows[s : s + 1], weights[s : s + 1], 0.0).astype(BF16)
            for s in range(rows.shape[0])
        ],
        axis=1,
    )


def spread_order():
    left = list(itertools.product(range(4), range(4), range(2)))[1:]
    ways = {0: (0.0, 0.0), 1: (1.0, 0.0), 2: (1.0, 1.0), 3: (0.0, 1.0)}

    def links(step):
        return np.array([way for axis in step[:2] for way in ways[axis]])

    used, order = np.zeros(4), []
    while left:
        step = min(left, key=lambda t: (np.max(used + links(t)), -np.sum(links(t)), t))
        left.remove(step)
        used = used + links(step)
        order.append(step)
    return order


def exchange_kernel(
    blks,
    subs,
    syn_hbm,
    obs_hbm,
    table_hbm,
    first_hbm,
    second_hbm,
    mask_hbm,
    weight_hbm,
    owner_hbm,
    element_hbm,
    summed,
    traces,
    table,
    first,
    second,
    mask,
    weight,
    owner,
    element,
    spec,
    halo,
    list_out,
    list_over,
    lists,
    lists_prev,
    labels,
    outgoing,
    received,
    load_sems,
    list_send,
    list_recv,
    over_send,
    over_recv,
    halo_send,
    halo_recv,
    entered,
    joined,
    y_send,
    y_recv,
    z_send,
    z_recv,
    all_send,
    all_recv,
):
    devices = blks * subs
    blk, sub = lax.axis_index("blk"), lax.axis_index("sub")
    me = blk * subs + sub
    rows = spec.shape[1]
    blocks = first.shape[0]
    def around(at, step, size):
        there = at + step
        return jnp.where(there >= size, there - size, there)

    subs_there = [around(sub, step, subs) for step in range(1, subs)]
    blks_there = [around(blk, step, blks) for step in range(1, blks)]
    blk_after, blk_before = blks_there[0], blks_there[-1]
    after = (jnp.where(sub == subs - 1, blk_after, blk), subs_there[0])
    before = (jnp.where(sub == 0, blk_before, blk), subs_there[-1])

    pairs = [
        (table_hbm, table),
        (syn_hbm.at[0], traces.at[0, pl.ds(0, rows)]),
        (obs_hbm.at[0], traces.at[0, pl.ds(rows, rows)]),
        (owner_hbm, owner),
        (element_hbm, element),
        (first_hbm, first),
        (second_hbm, second),
        (mask_hbm, mask),
        (weight_hbm, weight),
        (syn_hbm.at[1], traces.at[1, pl.ds(0, rows)]),
        (obs_hbm.at[1], traces.at[1, pl.ds(rows, rows)]),
        (syn_hbm.at[2], traces.at[2, pl.ds(0, rows)]),
        (obs_hbm.at[2], traces.at[2, pl.ds(rows, rows)]),
    ]
    loads = [
        pltpu.make_async_copy(src, dst, load_sems.at[i]) for i, (src, dst) in enumerate(pairs)
    ]
    for load in loads:
        load.start()

    z, y = lax.div(blk, 4), lax.rem(blk, 4)
    has_before, has_after = me > 0, me < devices - 1
    row_before, row_after = blk > 0, blk < blks - 1
    barrier = pltpu.get_barrier_semaphore()

    def greet(there):
        pl.semaphore_signal(barrier, inc=1, device_id=there, device_id_type=MESH)

    def greet_column(there, carry):
        greet((there, sub))
        return carry

    for there in subs_there:
        greet((blk, there))
    lax.fori_loop(blk + 1, blks, greet_column, 0)

    @pl.when((sub == 0) & row_before)
    def _():
        for s in range(subs):
            greet((blk_before, s))

    @pl.when((sub == subs - 1) & row_after)
    def _():
        greet((blk_after, 0))

    for i in range(3):
        pl.semaphore_signal(entered.at[i], inc=1)
    greetings = (
        (subs - 1)
        + jnp.where(row_after, 1, 0)
        + jnp.where((sub == 0) & row_before, 1, 0)
        + blk
    )

    def transform(c):
        both = dot_plain(traces[c], table[...]).astype(BF16)
        spec[2 * c] = both[:rows]
        spec[2 * c + 1] = both[rows:]

    for i in range(3):
        loads[i].wait()
    transform(0)

    pl.semaphore_wait(barrier, greetings)

    def halo_copies(c):
        q = pl.ds(2 * c, 2)
        return [
            pltpu.make_async_remote_copy(
                src_ref=spec.at[q, pl.ds(0, BLOCK)],
                dst_ref=halo.at[q, pl.ds(BLOCK, BLOCK)],
                send_sem=halo_send.at[0, c],
                recv_sem=halo_recv.at[0, c],
                device_id=before,
                device_id_type=MESH,
            ),
            pltpu.make_async_remote_copy(
                src_ref=spec.at[q, pl.ds(rows - BLOCK, BLOCK)],
                dst_ref=halo.at[q, pl.ds(0, BLOCK)],
                send_sem=halo_send.at[1, c],
                recv_sem=halo_recv.at[1, c],
                device_id=after,
                device_id_type=MESH,
            ),
        ]

    halos = [halo_copies(c) for c in range(3)]

    def start_halos(c):
        @pl.when(has_before)
        def _():
            halos[c][0].start()

        @pl.when(has_after)
        def _():
            halos[c][1].start()

    start_halos(0)

    def answer(there, carry):
        kind = jnp.where(lax.div(there, 4) == z, 0, jnp.where(z == 1, 1, 2))
        pl.semaphore_signal(
            entered.at[kind], inc=1, device_id=(there, sub), device_id_type=MESH
        )
        return carry

    @pl.when(z < 3)
    def _():
        lax.fori_loop(0, blk, answer, 0)


    for i in range(3, 5):
        loads[i].wait()
    lane = lax.broadcasted_iota(jnp.int32, (rows, rows), 1)
    line = lax.broadcasted_iota(jnp.int32, (rows, rows), 0)
    owner_row = owner[...]

    def column(row):
        return jnp.sum(jnp.where(lane == line, row, 0), axis=1, keepdims=True)

    owner_column, element_column = column(owner_row), column(element[...]).astype(F32)
    same = owner_column == owner_row
    rank_column = jnp.sum(jnp.where(same & (lane < line), 1, 0), axis=1, keepdims=True)
    label_rows = []
    for k in range(2):
        chosen = ((owner_column == lane) & (rank_column == k)).astype(F32)
        label_rows.append(
            jnp.sum(chosen * (element_column - rows), axis=0, keepdims=True) + float(rows)
        )

    for i in range(5, 9):
        loads[i].wait()
    base = (blk * blocks + lax.broadcasted_iota(jnp.int32, (blocks, NF), 0)) * BLOCK
    code = ((first[...] - base) * (2 * BLOCK) + (second[...] - base)).astype(F32)
    slot_weight = weight[...] * mask[...].astype(F32)
    zero_row = jnp.zeros((1, NF), F32)
    for s in range(subs):
        lines = [max(2 * s - 1, 0), 2 * s, 2 * s + 1]
        list_out[s] = jnp.concatenate(
            [code[i : i + 1] for i in lines]
            + [slot_weight[i : i + 1] for i in lines]
            + label_rows,
            axis=0,
        )
    list_over[...] = jnp.concatenate(
        [code[blocks - 1 : blocks]]
        + [zero_row] * 2
        + [slot_weight[blocks - 1 : blocks]]
        + [zero_row] * 4,
        axis=0,
    )
    lists[sub] = list_out[sub]

    for there in subs_there:
        pltpu.make_async_remote_copy(
            src_ref=list_out.at[there],
            dst_ref=lists.at[sub],
            send_sem=list_send,
            recv_sem=list_recv,
            device_id=(blk, there),
            device_id_type=MESH,
        ).start()
    over = pltpu.make_async_remote_copy(
        src_ref=list_over,
        dst_ref=lists_prev.at[sub],
        send_sem=over_send,
        recv_sem=over_recv,
        device_id=(blk_after, 0),
        device_id_type=MESH,
    )

    @pl.when(row_after)
    def _():
        over.start()


    for c in (1, 2):
        loads[7 + 2 * c].wait()
        loads[8 + 2 * c].wait()
        transform(c)
        start_halos(c)

    @pl.when(jnp.logical_not(has_before))
    def _():
        halo[:, :BLOCK] = jnp.zeros((6, BLOCK, 2 * NF), BF16)

    @pl.when(jnp.logical_not(has_after))
    def _():
        halo[:, BLOCK:] = jnp.zeros((6, BLOCK, 2 * NF), BF16)

    @pl.when(z == 3)
    def _():
        lax.fori_loop(0, blk, answer, 0)

    def tell_row(which):
        for there in subs_there:
            pl.semaphore_signal(
                joined.at[which], inc=1, device_id=(blk, there), device_id_type=MESH
            )

    @pl.when(z >= 2)
    def _():
        tell_row(0)

    rank_row = jnp.sum(jnp.where(same & (line < lane), 1, 0), axis=0, keepdims=True)
    target = owner_row * 4 + rank_row * 2
    slot = lax.broadcasted_iota(jnp.int32, (4 * devices, 2 * rows), 0)
    placement = (slot == jnp.concatenate([target, target + 1], axis=1)).astype(F32).astype(BF16)

    def stations(c):
        return (spec[2 * c], spec[2 * c + 1])

    own = [features(stations(c)) for c in range(3)]

    others = pl.ds(0, subs - 1)
    pltpu.make_async_copy(lists.at[others], lists.at[others], list_recv).wait()

    pl.semaphore_wait(entered.at[0], 4 - y)
    labels[z, y] = jnp.concatenate([lists[:, 6, :], lists[:, 7, :]], axis=0).astype(BF16)
    for step in range(1, 4):
        pltpu.make_async_remote_copy(
            src_ref=labels.at[z, y],
            dst_ref=labels.at[z, y],
            send_sem=y_send,
            recv_sem=y_recv,
            device_id=(z * 4 + around(y, step, 4), sub),
            device_id_type=MESH,
        ).start()

    @pl.when((sub == 0) & row_before)
    def _():
        pltpu.make_async_copy(lists_prev, lists_prev, over_recv).wait()

    @pl.when((sub == 0) & jnp.logical_not(row_before))
    def _():
        lists_prev[...] = jnp.zeros(lists_prev.shape, F32)

    @pl.when(sub != 0)
    def _():
        lists_prev[...] = lists[...]

    def unpacked(ref, k):
        codes = ref[:, k, :].astype(jnp.int32)
        return codes >> 7, codes & 127, ref[:, 3 + k, :]

    first0, second0, weight0 = unpacked(lists_prev, 0)
    first1, second1, weight1 = unpacked(lists, 1)
    first2, second2, weight2 = unpacked(lists, 2)
    to_prev = dot_rows(spread_weights(second0, weight0, BLOCK, BLOCK), spread(first0, rows, 0))
    upper = dot_rows(spread_weights(first1, weight1, BLOCK, 0), spread(second1, rows, 0))
    lower = dot_rows(spread_weights(first2, weight2, BLOCK, 0), spread(second2, rows, 0))
    half = lax.broadcasted_iota(jnp.int32, (BLOCK, rows), 1) >= BLOCK
    inside = jnp.where(half, pltpu.roll(lower, BLOCK, 1), 0.0)
    one_way = jnp.concatenate([upper, inside], axis=0)
    link_own = for_features(one_way + one_way.T)
    link_halo = for_features(jnp.concatenate([to_prev, jnp.where(half, lower, 0.0)], axis=0))
    inner = [dot_plain(link_own, own[c]) for c in range(3)]

    def adjoint(c):
        sums = inner[c] + dot_plain(link_halo, features((halo[2 * c], halo[2 * c + 1])))
        g1r, g1i, g2r, g2i = (sums[:, i * NF : (i + 1) * NF] for i in range(4))
        x, o = stations(c)
        xr, xi = x[:, :NF].astype(F32), x[:, NF:].astype(F32)
        dr, di = xr - o[:, :NF].astype(F32), xi - o[:, NF:].astype(F32)
        real = (xr * g1r - xi * g1i) + (dr * g2r - di * g2i)
        imag = (xr * g1i + xi * g1r) + (dr * g2i + di * g2r)
        return jnp.concatenate([real, imag], axis=0).astype(BF16)

    def handle(together):
        for c in together:

            @pl.when(has_after)
            def _():
                halos[c][0].wait_recv()

            @pl.when(has_before)
            def _():
                halos[c][1].wait_recv()

        placed = dot_plain(placement, jnp.concatenate([adjoint(c) for c in together], axis=1))
        for i, c in enumerate(together):
            outgoing[:, c] = (
                placed[:, i * NF : (i + 1) * NF].astype(BF16).reshape(devices, 4, NF)
            )

    handle((0, 1))

    pl.semaphore_wait(entered.at[1], 1 + jnp.where(z == 0, 4, 0))

    @pl.when(z < 2)
    def _():
        tell_row(0)

    handle((2,))

    def rest_entered(answers):
        pl.semaphore_wait(entered.at[2], 1 + answers)
        tell_row(1)

    @pl.when(z >= 2)
    def _():
        rest_entered(jnp.where(z == 2, 4, 0))

    def turns(at, size):
        return [at] + [around(at, step, size) for step in range(1, size)]

    core, chip = lax.rem(sub, 2), lax.div(me, 2)
    y_to, x_to = turns(y, 4), turns(lax.div(sub, 2), 4)
    core_to = [core, 1 - core]
    received[core, chip] = outgoing[me]

    def deliver(plane, step):
        dy, dx, other = step
        blk_to, sub_to = plane * 4 + y_to[dy], x_to[dx] * 2 + core_to[other]
        pltpu.make_async_remote_copy(
            src_ref=outgoing.at[blk_to * subs + sub_to],
            dst_ref=received.at[core, chip],
            send_sem=all_send,
            recv_sem=all_recv.at[other],
            device_id=(blk_to, sub_to),
            device_id_type=MESH,
        ).start()

    order = spread_order()

    def deliver_plane(plane, steps):
        for step in steps:
            deliver(plane, step)

        @pl.when(z != plane)
        def _():
            deliver(plane, (0, 0, 0))

    pl.semaphore_wait(joined.at[0], subs - 1)
    for step in order[:12]:
        deliver(0, step)

    @pl.when(z < 2)
    def _():
        rest_entered(8)

    some = pl.ds(0, 3)
    pltpu.make_async_copy(labels.at[0, some], labels.at[0, some], y_recv).wait()
    for step in range(1, 4):
        pltpu.make_async_remote_copy(
            src_ref=labels.at[z],
            dst_ref=labels.at[z],
            send_sem=z_send,
            recv_sem=z_recv,
            device_id=(around(z, step, 4) * 4 + y, sub),
            device_id_type=MESH,
        ).start()

    deliver_plane(0, order[12:])
    deliver_plane(1, order)
    pl.semaphore_wait(joined.at[1], subs - 1)
    deliver_plane(2, order)
    deliver_plane(3, order)

    arrived = lax.broadcasted_iota(jnp.int32, (2 * devices, 2 * devices), 1)
    held = lax.broadcasted_iota(jnp.int32, (2 * devices, 2 * devices), 0)
    sub_bits = subs.bit_length() - 1
    wanted = (
        ((arrived >> (sub_bits + 1)) << (sub_bits + 1))
        + (((arrived >> 1) & 1) << sub_bits)
        + (((arrived >> 2) & (subs // 2 - 1)) << 1)
    )
    owner_line = lax.broadcasted_iota(jnp.int32, (rows, 2 * devices), 0)
    repeat = [(held == wanted + of).astype(F32).astype(BF16) for of in (core, 1 - core)]
    pltpu.make_async_copy(labels.at[some], labels.at[some], z_recv).wait()
    by_owner = labels[...].reshape(2 * devices, NF)

    def collector(repeat):
        repeated = lax.dot_general(
            by_owner,
            repeat,
            (((0,), (0,)), ((), ())),
            preferred_element_type=F32,
        )
        label = jnp.sum(jnp.where(owner_line == me, repeated, 0.0), axis=0, keepdims=True)
        return jnp.concatenate(
            [
                ((label == owner_line.astype(F32)) & ((arrived[:rows] & 1) == i)).astype(F32)
                for i in range(2)
            ],
            axis=0,
        ).astype(BF16)

    collect_other, collect_same = collector(repeat[1]), collector(repeat[0])

    def sums(collect, source_core):
        values = [received[source_core, :, c].reshape(2 * devices, NF) for c in range(3)]
        return dot_plain(collect, jnp.concatenate(values, axis=1))

    pltpu.make_async_copy(received.at[0], received.at[0], all_recv.at[1]).wait()
    first_sums = sums(collect_other, 1 - core)
    most = pl.ds(0, devices // 2 - 1)
    pltpu.make_async_copy(received.at[0, most], received.at[0, most], all_recv.at[0]).wait()
    total = (first_sums + sums(collect_same, core)).astype(BF16)
    for c in range(3):
        summed[c * rows : (c + 1) * rows, :NF] = total[:rows, c * NF : (c + 1) * NF]
        summed[c * rows : (c + 1) * rows, NF:] = total[rows:, c * NF : (c + 1) * NF]

    for c in range(3):

        @pl.when(has_before)
        def _():
            halos[c][0].wait_send()

        @pl.when(has_after)
        def _():
            halos[c][1].wait_send()

    pltpu.make_async_copy(list_out.at[others], list_out.at[others], list_send).wait()

    @pl.when(row_after)
    def _():
        over.wait_send()

    pltpu.make_async_copy(labels.at[0, some], labels.at[0, some], y_send).wait()
    pltpu.make_async_copy(labels.at[some], labels.at[some], z_send).wait()
    most = pl.ds(0, devices - 1)
    pltpu.make_async_copy(outgoing.at[most], outgoing.at[most], all_send).wait()


def exchange(blks, subs, syn, obs, table, first, second, mask, weight, owner, element):
    devices = blks * subs
    samples, rows = syn.shape[2], syn.shape[1]
    in_hbm = pl.BlockSpec(memory_space=pltpu.HBM)
    dma = pltpu.SemaphoreType.DMA
    return pl.pallas_call(
        functools.partial(exchange_kernel, blks, subs),
        out_shape=pltpu.VMEM((3 * rows, 2 * NF), BF16),
        in_specs=[in_hbm] * 9,
        out_specs=pl.BlockSpec(memory_space=pltpu.VMEM),
        scratch_shapes=[
            pltpu.VMEM((3, 2 * rows, samples), BF16),
            pltpu.VMEM(table.shape, BF16),
            pltpu.VMEM(first.shape, jnp.int32),
            pltpu.VMEM(second.shape, jnp.int32),
            pltpu.VMEM(mask.shape, jnp.int32),
            pltpu.VMEM(weight.shape, F32),
            pltpu.VMEM(owner.shape, jnp.int32),
            pltpu.VMEM(element.shape, jnp.int32),
            pltpu.VMEM((6, rows, 2 * NF), BF16),
            pltpu.VMEM((6, 2 * BLOCK, 2 * NF), BF16),
            pltpu.VMEM((subs, 8, NF), F32),
            pltpu.VMEM((8, NF), F32),
            pltpu.VMEM((subs, 8, NF), F32),
            pltpu.VMEM((subs, 8, NF), F32),
            pltpu.VMEM((4, blks // 4, 2 * subs, NF), BF16),
            pltpu.VMEM((devices, 3, 4, NF), BF16),
            pltpu.VMEM((2, devices // 2, 3, 4, NF), BF16),
            dma((13,)),
            dma,
            dma,
            dma,
            dma,
            dma((2, 3)),
            dma((2, 3)),
            pltpu.SemaphoreType.REGULAR((3,)),
            pltpu.SemaphoreType.REGULAR((2,)),
            dma,
            dma,
            dma,
            dma,
            dma,
            dma((2,)),
        ],
        compiler_params=pltpu.CompilerParams(
            collective_id=0, has_side_effects=True, vmem_limit_bytes=60 * 2**20
        ),
        cost_estimate=pl.CostEstimate(
            flops=2 * 10**9, bytes_accessed=3 * 10**6, transcendentals=0
        ),
        name="exchange",
    )(syn, obs, table, first, second, mask, weight, owner, element)


def finish_kernel(summed, table, out, result, sems):
    samples = result.shape[1]
    chunk = samples // sems.shape[0]
    copies = []
    for n in range(sems.shape[0]):
        columns = pl.ds(n * chunk, chunk)
        result[:, columns] = dot_plain(summed[...], table[:, columns])
        copies.append(
            pltpu.make_async_copy(result.at[:, columns], out.at[:, columns], sems.at[n])
        )
        copies[-1].start()
    for copy in copies:
        copy.wait()


def finish(summed, table):
    count, samples = summed.shape[0], table.shape[1]
    in_vmem = pl.BlockSpec(memory_space=pltpu.VMEM)
    out = pl.pallas_call(
        finish_kernel,
        out_shape=jax.ShapeDtypeStruct((count, samples), F32),
        in_specs=[in_vmem] * 2,
        out_specs=pl.BlockSpec(memory_space=pl.ANY),
        scratch_shapes=[
            pltpu.VMEM((count, samples), F32),
            pltpu.SemaphoreType.DMA((4,)),
        ],
        compiler_params=pltpu.CompilerParams(vmem_limit_bytes=40 * 2**20),
        cost_estimate=pl.CostEstimate(
            flops=7 * 10**8, bytes_accessed=3 * 10**6, transcendentals=0
        ),
        name="finish",
    )(summed, table)
    return out.reshape(3, count // 3, samples)


def on_device(
    blks,
    subs,
    synthetic,
    observed,
    pair_first,
    pair_second,
    pair_mask,
    pair_weight,
    station_owner,
    station_element,
):
    rows, _, samples = synthetic.shape
    forward, inverse = dft_tables(samples, NF)
    summed = exchange(
        blks,
        subs,
        jnp.transpose(synthetic, (1, 0, 2)),
        jnp.transpose(observed, (1, 0, 2)),
        jnp.asarray(forward),
        pair_first,
        pair_second,
        pair_mask,
        pair_weight,
        station_owner.reshape(1, rows),
        station_element.reshape(1, rows),
    )
    out = finish(summed, jnp.asarray(inverse))
    return jnp.transpose(out, (1, 0, 2))


def solution(mesh):
    blks, subs = mesh.shape["blk"], mesh.shape["sub"]
    return jax.shard_map(
        functools.partial(on_device, blks, subs),
        mesh=mesh,
        in_specs=(
            P(("blk", "sub"), None, None),
            P(("blk", "sub"), None, None),
            P("blk", "sub"),
            P("blk", "sub"),
            P("blk", "sub"),
            P("blk", "sub"),
            P(("blk", "sub"), None),
            P(("blk", "sub")),
        ),
        out_specs=P(("blk", "sub"), None, None),
        check_vma=False,
    )
```

```python
import functools
import itertools
import math

import jax
import jax.numpy as jnp
import numpy as np
from jax import lax
from jax.experimental import pallas as pl
from jax.experimental.pallas import tpu as pltpu
from jax.sharding import PartitionSpec as P

MESH = pl.DeviceIdType.MESH
NF = 128
BLOCK = 64
F32 = jnp.float32
BF16 = jnp.bfloat16


def dft_tables(samples, freqs):
    phase = (np.arange(samples)[:, None] * np.arange(freqs)[None, :]) % samples
    angles = phase.astype(np.float64) * (2.0 * math.pi / samples)
    scale = 1.0 / math.sqrt(samples)
    cosine, sine = np.cos(angles) * scale, np.sin(angles) * scale
    forward = np.concatenate([cosine, -sine], axis=1).astype(np.float32)
    doubled = np.where(np.arange(freqs) == 0, 1.0, 2.0)[:, None]
    inverse = np.concatenate([cosine.T * doubled, -sine.T * doubled], axis=0)
    return forward.astype(jnp.bfloat16), inverse.astype(np.float32).astype(jnp.bfloat16)


def in_two(x):
    high = x.astype(BF16)
    return high, (x - high.astype(F32)).astype(BF16)


def dot_rows(a, b):
    return lax.dot_general(a, b, (((1,), (1,)), ((), ())), preferred_element_type=F32)


def dot_plain(a, b):
    return jnp.dot(a, b, preferred_element_type=F32)


def features(pair):
    xr, xi = pair[0][:, :NF].astype(F32), pair[0][:, NF:].astype(F32)
    o_r, o_i = pair[1][:, :NF].astype(F32), pair[1][:, NF:].astype(F32)
    dr, di = xr - o_r, xi - o_i
    parts = [dr * xr + di * xi, dr * xi - di * xr, o_r * xr + o_i * xi, o_r * xi - o_i * xr]
    both = [in_two(p) for p in parts]
    return jnp.concatenate(
        [jnp.concatenate([b[i] for b in both], axis=1) for i in range(2)], axis=0
    )


def for_features(links):
    return jnp.concatenate([links.astype(BF16)] * 2, axis=1)


def spread(rows, count, shift):
    index = lax.broadcasted_iota(jnp.int32, (count, NF), 0) + shift
    return jnp.concatenate(
        [(index == rows[s : s + 1]).astype(F32).astype(BF16) for s in range(rows.shape[0])], axis=1
    )


def spread_weights(rows, weights, count, shift):
    index = lax.broadcasted_iota(jnp.int32, (count, NF), 0) + shift
    return jnp.concatenate(
        [
            jnp.where(index == rows[s : s + 1], weights[s : s + 1], 0.0).astype(BF16)
            for s in range(rows.shape[0])
        ],
        axis=1,
    )


def spread_order():
    left = list(itertools.product(range(4), range(4), range(2)))[1:]
    ways = {0: (0.0, 0.0), 1: (1.0, 0.0), 2: (1.0, 1.0), 3: (0.0, 1.0)}

    def links(step):
        return np.array([way for axis in step[:2] for way in ways[axis]])

    used, order = np.zeros(4), []
    while left:
        step = min(left, key=lambda t: (np.max(used + links(t)), -np.sum(links(t)), t))
        left.remove(step)
        used = used + links(step)
        order.append(step)
    return order


def exchange_kernel(
    blks,
    subs,
    syn_hbm,
    obs_hbm,
    table_hbm,
    first_hbm,
    second_hbm,
    mask_hbm,
    weight_hbm,
    owner_hbm,
    element_hbm,
    summed,
    traces,
    table,
    first,
    second,
    mask,
    weight,
    owner,
    element,
    spec,
    halo,
    list_out,
    list_over,
    lists,
    lists_prev,
    labels,
    outgoing,
    received,
    load_sems,
    list_send,
    list_recv,
    over_send,
    over_recv,
    halo_send,
    halo_recv,
    entered,
    joined,
    y_send,
    y_recv,
    z_send,
    z_recv,
    all_send,
    all_recv,
):
    devices = blks * subs
    blk, sub = lax.axis_index("blk"), lax.axis_index("sub")
    me = blk * subs + sub
    rows = spec.shape[1]
    blocks = first.shape[0]
    def around(at, step, size):
        there = at + step
        return jnp.where(there >= size, there - size, there)

    subs_there = [around(sub, step, subs) for step in range(1, subs)]
    blks_there = [around(blk, step, blks) for step in range(1, blks)]
    blk_after, blk_before = blks_there[0], blks_there[-1]
    after = (jnp.where(sub == subs - 1, blk_after, blk), subs_there[0])
    before = (jnp.where(sub == 0, blk_before, blk), subs_there[-1])

    pairs = [
        (table_hbm, table),
        (syn_hbm.at[0], traces.at[0, pl.ds(0, rows)]),
        (obs_hbm.at[0], traces.at[0, pl.ds(rows, rows)]),
        (owner_hbm, owner),
        (element_hbm, element),
        (first_hbm, first),
        (second_hbm, second),
        (mask_hbm, mask),
        (weight_hbm, weight),
        (syn_hbm.at[1], traces.at[1, pl.ds(0, rows)]),
        (obs_hbm.at[1], traces.at[1, pl.ds(rows, rows)]),
        (syn_hbm.at[2], traces.at[2, pl.ds(0, rows)]),
        (obs_hbm.at[2], traces.at[2, pl.ds(rows, rows)]),
    ]
    loads = [
        pltpu.make_async_copy(src, dst, load_sems.at[i]) for i, (src, dst) in enumerate(pairs)
    ]
    for load in loads:
        load.start()

    z, y = lax.div(blk, 4), lax.rem(blk, 4)
    has_before, has_after = me > 0, me < devices - 1
    row_before, row_after = blk > 0, blk < blks - 1
    barrier = pltpu.get_barrier_semaphore()

    def greet(there):
        pl.semaphore_signal(barrier, inc=1, device_id=there, device_id_type=MESH)

    def greet_column(there, carry):
        greet((there, sub))
        return carry

    for there in subs_there:
        greet((blk, there))
    lax.fori_loop(blk + 1, blks, greet_column, 0)

    @pl.when((sub == 0) & row_before)
    def _():
        for s in range(subs):
            greet((blk_before, s))

    @pl.when((sub == subs - 1) & row_after)
    def _():
        greet((blk_after, 0))

    for i in range(3):
        pl.semaphore_signal(entered.at[i], inc=1)
    greetings = (
        (subs - 1)
        + jnp.where(row_after, 1, 0)
        + jnp.where((sub == 0) & row_before, 1, 0)
        + blk
    )

    def transform(c):
        both = dot_plain(traces[c], table[...]).astype(BF16)
        spec[2 * c] = both[:rows]
        spec[2 * c + 1] = both[rows:]

    for i in range(3):
        loads[i].wait()
    transform(0)

    pl.semaphore_wait(barrier, greetings)

    def halo_copies(c):
        q = pl.ds(2 * c, 2)
        return [
            pltpu.make_async_remote_copy(
                src_ref=spec.at[q, pl.ds(0, BLOCK)],
                dst_ref=halo.at[q, pl.ds(BLOCK, BLOCK)],
                send_sem=halo_send.at[0, c],
                recv_sem=halo_recv.at[0, c],
                device_id=before,
                device_id_type=MESH,
            ),
            pltpu.make_async_remote_copy(
                src_ref=spec.at[q, pl.ds(rows - BLOCK, BLOCK)],
                dst_ref=halo.at[q, pl.ds(0, BLOCK)],
                send_sem=halo_send.at[1, c],
                recv_sem=halo_recv.at[1, c],
                device_id=after,
                device_id_type=MESH,
            ),
        ]

    halos = [halo_copies(c) for c in range(3)]

    def start_halos(c):
        @pl.when(has_before)
        def _():
            halos[c][0].start()

        @pl.when(has_after)
        def _():
            halos[c][1].start()

    start_halos(0)

    def answer(there, carry):
        kind = jnp.where(lax.div(there, 4) == z, 0, jnp.where(z == 1, 1, 2))
        pl.semaphore_signal(
            entered.at[kind], inc=1, device_id=(there, sub), device_id_type=MESH
        )
        return carry

    @pl.when(z < 3)
    def _():
        lax.fori_loop(0, blk, answer, 0)


    for i in range(3, 5):
        loads[i].wait()
    lane = lax.broadcasted_iota(jnp.int32, (rows, rows), 1)
    line = lax.broadcasted_iota(jnp.int32, (rows, rows), 0)
    owner_row = owner[...]

    def column(row):
        return jnp.sum(jnp.where(lane == line, row, 0), axis=1, keepdims=True)

    owner_column, element_column = column(owner_row), column(element[...]).astype(F32)
    same = owner_column == owner_row
    rank_column = jnp.sum(jnp.where(same & (lane < line), 1, 0), axis=1, keepdims=True)
    label_rows = []
    for k in range(2):
        chosen = ((owner_column == lane) & (rank_column == k)).astype(F32)
        label_rows.append(
            jnp.sum(chosen * (element_column - rows), axis=0, keepdims=True) + float(rows)
        )

    for i in range(5, 9):
        loads[i].wait()
    base = (blk * blocks + lax.broadcasted_iota(jnp.int32, (blocks, NF), 0)) * BLOCK
    code = ((first[...] - base) * (2 * BLOCK) + (second[...] - base)).astype(F32)
    slot_weight = weight[...] * mask[...].astype(F32)
    zero_row = jnp.zeros((1, NF), F32)
    for s in range(subs):
        lines = [max(2 * s - 1, 0), 2 * s, 2 * s + 1]
        list_out[s] = jnp.concatenate(
            [code[i : i + 1] for i in lines]
            + [slot_weight[i : i + 1] for i in lines]
            + label_rows,
            axis=0,
        )
    list_over[...] = jnp.concatenate(
        [code[blocks - 1 : blocks]]
        + [zero_row] * 2
        + [slot_weight[blocks - 1 : blocks]]
        + [zero_row] * 4,
        axis=0,
    )
    lists[sub] = list_out[sub]

    for there in subs_there:
        pltpu.make_async_remote_copy(
            src_ref=list_out.at[there],
            dst_ref=lists.at[sub],
            send_sem=list_send,
            recv_sem=list_recv,
            device_id=(blk, there),
            device_id_type=MESH,
        ).start()
    over = pltpu.make_async_remote_copy(
        src_ref=list_over,
        dst_ref=lists_prev.at[sub],
        send_sem=over_send,
        recv_sem=over_recv,
        device_id=(blk_after, 0),
        device_id_type=MESH,
    )

    @pl.when(row_after)
    def _():
        over.start()


    for c in (1, 2):
        loads[7 + 2 * c].wait()
        loads[8 + 2 * c].wait()
        transform(c)
        start_halos(c)

    @pl.when(jnp.logical_not(has_before))
    def _():
        halo[:, :BLOCK] = jnp.zeros((6, BLOCK, 2 * NF), BF16)

    @pl.when(jnp.logical_not(has_after))
    def _():
        halo[:, BLOCK:] = jnp.zeros((6, BLOCK, 2 * NF), BF16)

    @pl.when(z == 3)
    def _():
        lax.fori_loop(0, blk, answer, 0)

    def tell_row(which):
        for there in subs_there:
            pl.semaphore_signal(
                joined.at[which], inc=1, device_id=(blk, there), device_id_type=MESH
            )

    @pl.when(z >= 2)
    def _():
        tell_row(0)

    rank_row = jnp.sum(jnp.where(same & (line < lane), 1, 0), axis=0, keepdims=True)
    target = owner_row * 4 + rank_row * 2
    slot = lax.broadcasted_iota(jnp.int32, (4 * devices, 2 * rows), 0)
    placement = (slot == jnp.concatenate([target, target + 1], axis=1)).astype(F32).astype(BF16)

    def stations(c):
        return (spec[2 * c], spec[2 * c + 1])

    own = [features(stations(c)) for c in range(3)]

    others = pl.ds(0, subs - 1)
    pltpu.make_async_copy(lists.at[others], lists.at[others], list_recv).wait()

    pl.semaphore_wait(entered.at[0], 4 - y)
    labels[z, y] = jnp.concatenate([lists[:, 6, :], lists[:, 7, :]], axis=0).astype(BF16)
    for step in range(1, 4):
        pltpu.make_async_remote_copy(
            src_ref=labels.at[z, y],
            dst_ref=labels.at[z, y],
            send_sem=y_send,
            recv_sem=y_recv,
            device_id=(z * 4 + around(y, step, 4), sub),
            device_id_type=MESH,
        ).start()

    @pl.when((sub == 0) & row_before)
    def _():
        pltpu.make_async_copy(lists_prev, lists_prev, over_recv).wait()

    @pl.when((sub == 0) & jnp.logical_not(row_before))
    def _():
        lists_prev[...] = jnp.zeros(lists_prev.shape, F32)

    @pl.when(sub != 0)
    def _():
        lists_prev[...] = lists[...]

    def unpacked(ref, k):
        codes = ref[:, k, :].astype(jnp.int32)
        return codes >> 7, codes & 127, ref[:, 3 + k, :]

    first0, second0, weight0 = unpacked(lists_prev, 0)
    first1, second1, weight1 = unpacked(lists, 1)
    first2, second2, weight2 = unpacked(lists, 2)
    to_prev = dot_rows(spread_weights(second0, weight0, BLOCK, BLOCK), spread(first0, rows, 0))
    upper = dot_rows(spread_weights(first1, weight1, BLOCK, 0), spread(second1, rows, 0))
    lower = dot_rows(spread_weights(first2, weight2, BLOCK, 0), spread(second2, rows, 0))
    half = lax.broadcasted_iota(jnp.int32, (BLOCK, rows), 1) >= BLOCK
    inside = jnp.where(half, pltpu.roll(lower, BLOCK, 1), 0.0)
    one_way = jnp.concatenate([upper, inside], axis=0)
    link_own = for_features(one_way + one_way.T)
    link_halo = for_features(jnp.concatenate([to_prev, jnp.where(half, lower, 0.0)], axis=0))
    inner = [dot_plain(link_own, own[c]) for c in range(3)]

    def adjoint(c):
        sums = inner[c] + dot_plain(link_halo, features((halo[2 * c], halo[2 * c + 1])))
        g1r, g1i, g2r, g2i = (sums[:, i * NF : (i + 1) * NF] for i in range(4))
        x, o = stations(c)
        xr, xi = x[:, :NF].astype(F32), x[:, NF:].astype(F32)
        dr, di = xr - o[:, :NF].astype(F32), xi - o[:, NF:].astype(F32)
        real = (xr * g1r - xi * g1i) + (dr * g2r - di * g2i)
        imag = (xr * g1i + xi * g1r) + (dr * g2i + di * g2r)
        return jnp.concatenate([real, imag], axis=0).astype(BF16)

    def handle(together):
        for c in together:

            @pl.when(has_after)
            def _():
                halos[c][0].wait_recv()

            @pl.when(has_before)
            def _():
                halos[c][1].wait_recv()

        placed = dot_plain(placement, jnp.concatenate([adjoint(c) for c in together], axis=1))
        for i, c in enumerate(together):
            outgoing[:, c] = (
                placed[:, i * NF : (i + 1) * NF].astype(BF16).reshape(devices, 4, NF)
            )

    handle((0, 1))

    pl.semaphore_wait(entered.at[1], 1 + jnp.where(z == 0, 4, 0))

    @pl.when(z < 2)
    def _():
        tell_row(0)

    handle((2,))

    def rest_entered(answers):
        pl.semaphore_wait(entered.at[2], 1 + answers)
        tell_row(1)

    @pl.when(z >= 2)
    def _():
        rest_entered(jnp.where(z == 2, 4, 0))

    def turns(at, size):
        return [at] + [around(at, step, size) for step in range(1, size)]

    core, chip = lax.rem(sub, 2), lax.div(me, 2)
    y_to, x_to = turns(y, 4), turns(lax.div(sub, 2), 4)
    core_to = [core, 1 - core]
    received[core, chip] = outgoing[me]

    def deliver(plane, step):
        dy, dx, other = step
        blk_to, sub_to = plane * 4 + y_to[dy], x_to[dx] * 2 + core_to[other]
        pltpu.make_async_remote_copy(
            src_ref=outgoing.at[blk_to * subs + sub_to],
            dst_ref=received.at[core, chip],
            send_sem=all_send,
            recv_sem=all_recv.at[other],
            device_id=(blk_to, sub_to),
            device_id_type=MESH,
        ).start()

    order = spread_order()

    def deliver_planes(planes, steps):
        for step in steps:
            for plane in planes:
                deliver(plane, step)
        for plane in planes:

            @pl.when(z != plane)
            def _():
                deliver(plane, (0, 0, 0))

    pl.semaphore_wait(joined.at[0], subs - 1)
    for step in order[:20]:
        deliver(0, step)

    @pl.when(z < 2)
    def _():
        rest_entered(8)

    some = pl.ds(0, 3)
    pltpu.make_async_copy(labels.at[0, some], labels.at[0, some], y_recv).wait()
    for step in range(1, 4):
        pltpu.make_async_remote_copy(
            src_ref=labels.at[z],
            dst_ref=labels.at[z],
            send_sem=z_send,
            recv_sem=z_recv,
            device_id=(around(z, step, 4) * 4 + y, sub),
            device_id_type=MESH,
        ).start()

    deliver_planes((0,), order[20:])
    deliver_planes((1,), order)
    pl.semaphore_wait(joined.at[1], subs - 1)
    deliver_planes((2, 3), order)

    arrived = lax.broadcasted_iota(jnp.int32, (2 * devices, 2 * devices), 1)
    held = lax.broadcasted_iota(jnp.int32, (2 * devices, 2 * devices), 0)
    sub_bits = subs.bit_length() - 1
    wanted = (
        ((arrived >> (sub_bits + 1)) << (sub_bits + 1))
        + (((arrived >> 1) & 1) << sub_bits)
        + (((arrived >> 2) & (subs // 2 - 1)) << 1)
    )
    owner_line = lax.broadcasted_iota(jnp.int32, (rows, 2 * devices), 0)
    repeat = [(held == wanted + of).astype(F32).astype(BF16) for of in (core, 1 - core)]
    pltpu.make_async_copy(labels.at[some], labels.at[some], z_recv).wait()
    by_owner = labels[...].reshape(2 * devices, NF)

    def collector(repeat):
        repeated = lax.dot_general(
            by_owner,
            repeat,
            (((0,), (0,)), ((), ())),
            preferred_element_type=F32,
        )
        label = jnp.sum(jnp.where(owner_line == me, repeated, 0.0), axis=0, keepdims=True)
        return jnp.concatenate(
            [
                ((label == owner_line.astype(F32)) & ((arrived[:rows] & 1) == i)).astype(F32)
                for i in range(2)
            ],
            axis=0,
        ).astype(BF16)

    collect_other, collect_same = collector(repeat[1]), collector(repeat[0])

    def sums(collect, source_core):
        values = [received[source_core, :, c].reshape(2 * devices, NF) for c in range(3)]
        return dot_plain(collect, jnp.concatenate(values, axis=1))

    pltpu.make_async_copy(received.at[0], received.at[0], all_recv.at[1]).wait()
    first_sums = sums(collect_other, 1 - core)
    most = pl.ds(0, devices // 2 - 1)
    pltpu.make_async_copy(received.at[0, most], received.at[0, most], all_recv.at[0]).wait()
    total = (first_sums + sums(collect_same, core)).astype(BF16)
    for c in range(3):
        summed[c * rows : (c + 1) * rows, :NF] = total[:rows, c * NF : (c + 1) * NF]
        summed[c * rows : (c + 1) * rows, NF:] = total[rows:, c * NF : (c + 1) * NF]

    for c in range(3):

        @pl.when(has_before)
        def _():
            halos[c][0].wait_send()

        @pl.when(has_after)
        def _():
            halos[c][1].wait_send()

    pltpu.make_async_copy(list_out.at[others], list_out.at[others], list_send).wait()

    @pl.when(row_after)
    def _():
        over.wait_send()

    pltpu.make_async_copy(labels.at[0, some], labels.at[0, some], y_send).wait()
    pltpu.make_async_copy(labels.at[some], labels.at[some], z_send).wait()
    most = pl.ds(0, devices - 1)
    pltpu.make_async_copy(outgoing.at[most], outgoing.at[most], all_send).wait()


def exchange(blks, subs, syn, obs, table, first, second, mask, weight, owner, element):
    devices = blks * subs
    samples, rows = syn.shape[2], syn.shape[1]
    in_hbm = pl.BlockSpec(memory_space=pltpu.HBM)
    dma = pltpu.SemaphoreType.DMA
    return pl.pallas_call(
        functools.partial(exchange_kernel, blks, subs),
        out_shape=pltpu.VMEM((3 * rows, 2 * NF), BF16),
        in_specs=[in_hbm] * 9,
        out_specs=pl.BlockSpec(memory_space=pltpu.VMEM),
        scratch_shapes=[
            pltpu.VMEM((3, 2 * rows, samples), BF16),
            pltpu.VMEM(table.shape, BF16),
            pltpu.VMEM(first.shape, jnp.int32),
            pltpu.VMEM(second.shape, jnp.int32),
            pltpu.VMEM(mask.shape, jnp.int32),
            pltpu.VMEM(weight.shape, F32),
            pltpu.VMEM(owner.shape, jnp.int32),
            pltpu.VMEM(element.shape, jnp.int32),
            pltpu.VMEM((6, rows, 2 * NF), BF16),
            pltpu.VMEM((6, 2 * BLOCK, 2 * NF), BF16),
            pltpu.VMEM((subs, 8, NF), F32),
            pltpu.VMEM((8, NF), F32),
            pltpu.VMEM((subs, 8, NF), F32),
            pltpu.VMEM((subs, 8, NF), F32),
            pltpu.VMEM((4, blks // 4, 2 * subs, NF), BF16),
            pltpu.VMEM((devices, 3, 4, NF), BF16),
            pltpu.VMEM((2, devices // 2, 3, 4, NF), BF16),
            dma((13,)),
            dma,
            dma,
            dma,
            dma,
            dma((2, 3)),
            dma((2, 3)),
            pltpu.SemaphoreType.REGULAR((3,)),
            pltpu.SemaphoreType.REGULAR((2,)),
            dma,
            dma,
            dma,
            dma,
            dma,
            dma((2,)),
        ],
        compiler_params=pltpu.CompilerParams(
            collective_id=0, has_side_effects=True, vmem_limit_bytes=60 * 2**20
        ),
        cost_estimate=pl.CostEstimate(
            flops=2 * 10**9, bytes_accessed=3 * 10**6, transcendentals=0
        ),
        name="exchange",
    )(syn, obs, table, first, second, mask, weight, owner, element)


def finish_kernel(summed, table, out, result, sems):
    samples = result.shape[1]
    chunk = samples // sems.shape[0]
    copies = []
    for n in range(sems.shape[0]):
        columns = pl.ds(n * chunk, chunk)
        result[:, columns] = dot_plain(summed[...], table[:, columns])
        copies.append(
            pltpu.make_async_copy(result.at[:, columns], out.at[:, columns], sems.at[n])
        )
        copies[-1].start()
    for copy in copies:
        copy.wait()


def finish(summed, table):
    count, samples = summed.shape[0], table.shape[1]
    in_vmem = pl.BlockSpec(memory_space=pltpu.VMEM)
    out = pl.pallas_call(
        finish_kernel,
        out_shape=jax.ShapeDtypeStruct((count, samples), F32),
        in_specs=[in_vmem] * 2,
        out_specs=pl.BlockSpec(memory_space=pl.ANY),
        scratch_shapes=[
            pltpu.VMEM((count, samples), F32),
            pltpu.SemaphoreType.DMA((4,)),
        ],
        compiler_params=pltpu.CompilerParams(vmem_limit_bytes=40 * 2**20),
        cost_estimate=pl.CostEstimate(
            flops=7 * 10**8, bytes_accessed=3 * 10**6, transcendentals=0
        ),
        name="finish",
    )(summed, table)
    return out.reshape(3, count // 3, samples)


def on_device(
    blks,
    subs,
    synthetic,
    observed,
    pair_first,
    pair_second,
    pair_mask,
    pair_weight,
    station_owner,
    station_element,
):
    rows, _, samples = synthetic.shape
    forward, inverse = dft_tables(samples, NF)
    summed = exchange(
        blks,
        subs,
        jnp.transpose(synthetic, (1, 0, 2)),
        jnp.transpose(observed, (1, 0, 2)),
        jnp.asarray(forward),
        pair_first,
        pair_second,
        pair_mask,
        pair_weight,
        station_owner.reshape(1, rows),
        station_element.reshape(1, rows),
    )
    out = finish(summed, jnp.asarray(inverse))
    return jnp.transpose(out, (1, 0, 2))


def solution(mesh):
    blks, subs = mesh.shape["blk"], mesh.shape["sub"]
    return jax.shard_map(
        functools.partial(on_device, blks, subs),
        mesh=mesh,
        in_specs=(
            P(("blk", "sub"), None, None),
            P(("blk", "sub"), None, None),
            P("blk", "sub"),
            P("blk", "sub"),
            P("blk", "sub"),
            P("blk", "sub"),
            P(("blk", "sub"), None),
            P(("blk", "sub")),
        ),
        out_specs=P(("blk", "sub"), None, None),
        check_vma=False,
    )
```

```python
import functools
import itertools
import math

import jax
import jax.numpy as jnp
import numpy as np
from jax import lax
from jax.experimental import pallas as pl
from jax.experimental.pallas import tpu as pltpu
from jax.sharding import PartitionSpec as P

MESH = pl.DeviceIdType.MESH
NF = 128
BLOCK = 64
F32 = jnp.float32
BF16 = jnp.bfloat16


def dft_tables(samples, freqs):
    phase = (np.arange(samples)[:, None] * np.arange(freqs)[None, :]) % samples
    angles = phase.astype(np.float64) * (2.0 * math.pi / samples)
    scale = 1.0 / math.sqrt(samples)
    cosine, sine = np.cos(angles) * scale, np.sin(angles) * scale
    forward = np.concatenate([cosine, -sine], axis=1).astype(np.float32)
    doubled = np.where(np.arange(freqs) == 0, 1.0, 2.0)[:, None]
    inverse = np.concatenate([cosine.T * doubled, -sine.T * doubled], axis=0)
    return forward.astype(jnp.bfloat16), inverse.astype(np.float32).astype(jnp.bfloat16)


def in_two(x):
    high = x.astype(BF16)
    return high, (x - high.astype(F32)).astype(BF16)


def dot_rows(a, b):
    return lax.dot_general(a, b, (((1,), (1,)), ((), ())), preferred_element_type=F32)


def dot_plain(a, b):
    return jnp.dot(a, b, preferred_element_type=F32)


def features(pair):
    xr, xi = pair[0][:, :NF].astype(F32), pair[0][:, NF:].astype(F32)
    o_r, o_i = pair[1][:, :NF].astype(F32), pair[1][:, NF:].astype(F32)
    dr, di = xr - o_r, xi - o_i
    parts = [dr * xr + di * xi, dr * xi - di * xr, o_r * xr + o_i * xi, o_r * xi - o_i * xr]
    both = [in_two(p) for p in parts]
    return jnp.concatenate(
        [jnp.concatenate([b[i] for b in both], axis=1) for i in range(2)], axis=0
    )


def for_features(links):
    return jnp.concatenate([links.astype(BF16)] * 2, axis=1)


def spread(rows, count, shift):
    index = lax.broadcasted_iota(jnp.int32, (count, NF), 0) + shift
    return jnp.concatenate(
        [(index == rows[s : s + 1]).astype(F32).astype(BF16) for s in range(rows.shape[0])], axis=1
    )


def spread_weights(rows, weights, count, shift):
    index = lax.broadcasted_iota(jnp.int32, (count, NF), 0) + shift
    return jnp.concatenate(
        [
            jnp.where(index == rows[s : s + 1], weights[s : s + 1], 0.0).astype(BF16)
            for s in range(rows.shape[0])
        ],
        axis=1,
    )


def spread_order():
    left = list(itertools.product(range(4), range(4), range(2)))[1:]
    ways = {0: (0.0, 0.0), 1: (1.0, 0.0), 2: (1.0, 1.0), 3: (0.0, 1.0)}

    def links(step):
        return np.array([way for axis in step[:2] for way in ways[axis]])

    used, order = np.zeros(4), []
    while left:
        step = min(left, key=lambda t: (np.max(used + links(t)), -np.sum(links(t)), t))
        left.remove(step)
        used = used + links(step)
        order.append(step)
    return order


def exchange_kernel(
    blks,
    subs,
    syn_hbm,
    obs_hbm,
    table_hbm,
    first_hbm,
    second_hbm,
    mask_hbm,
    weight_hbm,
    owner_hbm,
    element_hbm,
    summed,
    traces,
    table,
    first,
    second,
    mask,
    weight,
    owner,
    element,
    spec,
    halo,
    list_out,
    list_over,
    lists,
    lists_prev,
    labels,
    outgoing,
    received,
    load_sems,
    list_send,
    list_recv,
    over_send,
    over_recv,
    halo_send,
    halo_recv,
    entered,
    joined,
    y_send,
    y_recv,
    z_send,
    z_recv,
    all_send,
    all_recv,
):
    devices = blks * subs
    blk, sub = lax.axis_index("blk"), lax.axis_index("sub")
    me = blk * subs + sub
    rows = spec.shape[1]
    blocks = first.shape[0]
    def around(at, step, size):
        there = at + step
        return jnp.where(there >= size, there - size, there)

    subs_there = [around(sub, step, subs) for step in range(1, subs)]
    blks_there = [around(blk, step, blks) for step in range(1, blks)]
    blk_after, blk_before = blks_there[0], blks_there[-1]
    after = (jnp.where(sub == subs - 1, blk_after, blk), subs_there[0])
    before = (jnp.where(sub == 0, blk_before, blk), subs_there[-1])

    pairs = [
        (table_hbm, table),
        (syn_hbm.at[0], traces.at[0, pl.ds(0, rows)]),
        (obs_hbm.at[0], traces.at[0, pl.ds(rows, rows)]),
        (owner_hbm, owner),
        (element_hbm, element),
        (first_hbm, first),
        (second_hbm, second),
        (mask_hbm, mask),
        (weight_hbm, weight),
        (syn_hbm.at[1], traces.at[1, pl.ds(0, rows)]),
        (obs_hbm.at[1], traces.at[1, pl.ds(rows, rows)]),
        (syn_hbm.at[2], traces.at[2, pl.ds(0, rows)]),
        (obs_hbm.at[2], traces.at[2, pl.ds(rows, rows)]),
    ]
    loads = [
        pltpu.make_async_copy(src, dst, load_sems.at[i]) for i, (src, dst) in enumerate(pairs)
    ]
    for load in loads:
        load.start()

    z, y = lax.div(blk, 4), lax.rem(blk, 4)
    has_before, has_after = me > 0, me < devices - 1
    row_before, row_after = blk > 0, blk < blks - 1
    barrier = pltpu.get_barrier_semaphore()

    def greet(there):
        pl.semaphore_signal(barrier, inc=1, device_id=there, device_id_type=MESH)

    def greet_column(there, carry):
        greet((there, sub))
        return carry

    for there in subs_there:
        greet((blk, there))
    lax.fori_loop(blk + 1, blks, greet_column, 0)

    @pl.when((sub == 0) & row_before)
    def _():
        for s in range(subs):
            greet((blk_before, s))

    @pl.when((sub == subs - 1) & row_after)
    def _():
        greet((blk_after, 0))

    for i in range(3):
        pl.semaphore_signal(entered.at[i], inc=1)
    greetings = (
        (subs - 1)
        + jnp.where(row_after, 1, 0)
        + jnp.where((sub == 0) & row_before, 1, 0)
        + blk
    )

    def transform(c):
        both = dot_plain(traces[c], table[...]).astype(BF16)
        spec[2 * c] = both[:rows]
        spec[2 * c + 1] = both[rows:]

    for i in range(3):
        loads[i].wait()
    transform(0)

    pl.semaphore_wait(barrier, greetings)

    def halo_copies(c):
        q = pl.ds(2 * c, 2)
        return [
            pltpu.make_async_remote_copy(
                src_ref=spec.at[q, pl.ds(0, BLOCK)],
                dst_ref=halo.at[q, pl.ds(BLOCK, BLOCK)],
                send_sem=halo_send.at[0, c],
                recv_sem=halo_recv.at[0, c],
                device_id=before,
                device_id_type=MESH,
            ),
            pltpu.make_async_remote_copy(
                src_ref=spec.at[q, pl.ds(rows - BLOCK, BLOCK)],
                dst_ref=halo.at[q, pl.ds(0, BLOCK)],
                send_sem=halo_send.at[1, c],
                recv_sem=halo_recv.at[1, c],
                device_id=after,
                device_id_type=MESH,
            ),
        ]

    halos = [halo_copies(c) for c in range(3)]

    def start_halos(c):
        @pl.when(has_before)
        def _():
            halos[c][0].start()

        @pl.when(has_after)
        def _():
            halos[c][1].start()

    start_halos(0)

    def answer(there, carry):
        kind = jnp.where(lax.div(there, 4) == z, 0, jnp.where(z == 1, 1, 2))
        pl.semaphore_signal(
            entered.at[kind], inc=1, device_id=(there, sub), device_id_type=MESH
        )
        return carry

    @pl.when(z < 3)
    def _():
        lax.fori_loop(0, blk, answer, 0)


    for i in range(3, 5):
        loads[i].wait()
    lane = lax.broadcasted_iota(jnp.int32, (rows, rows), 1)
    line = lax.broadcasted_iota(jnp.int32, (rows, rows), 0)
    owner_row = owner[...]

    def column(row):
        return jnp.sum(jnp.where(lane == line, row, 0), axis=1, keepdims=True)

    owner_column, element_column = column(owner_row), column(element[...]).astype(F32)
    same = owner_column == owner_row
    rank_column = jnp.sum(jnp.where(same & (lane < line), 1, 0), axis=1, keepdims=True)
    label_rows = []
    for k in range(2):
        chosen = ((owner_column == lane) & (rank_column == k)).astype(F32)
        label_rows.append(
            jnp.sum(chosen * (element_column - rows), axis=0, keepdims=True) + float(rows)
        )

    for i in range(5, 9):
        loads[i].wait()
    base = (blk * blocks + lax.broadcasted_iota(jnp.int32, (blocks, NF), 0)) * BLOCK
    code = ((first[...] - base) * (2 * BLOCK) + (second[...] - base)).astype(F32)
    slot_weight = weight[...] * mask[...].astype(F32)
    zero_row = jnp.zeros((1, NF), F32)
    for s in range(subs):
        lines = [max(2 * s - 1, 0), 2 * s, 2 * s + 1]
        list_out[s] = jnp.concatenate(
            [code[i : i + 1] for i in lines]
            + [slot_weight[i : i + 1] for i in lines]
            + label_rows,
            axis=0,
        )
    list_over[...] = jnp.concatenate(
        [code[blocks - 1 : blocks]]
        + [zero_row] * 2
        + [slot_weight[blocks - 1 : blocks]]
        + [zero_row] * 4,
        axis=0,
    )
    lists[sub] = list_out[sub]

    for there in subs_there:
        pltpu.make_async_remote_copy(
            src_ref=list_out.at[there],
            dst_ref=lists.at[sub],
            send_sem=list_send,
            recv_sem=list_recv,
            device_id=(blk, there),
            device_id_type=MESH,
        ).start()
    over = pltpu.make_async_remote_copy(
        src_ref=list_over,
        dst_ref=lists_prev.at[sub],
        send_sem=over_send,
        recv_sem=over_recv,
        device_id=(blk_after, 0),
        device_id_type=MESH,
    )

    @pl.when(row_after)
    def _():
        over.start()


    for c in (1, 2):
        loads[7 + 2 * c].wait()
        loads[8 + 2 * c].wait()
        transform(c)
        start_halos(c)

    @pl.when(jnp.logical_not(has_before))
    def _():
        halo[:, :BLOCK] = jnp.zeros((6, BLOCK, 2 * NF), BF16)

    @pl.when(jnp.logical_not(has_after))
    def _():
        halo[:, BLOCK:] = jnp.zeros((6, BLOCK, 2 * NF), BF16)

    @pl.when(z == 3)
    def _():
        lax.fori_loop(0, blk, answer, 0)

    def tell_row(which):
        for there in subs_there:
            pl.semaphore_signal(
                joined.at[which], inc=1, device_id=(blk, there), device_id_type=MESH
            )

    @pl.when(z >= 2)
    def _():
        tell_row(0)

    rank_row = jnp.sum(jnp.where(same & (line < lane), 1, 0), axis=0, keepdims=True)
    target = owner_row * 4 + rank_row * 2
    slot = lax.broadcasted_iota(jnp.int32, (4 * devices, 2 * rows), 0)
    placement = (slot == jnp.concatenate([target, target + 1], axis=1)).astype(F32).astype(BF16)

    def stations(c):
        return (spec[2 * c], spec[2 * c + 1])

    own = [features(stations(c)) for c in range(3)]

    others = pl.ds(0, subs - 1)
    pltpu.make_async_copy(lists.at[others], lists.at[others], list_recv).wait()

    pl.semaphore_wait(entered.at[0], 4 - y)
    labels[z, y] = jnp.concatenate([lists[:, 6, :], lists[:, 7, :]], axis=0).astype(BF16)
    for step in range(1, 4):
        pltpu.make_async_remote_copy(
            src_ref=labels.at[z, y],
            dst_ref=labels.at[z, y],
            send_sem=y_send,
            recv_sem=y_recv,
            device_id=(z * 4 + around(y, step, 4), sub),
            device_id_type=MESH,
        ).start()

    @pl.when((sub == 0) & row_before)
    def _():
        pltpu.make_async_copy(lists_prev, lists_prev, over_recv).wait()

    @pl.when((sub == 0) & jnp.logical_not(row_before))
    def _():
        lists_prev[...] = jnp.zeros(lists_prev.shape, F32)

    @pl.when(sub != 0)
    def _():
        lists_prev[...] = lists[...]

    def unpacked(ref, k):
        codes = ref[:, k, :].astype(jnp.int32)
        return codes >> 7, codes & 127, ref[:, 3 + k, :]

    first0, second0, weight0 = unpacked(lists_prev, 0)
    first1, second1, weight1 = unpacked(lists, 1)
    first2, second2, weight2 = unpacked(lists, 2)
    to_prev = dot_rows(spread_weights(second0, weight0, BLOCK, BLOCK), spread(first0, rows, 0))
    upper = dot_rows(spread_weights(first1, weight1, BLOCK, 0), spread(second1, rows, 0))
    lower = dot_rows(spread_weights(first2, weight2, BLOCK, 0), spread(second2, rows, 0))
    half = lax.broadcasted_iota(jnp.int32, (BLOCK, rows), 1) >= BLOCK
    inside = jnp.where(half, pltpu.roll(lower, BLOCK, 1), 0.0)
    one_way = jnp.concatenate([upper, inside], axis=0)
    link_own = for_features(one_way + one_way.T)
    link_halo = for_features(jnp.concatenate([to_prev, jnp.where(half, lower, 0.0)], axis=0))
    inner = [dot_plain(link_own, own[c]) for c in range(3)]

    def adjoint(c):
        sums = inner[c] + dot_plain(link_halo, features((halo[2 * c], halo[2 * c + 1])))
        g1r, g1i, g2r, g2i = (sums[:, i * NF : (i + 1) * NF] for i in range(4))
        x, o = stations(c)
        xr, xi = x[:, :NF].astype(F32), x[:, NF:].astype(F32)
        dr, di = xr - o[:, :NF].astype(F32), xi - o[:, NF:].astype(F32)
        real = (xr * g1r - xi * g1i) + (dr * g2r - di * g2i)
        imag = (xr * g1i + xi * g1r) + (dr * g2i + di * g2r)
        return jnp.concatenate([real, imag], axis=0).astype(BF16)

    def handle(together):
        for c in together:

            @pl.when(has_after)
            def _():
                halos[c][0].wait_recv()

            @pl.when(has_before)
            def _():
                halos[c][1].wait_recv()

        placed = dot_plain(placement, jnp.concatenate([adjoint(c) for c in together], axis=1))
        for i, c in enumerate(together):
            outgoing[:, c] = (
                placed[:, i * NF : (i + 1) * NF].astype(BF16).reshape(devices, 4, NF)
            )

    handle((0, 1))

    pl.semaphore_wait(entered.at[1], 1 + jnp.where(z == 0, 4, 0))

    @pl.when(z < 2)
    def _():
        tell_row(0)

    handle((2,))

    def rest_entered(answers):
        pl.semaphore_wait(entered.at[2], 1 + answers)
        tell_row(1)

    @pl.when(z >= 2)
    def _():
        rest_entered(jnp.where(z == 2, 4, 0))

    def turns(at, size):
        return [at] + [around(at, step, size) for step in range(1, size)]

    core, chip = lax.rem(sub, 2), lax.div(me, 2)
    y_to, x_to = turns(y, 4), turns(lax.div(sub, 2), 4)
    core_to = [core, 1 - core]
    received[core, chip] = outgoing[me]

    def deliver(plane, step):
        dy, dx, other = step
        blk_to, sub_to = plane * 4 + y_to[dy], x_to[dx] * 2 + core_to[other]
        pltpu.make_async_remote_copy(
            src_ref=outgoing.at[blk_to * subs + sub_to],
            dst_ref=received.at[core, chip],
            send_sem=all_send,
            recv_sem=all_recv.at[other],
            device_id=(blk_to, sub_to),
            device_id_type=MESH,
        ).start()

    order = spread_order()

    def deliver_planes(planes, steps):
        for step in steps:
            for plane in planes:
                deliver(plane, step)
        for plane in planes:

            @pl.when(z != plane)
            def _():
                deliver(plane, (0, 0, 0))

    pl.semaphore_wait(joined.at[0], subs - 1)
    some = pl.ds(0, 3)

    def labels_along_z():
        pltpu.make_async_copy(labels.at[0, some], labels.at[0, some], y_recv).wait()
        for step in range(1, 4):
            pltpu.make_async_remote_copy(
                src_ref=labels.at[z],
                dst_ref=labels.at[z],
                send_sem=z_send,
                recv_sem=z_recv,
                device_id=(around(z, step, 4) * 4 + y, sub),
                device_id_type=MESH,
            ).start()

    for step in order[:14]:
        deliver(0, step)

    @pl.when(z >= 2)
    def _():
        labels_along_z()

    deliver_planes((0,), order[14:])

    @pl.when(z < 2)
    def _():
        rest_entered(8)
        labels_along_z()

    deliver_planes((1,), order)
    pl.semaphore_wait(joined.at[1], subs - 1)
    deliver_planes((2, 3), order)

    arrived = lax.broadcasted_iota(jnp.int32, (2 * devices, 2 * devices), 1)
    held = lax.broadcasted_iota(jnp.int32, (2 * devices, 2 * devices), 0)
    sub_bits = subs.bit_length() - 1
    wanted = (
        ((arrived >> (sub_bits + 1)) << (sub_bits + 1))
        + (((arrived >> 1) & 1) << sub_bits)
        + (((arrived >> 2) & (subs // 2 - 1)) << 1)
    )
    owner_line = lax.broadcasted_iota(jnp.int32, (rows, 2 * devices), 0)
    repeat = [(held == wanted + of).astype(F32).astype(BF16) for of in (core, 1 - core)]
    pltpu.make_async_copy(labels.at[some], labels.at[some], z_recv).wait()
    by_owner = labels[...].reshape(2 * devices, NF)

    def collector(repeat):
        repeated = lax.dot_general(
            by_owner,
            repeat,
            (((0,), (0,)), ((), ())),
            preferred_element_type=F32,
        )
        label = jnp.sum(jnp.where(owner_line == me, repeated, 0.0), axis=0, keepdims=True)
        return jnp.concatenate(
            [
                ((label == owner_line.astype(F32)) & ((arrived[:rows] & 1) == i)).astype(F32)
                for i in range(2)
            ],
            axis=0,
        ).astype(BF16)

    collect_other, collect_same = collector(repeat[1]), collector(repeat[0])

    def sums(collect, source_core):
        values = [received[source_core, :, c].reshape(2 * devices, NF) for c in range(3)]
        return dot_plain(collect, jnp.concatenate(values, axis=1))

    pltpu.make_async_copy(received.at[0], received.at[0], all_recv.at[1]).wait()
    first_sums = sums(collect_other, 1 - core)
    most = pl.ds(0, devices // 2 - 1)
    pltpu.make_async_copy(received.at[0, most], received.at[0, most], all_recv.at[0]).wait()
    total = (first_sums + sums(collect_same, core)).astype(BF16)
    for c in range(3):
        summed[c * rows : (c + 1) * rows, :NF] = total[:rows, c * NF : (c + 1) * NF]
        summed[c * rows : (c + 1) * rows, NF:] = total[rows:, c * NF : (c + 1) * NF]

    for c in range(3):

        @pl.when(has_before)
        def _():
            halos[c][0].wait_send()

        @pl.when(has_after)
        def _():
            halos[c][1].wait_send()

    pltpu.make_async_copy(list_out.at[others], list_out.at[others], list_send).wait()

    @pl.when(row_after)
    def _():
        over.wait_send()

    pltpu.make_async_copy(labels.at[0, some], labels.at[0, some], y_send).wait()
    pltpu.make_async_copy(labels.at[some], labels.at[some], z_send).wait()
    most = pl.ds(0, devices - 1)
    pltpu.make_async_copy(outgoing.at[most], outgoing.at[most], all_send).wait()


def exchange(blks, subs, syn, obs, table, first, second, mask, weight, owner, element):
    devices = blks * subs
    samples, rows = syn.shape[2], syn.shape[1]
    in_hbm = pl.BlockSpec(memory_space=pltpu.HBM)
    dma = pltpu.SemaphoreType.DMA
    return pl.pallas_call(
        functools.partial(exchange_kernel, blks, subs),
        out_shape=pltpu.VMEM((3 * rows, 2 * NF), BF16),
        in_specs=[in_hbm] * 9,
        out_specs=pl.BlockSpec(memory_space=pltpu.VMEM),
        scratch_shapes=[
            pltpu.VMEM((3, 2 * rows, samples), BF16),
            pltpu.VMEM(table.shape, BF16),
            pltpu.VMEM(first.shape, jnp.int32),
            pltpu.VMEM(second.shape, jnp.int32),
            pltpu.VMEM(mask.shape, jnp.int32),
            pltpu.VMEM(weight.shape, F32),
            pltpu.VMEM(owner.shape, jnp.int32),
            pltpu.VMEM(element.shape, jnp.int32),
            pltpu.VMEM((6, rows, 2 * NF), BF16),
            pltpu.VMEM((6, 2 * BLOCK, 2 * NF), BF16),
            pltpu.VMEM((subs, 8, NF), F32),
            pltpu.VMEM((8, NF), F32),
            pltpu.VMEM((subs, 8, NF), F32),
            pltpu.VMEM((subs, 8, NF), F32),
            pltpu.VMEM((4, blks // 4, 2 * subs, NF), BF16),
            pltpu.VMEM((devices, 3, 4, NF), BF16),
            pltpu.VMEM((2, devices // 2, 3, 4, NF), BF16),
            dma((13,)),
            dma,
            dma,
            dma,
            dma,
            dma((2, 3)),
            dma((2, 3)),
            pltpu.SemaphoreType.REGULAR((3,)),
            pltpu.SemaphoreType.REGULAR((2,)),
            dma,
            dma,
            dma,
            dma,
            dma,
            dma((2,)),
        ],
        compiler_params=pltpu.CompilerParams(
            collective_id=0, has_side_effects=True, vmem_limit_bytes=60 * 2**20
        ),
        cost_estimate=pl.CostEstimate(
            flops=2 * 10**9, bytes_accessed=3 * 10**6, transcendentals=0
        ),
        name="exchange",
    )(syn, obs, table, first, second, mask, weight, owner, element)


def finish_kernel(summed, table, out, result, sems):
    samples = result.shape[1]
    chunk = samples // sems.shape[0]
    copies = []
    for n in range(sems.shape[0]):
        columns = pl.ds(n * chunk, chunk)
        result[:, columns] = dot_plain(summed[...], table[:, columns])
        copies.append(
            pltpu.make_async_copy(result.at[:, columns], out.at[:, columns], sems.at[n])
        )
        copies[-1].start()
    for copy in copies:
        copy.wait()


def finish(summed, table):
    count, samples = summed.shape[0], table.shape[1]
    in_vmem = pl.BlockSpec(memory_space=pltpu.VMEM)
    out = pl.pallas_call(
        finish_kernel,
        out_shape=jax.ShapeDtypeStruct((count, samples), F32),
        in_specs=[in_vmem] * 2,
        out_specs=pl.BlockSpec(memory_space=pl.ANY),
        scratch_shapes=[
            pltpu.VMEM((count, samples), F32),
            pltpu.SemaphoreType.DMA((4,)),
        ],
        compiler_params=pltpu.CompilerParams(vmem_limit_bytes=40 * 2**20),
        cost_estimate=pl.CostEstimate(
            flops=7 * 10**8, bytes_accessed=3 * 10**6, transcendentals=0
        ),
        name="finish",
    )(summed, table)
    return out.reshape(3, count // 3, samples)


def on_device(
    blks,
    subs,
    synthetic,
    observed,
    pair_first,
    pair_second,
    pair_mask,
    pair_weight,
    station_owner,
    station_element,
):
    rows, _, samples = synthetic.shape
    forward, inverse = dft_tables(samples, NF)
    summed = exchange(
        blks,
        subs,
        jnp.transpose(synthetic, (1, 0, 2)),
        jnp.transpose(observed, (1, 0, 2)),
        jnp.asarray(forward),
        pair_first,
        pair_second,
        pair_mask,
        pair_weight,
        station_owner.reshape(1, rows),
        station_element.reshape(1, rows),
    )
    out = finish(summed, jnp.asarray(inverse))
    return jnp.transpose(out, (1, 0, 2))


def solution(mesh):
    blks, subs = mesh.shape["blk"], mesh.shape["sub"]
    return jax.shard_map(
        functools.partial(on_device, blks, subs),
        mesh=mesh,
        in_specs=(
            P(("blk", "sub"), None, None),
            P(("blk", "sub"), None, None),
            P("blk", "sub"),
            P("blk", "sub"),
            P("blk", "sub"),
            P("blk", "sub"),
            P(("blk", "sub"), None),
            P(("blk", "sub")),
        ),
        out_specs=P(("blk", "sub"), None, None),
        check_vma=False,
    )
```
